32 devices in a mesh: lat: 8 (over z, y), var: 4 (over x, core).
Axes of the slice: x: 2, y: 2, z: 4, core: 2. Of those that a mesh axis runs over, the one named last changes fastest.
Arguments:
- control: bfloat16 [4, 8, 64, 3072], P('var', 'lat'), may hold values from -6 to 6
- row_order: int32 [8], replicated, may hold values from 0 to 7, each once
- row_length: int32 [8], replicated, may hold values from 16 to 3072, as said below
- vertical: bfloat16 [4, 64, 64], P('var'), may hold values from -0.75 to 0.75
- amplitude: float32 [4, 768], P('var'), may hold values from 0.3 to 3
- meridional: bfloat16 [4, 8, 8], P('var'), may hold values from -16 to 16
- balance: bfloat16 [4, 64, 64], P('var'), may hold values from -0.75 to 0.75
Outputs:
- increment: bfloat16 [4, 8, 64, 3072], P('var', 'lat')
The draws below stay inside these ranges and needn't reach their ends.
Inputs may be any that keep to these rules, and one draw needn't show every extreme that they name: `row_length`: each a multiple of 4; the two middle latitude rows have exactly 3072 longitudes and the first and last rows 16.
All inputs are finite; a program needn't handle non-finite values.
Results may differ from the reference program's by a relative error of at most 0.0078.
Values may be sent and summed in bfloat16 or wider, within the bound.
No kernel may reach another device: no remote copies, remote signals or barrier semaphores. Data moves between devices by JAX's collectives and lax.ppermute only.
A program may use at most 64 MiB of HBM per device.

```python
import math
import jax
import jax.numpy as jnp
from jax import lax

NLON = 3072
LEV = 64
WAVES = 768
VARS = 4
NLAT = 8


def draw_row_length(key, part):
    latitude = jnp.arange(NLAT, dtype=jnp.int32)
    halfway = NLAT // 2
    distance = jnp.minimum(latitude, NLAT - 1 - latitude)
    base_len = 16 + (NLON - 16) * distance // max(halfway - 1, 1)
    base_len = base_len // 4 * 4
    jitter = 4 * jax.random.randint(key, (NLAT,), 0, 4)
    lengths = jnp.maximum(base_len - jitter, 16)
    return jnp.where(distance == halfway - 1, NLON, lengths).astype(jnp.int32)


def draw_meridional(key, part):
    noise_key = jax.random.fold_in(key, 11)
    position = jnp.arange(NLAT).astype(jnp.float32)
    spread = (position[:, None] - position[None, :]) / (NLAT / 3.0)
    envelope = jnp.exp(-spread * spread)
    noise = jnp.clip(jax.random.normal(noise_key, (VARS, NLAT, NLAT), jnp.float32), -3.0, 3.0)
    matrix = jnp.eye(NLAT, dtype=jnp.float32)[None] + noise * envelope[None] * (2.0 / math.sqrt(NLAT))
    return matrix.astype(jnp.bfloat16)


def block_scale(rng, dims, split, smallest, top_value):
    def one(dim, blocks):
        heights = jax.random.uniform(jax.random.fold_in(jax.random.fold_in(rng, 6), dim), (blocks,), jnp.float32, smallest / len(split), top_value / len(split))
        return jnp.repeat(jnp.exp(heights), dims[dim] // blocks).reshape((-1,) + (1,) * (len(dims) - dim - 1))

    gain = one(*split[0])
    for cut in split[1:]:
        gain = gain * one(*cut)
    return gain


def bell_draw(key, extent, deviation, bound, pieces=(), held_as=jnp.bfloat16):
    level = block_scale(key, extent, pieces, -0.22, 0.18) if pieces else 1.0
    entries = jax.random.normal(key, extent, jnp.float32) * deviation * level
    return jnp.minimum(jnp.maximum(entries, -bound), bound).astype(held_as)


def setup_inputs(seed: int = 0) -> dict:
    splits = jax.random.split(jax.random.key(seed), 8)
    return {
        "control": bell_draw(splits[0], (VARS, NLAT, LEV, NLON), 1.0, 6.0, ((0, 4), (1, 8))),
        "row_order": jax.random.permutation(splits[1], NLAT).astype(jnp.int32),
        "row_length": draw_row_length(jax.random.fold_in(splits[7], 71), 0),
        "vertical": bell_draw(splits[3], (VARS, LEV, LEV), LEV ** -0.5, 0.75, ((0, 4),)),
        "amplitude": jnp.clip(jnp.exp(math.log(3.0) - 2.3025851 * jax.random.uniform(splits[4], (VARS, WAVES), jnp.float32) ** block_scale(splits[4], (VARS, WAVES), ((0, 4),), -0.2, 0.2)), 0.3, 3.0),
        "meridional": draw_meridional(jax.random.fold_in(splits[7], 71), 0),
        "balance": bell_draw(splits[6], (VARS, LEV, LEV), LEV ** -0.5, 0.75, ((0, 4),)),
    }


def zonal_basis(lengths, offset, width, waves):
    columns = offset + jnp.arange(width, dtype=jnp.int32)
    wavenum = jnp.arange(waves, dtype=jnp.int32)
    period = lengths.astype(jnp.int32)[:, None, None]
    phases = (columns[None, :, None] * wavenum[None, None, :]) % period
    angles = (2.0 * math.pi) * phases.astype(jnp.float32) / period.astype(jnp.float32)
    inside = (columns[None, :, None] < period) & (wavenum[None, None, :] <= (period - 1) // 2)
    cosine = jnp.where(inside, jnp.cos(angles), 0.0)
    sines = jnp.where(inside, jnp.sin(angles), 0.0)
    return jnp.concatenate([cosine, sines], axis=2)


def wave_scaling(lengths, waves):
    wavenum = jnp.arange(waves, dtype=jnp.int32)
    factor = jnp.where(wavenum == 0, 1.0, 2.0).astype(jnp.float32)
    factor = jnp.concatenate([factor, factor])
    return factor[None, :] / lengths.astype(jnp.float32)[:, None]


def reference(control, row_order, row_length, vertical, amplitude, meridional, balance):
    lat_total = control.shape[1]
    lon_count = control.shape[3]
    waves = amplitude.shape[1]
    slot_len = row_length[row_order]
    amp_both = jnp.concatenate([amplitude, amplitude], axis=1)
    vert_float = vertical.astype(jnp.float32)

    def analyse(inputs_row):
        fields, length = inputs_row
        lengths = length[None]
        basis_tab = zonal_basis(lengths, 0, lon_count, waves)
        analysis_tab = (basis_tab * wave_scaling(lengths, waves)[:, None, :]).astype(jnp.bfloat16)[0]
        levels = jnp.einsum('vml,vlj->vmj', vert_float, fields.astype(jnp.float32)).astype(jnp.bfloat16)
        summed = jnp.einsum('vmj,jc->vmc', levels.astype(jnp.float32), analysis_tab.astype(jnp.float32))
        return (summed * amp_both[:, None, :]).astype(jnp.bfloat16)

    coeffs = lax.map(analyse, (jnp.moveaxis(control, 1, 0), slot_len))
    blended = []
    for var_idx in range(VARS):
        slot_mat = meridional[var_idx][row_order][:, row_order].astype(jnp.float32)
        flattened = coeffs[:, var_idx].reshape(lat_total, -1).astype(jnp.float32)
        product = jnp.dot(slot_mat, flattened, preferred_element_type=jnp.float32).astype(jnp.bfloat16)
        blended.append(product.reshape(lat_total, coeffs.shape[2], coeffs.shape[3]))
    balanced = [blended[0]]
    for var_idx in range(1, VARS):
        lifted = jnp.einsum('ml,plc->pmc', balance[var_idx].astype(jnp.float32), blended[0].astype(jnp.float32))
        balanced.append((blended[var_idx].astype(jnp.float32) + lifted).astype(jnp.bfloat16))
    stacked = jnp.stack(balanced, axis=1)

    def synthesise(inputs_row):
        spectra, length = inputs_row
        basis_tab = zonal_basis(length[None], 0, lon_count, waves)[0].astype(jnp.bfloat16)
        return jnp.einsum('vmc,jc->vmj', spectra.astype(jnp.float32), basis_tab.astype(jnp.float32)).astype(jnp.bfloat16)

    output = lax.map(synthesise, (stacked, slot_len))
    return jnp.moveaxis(output, 0, 1)
```

```python
import functools

import jax
import jax.numpy as jnp
from jax import lax
from jax.experimental import pallas as pl
from jax.experimental.pallas import tpu as pltpu
from jax.sharding import PartitionSpec as P

RADIX = 4
LANES = 128
SUBLANES = 8
STRIP = 16
F32 = jnp.float32
BF16 = jnp.bfloat16

COS_POLY = (1, -19.7392044, 64.9391174, -85.4501419, 60.1676292, -25.9675999, 6.52865839)
SIN_POLY = (6.28318501, -41.3415909, 81.5999451, -76.6144714, 41.3428841, -12.4712439)

VMEM = pl.BlockSpec(memory_space=pltpu.VMEM)
SMEM = pl.BlockSpec(memory_space=pltpu.SMEM)
PARAMS = pltpu.CompilerParams(vmem_limit_bytes=48 * 1024 * 1024)


def iota(shape, dim):
    return lax.broadcasted_iota(jnp.int32, shape, dim)


def horner(poly, x):
    total = jnp.full_like(x, poly[-1])
    for term in poly[-2::-1]:
        total = total * x + term
    return total


def cos_sin(turns):
    turns = turns - jnp.round(turns)
    square = turns * turns
    return horner(COS_POLY, square), horner(SIN_POLY, square) * turns


def ceil_div(a, b):
    return -(-a // b)


def round_up(a, b):
    return ceil_div(a, b) * b


def dot(a, b, contract=((1,), (0,))):
    return lax.dot_general(a, b, (contract, ((), ())), preferred_element_type=F32)


class Sizes:
    def __init__(self, lat_total, var_total, levels, lons, waves):
        self.lat, self.var, self.levels, self.lons, self.waves = lat_total, var_total, levels, lons, waves
        self.devices = lat_total * var_total
        self.points = lons // RADIX
        self.kaps = waves // RADIX
        self.rows = round_up(ceil_div(waves, self.devices), SUBLANES)
        assert self.kaps % self.rows == 0 and 2 * levels == LANES and lat_total <= LANES
        self.bal_rows = ceil_div(levels, lat_total)
        if lat_total <= LANES - levels:
            self.mer_row, self.mer_lane = 0, levels
        else:
            self.mer_row, self.mer_lane = self.bal_rows, 0
        self.par_rows = round_up(max(self.bal_rows, self.mer_row + 1), SUBLANES)
        self.packet = round_up(self.rows + self.par_rows, STRIP)


def own_length(order_ref, length_ref):
    slot = lax.axis_index("lat")
    row = order_ref[slot]
    return slot, row, length_ref[row]


def analysis_kernel(
    z, order_ref, length_ref, control_ref, vert_ref, amp_ref, mer_ref, bal_ref, packet_ref, basis_ref, twiddle_ref,
    field_ref, parts_ref,
):
    slot, row, length = own_length(order_ref, length_ref)
    quarter = length // RADIX
    field_ref[:, z.lons :] = jnp.zeros((z.levels, LANES), F32)
    field_ref[:, : z.lons] = dot(vert_ref[0], control_ref[0, 0])
    points = iota((1, z.points), 1)
    inside = points < quarter
    step = points.astype(F32) / jnp.full((1, z.points), quarter, jnp.int32).astype(F32)
    for at in range(0, z.kaps, STRIP):
        kap = (at + iota((STRIP, z.points), 0)).astype(F32)
        cosine, sine = cos_sin(kap * step)
        basis_ref[at : at + STRIP, :] = jnp.where(inside, cosine, 0.0).astype(BF16)
        basis_ref[z.kaps + at : z.kaps + at + STRIP, :] = jnp.where(inside, sine, 0.0).astype(BF16)
    tw_row = iota((2 * RADIX, z.points), 0)
    period = jnp.full((1, z.points), length, jnp.int32).astype(F32)
    tw_cos, tw_sin = cos_sin((tw_row % RADIX).astype(F32) * (points.astype(F32) / period))
    twiddle_ref[...] = jnp.where(tw_row < RADIX, tw_cos, tw_sin)
    starts = [quarter * j1 for j1 in range(1, RADIX)]
    bases = [pl.multiple_of(s // LANES * LANES, LANES) for s in starts]
    shifts = [(LANES - (s - b)) % LANES for s, b in zip(starts, bases)]
    lane = iota((STRIP, LANES), 1)
    for at in range(0, z.levels, STRIP):
        rows = slice(at, at + STRIP)

        def quarter_of(base, shift):
            wide = field_ref[rows, pl.ds(base, z.points + LANES)]
            tiles = [
                pltpu.roll(wide[:, c : c + LANES], shift, 1) for c in range(0, z.points + LANES, LANES)
            ]
            keep = (lane < shift) | (shift == 0)
            return jnp.concatenate([jnp.where(keep, a, b) for a, b in zip(tiles, tiles[1:])], axis=1)

        first = field_ref[rows, : z.points]
        second, third, fourth = [quarter_of(b, s) for b, s in zip(bases, shifts)]
        even, odd = first + third, second + fourth
        real, imag = first - third, second - fourth
        cos1, cos2, cos3 = [twiddle_ref[r : r + 1, :] for r in (1, 2, 3)]
        sin1, sin2, sin3 = [twiddle_ref[RADIX + r : RADIX + r + 1, :] for r in (1, 2, 3)]
        turned = even - odd
        parts = (
            (even + odd, None),
            (real * cos1 - imag * sin1, real * sin1 + imag * cos1),
            (turned * cos2, turned * sin2),
            (real * cos3 + imag * sin3, real * sin3 - imag * cos3),
        )
        for r, pair in enumerate(parts):
            for half, part in enumerate(pair):
                part = jnp.zeros((STRIP, z.points), F32) if part is None else part
                to = (2 * r + half) * z.levels + at
                parts_ref[to : to + STRIP, :] = part.astype(BF16)
    bal_at = slot * z.bal_rows + iota((z.par_rows, z.levels), 0)
    bal_pick = (iota((z.par_rows, z.levels), 1) == bal_at) & (iota((z.par_rows, z.levels), 0) < z.bal_rows)
    bal_part = dot(bal_pick.astype(F32).astype(BF16), bal_ref[0])
    params = jnp.concatenate([bal_part, jnp.zeros((z.par_rows, LANES - z.levels), F32)], axis=1)
    mer_pick = (iota((z.par_rows, z.lat), 1) == row) & (iota((z.par_rows, z.lat), 0) == z.mer_row)
    mer_part = dot(mer_pick.astype(F32).astype(BF16), mer_ref[0])
    mer_place = iota((z.lat, LANES), 1) == iota((z.lat, LANES), 0) + z.mer_lane
    params = params + dot(mer_part.astype(BF16), mer_place.astype(F32).astype(BF16))
    if z.packet > z.rows + z.par_rows:
        params = jnp.concatenate([params, jnp.zeros((z.packet - z.rows - z.par_rows, LANES), F32)], axis=0)
    product = dot(basis_ref[...], parts_ref[...], ((1,), (1,)))
    count = z.kaps // z.rows
    sign = jnp.where(iota((1, LANES), 1) < z.levels, -1.0, 1.0).astype(F32)
    group = LANES // RADIX
    for r in range(RADIX):
        from_cos = product[: z.kaps, r * LANES : (r + 1) * LANES]
        from_sin = product[z.kaps :, r * LANES : (r + 1) * LANES]
        both = from_cos + pltpu.roll(from_sin, z.levels, 1) * sign
        picked = iota((group, LANES), 1) == iota((group, LANES), 0) * RADIX + r
        amp = jnp.concatenate(
            [
                jnp.sum(jnp.where(picked, amp_ref[:, c : c + LANES], 0.0), axis=1, keepdims=True)
                for c in range(0, z.waves, LANES)
            ],
            axis=0,
        )
        wave = iota((z.kaps, 1), 0) * RADIX + r
        weight = jnp.where(wave == 0, 1.0, 2.0) / jnp.full((z.kaps, 1), length, jnp.int32).astype(F32)
        weight = jnp.where(wave <= (length - 1) // 2, weight, 0.0)
        both = (both * (weight * amp)).reshape(count, z.rows, LANES)
        for i in range(count):
            packet_ref[r * count + i] = jnp.concatenate([both[i], params], axis=0).astype(BF16)
    for i in range(RADIX * count, z.devices):
        packet_ref[i] = jnp.concatenate([jnp.zeros((z.rows, LANES), F32), params], axis=0).astype(BF16)


def mixing_kernel(z, order_ref, packet_ref, out_ref):
    size = z.lat * z.rows
    col_slot = iota((1, size), 1) // z.rows
    col_row = jnp.zeros((1, size), jnp.int32)
    for t in range(z.lat):
        col_row = jnp.where(col_slot == t, order_ref[t], col_row)
    to_cols = (iota((LANES, size), 0) == col_row + z.mer_lane).astype(F32).astype(BF16)
    par = z.lat * z.par_rows
    from_par = iota((size, par), 0) // z.rows * z.par_rows + z.mer_row == iota((size, par), 1)
    from_par = from_par.astype(F32).astype(BF16)
    same = iota((size, size), 0) % z.rows == iota((size, size), 1) % z.rows
    halves = iota((LANES, LANES), 0) // z.levels == iota((LANES, LANES), 1) // z.levels
    streams = None
    for v in range(z.var):
        whole = packet_ref[:, v].astype(F32)
        coeffs = whole[:, : z.rows].reshape(size, LANES).astype(BF16)
        params = whole[:, z.rows : z.rows + z.par_rows].reshape(par, LANES).astype(BF16)
        slot_rows = dot(params, to_cols).astype(BF16)
        mix = jnp.where(same, dot(from_par, slot_rows), 0.0).astype(BF16)
        blended = dot(mix, coeffs)
        if v == 0:
            stream = blended.astype(BF16)
        else:
            if z.bal_rows == z.par_rows and z.lat * z.bal_rows == z.levels:
                balance = params.astype(F32)
            else:
                level = iota((z.levels, par), 0)
                pick = iota((z.levels, par), 1) == level // z.bal_rows * z.par_rows + level % z.bal_rows
                balance = dot(pick.astype(F32).astype(BF16), params)
            balance = balance[:, : z.levels]
            balance = jnp.concatenate([balance, balance], axis=1)
            balance = jnp.where(halves, jnp.concatenate([balance, balance], axis=0), 0.0).astype(BF16)
            blended = blended + dot(stream, balance, ((1,), (1,)))
        blended = blended.reshape(z.lat, z.rows, LANES)
        for s in range(z.lat):
            out_ref[s, v] = blended[s].astype(BF16)


def synthesis_kernel(z, order_ref, length_ref, spectra_ref, basis_ref, twiddle_ref, out_ref, field_ref, parts_ref):
    _, _, length = own_length(order_ref, length_ref)
    quarter = length // RADIX
    used = z.waves // z.rows
    spectra = spectra_ref[:used].astype(F32).reshape(z.waves, LANES)
    at = iota((z.waves, 1), 0)
    wave = at % z.kaps * RADIX + at // z.kaps
    spectra = jnp.where(wave <= (length - 1) // 2, spectra, 0.0)
    cosine, sine = basis_ref[: z.kaps], basis_ref[z.kaps :]
    for r in range(RADIX):
        turned = spectra[r * z.kaps : (r + 1) * z.kaps].T.astype(BF16)
        parts_ref[2 * r] = dot(turned, cosine)
        parts_ref[2 * r + 1] = dot(turned, sine)
    starts = [quarter * j1 for j1 in range(1, RADIX)]
    bases = [pl.multiple_of(s // LANES * LANES, LANES) for s in starts]
    shifts = [s - b for s, b in zip(starts, bases)]
    field_ref[:, z.points :] = jnp.zeros((z.levels, z.lons + LANES - z.points), F32)
    lane = iota((STRIP, LANES), 1)
    for at in range(0, z.levels, STRIP):
        rows = slice(at, at + STRIP)
        below = slice(z.levels + at, z.levels + at + STRIP)
        cos1, cos2, cos3 = [twiddle_ref[r : r + 1, :] for r in (1, 2, 3)]
        sin1, sin2, sin3 = [twiddle_ref[RADIX + r : RADIX + r + 1, :] for r in (1, 2, 3)]

        def real(r):
            return parts_ref[2 * r, rows] + parts_ref[2 * r + 1, below]

        def imag(r):
            return parts_ref[2 * r + 1, rows] - parts_ref[2 * r, below]

        w0 = real(0)
        w2 = real(2) * cos2 - imag(2) * sin2
        re1, im1, re3, im3 = real(1), imag(1), real(3), imag(3)
        cross = (re1 * cos1 - im1 * sin1) + (re3 * cos3 - im3 * sin3)
        turn = (re1 * sin1 + im1 * cos1) - (re3 * sin3 + im3 * cos3)
        even, odd = w0 + w2, w0 - w2
        field_ref[rows, : z.points] = even + cross
        for base, shift, part in zip(bases, shifts, (odd - turn, even - cross, odd + turn)):
            tiles = [pltpu.roll(part[:, c : c + LANES], shift, 1) for c in range(0, z.points, LANES)]
            zero = jnp.zeros((STRIP, LANES), F32)
            moved = [jnp.where(lane < shift, a, b) for a, b in zip([zero] + tiles, tiles + [zero])]
            to = pl.ds(base, z.points + LANES)
            field_ref[rows, to] = field_ref[rows, to] + jnp.concatenate(moved, axis=1)
        out_ref[0, 0, rows, :] = field_ref[rows, : z.lons].astype(BF16)


def body(z, control, row_order, row_length, vertical, amplitude, meridional, balance):
    packets, basis, twiddle = pl.pallas_call(
        functools.partial(analysis_kernel, z),
        out_shape=(
            jax.ShapeDtypeStruct((z.devices, z.packet, LANES), BF16),
            jax.ShapeDtypeStruct((2 * z.kaps, z.points), BF16),
            jax.ShapeDtypeStruct((2 * RADIX, z.points), F32),
        ),
        in_specs=[SMEM, SMEM] + [VMEM] * 5,
        out_specs=(VMEM, VMEM, VMEM),
        scratch_shapes=[
            pltpu.VMEM((z.levels, z.lons + LANES), F32),
            pltpu.VMEM((2 * RADIX * z.levels, z.points), BF16),
        ],
        compiler_params=PARAMS,
        name="analysis",
    )(row_order, row_length, control, vertical, amplitude, meridional, balance)
    packets = lax.all_to_all(packets, ("lat", "var"), 0, 0, tiled=True)
    balanced = pl.pallas_call(
        functools.partial(mixing_kernel, z),
        out_shape=jax.ShapeDtypeStruct((z.lat, z.var, z.rows, LANES), BF16),
        in_specs=[SMEM, VMEM],
        out_specs=VMEM,
        compiler_params=PARAMS,
        name="mixing",
    )(row_order, packets.reshape(z.lat, z.var, z.packet, LANES))
    balanced = balanced.reshape(z.devices, z.rows, LANES)
    balanced = lax.all_to_all(balanced, ("lat", "var"), 0, 0, tiled=True)
    return pl.pallas_call(
        functools.partial(synthesis_kernel, z),
        out_shape=jax.ShapeDtypeStruct(control.shape, BF16),
        in_specs=[SMEM, SMEM] + [VMEM] * 3,
        out_specs=VMEM,
        scratch_shapes=[
            pltpu.VMEM((z.levels, z.lons + LANES), F32),
            pltpu.VMEM((2 * RADIX, 2 * z.levels, z.points), F32),
        ],
        compiler_params=PARAMS,
        name="synthesis",
    )(row_order, row_length, balanced, basis, twiddle)


def solution(mesh):
    placed = (
        P("var", "lat", None, None),
        P(),
        P(),
        P("var", None, None),
        P("var", None),
        P("var", None, None),
        P("var", None, None),
    )

    def run(control, row_order, row_length, vertical, amplitude, meridional, balance):
        lat_total, var_total = mesh.shape["lat"], mesh.shape["var"]
        assert control.shape[0] == var_total and control.shape[1] == lat_total
        z = Sizes(lat_total, var_total, control.shape[2], control.shape[3], amplitude.shape[1])
        return jax.shard_map(
            functools.partial(body, z),
            mesh=mesh,
            in_specs=placed,
            out_specs=P("var", "lat", None, None),
            check_vma=False,
        )(control, row_order, row_length, vertical, amplitude, meridional, balance)

    return run
```

```python
import functools

import jax
import jax.numpy as jnp
from jax import lax
from jax.experimental import pallas as pl
from jax.experimental.pallas import tpu as pltpu
from jax.sharding import PartitionSpec as P

RADIX = 4
LANES = 128
SUBLANES = 8
STRIP = 16
F32 = jnp.float32
BF16 = jnp.bfloat16

COS_POLY = (1, -19.7392044, 64.9391174, -85.4501419, 60.1676292, -25.9675999, 6.52865839)
SIN_POLY = (6.28318501, -41.3415909, 81.5999451, -76.6144714, 41.3428841, -12.4712439)

VMEM = pl.BlockSpec(memory_space=pltpu.VMEM)
HBM = pl.BlockSpec(memory_space=pltpu.HBM)
PARAMS = pltpu.CompilerParams(vmem_limit_bytes=32 * 1024 * 1024)
ALL_VMEM = pltpu.CompilerParams(vmem_limit_bytes=58 * 1024 * 1024)


def iota(shape, dim):
    return lax.broadcasted_iota(jnp.int32, shape, dim)


def horner(poly, x):
    total = jnp.full_like(x, poly[-1])
    for term in poly[-2::-1]:
        total = total * x + term
    return total


def cos_sin(turns):
    turns = turns - jnp.round(turns)
    square = turns * turns
    return horner(COS_POLY, square), horner(SIN_POLY, square) * turns


def ceil_div(a, b):
    return -(-a // b)


def round_up(a, b):
    return ceil_div(a, b) * b


def dot(a, b, contract=((1,), (0,))):
    return lax.dot_general(a, b, (contract, ((), ())), preferred_element_type=F32)


class Sizes:
    def __init__(self, lat_total, var_total, levels, lons, waves):
        self.lat, self.var, self.levels, self.lons, self.waves = lat_total, var_total, levels, lons, waves
        self.devices = lat_total * var_total
        self.points = lons // RADIX
        self.kaps = waves // RADIX
        self.rows = round_up(ceil_div(waves, self.devices), SUBLANES)
        assert self.kaps % self.rows == 0 and 2 * levels == LANES and lat_total <= LANES
        self.bal_rows = ceil_div(levels, lat_total)
        if lat_total <= LANES - levels:
            self.mer_row, self.mer_lane = 0, levels
        else:
            self.mer_row, self.mer_lane = self.bal_rows, 0
        self.par_rows = round_up(max(self.bal_rows, self.mer_row + 1), SUBLANES)
        self.packet = round_up(self.rows + self.par_rows, STRIP)


def own_length(order_ref, length_ref):
    slot = lax.axis_index("lat")
    row = order_ref[slot]
    return slot, row, length_ref[row]


def fetch(sources, targets, sems):
    copies = [pltpu.make_async_copy(s, t, sems.at[i]) for i, (s, t) in enumerate(zip(sources, targets))]
    for copy in copies:
        copy.start()
    return copies


def analysis_kernel(
    z, order_in, length_in, control_in, vert_in, amp_in, mer_in, bal_in,
    packet_out, basis_out, twiddle_out, period_out, pick_out,
    order_ref, length_ref, control_ref, vert_ref, amp_ref, mer_ref, bal_ref, sems, field_ref, parts_ref,
    packet_ref, basis_ref, twiddle_ref, period_ref, pick_ref, out_sems,
):
    copies = fetch(
        (order_in, length_in, control_in, vert_in, amp_in, mer_in, bal_in),
        (order_ref, length_ref, control_ref, vert_ref, amp_ref, mer_ref, bal_ref),
        sems,
    )
    field_ref[:, z.lons :] = jnp.zeros((z.levels, LANES), F32)
    for copy in copies[:2]:
        copy.wait()
    slot, row, length = own_length(order_ref, length_ref)
    quarter = length // RADIX
    period_ref[...] = jnp.full(period_ref.shape, length, jnp.int32)
    size = z.lat * z.rows
    col_slot = iota((1, size), 1) // z.rows
    col_row = jnp.zeros((1, size), jnp.int32)
    for t in range(z.lat):
        col_row = jnp.where(col_slot == t, order_ref[t], col_row)
    pick_ref[...] = (iota((LANES, size), 0) == col_row + z.mer_lane).astype(F32).astype(BF16)
    points = iota((1, z.points), 1)
    inside = points < quarter
    step = points.astype(F32) / jnp.full((1, z.points), quarter, jnp.int32).astype(F32)
    for at in range(0, z.kaps, STRIP):
        if at == z.kaps // 2 // STRIP * STRIP:
            for copy in copies[2:]:
                copy.wait()
            field_ref[:, : z.lons] = dot(vert_ref[0], control_ref[0, 0])
        kap = (at + iota((STRIP, z.points), 0)).astype(F32)
        cosine, sine = cos_sin(kap * step)
        basis_ref[at : at + STRIP, :] = jnp.where(inside, cosine, 0.0).astype(BF16)
        basis_ref[z.kaps + at : z.kaps + at + STRIP, :] = jnp.where(inside, sine, 0.0).astype(BF16)
    tw_row = iota((2 * RADIX, z.points), 0)
    period = jnp.full((1, z.points), length, jnp.int32).astype(F32)
    tw_cos, tw_sin = cos_sin((tw_row % RADIX).astype(F32) * (points.astype(F32) / period))
    twiddle_ref[...] = jnp.where(tw_row < RADIX, tw_cos, tw_sin)
    sent = fetch(
        (basis_ref, twiddle_ref, period_ref, pick_ref),
        (basis_out, twiddle_out, period_out, pick_out),
        out_sems.at[pl.ds(RADIX + 1, 4)],
    )
    starts = [quarter * j1 for j1 in range(1, RADIX)]
    bases = [pl.multiple_of(s // LANES * LANES, LANES) for s in starts]
    shifts = [(LANES - (s - b)) % LANES for s, b in zip(starts, bases)]
    lane = iota((STRIP, LANES), 1)
    for at in range(0, z.levels, STRIP):
        rows = slice(at, at + STRIP)

        def quarter_of(base, shift):
            wide = field_ref[rows, pl.ds(base, z.points + LANES)]
            tiles = [
                pltpu.roll(wide[:, c : c + LANES], shift, 1) for c in range(0, z.points + LANES, LANES)
            ]
            keep = (lane < shift) | (shift == 0)
            return jnp.concatenate([jnp.where(keep, a, b) for a, b in zip(tiles, tiles[1:])], axis=1)

        first = field_ref[rows, : z.points]
        second, third, fourth = [quarter_of(b, s) for b, s in zip(bases, shifts)]
        even, odd = first + third, second + fourth
        real, imag = first - third, second - fourth
        cos1, cos2, cos3 = [twiddle_ref[r : r + 1, :] for r in (1, 2, 3)]
        sin1, sin2, sin3 = [twiddle_ref[RADIX + r : RADIX + r + 1, :] for r in (1, 2, 3)]
        turned = even - odd
        parts = (
            (even + odd, None),
            (real * cos1 - imag * sin1, real * sin1 + imag * cos1),
            (turned * cos2, turned * sin2),
            (real * cos3 + imag * sin3, real * sin3 - imag * cos3),
        )
        for r, pair in enumerate(parts):
            for half, part in enumerate(pair):
                part = jnp.zeros((STRIP, z.points), F32) if part is None else part
                to = (2 * r + half) * z.levels + at
                parts_ref[to : to + STRIP, :] = part.astype(BF16)
    bal_at = slot * z.bal_rows + iota((z.par_rows, z.levels), 0)
    bal_pick = (iota((z.par_rows, z.levels), 1) == bal_at) & (iota((z.par_rows, z.levels), 0) < z.bal_rows)
    bal_part = dot(bal_pick.astype(F32).astype(BF16), bal_ref[0])
    params = jnp.concatenate([bal_part, jnp.zeros((z.par_rows, LANES - z.levels), F32)], axis=1)
    mer_pick = (iota((z.par_rows, z.lat), 1) == row) & (iota((z.par_rows, z.lat), 0) == z.mer_row)
    mer_part = dot(mer_pick.astype(F32).astype(BF16), mer_ref[0])
    mer_place = iota((z.lat, LANES), 1) == iota((z.lat, LANES), 0) + z.mer_lane
    params = params + dot(mer_part.astype(BF16), mer_place.astype(F32).astype(BF16))
    if z.packet > z.rows + z.par_rows:
        params = jnp.concatenate([params, jnp.zeros((z.packet - z.rows - z.par_rows, LANES), F32)], axis=0)
    product = dot(basis_ref[...], parts_ref[...], ((1,), (1,)))
    count = z.kaps // z.rows
    sign = jnp.where(iota((1, LANES), 1) < z.levels, -1.0, 1.0).astype(F32)
    group = LANES // RADIX
    for r in range(RADIX):
        from_cos = product[: z.kaps, r * LANES : (r + 1) * LANES]
        from_sin = product[z.kaps :, r * LANES : (r + 1) * LANES]
        both = from_cos + pltpu.roll(from_sin, z.levels, 1) * sign
        picked = iota((group, LANES), 1) == iota((group, LANES), 0) * RADIX + r
        amp = jnp.concatenate(
            [
                jnp.sum(jnp.where(picked, amp_ref[:, c : c + LANES], 0.0), axis=1, keepdims=True)
                for c in range(0, z.waves, LANES)
            ],
            axis=0,
        )
        wave = iota((z.kaps, 1), 0) * RADIX + r
        weight = jnp.where(wave == 0, 1.0, 2.0) / jnp.full((z.kaps, 1), length, jnp.int32).astype(F32)
        weight = jnp.where(wave <= (length - 1) // 2, weight, 0.0)
        both = (both * (weight * amp)).reshape(count, z.rows, LANES)
        for i in range(count):
            packet_ref[r * count + i] = jnp.concatenate([both[i], params], axis=0).astype(BF16)
        part = pl.ds(r * count, count)
        sent += fetch((packet_ref.at[part],), (packet_out.at[part],), out_sems.at[pl.ds(r, 1)])
    if z.devices > RADIX * count:
        for i in range(RADIX * count, z.devices):
            packet_ref[i] = jnp.concatenate([jnp.zeros((z.rows, LANES), F32), params], axis=0).astype(BF16)
        part = pl.ds(RADIX * count, z.devices - RADIX * count)
        sent += fetch((packet_ref.at[part],), (packet_out.at[part],), out_sems.at[pl.ds(RADIX, 1)])
    for copy in sent:
        copy.wait()


def mixing_kernel(z, packet_ref, pick_ref, out_ref):
    size = z.lat * z.rows
    to_cols = pick_ref[...]
    par = z.lat * z.par_rows
    from_par = iota((size, par), 0) // z.rows * z.par_rows + z.mer_row == iota((size, par), 1)
    from_par = from_par.astype(F32).astype(BF16)
    same = iota((size, size), 0) % z.rows == iota((size, size), 1) % z.rows
    halves = iota((LANES, LANES), 0) // z.levels == iota((LANES, LANES), 1) // z.levels
    streams = None
    for v in range(z.var):
        whole = packet_ref[:, v].astype(F32)
        coeffs = whole[:, : z.rows].reshape(size, LANES).astype(BF16)
        params = whole[:, z.rows : z.rows + z.par_rows].reshape(par, LANES).astype(BF16)
        slot_rows = dot(params, to_cols).astype(BF16)
        mix = jnp.where(same, dot(from_par, slot_rows), 0.0).astype(BF16)
        blended = dot(mix, coeffs)
        if v == 0:
            stream = blended.astype(BF16)
        else:
            if z.bal_rows == z.par_rows and z.lat * z.bal_rows == z.levels:
                balance = params.astype(F32)
            else:
                level = iota((z.levels, par), 0)
                pick = iota((z.levels, par), 1) == level // z.bal_rows * z.par_rows + level % z.bal_rows
                balance = dot(pick.astype(F32).astype(BF16), params)
            balance = balance[:, : z.levels]
            balance = jnp.concatenate([balance, balance], axis=1)
            balance = jnp.where(halves, jnp.concatenate([balance, balance], axis=0), 0.0).astype(BF16)
            blended = blended + dot(stream, balance, ((1,), (1,)))
        blended = blended.reshape(z.lat, z.rows, LANES)
        for s in range(z.lat):
            out_ref[s, v] = blended[s].astype(BF16)


def synthesis_kernel(
    z, order_in, length_in, spectra_ref, basis_ref, twiddle_ref, period_ref, out_ref,
    order_ref, length_ref, sems, field_ref, parts_ref,
):
    copies = fetch((order_in, length_in), (order_ref, length_ref), sems)
    used = z.waves // z.rows
    spectra = spectra_ref[:used].astype(F32).reshape(z.waves, LANES)
    at = iota((z.waves, LANES), 0)
    wave = at % z.kaps * RADIX + at // z.kaps
    spectra = jnp.where(wave <= (period_ref[0:1] - 1) // 2, spectra, 0.0)
    cosine, sine = basis_ref[: z.kaps], basis_ref[z.kaps :]
    for r in range(RADIX):
        turned = spectra[r * z.kaps : (r + 1) * z.kaps].T.astype(BF16)
        parts_ref[2 * r] = dot(turned, cosine)
        parts_ref[2 * r + 1] = dot(turned, sine)
    for copy in copies:
        copy.wait()
    _, _, length = own_length(order_ref, length_ref)
    quarter = length // RADIX
    starts = [quarter * j1 for j1 in range(1, RADIX)]
    bases = [pl.multiple_of(s // LANES * LANES, LANES) for s in starts]
    shifts = [s - b for s, b in zip(starts, bases)]
    field_ref[:, z.points :] = jnp.zeros((z.levels, z.lons + LANES - z.points), F32)
    lane = iota((STRIP, LANES), 1)
    for at in range(0, z.levels, STRIP):
        rows = slice(at, at + STRIP)
        below = slice(z.levels + at, z.levels + at + STRIP)
        cos1, cos2, cos3 = [twiddle_ref[r : r + 1, :] for r in (1, 2, 3)]
        sin1, sin2, sin3 = [twiddle_ref[RADIX + r : RADIX + r + 1, :] for r in (1, 2, 3)]

        def real(r):
            return parts_ref[2 * r, rows] + parts_ref[2 * r + 1, below]

        def imag(r):
            return parts_ref[2 * r + 1, rows] - parts_ref[2 * r, below]

        w0 = real(0)
        w2 = real(2) * cos2 - imag(2) * sin2
        re1, im1, re3, im3 = real(1), imag(1), real(3), imag(3)
        cross = (re1 * cos1 - im1 * sin1) + (re3 * cos3 - im3 * sin3)
        turn = (re1 * sin1 + im1 * cos1) - (re3 * sin3 + im3 * cos3)
        even, odd = w0 + w2, w0 - w2
        field_ref[rows, : z.points] = even + cross
        for base, shift, part in zip(bases, shifts, (odd - turn, even - cross, odd + turn)):
            tiles = [pltpu.roll(part[:, c : c + LANES], shift, 1) for c in range(0, z.points, LANES)]
            zero = jnp.zeros((STRIP, LANES), F32)
            moved = [jnp.where(lane < shift, a, b) for a, b in zip([zero] + tiles, tiles + [zero])]
            to = pl.ds(base, z.points + LANES)
            field_ref[rows, to] = field_ref[rows, to] + jnp.concatenate(moved, axis=1)
        out_ref[0, 0, rows, :] = field_ref[rows, : z.lons].astype(BF16)


def body(z, control, row_order, row_length, vertical, amplitude, meridional, balance):
    order_scratch = pltpu.SMEM(row_order.shape, jnp.int32)
    length_scratch = pltpu.SMEM(row_length.shape, jnp.int32)
    field_scratch = pltpu.VMEM((z.levels, z.lons + LANES), F32)
    in_vmem = [pltpu.VMEM(x.shape, x.dtype) for x in (control, vertical, amplitude, meridional, balance)]
    made = (
        jax.ShapeDtypeStruct((z.devices, z.packet, LANES), BF16),
        jax.ShapeDtypeStruct((2 * z.kaps, z.points), BF16),
        jax.ShapeDtypeStruct((2 * RADIX, z.points), F32),
        jax.ShapeDtypeStruct((SUBLANES, LANES), jnp.int32),
        jax.ShapeDtypeStruct((LANES, z.lat * z.rows), BF16),
    )
    packets, basis, twiddle, period, pick = pl.pallas_call(
        functools.partial(analysis_kernel, z),
        out_shape=made,
        in_specs=[HBM] * 7,
        out_specs=(HBM,) * 5,
        scratch_shapes=[
            order_scratch,
            length_scratch,
            *in_vmem,
            pltpu.SemaphoreType.DMA((7,)),
            field_scratch,
            pltpu.VMEM((2 * RADIX * z.levels, z.points), BF16),
            *[pltpu.VMEM(x.shape, x.dtype) for x in made],
            pltpu.SemaphoreType.DMA((RADIX + 5,)),
        ],
        compiler_params=ALL_VMEM,
        name="analysis",
    )(row_order, row_length, control, vertical, amplitude, meridional, balance)
    packets = lax.all_to_all(packets, ("lat", "var"), 0, 0, tiled=True)
    balanced = pl.pallas_call(
        functools.partial(mixing_kernel, z),
        out_shape=jax.ShapeDtypeStruct((z.lat, z.var, z.rows, LANES), BF16),
        in_specs=[VMEM, VMEM],
        out_specs=VMEM,
        compiler_params=PARAMS,
        name="mixing",
    )(packets.reshape(z.lat, z.var, z.packet, LANES), pick)
    balanced = balanced.reshape(z.devices, z.rows, LANES)
    balanced = lax.all_to_all(balanced, ("lat", "var"), 0, 0, tiled=True)
    return pl.pallas_call(
        functools.partial(synthesis_kernel, z),
        out_shape=jax.ShapeDtypeStruct(control.shape, BF16),
        in_specs=[HBM, HBM] + [VMEM] * 4,
        out_specs=VMEM,
        scratch_shapes=[
            order_scratch,
            length_scratch,
            pltpu.SemaphoreType.DMA((2,)),
            field_scratch,
            pltpu.VMEM((2 * RADIX, 2 * z.levels, z.points), F32),
        ],
        compiler_params=PARAMS,
        name="synthesis",
    )(row_order, row_length, balanced, basis, twiddle, period)


def solution(mesh):
    placed = (
        P("var", "lat", None, None),
        P(),
        P(),
        P("var", None, None),
        P("var", None),
        P("var", None, None),
        P("var", None, None),
    )

    def run(control, row_order, row_length, vertical, amplitude, meridional, balance):
        lat_total, var_total = mesh.shape["lat"], mesh.shape["var"]
        assert control.shape[0] == var_total and control.shape[1] == lat_total
        z = Sizes(lat_total, var_total, control.shape[2], control.shape[3], amplitude.shape[1])
        return jax.shard_map(
            functools.partial(body, z),
            mesh=mesh,
            in_specs=placed,
            out_specs=P("var", "lat", None, None),
            check_vma=False,
        )(control, row_order, row_length, vertical, amplitude, meridional, balance)

    return run
```

```python
import functools

import jax
import jax.numpy as jnp
from jax import lax
from jax.experimental import pallas as pl
from jax.experimental.pallas import tpu as pltpu
from jax.sharding import PartitionSpec as P

RADIX = 4
LANES = 128
SUBLANES = 8
STRIP = 16
F32 = jnp.float32
BF16 = jnp.bfloat16

COS_POLY = (1, -19.7392044, 64.9391174, -85.4501419, 60.1676292, -25.9675999, 6.52865839)
SIN_POLY = (6.28318501, -41.3415909, 81.5999451, -76.6144714, 41.3428841, -12.4712439)

VMEM = pl.BlockSpec(memory_space=pltpu.VMEM)
HBM = pl.BlockSpec(memory_space=pltpu.HBM)
PARAMS = pltpu.CompilerParams(vmem_limit_bytes=32 * 1024 * 1024)
ALL_VMEM = pltpu.CompilerParams(vmem_limit_bytes=58 * 1024 * 1024)


def iota(shape, dim):
    return lax.broadcasted_iota(jnp.int32, shape, dim)


def horner(poly, x):
    total = jnp.full_like(x, poly[-1])
    for term in poly[-2::-1]:
        total = total * x + term
    return total


def cos_sin(turns):
    turns = turns - jnp.round(turns)
    square = turns * turns
    return horner(COS_POLY, square), horner(SIN_POLY, square) * turns


def ceil_div(a, b):
    return -(-a // b)


def round_up(a, b):
    return ceil_div(a, b) * b


def dot(a, b, contract=((1,), (0,))):
    return lax.dot_general(a, b, (contract, ((), ())), preferred_element_type=F32)


class Sizes:
    def __init__(self, lat_total, var_total, levels, lons, waves):
        self.lat, self.var, self.levels, self.lons, self.waves = lat_total, var_total, levels, lons, waves
        self.devices = lat_total * var_total
        self.points = lons // RADIX
        self.kaps = waves // RADIX
        self.rows = round_up(ceil_div(waves, self.devices), SUBLANES)
        assert self.kaps % self.rows == 0 and 2 * levels == LANES and lat_total <= LANES
        self.mixed = lat_total * self.rows
        self.params = round_up(levels + lat_total, STRIP)


def own_length(order_ref, length_ref):
    slot = lax.axis_index("lat")
    row = order_ref[slot]
    return slot, row, length_ref[row]


def fetch(sources, targets, sems):
    copies = [pltpu.make_async_copy(s, t, sems.at[i]) for i, (s, t) in enumerate(zip(sources, targets))]
    for copy in copies:
        copy.start()
    return copies


def slot_matrix(z, order_ref, mer_ref):
    slot = iota((z.lat, z.lat), 0)
    row = jnp.zeros((z.lat, z.lat), jnp.int32)
    for t in range(z.lat):
        row = jnp.where(slot == t, order_ref[t], row)
    pick = (row == iota((z.lat, z.lat), 1)).astype(F32).astype(BF16)
    return dot(dot(pick, mer_ref[0]).astype(BF16), pick, ((1,), (1,)))


def analysis_kernel(
    z, order_in, length_in, control_in, vert_in, amp_in, mer_in, bal_in,
    packet_out, params_out, basis_out, twiddle_out, period_out,
    order_ref, length_ref, control_ref, vert_ref, amp_ref, mer_ref, bal_ref, sems, field_ref, parts_ref,
    packet_ref, params_ref, basis_ref, twiddle_ref, period_ref, out_sems,
):
    copies = fetch(
        (order_in, length_in, control_in, vert_in, amp_in, mer_in, bal_in),
        (order_ref, length_ref, control_ref, vert_ref, amp_ref, mer_ref, bal_ref),
        sems,
    )
    field_ref[:, z.lons :] = jnp.zeros((z.levels, LANES), F32)
    for copy in copies[:2]:
        copy.wait()
    slot, row, length = own_length(order_ref, length_ref)
    quarter = length // RADIX
    period_ref[...] = jnp.full(period_ref.shape, length, jnp.int32)
    points = iota((1, z.points), 1)
    inside = points < quarter
    step = points.astype(F32) / jnp.full((1, z.points), quarter, jnp.int32).astype(F32)
    for at in range(0, z.kaps, STRIP):
        if at == z.kaps // 2 // STRIP * STRIP:
            for copy in copies[2:]:
                copy.wait()
            field_ref[:, : z.lons] = dot(vert_ref[0], control_ref[0, 0])
            params_ref[...] = jnp.zeros(params_ref.shape, BF16)
            params_ref[: z.levels] = jnp.concatenate([bal_ref[0], bal_ref[0]], axis=1)
            params_ref[z.levels : z.levels + z.lat, : z.lat] = slot_matrix(z, order_ref, mer_ref).astype(BF16)
        kap = (at + iota((STRIP, z.points), 0)).astype(F32)
        cosine, sine = cos_sin(kap * step)
        basis_ref[at : at + STRIP, :] = jnp.where(inside, cosine, 0.0).astype(BF16)
        basis_ref[z.kaps + at : z.kaps + at + STRIP, :] = jnp.where(inside, sine, 0.0).astype(BF16)
    tw_row = iota((2 * RADIX, z.points), 0)
    period = jnp.full((1, z.points), length, jnp.int32).astype(F32)
    tw_cos, tw_sin = cos_sin((tw_row % RADIX).astype(F32) * (points.astype(F32) / period))
    twiddle_ref[...] = jnp.where(tw_row < RADIX, tw_cos, tw_sin)
    sent = fetch(
        (params_ref, basis_ref, twiddle_ref, period_ref),
        (params_out, basis_out, twiddle_out, period_out),
        out_sems.at[pl.ds(RADIX + 1, 4)],
    )
    starts = [quarter * j1 for j1 in range(1, RADIX)]
    bases = [pl.multiple_of(s // LANES * LANES, LANES) for s in starts]
    shifts = [(LANES - (s - b)) % LANES for s, b in zip(starts, bases)]
    lane = iota((STRIP, LANES), 1)
    for at in range(0, z.levels, STRIP):
        rows = slice(at, at + STRIP)

        def quarter_of(base, shift):
            wide = field_ref[rows, pl.ds(base, z.points + LANES)]
            tiles = [
                pltpu.roll(wide[:, c : c + LANES], shift, 1) for c in range(0, z.points + LANES, LANES)
            ]
            keep = (lane < shift) | (shift == 0)
            return jnp.concatenate([jnp.where(keep, a, b) for a, b in zip(tiles, tiles[1:])], axis=1)

        first = field_ref[rows, : z.points]
        second, third, fourth = [quarter_of(b, s) for b, s in zip(bases, shifts)]
        even, odd = first + third, second + fourth
        real, imag = first - third, second - fourth
        cos1, cos2, cos3 = [twiddle_ref[r : r + 1, :] for r in (1, 2, 3)]
        sin1, sin2, sin3 = [twiddle_ref[RADIX + r : RADIX + r + 1, :] for r in (1, 2, 3)]
        turned = even - odd
        parts = (
            (even + odd, None),
            (real * cos1 - imag * sin1, real * sin1 + imag * cos1),
            (turned * cos2, turned * sin2),
            (real * cos3 + imag * sin3, real * sin3 - imag * cos3),
        )
        for r, pair in enumerate(parts):
            for half, part in enumerate(pair):
                part = jnp.zeros((STRIP, z.points), F32) if part is None else part
                to = (2 * r + half) * z.levels + at
                parts_ref[to : to + STRIP, :] = part.astype(BF16)
    product = dot(basis_ref[...], parts_ref[...], ((1,), (1,)))
    count = z.kaps // z.rows
    sign = jnp.where(iota((1, LANES), 1) < z.levels, -1.0, 1.0).astype(F32)
    group = LANES // RADIX
    for r in range(RADIX):
        from_cos = product[: z.kaps, r * LANES : (r + 1) * LANES]
        from_sin = product[z.kaps :, r * LANES : (r + 1) * LANES]
        both = from_cos + pltpu.roll(from_sin, z.levels, 1) * sign
        picked = iota((group, LANES), 1) == iota((group, LANES), 0) * RADIX + r
        amp = jnp.concatenate(
            [
                jnp.sum(jnp.where(picked, amp_ref[:, c : c + LANES], 0.0), axis=1, keepdims=True)
                for c in range(0, z.waves, LANES)
            ],
            axis=0,
        )
        wave = iota((z.kaps, 1), 0) * RADIX + r
        weight = jnp.where(wave == 0, 1.0, 2.0) / jnp.full((z.kaps, 1), length, jnp.int32).astype(F32)
        weight = jnp.where(wave <= (length - 1) // 2, weight, 0.0)
        both = (both * (weight * amp)).reshape(count, z.rows, LANES)
        for i in range(count):
            packet_ref[r * count + i] = both[i].astype(BF16)
        part = pl.ds(r * count, count)
        sent += fetch((packet_ref.at[part],), (packet_out.at[part],), out_sems.at[pl.ds(r, 1)])
    if z.devices > RADIX * count:
        for i in range(RADIX * count, z.devices):
            packet_ref[i] = jnp.zeros((z.rows, LANES), BF16)
        part = pl.ds(RADIX * count, z.devices - RADIX * count)
        sent += fetch((packet_ref.at[part],), (packet_out.at[part],), out_sems.at[pl.ds(RADIX, 1)])
    for copy in sent:
        copy.wait()


def mixing_kernel(z, *refs):
    packet_ref, *given, out_ref, params_ref = refs
    own = lax.axis_index("var")
    for step, ref in enumerate(given):
        params_ref[(own + step) % z.var] = ref[...]
    size = z.mixed
    to_cols = (iota((z.lat, size), 0) == iota((z.lat, size), 1) // z.rows).astype(F32).astype(BF16)
    same = iota((size, size), 0) % z.rows == iota((size, size), 1) % z.rows
    halves = iota((LANES, LANES), 0) // z.levels == iota((LANES, LANES), 1) // z.levels
    stream = None
    for v in range(z.var):
        coeffs = packet_ref[:, v].astype(F32).reshape(size, LANES).astype(BF16)
        meridional = params_ref[v, z.levels :].astype(F32)[: z.lat, : z.lat].astype(BF16)
        slot_cols = dot(meridional, to_cols).astype(BF16)
        mix = jnp.where(same, dot(to_cols, slot_cols, ((0,), (0,))), 0.0).astype(BF16)
        blended = dot(mix, coeffs)
        if v == 0:
            stream = blended.astype(BF16)
        else:
            balance = params_ref[v, : z.levels].astype(F32)
            balance = jnp.where(halves, jnp.concatenate([balance, balance], axis=0), 0.0).astype(BF16)
            blended = blended + dot(stream, balance, ((1,), (1,)))
        blended = blended.reshape(z.lat, z.rows, LANES)
        for s in range(z.lat):
            out_ref[s, v] = blended[s].astype(BF16)


def synthesis_kernel(
    z, order_in, length_in, spectra_ref, basis_ref, twiddle_ref, period_ref, out_ref,
    order_ref, length_ref, sems, field_ref, parts_ref,
):
    copies = fetch((order_in, length_in), (order_ref, length_ref), sems)
    used = z.waves // z.rows
    spectra = spectra_ref[:used].astype(F32).reshape(z.waves, LANES)
    at = iota((z.waves, LANES), 0)
    wave = at % z.kaps * RADIX + at // z.kaps
    spectra = jnp.where(wave <= (period_ref[0:1] - 1) // 2, spectra, 0.0)
    cosine, sine = basis_ref[: z.kaps], basis_ref[z.kaps :]
    for r in range(RADIX):
        turned = spectra[r * z.kaps : (r + 1) * z.kaps].T.astype(BF16)
        parts_ref[2 * r] = dot(turned, cosine)
        parts_ref[2 * r + 1] = dot(turned, sine)
    for copy in copies:
        copy.wait()
    _, _, length = own_length(order_ref, length_ref)
    quarter = length // RADIX
    starts = [quarter * j1 for j1 in range(1, RADIX)]
    bases = [pl.multiple_of(s // LANES * LANES, LANES) for s in starts]
    shifts = [s - b for s, b in zip(starts, bases)]
    field_ref[:, z.points :] = jnp.zeros((z.levels, z.lons + LANES - z.points), F32)
    lane = iota((STRIP, LANES), 1)
    for at in range(0, z.levels, STRIP):
        rows = slice(at, at + STRIP)
        below = slice(z.levels + at, z.levels + at + STRIP)
        cos1, cos2, cos3 = [twiddle_ref[r : r + 1, :] for r in (1, 2, 3)]
        sin1, sin2, sin3 = [twiddle_ref[RADIX + r : RADIX + r + 1, :] for r in (1, 2, 3)]

        def real(r):
            return parts_ref[2 * r, rows] + parts_ref[2 * r + 1, below]

        def imag(r):
            return parts_ref[2 * r + 1, rows] - parts_ref[2 * r, below]

        w0 = real(0)
        w2 = real(2) * cos2 - imag(2) * sin2
        re1, im1, re3, im3 = real(1), imag(1), real(3), imag(3)
        cross = (re1 * cos1 - im1 * sin1) + (re3 * cos3 - im3 * sin3)
        turn = (re1 * sin1 + im1 * cos1) - (re3 * sin3 + im3 * cos3)
        even, odd = w0 + w2, w0 - w2
        field_ref[rows, : z.points] = even + cross
        for base, shift, part in zip(bases, shifts, (odd - turn, even - cross, odd + turn)):
            tiles = [pltpu.roll(part[:, c : c + LANES], shift, 1) for c in range(0, z.points, LANES)]
            zero = jnp.zeros((STRIP, LANES), F32)
            moved = [jnp.where(lane < shift, a, b) for a, b in zip([zero] + tiles, tiles + [zero])]
            to = pl.ds(base, z.points + LANES)
            field_ref[rows, to] = field_ref[rows, to] + jnp.concatenate(moved, axis=1)
        out_ref[0, 0, rows, :] = field_ref[rows, : z.lons].astype(BF16)


def body(z, control, row_order, row_length, vertical, amplitude, meridional, balance):
    order_scratch = pltpu.SMEM(row_order.shape, jnp.int32)
    length_scratch = pltpu.SMEM(row_length.shape, jnp.int32)
    field_scratch = pltpu.VMEM((z.levels, z.lons + LANES), F32)
    in_vmem = [pltpu.VMEM(x.shape, x.dtype) for x in (control, vertical, amplitude, meridional, balance)]
    made = (
        jax.ShapeDtypeStruct((z.devices, z.rows, LANES), BF16),
        jax.ShapeDtypeStruct((z.params, LANES), BF16),
        jax.ShapeDtypeStruct((2 * z.kaps, z.points), BF16),
        jax.ShapeDtypeStruct((2 * RADIX, z.points), F32),
        jax.ShapeDtypeStruct((SUBLANES, LANES), jnp.int32),
    )
    packets, params, basis, twiddle, period = pl.pallas_call(
        functools.partial(analysis_kernel, z),
        out_shape=made,
        in_specs=[HBM] * 7,
        out_specs=(HBM,) * 5,
        scratch_shapes=[
            order_scratch,
            length_scratch,
            *in_vmem,
            pltpu.SemaphoreType.DMA((7,)),
            field_scratch,
            pltpu.VMEM((2 * RADIX * z.levels, z.points), BF16),
            *[pltpu.VMEM(x.shape, x.dtype) for x in made],
            pltpu.SemaphoreType.DMA((RADIX + 5,)),
        ],
        compiler_params=ALL_VMEM,
        name="analysis",
    )(row_order, row_length, control, vertical, amplitude, meridional, balance)
    given = [params]
    for step in range(1, z.var):
        given.append(lax.ppermute(params, "var", [((i + step) % z.var, i) for i in range(z.var)]))
    packets = lax.all_to_all(packets, ("lat", "var"), 0, 0, tiled=True)
    balanced = pl.pallas_call(
        functools.partial(mixing_kernel, z),
        out_shape=jax.ShapeDtypeStruct((z.lat, z.var, z.rows, LANES), BF16),
        in_specs=[VMEM] * (1 + z.var),
        out_specs=VMEM,
        scratch_shapes=[pltpu.VMEM((z.var, z.params, LANES), BF16)],
        compiler_params=PARAMS,
        name="mixing",
    )(packets.reshape(z.lat, z.var, z.rows, LANES), *given)
    balanced = balanced.reshape(z.devices, z.rows, LANES)
    balanced = lax.all_to_all(balanced, ("lat", "var"), 0, 0, tiled=True)
    return pl.pallas_call(
        functools.partial(synthesis_kernel, z),
        out_shape=jax.ShapeDtypeStruct(control.shape, BF16),
        in_specs=[HBM, HBM] + [VMEM] * 4,
        out_specs=VMEM,
        scratch_shapes=[
            order_scratch,
            length_scratch,
            pltpu.SemaphoreType.DMA((2,)),
            field_scratch,
            pltpu.VMEM((2 * RADIX, 2 * z.levels, z.points), F32),
        ],
        compiler_params=PARAMS,
        name="synthesis",
    )(row_order, row_length, balanced, basis, twiddle, period)


def solution(mesh):
    placed = (
        P("var", "lat", None, None),
        P(),
        P(),
        P("var", None, None),
        P("var", None),
        P("var", None, None),
        P("var", None, None),
    )

    def run(control, row_order, row_length, vertical, amplitude, meridional, balance):
        lat_total, var_total = mesh.shape["lat"], mesh.shape["var"]
        assert control.shape[0] == var_total and control.shape[1] == lat_total
        z = Sizes(lat_total, var_total, control.shape[2], control.shape[3], amplitude.shape[1])
        return jax.shard_map(
            functools.partial(body, z),
            mesh=mesh,
            in_specs=placed,
            out_specs=P("var", "lat", None, None),
            check_vma=False,
        )(control, row_order, row_length, vertical, amplitude, meridional, balance)

    return run
```

```python
import functools

import jax
import jax.numpy as jnp
from jax import lax
from jax.experimental import pallas as pl
from jax.experimental.pallas import tpu as pltpu
from jax.sharding import PartitionSpec as P

RADIX = 4
LANES = 128
SUBLANES = 8
STRIP = 16
F32 = jnp.float32
BF16 = jnp.bfloat16

COS_POLY = (1, -19.7392044, 64.9391174, -85.4501419, 60.1676292, -25.9675999, 6.52865839)
SIN_POLY = (6.28318501, -41.3415909, 81.5999451, -76.6144714, 41.3428841, -12.4712439)

VMEM = pl.BlockSpec(memory_space=pltpu.VMEM)
HBM = pl.BlockSpec(memory_space=pltpu.HBM)
PARAMS = pltpu.CompilerParams(vmem_limit_bytes=32 * 1024 * 1024)
ALL_VMEM = pltpu.CompilerParams(vmem_limit_bytes=58 * 1024 * 1024)


def iota(shape, dim):
    return lax.broadcasted_iota(jnp.int32, shape, dim)


def horner(poly, x):
    total = jnp.full_like(x, poly[-1])
    for term in poly[-2::-1]:
        total = total * x + term
    return total


def cos_sin(turns):
    turns = turns - jnp.round(turns)
    square = turns * turns
    return horner(COS_POLY, square), horner(SIN_POLY, square) * turns


def ceil_div(a, b):
    return -(-a // b)


def round_up(a, b):
    return ceil_div(a, b) * b


def dot(a, b, contract=((1,), (0,))):
    return lax.dot_general(a, b, (contract, ((), ())), preferred_element_type=F32)


class Sizes:
    def __init__(self, lat_total, var_total, levels, lons, waves):
        self.lat, self.var, self.levels, self.lons, self.waves = lat_total, var_total, levels, lons, waves
        self.devices = lat_total * var_total
        self.points = lons // RADIX
        self.kaps = waves // RADIX
        self.rows = round_up(ceil_div(waves, self.devices), SUBLANES)
        assert self.kaps % self.rows == 0 and 2 * levels == LANES and lat_total <= LANES
        self.mixed = lat_total * self.rows
        self.params = round_up(levels + lat_total, STRIP)


def own_length(order_ref, length_ref):
    slot = lax.axis_index("lat")
    row = order_ref[slot]
    return slot, row, length_ref[row]


def fetch(sources, targets, sems):
    copies = [pltpu.make_async_copy(s, t, sems.at[i]) for i, (s, t) in enumerate(zip(sources, targets))]
    for copy in copies:
        copy.start()
    return copies


def slot_matrix(z, order_ref, mer_ref):
    slot = iota((z.lat, z.lat), 0)
    row = jnp.zeros((z.lat, z.lat), jnp.int32)
    for t in range(z.lat):
        row = jnp.where(slot == t, order_ref[t], row)
    pick = (row == iota((z.lat, z.lat), 1)).astype(F32).astype(BF16)
    return dot(dot(pick, mer_ref[0]).astype(BF16), pick, ((1,), (1,)))


def analysis_kernel(
    z, order_in, length_in, control_in, vert_in, amp_in, mer_in, bal_in,
    packet_out, params_out, basis_out, twiddle_out,
    order_ref, length_ref, control_ref, vert_ref, amp_ref, mer_ref, bal_ref, sems, field_ref, parts_ref,
    packet_ref, params_ref, basis_ref, twiddle_ref, out_sems,
):
    copies = fetch(
        (order_in, length_in, control_in, vert_in, amp_in, mer_in, bal_in),
        (order_ref, length_ref, control_ref, vert_ref, amp_ref, mer_ref, bal_ref),
        sems,
    )
    field_ref[:, z.lons :] = jnp.zeros((z.levels, LANES), F32)
    for copy in copies[:2]:
        copy.wait()
    slot, row, length = own_length(order_ref, length_ref)
    quarter = length // RADIX
    points = iota((1, z.points), 1)
    inside = points < quarter
    step = points.astype(F32) / jnp.full((1, z.points), quarter, jnp.int32).astype(F32)
    for at in range(0, z.kaps, STRIP):
        if at == z.kaps // 2 // STRIP * STRIP:
            for copy in copies[2:]:
                copy.wait()
            field_ref[:, : z.lons] = dot(vert_ref[0], control_ref[0, 0])
            params_ref[...] = jnp.zeros(params_ref.shape, BF16)
            params_ref[: z.levels] = jnp.concatenate([bal_ref[0], bal_ref[0]], axis=1)
            params_ref[z.levels : z.levels + z.lat, : z.lat] = slot_matrix(z, order_ref, mer_ref).astype(BF16)
        kap = (at + iota((STRIP, z.points), 0)).astype(F32)
        cosine, sine = cos_sin(kap * step)
        basis_ref[at : at + STRIP, :] = jnp.where(inside, cosine, 0.0).astype(BF16)
        basis_ref[z.kaps + at : z.kaps + at + STRIP, :] = jnp.where(inside, sine, 0.0).astype(BF16)
    tw_row = iota((2 * RADIX, z.points), 0)
    period = jnp.full((1, z.points), length, jnp.int32).astype(F32)
    tw_cos, tw_sin = cos_sin((tw_row % RADIX).astype(F32) * (points.astype(F32) / period))
    twiddle_ref[: 2 * RADIX] = jnp.where(tw_row < RADIX, tw_cos, tw_sin)
    twiddle_ref[2 * RADIX :] = jnp.broadcast_to(period, (SUBLANES, z.points))
    sent = fetch(
        (params_ref, basis_ref, twiddle_ref),
        (params_out, basis_out, twiddle_out),
        out_sems.at[pl.ds(RADIX + 1, 3)],
    )
    starts = [quarter * j1 for j1 in range(1, RADIX)]
    bases = [pl.multiple_of(s // LANES * LANES, LANES) for s in starts]
    shifts = [(LANES - (s - b)) % LANES for s, b in zip(starts, bases)]
    lane = iota((STRIP, LANES), 1)
    for at in range(0, z.levels, STRIP):
        rows = slice(at, at + STRIP)

        def quarter_of(base, shift):
            wide = field_ref[rows, pl.ds(base, z.points + LANES)]
            tiles = [
                pltpu.roll(wide[:, c : c + LANES], shift, 1) for c in range(0, z.points + LANES, LANES)
            ]
            keep = (lane < shift) | (shift == 0)
            return jnp.concatenate([jnp.where(keep, a, b) for a, b in zip(tiles, tiles[1:])], axis=1)

        first = field_ref[rows, : z.points]
        second, third, fourth = [quarter_of(b, s) for b, s in zip(bases, shifts)]
        even, odd = first + third, second + fourth
        real, imag = first - third, second - fourth
        cos1, cos2, cos3 = [twiddle_ref[r : r + 1, :] for r in (1, 2, 3)]
        sin1, sin2, sin3 = [twiddle_ref[RADIX + r : RADIX + r + 1, :] for r in (1, 2, 3)]
        turned = even - odd
        parts = (
            (even + odd, None),
            (real * cos1 - imag * sin1, real * sin1 + imag * cos1),
            (turned * cos2, turned * sin2),
            (real * cos3 + imag * sin3, real * sin3 - imag * cos3),
        )
        for r, pair in enumerate(parts):
            for half, part in enumerate(pair):
                part = jnp.zeros((STRIP, z.points), F32) if part is None else part
                to = (2 * r + half) * z.levels + at
                parts_ref[to : to + STRIP, :] = part.astype(BF16)
    product = dot(basis_ref[...], parts_ref[...], ((1,), (1,)))
    count = z.kaps // z.rows
    sign = jnp.where(iota((1, LANES), 1) < z.levels, -1.0, 1.0).astype(F32)
    group = LANES // RADIX
    for r in range(RADIX):
        from_cos = product[: z.kaps, r * LANES : (r + 1) * LANES]
        from_sin = product[z.kaps :, r * LANES : (r + 1) * LANES]
        both = from_cos + pltpu.roll(from_sin, z.levels, 1) * sign
        picked = iota((group, LANES), 1) == iota((group, LANES), 0) * RADIX + r
        amp = jnp.concatenate(
            [
                jnp.sum(jnp.where(picked, amp_ref[:, c : c + LANES], 0.0), axis=1, keepdims=True)
                for c in range(0, z.waves, LANES)
            ],
            axis=0,
        )
        wave = iota((z.kaps, 1), 0) * RADIX + r
        weight = jnp.where(wave == 0, 1.0, 2.0) / jnp.full((z.kaps, 1), length, jnp.int32).astype(F32)
        weight = jnp.where(wave <= (length - 1) // 2, weight, 0.0)
        both = (both * (weight * amp)).reshape(count, z.rows, LANES)
        for i in range(count):
            packet_ref[r * count + i] = both[i].astype(BF16)
        part = pl.ds(r * count, count)
        sent += fetch((packet_ref.at[part],), (packet_out.at[part],), out_sems.at[pl.ds(r, 1)])
    if z.devices > RADIX * count:
        for i in range(RADIX * count, z.devices):
            packet_ref[i] = jnp.zeros((z.rows, LANES), BF16)
        part = pl.ds(RADIX * count, z.devices - RADIX * count)
        sent += fetch((packet_ref.at[part],), (packet_out.at[part],), out_sems.at[pl.ds(RADIX, 1)])
    for copy in sent:
        copy.wait()


def mixing_kernel(z, packet_ref, given_ref, out_ref):
    own = lax.axis_index("var")
    size = z.mixed
    to_cols = (iota((z.lat, size), 0) == iota((z.lat, size), 1) // z.rows).astype(F32).astype(BF16)
    same = iota((size, size), 0) % z.rows == iota((size, size), 1) % z.rows
    halves = iota((LANES, LANES), 0) // z.levels == iota((LANES, LANES), 1) // z.levels
    stream = None
    for v in range(z.var):
        coeffs = packet_ref[:, v].astype(F32).reshape(size, LANES).astype(BF16)
        step = (v + z.var - own) % z.var
        meridional = given_ref[step, z.levels :].astype(F32)[: z.lat, : z.lat].astype(BF16)
        slot_cols = dot(meridional, to_cols).astype(BF16)
        mix = jnp.where(same, dot(to_cols, slot_cols, ((0,), (0,))), 0.0).astype(BF16)
        blended = dot(mix, coeffs)
        if v == 0:
            stream = blended.astype(BF16)
        else:
            balance = given_ref[step, : z.levels].astype(F32)
            balance = jnp.where(halves, jnp.concatenate([balance, balance], axis=0), 0.0).astype(BF16)
            blended = blended + dot(stream, balance, ((1,), (1,)))
        blended = blended.reshape(z.lat, z.rows, LANES)
        for s in range(z.lat):
            out_ref[s, v] = blended[s].astype(BF16)


def synthesis_kernel(
    z, spectra_ref, basis_ref, twiddle_ref, out_ref, field_ref, parts_ref,
):
    period = twiddle_ref[2 * RADIX :, :LANES].astype(jnp.int32)
    length = jnp.max(period)
    used = z.waves // z.rows
    spectra = spectra_ref[:used].astype(F32).reshape(z.waves, LANES)
    at = iota((z.waves, LANES), 0)
    wave = at % z.kaps * RADIX + at // z.kaps
    spectra = jnp.where(wave <= (period[0:1] - 1) // 2, spectra, 0.0)
    cosine, sine = basis_ref[: z.kaps], basis_ref[z.kaps :]
    for r in range(RADIX):
        turned = spectra[r * z.kaps : (r + 1) * z.kaps].T.astype(BF16)
        parts_ref[2 * r] = dot(turned, cosine)
        parts_ref[2 * r + 1] = dot(turned, sine)
    quarter = length // RADIX
    starts = [quarter * j1 for j1 in range(1, RADIX)]
    bases = [pl.multiple_of(s // LANES * LANES, LANES) for s in starts]
    shifts = [s - b for s, b in zip(starts, bases)]
    field_ref[:, z.points :] = jnp.zeros((z.levels, z.lons + LANES - z.points), F32)
    lane = iota((STRIP, LANES), 1)
    for at in range(0, z.levels, STRIP):
        rows = slice(at, at + STRIP)
        below = slice(z.levels + at, z.levels + at + STRIP)
        cos1, cos2, cos3 = [twiddle_ref[r : r + 1, :] for r in (1, 2, 3)]
        sin1, sin2, sin3 = [twiddle_ref[RADIX + r : RADIX + r + 1, :] for r in (1, 2, 3)]

        def real(r):
            return parts_ref[2 * r, rows] + parts_ref[2 * r + 1, below]

        def imag(r):
            return parts_ref[2 * r + 1, rows] - parts_ref[2 * r, below]

        w0 = real(0)
        w2 = real(2) * cos2 - imag(2) * sin2
        re1, im1, re3, im3 = real(1), imag(1), real(3), imag(3)
        cross = (re1 * cos1 - im1 * sin1) + (re3 * cos3 - im3 * sin3)
        turn = (re1 * sin1 + im1 * cos1) - (re3 * sin3 + im3 * cos3)
        even, odd = w0 + w2, w0 - w2
        field_ref[rows, : z.points] = even + cross
        for base, shift, part in zip(bases, shifts, (odd - turn, even - cross, odd + turn)):
            tiles = [pltpu.roll(part[:, c : c + LANES], shift, 1) for c in range(0, z.points, LANES)]
            zero = jnp.zeros((STRIP, LANES), F32)
            moved = [jnp.where(lane < shift, a, b) for a, b in zip([zero] + tiles, tiles + [zero])]
            to = pl.ds(base, z.points + LANES)
            field_ref[rows, to] = field_ref[rows, to] + jnp.concatenate(moved, axis=1)
        out_ref[0, 0, rows, :] = field_ref[rows, : z.lons].astype(BF16)


def body(z, control, row_order, row_length, vertical, amplitude, meridional, balance):
    field_scratch = pltpu.VMEM((z.levels, z.lons + LANES), F32)
    in_vmem = [pltpu.VMEM(x.shape, x.dtype) for x in (control, vertical, amplitude, meridional, balance)]
    made = (
        jax.ShapeDtypeStruct((z.devices, z.rows, LANES), BF16),
        jax.ShapeDtypeStruct((z.params, LANES), BF16),
        jax.ShapeDtypeStruct((2 * z.kaps, z.points), BF16),
        jax.ShapeDtypeStruct((2 * RADIX + SUBLANES, z.points), F32),
    )
    packets, params, basis, twiddle = pl.pallas_call(
        functools.partial(analysis_kernel, z),
        out_shape=made,
        in_specs=[HBM] * 7,
        out_specs=(HBM,) * 4,
        scratch_shapes=[
            pltpu.SMEM(row_order.shape, jnp.int32),
            pltpu.SMEM(row_length.shape, jnp.int32),
            *in_vmem,
            pltpu.SemaphoreType.DMA((7,)),
            field_scratch,
            pltpu.VMEM((2 * RADIX * z.levels, z.points), BF16),
            *[pltpu.VMEM(x.shape, x.dtype) for x in made],
            pltpu.SemaphoreType.DMA((RADIX + 4,)),
        ],
        compiler_params=ALL_VMEM,
        name="analysis",
    )(row_order, row_length, control, vertical, amplitude, meridional, balance)
    given = [params]
    for step in range(1, z.var):
        given.append(lax.ppermute(params, "var", [((i + step) % z.var, i) for i in range(z.var)]))
    packets = lax.all_to_all(packets, ("lat", "var"), 0, 0, tiled=True)
    balanced = pl.pallas_call(
        functools.partial(mixing_kernel, z),
        out_shape=jax.ShapeDtypeStruct((z.lat, z.var, z.rows, LANES), BF16),
        in_specs=[VMEM, VMEM],
        out_specs=VMEM,
        compiler_params=PARAMS,
        name="mixing",
    )(packets.reshape(z.lat, z.var, z.rows, LANES), jnp.stack(given))
    balanced = balanced.reshape(z.devices, z.rows, LANES)
    balanced = lax.all_to_all(balanced, ("lat", "var"), 0, 0, tiled=True)
    return pl.pallas_call(
        functools.partial(synthesis_kernel, z),
        out_shape=jax.ShapeDtypeStruct(control.shape, BF16),
        in_specs=[VMEM] * 3,
        out_specs=VMEM,
        scratch_shapes=[
            field_scratch,
            pltpu.VMEM((2 * RADIX, 2 * z.levels, z.points), F32),
        ],
        compiler_params=PARAMS,
        name="synthesis",
    )(balanced, basis, twiddle)


def solution(mesh):
    placed = (
        P("var", "lat", None, None),
        P(),
        P(),
        P("var", None, None),
        P("var", None),
        P("var", None, None),
        P("var", None, None),
    )

    def run(control, row_order, row_length, vertical, amplitude, meridional, balance):
        lat_total, var_total = mesh.shape["lat"], mesh.shape["var"]
        assert control.shape[0] == var_total and control.shape[1] == lat_total
        z = Sizes(lat_total, var_total, control.shape[2], control.shape[3], amplitude.shape[1])
        return jax.shard_map(
            functools.partial(body, z),
            mesh=mesh,
            in_specs=placed,
            out_specs=P("var", "lat", None, None),
            check_vma=False,
        )(control, row_order, row_length, vertical, amplitude, meridional, balance)

    return run
```

```python
import functools

import jax
import jax.numpy as jnp
from jax import lax
from jax.experimental import pallas as pl
from jax.experimental.pallas import tpu as pltpu
from jax.sharding import PartitionSpec as P

RADIX = 4
LANES = 128
SUBLANES = 8
STRIP = 16
F32 = jnp.float32
BF16 = jnp.bfloat16

COS_POLY = (1, -19.7392044, 64.9391174, -85.4501419, 60.1676292, -25.9675999, 6.52865839)
SIN_POLY = (6.28318501, -41.3415909, 81.5999451, -76.6144714, 41.3428841, -12.4712439)

VMEM = pl.BlockSpec(memory_space=pltpu.VMEM)
HBM = pl.BlockSpec(memory_space=pltpu.HBM)
PARAMS = pltpu.CompilerParams(vmem_limit_bytes=32 * 1024 * 1024)
ALL_VMEM = pltpu.CompilerParams(vmem_limit_bytes=58 * 1024 * 1024)


def iota(shape, dim):
    return lax.broadcasted_iota(jnp.int32, shape, dim)


def horner(poly, x):
    total = jnp.full_like(x, poly[-1])
    for term in poly[-2::-1]:
        total = total * x + term
    return total


def cos_sin(turns):
    turns = turns - jnp.round(turns)
    square = turns * turns
    return horner(COS_POLY, square), horner(SIN_POLY, square) * turns


def ceil_div(a, b):
    return -(-a // b)


def round_up(a, b):
    return ceil_div(a, b) * b


def dot(a, b, contract=((1,), (0,))):
    return lax.dot_general(a, b, (contract, ((), ())), preferred_element_type=F32)


class Sizes:
    def __init__(self, lat_total, var_total, levels, lons, waves):
        self.lat, self.var, self.levels, self.lons, self.waves = lat_total, var_total, levels, lons, waves
        self.devices = lat_total * var_total
        self.points = lons // RADIX
        self.kaps = waves // RADIX
        self.rows = round_up(ceil_div(waves, self.devices), SUBLANES)
        assert self.kaps % self.rows == 0 and 2 * levels == LANES and lat_total <= LANES
        self.mixed = lat_total * self.rows
        self.params = round_up(levels + lat_total, STRIP)


def own_length(order_ref, length_ref):
    slot = lax.axis_index("lat")
    row = order_ref[slot]
    return slot, row, length_ref[row]


def fetch(sources, targets, sems):
    copies = [pltpu.make_async_copy(s, t, sems.at[i]) for i, (s, t) in enumerate(zip(sources, targets))]
    for copy in copies:
        copy.start()
    return copies


def slot_matrix(z, order_ref, mer_ref):
    slot = iota((z.lat, z.lat), 0)
    row = jnp.zeros((z.lat, z.lat), jnp.int32)
    for t in range(z.lat):
        row = jnp.where(slot == t, order_ref[t], row)
    pick = (row == iota((z.lat, z.lat), 1)).astype(F32).astype(BF16)
    return dot(dot(pick, mer_ref[0]).astype(BF16), pick, ((1,), (1,)))


def analysis_kernel(
    z, order_in, length_in, control_in, vert_in, amp_in, mer_in, bal_in,
    packet_out, params_out, basis_out, twiddle_out,
    order_ref, length_ref, control_ref, vert_ref, amp_ref, mer_ref, bal_ref, sems, field_ref, parts_ref,
    packet_ref, params_ref, basis_ref, twiddle_ref, out_sems,
):
    copies = fetch(
        (order_in, length_in, control_in, vert_in, amp_in, mer_in, bal_in),
        (order_ref, length_ref, control_ref, vert_ref, amp_ref, mer_ref, bal_ref),
        sems,
    )
    field_ref[:, z.lons :] = jnp.zeros((z.levels, LANES), F32)
    for copy in copies[:2]:
        copy.wait()
    slot, row, length = own_length(order_ref, length_ref)
    quarter = length // RADIX
    points = iota((1, z.points), 1)
    inside = points < quarter
    step = points.astype(F32) / jnp.full((1, z.points), quarter, jnp.int32).astype(F32)
    for at in range(0, z.kaps, STRIP):
        if at == z.kaps // 2 // STRIP * STRIP:
            for copy in copies[2:]:
                copy.wait()
            field_ref[:, : z.lons] = dot(vert_ref[0], control_ref[0, 0])
            params_ref[...] = jnp.zeros(params_ref.shape, BF16)
            params_ref[: z.levels] = jnp.concatenate([bal_ref[0], bal_ref[0]], axis=1)
            params_ref[z.levels : z.levels + z.lat, : z.lat] = slot_matrix(z, order_ref, mer_ref).astype(BF16)
        kap = (at + iota((STRIP, z.points), 0)).astype(F32)
        cosine, sine = cos_sin(kap * step)
        basis_ref[at : at + STRIP, :] = jnp.where(inside, cosine, 0.0).astype(BF16)
        basis_ref[z.kaps + at : z.kaps + at + STRIP, :] = jnp.where(inside, sine, 0.0).astype(BF16)
    tw_row = iota((2 * RADIX, z.points), 0)
    period = jnp.full((1, z.points), length, jnp.int32).astype(F32)
    tw_cos, tw_sin = cos_sin((tw_row % RADIX).astype(F32) * (points.astype(F32) / period))
    twiddle_ref[: 2 * RADIX] = jnp.where(tw_row < RADIX, tw_cos, tw_sin)
    twiddle_ref[2 * RADIX :] = jnp.broadcast_to(period, (SUBLANES, z.points))
    sent = fetch(
        (params_ref, basis_ref, twiddle_ref),
        (params_out, basis_out, twiddle_out),
        out_sems.at[pl.ds(RADIX + 1, 3)],
    )
    starts = [quarter * j1 for j1 in range(1, RADIX)]
    bases = [pl.multiple_of(s // LANES * LANES, LANES) for s in starts]
    shifts = [(LANES - (s - b)) % LANES for s, b in zip(starts, bases)]
    lane = iota((STRIP, LANES), 1)
    for at in range(0, z.levels, STRIP):
        rows = slice(at, at + STRIP)

        def quarter_of(base, shift):
            wide = field_ref[rows, pl.ds(base, z.points + LANES)]
            tiles = [
                pltpu.roll(wide[:, c : c + LANES], shift, 1) for c in range(0, z.points + LANES, LANES)
            ]
            keep = (lane < shift) | (shift == 0)
            return jnp.concatenate([jnp.where(keep, a, b) for a, b in zip(tiles, tiles[1:])], axis=1)

        first = field_ref[rows, : z.points]
        second, third, fourth = [quarter_of(b, s) for b, s in zip(bases, shifts)]
        even, odd = first + third, second + fourth
        real, imag = first - third, second - fourth
        cos1, cos2, cos3 = [twiddle_ref[r : r + 1, :] for r in (1, 2, 3)]
        sin1, sin2, sin3 = [twiddle_ref[RADIX + r : RADIX + r + 1, :] for r in (1, 2, 3)]
        turned = even - odd
        parts = (
            (even + odd, None),
            (real * cos1 - imag * sin1, real * sin1 + imag * cos1),
            (turned * cos2, turned * sin2),
            (real * cos3 + imag * sin3, real * sin3 - imag * cos3),
        )
        for r, pair in enumerate(parts):
            for half, part in enumerate(pair):
                part = jnp.zeros((STRIP, z.points), F32) if part is None else part
                to = (2 * r + half) * z.levels + at
                parts_ref[to : to + STRIP, :] = part.astype(BF16)
    product = dot(basis_ref[...], parts_ref[...], ((1,), (1,)))
    count = z.kaps // z.rows
    sign = jnp.where(iota((1, LANES), 1) < z.levels, -1.0, 1.0).astype(F32)
    group = LANES // RADIX
    for r in range(RADIX):
        from_cos = product[: z.kaps, r * LANES : (r + 1) * LANES]
        from_sin = product[z.kaps :, r * LANES : (r + 1) * LANES]
        both = from_cos + pltpu.roll(from_sin, z.levels, 1) * sign
        picked = iota((group, LANES), 1) == iota((group, LANES), 0) * RADIX + r
        amp = jnp.concatenate(
            [
                jnp.sum(jnp.where(picked, amp_ref[:, c : c + LANES], 0.0), axis=1, keepdims=True)
                for c in range(0, z.waves, LANES)
            ],
            axis=0,
        )
        wave = iota((z.kaps, 1), 0) * RADIX + r
        weight = jnp.where(wave == 0, 1.0, 2.0) / jnp.full((z.kaps, 1), length, jnp.int32).astype(F32)
        weight = jnp.where(wave <= (length - 1) // 2, weight, 0.0)
        both = (both * (weight * amp)).reshape(count, z.rows, LANES)
        for i in range(count):
            packet_ref[r * count + i] = both[i].astype(BF16)
        part = pl.ds(r * count, count)
        sent += fetch((packet_ref.at[part],), (packet_out.at[part],), out_sems.at[pl.ds(r, 1)])
    if z.devices > RADIX * count:
        for i in range(RADIX * count, z.devices):
            packet_ref[i] = jnp.zeros((z.rows, LANES), BF16)
        part = pl.ds(RADIX * count, z.devices - RADIX * count)
        sent += fetch((packet_ref.at[part],), (packet_out.at[part],), out_sems.at[pl.ds(RADIX, 1)])
    for copy in sent:
        copy.wait()


def mixing_kernel(z, packet_ref, given_ref, out_ref):
    own = lax.axis_index("var")
    size = z.mixed
    to_cols = (iota((z.lat, size), 0) == iota((z.lat, size), 1) // z.rows).astype(F32).astype(BF16)
    same = iota((size, size), 0) % z.rows == iota((size, size), 1) % z.rows
    halves = iota((LANES, LANES), 0) // z.levels == iota((LANES, LANES), 1) // z.levels
    stream = None
    for v in range(z.var):
        coeffs = packet_ref[v].astype(F32).reshape(size, LANES).astype(BF16)
        step = (v + z.var - own) % z.var
        meridional = given_ref[step, z.levels :].astype(F32)[: z.lat, : z.lat].astype(BF16)
        slot_cols = dot(meridional, to_cols).astype(BF16)
        mix = jnp.where(same, dot(to_cols, slot_cols, ((0,), (0,))), 0.0).astype(BF16)
        blended = dot(mix, coeffs)
        if v == 0:
            stream = blended.astype(BF16)
        else:
            balance = given_ref[step, : z.levels].astype(F32)
            balance = jnp.where(halves, jnp.concatenate([balance, balance], axis=0), 0.0).astype(BF16)
            blended = blended + dot(stream, balance, ((1,), (1,)))
        blended = blended.reshape(z.lat, z.rows, LANES)
        for s in range(z.lat):
            out_ref[v, s] = blended[s].astype(BF16)


def synthesis_kernel(
    z, spectra_ref, basis_ref, twiddle_ref, out_ref, field_ref, parts_ref,
):
    period = twiddle_ref[2 * RADIX :, :LANES].astype(jnp.int32)
    length = jnp.max(period)
    used = z.waves // z.rows
    spectra = spectra_ref[:used].astype(F32).reshape(z.waves, LANES)
    at = iota((z.waves, LANES), 0)
    wave = at % z.kaps * RADIX + at // z.kaps
    spectra = jnp.where(wave <= (period[0:1] - 1) // 2, spectra, 0.0)
    cosine, sine = basis_ref[: z.kaps], basis_ref[z.kaps :]
    for r in range(RADIX):
        turned = spectra[r * z.kaps : (r + 1) * z.kaps].T.astype(BF16)
        parts_ref[2 * r] = dot(turned, cosine)
        parts_ref[2 * r + 1] = dot(turned, sine)
    quarter = length // RADIX
    starts = [quarter * j1 for j1 in range(1, RADIX)]
    bases = [pl.multiple_of(s // LANES * LANES, LANES) for s in starts]
    shifts = [s - b for s, b in zip(starts, bases)]
    field_ref[:, z.points :] = jnp.zeros((z.levels, z.lons + LANES - z.points), F32)
    lane = iota((STRIP, LANES), 1)
    for at in range(0, z.levels, STRIP):
        rows = slice(at, at + STRIP)
        below = slice(z.levels + at, z.levels + at + STRIP)
        cos1, cos2, cos3 = [twiddle_ref[r : r + 1, :] for r in (1, 2, 3)]
        sin1, sin2, sin3 = [twiddle_ref[RADIX + r : RADIX + r + 1, :] for r in (1, 2, 3)]

        def real(r):
            return parts_ref[2 * r, rows] + parts_ref[2 * r + 1, below]

        def imag(r):
            return parts_ref[2 * r + 1, rows] - parts_ref[2 * r, below]

        w0 = real(0)
        w2 = real(2) * cos2 - imag(2) * sin2
        re1, im1, re3, im3 = real(1), imag(1), real(3), imag(3)
        cross = (re1 * cos1 - im1 * sin1) + (re3 * cos3 - im3 * sin3)
        turn = (re1 * sin1 + im1 * cos1) - (re3 * sin3 + im3 * cos3)
        even, odd = w0 + w2, w0 - w2
        field_ref[rows, : z.points] = even + cross
        for base, shift, part in zip(bases, shifts, (odd - turn, even - cross, odd + turn)):
            tiles = [pltpu.roll(part[:, c : c + LANES], shift, 1) for c in range(0, z.points, LANES)]
            zero = jnp.zeros((STRIP, LANES), F32)
            moved = [jnp.where(lane < shift, a, b) for a, b in zip([zero] + tiles, tiles + [zero])]
            to = pl.ds(base, z.points + LANES)
            field_ref[rows, to] = field_ref[rows, to] + jnp.concatenate(moved, axis=1)
        out_ref[0, 0, rows, :] = field_ref[rows, : z.lons].astype(BF16)


def body(z, control, row_order, row_length, vertical, amplitude, meridional, balance):
    field_scratch = pltpu.VMEM((z.levels, z.lons + LANES), F32)
    in_vmem = [pltpu.VMEM(x.shape, x.dtype) for x in (control, vertical, amplitude, meridional, balance)]
    made = (
        jax.ShapeDtypeStruct((z.devices, z.rows, LANES), BF16),
        jax.ShapeDtypeStruct((z.params, LANES), BF16),
        jax.ShapeDtypeStruct((2 * z.kaps, z.points), BF16),
        jax.ShapeDtypeStruct((2 * RADIX + SUBLANES, z.points), F32),
    )
    packets, params, basis, twiddle = pl.pallas_call(
        functools.partial(analysis_kernel, z),
        out_shape=made,
        in_specs=[HBM] * 7,
        out_specs=(HBM,) * 4,
        scratch_shapes=[
            pltpu.SMEM(row_order.shape, jnp.int32),
            pltpu.SMEM(row_length.shape, jnp.int32),
            *in_vmem,
            pltpu.SemaphoreType.DMA((7,)),
            field_scratch,
            pltpu.VMEM((2 * RADIX * z.levels, z.points), BF16),
            *[pltpu.VMEM(x.shape, x.dtype) for x in made],
            pltpu.SemaphoreType.DMA((RADIX + 4,)),
        ],
        compiler_params=ALL_VMEM,
        name="analysis",
    )(row_order, row_length, control, vertical, amplitude, meridional, balance)
    given = [params]
    for step in range(1, z.var):
        given.append(lax.ppermute(params, "var", [((i + step) % z.var, i) for i in range(z.var)]))
    packets = lax.all_to_all(packets, ("var", "lat"), 0, 0, tiled=True)
    balanced = pl.pallas_call(
        functools.partial(mixing_kernel, z),
        out_shape=jax.ShapeDtypeStruct((z.var, z.lat, z.rows, LANES), BF16),
        in_specs=[VMEM, VMEM],
        out_specs=VMEM,
        compiler_params=PARAMS,
        name="mixing",
    )(packets.reshape(z.var, z.lat, z.rows, LANES), jnp.stack(given))
    balanced = balanced.reshape(z.devices, z.rows, LANES)
    balanced = lax.all_to_all(balanced, ("var", "lat"), 0, 0, tiled=True)
    return pl.pallas_call(
        functools.partial(synthesis_kernel, z),
        out_shape=jax.ShapeDtypeStruct(control.shape, BF16),
        in_specs=[VMEM] * 3,
        out_specs=VMEM,
        scratch_shapes=[
            field_scratch,
            pltpu.VMEM((2 * RADIX, 2 * z.levels, z.points), F32),
        ],
        compiler_params=PARAMS,
        name="synthesis",
    )(balanced, basis, twiddle)


def solution(mesh):
    placed = (
        P("var", "lat", None, None),
        P(),
        P(),
        P("var", None, None),
        P("var", None),
        P("var", None, None),
        P("var", None, None),
    )

    def run(control, row_order, row_length, vertical, amplitude, meridional, balance):
        lat_total, var_total = mesh.shape["lat"], mesh.shape["var"]
        assert control.shape[0] == var_total and control.shape[1] == lat_total
        z = Sizes(lat_total, var_total, control.shape[2], control.shape[3], amplitude.shape[1])
        return jax.shard_map(
            functools.partial(body, z),
            mesh=mesh,
            in_specs=placed,
            out_specs=P("var", "lat", None, None),
            check_vma=False,
        )(control, row_order, row_length, vertical, amplitude, meridional, balance)

    return run
```

```python
import functools

import jax
import jax.numpy as jnp
from jax import lax
from jax.experimental import pallas as pl
from jax.experimental.pallas import tpu as pltpu
from jax.sharding import PartitionSpec as P

RADIX = 4
LANES = 128
SUBLANES = 8
STRIP = 16
F32 = jnp.float32
BF16 = jnp.bfloat16

COS_POLY = (1, -19.7392044, 64.9391174, -85.4501419, 60.1676292, -25.9675999, 6.52865839)
SIN_POLY = (6.28318501, -41.3415909, 81.5999451, -76.6144714, 41.3428841, -12.4712439)

VMEM = pl.BlockSpec(memory_space=pltpu.VMEM)
HBM = pl.BlockSpec(memory_space=pltpu.HBM)
PARAMS = pltpu.CompilerParams(vmem_limit_bytes=32 * 1024 * 1024)
ALL_VMEM = pltpu.CompilerParams(vmem_limit_bytes=58 * 1024 * 1024)


def iota(shape, dim):
    return lax.broadcasted_iota(jnp.int32, shape, dim)


def horner(poly, x):
    total = jnp.full_like(x, poly[-1])
    for term in poly[-2::-1]:
        total = total * x + term
    return total


def cos_sin(turns):
    turns = turns - jnp.round(turns)
    square = turns * turns
    return horner(COS_POLY, square), horner(SIN_POLY, square) * turns


def ceil_div(a, b):
    return -(-a // b)


def round_up(a, b):
    return ceil_div(a, b) * b


def dot(a, b, contract=((1,), (0,))):
    return lax.dot_general(a, b, (contract, ((), ())), preferred_element_type=F32)


class Sizes:
    def __init__(self, lat_total, var_total, levels, lons, waves):
        self.lat, self.var, self.levels, self.lons, self.waves = lat_total, var_total, levels, lons, waves
        self.points = lons // RADIX
        self.kaps = waves // RADIX
        self.rows = round_up(ceil_div(waves, lat_total), SUBLANES)
        self.used = waves // self.rows
        assert self.kaps % self.rows == 0 and 2 * levels == LANES and lat_total <= LANES
        self.paired = lat_total <= 16 and lat_total & (lat_total - 1) == 0
        self.pieces = lat_total if self.paired else 1
        self.piece = (self.rows, LANES) if self.paired else (lat_total, self.rows, LANES)

    def peer(self, slot, i):
        return slot ^ i if self.paired else i


def piece_of(z, refs, i):
    return refs[i][...] if z.paired else refs[0][i]


def put_piece(z, refs, i, value):
    if z.paired:
        refs[i][...] = value
    else:
        refs[0][i] = value


def own_length(order_ref, length_ref):
    slot = lax.axis_index("lat")
    row = order_ref[slot]
    return slot, row, length_ref[row]


def fetch(sources, targets, sems):
    copies = [pltpu.make_async_copy(s, t, sems.at[i]) for i, (s, t) in enumerate(zip(sources, targets))]
    for copy in copies:
        copy.start()
    return copies


def peer_weights(z, slot, order_ref, mer_ref):
    peer = iota((z.lat, z.lat), 0)
    row = jnp.zeros((z.lat, z.lat), jnp.int32)
    for i in range(z.lat):
        row = jnp.where(peer == i, order_ref[z.peer(slot, i)], row)
    pick = (row == iota((z.lat, z.lat), 1)).astype(F32).astype(BF16)
    factor = dot(dot(pick, mer_ref[0]).astype(BF16), pick, ((1,), (1,)))
    pairs = z.lat * z.lat
    spread = (iota((pairs, z.lat), 0) // z.lat == iota((pairs, z.lat), 1)).astype(F32).astype(BF16)
    spread = dot(spread, factor.astype(BF16))
    spread = jnp.where(iota((pairs, z.lat), 0) % z.lat == iota((pairs, z.lat), 1), spread, 0.0)
    return jnp.broadcast_to(jnp.sum(spread, axis=1, keepdims=True), (pairs, LANES))


def analysis_kernel(z, *refs):
    given, refs = refs[:6], refs[6:]
    chunk_outs, refs = refs[: z.pieces], refs[z.pieces :]
    made_outs, refs = refs[:3], refs[3:]
    held, refs = refs[:6], refs[6:]
    order_ref, length_ref, control_ref, vert_ref, amp_ref, mer_ref = held
    made_refs, refs = refs[:3], refs[3:]
    basis_ref, twiddle_ref, weight_ref = made_refs
    sems, out_sems, field_ref, parts_ref, chunk_ref = refs
    copies = fetch(given, held, sems)
    field_ref[:, z.lons :] = jnp.zeros((z.levels, LANES), F32)
    for copy in copies[:2]:
        copy.wait()
    slot, row, length = own_length(order_ref, length_ref)
    quarter = length // RADIX
    points = iota((1, z.points), 1)
    inside = points < quarter
    step = points.astype(F32) / jnp.full((1, z.points), quarter, jnp.int32).astype(F32)
    for at in range(0, z.kaps, STRIP):
        if at == z.kaps // 2 // STRIP * STRIP:
            for copy in copies[2:]:
                copy.wait()
            field_ref[:, : z.lons] = dot(vert_ref[0], control_ref[0, 0])
            weight_ref[...] = peer_weights(z, slot, order_ref, mer_ref)
        kap = (at + iota((STRIP, z.points), 0)).astype(F32)
        cosine, sine = cos_sin(kap * step)
        basis_ref[at : at + STRIP, :] = jnp.where(inside, cosine, 0.0).astype(BF16)
        basis_ref[z.kaps + at : z.kaps + at + STRIP, :] = jnp.where(inside, sine, 0.0).astype(BF16)
    tw_row = iota((2 * RADIX, z.points), 0)
    period = jnp.full((1, z.points), length, jnp.int32).astype(F32)
    tw_cos, tw_sin = cos_sin((tw_row % RADIX).astype(F32) * (points.astype(F32) / period))
    twiddle_ref[: 2 * RADIX] = jnp.where(tw_row < RADIX, tw_cos, tw_sin)
    twiddle_ref[2 * RADIX :] = jnp.broadcast_to(period, (SUBLANES, z.points))
    sent = fetch(made_refs, made_outs, out_sems.at[pl.ds(z.pieces, 3)])
    starts = [quarter * j1 for j1 in range(1, RADIX)]
    bases = [pl.multiple_of(s // LANES * LANES, LANES) for s in starts]
    shifts = [(LANES - (s - b)) % LANES for s, b in zip(starts, bases)]
    lane = iota((STRIP, LANES), 1)
    for at in range(0, z.levels, STRIP):
        rows = slice(at, at + STRIP)

        def quarter_of(base, shift):
            wide = field_ref[rows, pl.ds(base, z.points + LANES)]
            tiles = [
                pltpu.roll(wide[:, c : c + LANES], shift, 1) for c in range(0, z.points + LANES, LANES)
            ]
            keep = (lane < shift) | (shift == 0)
            return jnp.concatenate([jnp.where(keep, a, b) for a, b in zip(tiles, tiles[1:])], axis=1)

        first = field_ref[rows, : z.points]
        second, third, fourth = [quarter_of(b, s) for b, s in zip(bases, shifts)]
        even, odd = first + third, second + fourth
        real, imag = first - third, second - fourth
        cos1, cos2, cos3 = [twiddle_ref[r : r + 1, :] for r in (1, 2, 3)]
        sin1, sin2, sin3 = [twiddle_ref[RADIX + r : RADIX + r + 1, :] for r in (1, 2, 3)]
        turned = even - odd
        parts = (
            (even + odd, None),
            (real * cos1 - imag * sin1, real * sin1 + imag * cos1),
            (turned * cos2, turned * sin2),
            (real * cos3 + imag * sin3, real * sin3 - imag * cos3),
        )
        for r, pair in enumerate(parts):
            for half, part in enumerate(pair):
                part = jnp.zeros((STRIP, z.points), F32) if part is None else part
                to = (2 * r + half) * z.levels + at
                parts_ref[to : to + STRIP, :] = part.astype(BF16)
    product = dot(basis_ref[...], parts_ref[...], ((1,), (1,)))
    count = z.kaps // z.rows
    sign = jnp.where(iota((1, LANES), 1) < z.levels, -1.0, 1.0).astype(F32)
    group = LANES // RADIX
    for r in range(RADIX):
        from_cos = product[: z.kaps, r * LANES : (r + 1) * LANES]
        from_sin = product[z.kaps :, r * LANES : (r + 1) * LANES]
        both = from_cos + pltpu.roll(from_sin, z.levels, 1) * sign
        picked = iota((group, LANES), 1) == iota((group, LANES), 0) * RADIX + r
        amp = jnp.concatenate(
            [
                jnp.sum(jnp.where(picked, amp_ref[:, c : c + LANES], 0.0), axis=1, keepdims=True)
                for c in range(0, z.waves, LANES)
            ],
            axis=0,
        )
        wave = iota((z.kaps, 1), 0) * RADIX + r
        weight = jnp.where(wave == 0, 1.0, 2.0) / jnp.full((z.kaps, 1), length, jnp.int32).astype(F32)
        weight = jnp.where(wave <= (length - 1) // 2, weight, 0.0)
        both = (both * (weight * amp)).reshape(count, z.rows, LANES)
        for i in range(count):
            chunk_ref[r * count + i] = both[i].astype(BF16)
    for i in range(z.used, z.lat):
        chunk_ref[i] = jnp.zeros((z.rows, LANES), BF16)
    sources = [chunk_ref.at[z.peer(slot, i)] for i in range(z.lat)] if z.paired else [chunk_ref]
    sent += fetch(sources, chunk_outs, out_sems)
    for copy in sent:
        copy.wait()


def mixing_kernel(z, weight_ref, *refs):
    chunk_refs, out_ref = refs[: z.pieces], refs[-1]

    def mix(i):
        total = weight_ref[pl.ds(i * z.lat, 1)] * piece_of(z, chunk_refs, 0).astype(F32)
        for j in range(1, z.lat):
            total = total + weight_ref[pl.ds(i * z.lat + j, 1)] * piece_of(z, chunk_refs, j).astype(F32)
        out_ref[i] = total.astype(BF16)

    if z.paired:
        for i in range(z.lat):
            mix(i)
    else:
        lax.fori_loop(0, z.lat, lambda i, none: mix(i), None)


def balance_kernel(z, bal_ref, own_ref, *refs):
    stream_refs, out_refs = refs[: z.var - 1], refs[z.var - 1 :]
    own = lax.axis_index("var")
    balance = bal_ref[0].astype(F32)
    balance = jnp.concatenate([balance, balance], axis=1)
    balance = jnp.concatenate([balance, balance], axis=0)
    halves = iota((LANES, LANES), 0) // z.levels == iota((LANES, LANES), 1) // z.levels
    balance = jnp.where(halves & (own > 0), balance, 0.0).astype(BF16)
    for i in range(z.lat):
        stream = stream_refs[0][i].astype(F32)
        for v in range(2, z.var):
            stream = jnp.where(own == v, stream_refs[v - 1][i].astype(F32), stream)
        lifted = dot(stream.astype(BF16), balance, ((1,), (1,)))
        put_piece(z, out_refs, i, (own_ref[i].astype(F32) + lifted).astype(BF16))


def synthesis_kernel(
    z, basis_ref, twiddle_ref, *refs,
):
    chunk_refs, (out_ref, field_ref, parts_ref, spectra_ref) = refs[: z.pieces], refs[z.pieces :]
    slot = lax.axis_index("lat")
    for i in range(z.lat):
        spectra_ref[z.peer(slot, i)] = piece_of(z, chunk_refs, i)
    period = twiddle_ref[2 * RADIX :, :LANES].astype(jnp.int32)
    length = jnp.max(period)
    spectra = spectra_ref[: z.used].astype(F32).reshape(z.waves, LANES)
    at = iota((z.waves, LANES), 0)
    wave = at % z.kaps * RADIX + at // z.kaps
    spectra = jnp.where(wave <= (period[0:1] - 1) // 2, spectra, 0.0)
    cosine, sine = basis_ref[: z.kaps], basis_ref[z.kaps :]
    for r in range(RADIX):
        turned = spectra[r * z.kaps : (r + 1) * z.kaps].T.astype(BF16)
        parts_ref[2 * r] = dot(turned, cosine)
        parts_ref[2 * r + 1] = dot(turned, sine)
    quarter = length // RADIX
    starts = [quarter * j1 for j1 in range(1, RADIX)]
    bases = [pl.multiple_of(s // LANES * LANES, LANES) for s in starts]
    shifts = [s - b for s, b in zip(starts, bases)]
    field_ref[:, z.points :] = jnp.zeros((z.levels, z.lons + LANES - z.points), F32)
    lane = iota((STRIP, LANES), 1)
    for at in range(0, z.levels, STRIP):
        rows = slice(at, at + STRIP)
        below = slice(z.levels + at, z.levels + at + STRIP)
        cos1, cos2, cos3 = [twiddle_ref[r : r + 1, :] for r in (1, 2, 3)]
        sin1, sin2, sin3 = [twiddle_ref[RADIX + r : RADIX + r + 1, :] for r in (1, 2, 3)]

        def real(r):
            return parts_ref[2 * r, rows] + parts_ref[2 * r + 1, below]

        def imag(r):
            return parts_ref[2 * r + 1, rows] - parts_ref[2 * r, below]

        w0 = real(0)
        w2 = real(2) * cos2 - imag(2) * sin2
        re1, im1, re3, im3 = real(1), imag(1), real(3), imag(3)
        cross = (re1 * cos1 - im1 * sin1) + (re3 * cos3 - im3 * sin3)
        turn = (re1 * sin1 + im1 * cos1) - (re3 * sin3 + im3 * cos3)
        even, odd = w0 + w2, w0 - w2
        field_ref[rows, : z.points] = even + cross
        for base, shift, part in zip(bases, shifts, (odd - turn, even - cross, odd + turn)):
            tiles = [pltpu.roll(part[:, c : c + LANES], shift, 1) for c in range(0, z.points, LANES)]
            zero = jnp.zeros((STRIP, LANES), F32)
            moved = [jnp.where(lane < shift, a, b) for a, b in zip([zero] + tiles, tiles + [zero])]
            to = pl.ds(base, z.points + LANES)
            field_ref[rows, to] = field_ref[rows, to] + jnp.concatenate(moved, axis=1)
        out_ref[0, 0, rows, :] = field_ref[rows, : z.lons].astype(BF16)


def exchange(z, chunks):
    if not z.paired:
        return [lax.all_to_all(chunks[0], "lat", 0, 0, tiled=True)]
    swapped = [
        lax.ppermute(chunks[i], "lat", [(slot, slot ^ i) for slot in range(z.lat)]) for i in range(z.lat - 1, 0, -1)
    ]
    return chunks[:1] + swapped[::-1]


def spread_first(z, blended):
    held = {0: blended}
    for v in sorted(range(1, z.var), key=lambda v: (v.bit_count(), -v)):
        source = v & (v - 1)
        held[v] = lax.ppermute(held[source], "var", [(source, v)])
    return [held[v] for v in range(1, z.var)]


def body(z, control, row_order, row_length, vertical, amplitude, meridional, balance):
    arguments = (row_order, row_length, control, vertical, amplitude, meridional)
    chunk_shapes = [jax.ShapeDtypeStruct(z.piece, BF16)] * z.pieces
    made = [
        jax.ShapeDtypeStruct((2 * z.kaps, z.points), BF16),
        jax.ShapeDtypeStruct((2 * RADIX + SUBLANES, z.points), F32),
        jax.ShapeDtypeStruct((z.lat * z.lat, LANES), F32),
    ]
    *chunks, basis, twiddle, weights = pl.pallas_call(
        functools.partial(analysis_kernel, z),
        out_shape=chunk_shapes + made,
        in_specs=[HBM] * len(arguments),
        out_specs=[HBM] * (z.pieces + len(made)),
        scratch_shapes=[
            *[pltpu.SMEM(x.shape, x.dtype) for x in arguments[:2]],
            *[pltpu.VMEM(x.shape, x.dtype) for x in arguments[2:]],
            *[pltpu.VMEM(x.shape, x.dtype) for x in made],
            pltpu.SemaphoreType.DMA((len(arguments),)),
            pltpu.SemaphoreType.DMA((z.pieces + len(made),)),
            pltpu.VMEM((z.levels, z.lons + LANES), F32),
            pltpu.VMEM((2 * RADIX * z.levels, z.points), BF16),
            pltpu.VMEM((z.lat, z.rows, LANES), BF16),
        ],
        compiler_params=ALL_VMEM,
        name="analysis",
    )(*arguments)
    blended = pl.pallas_call(
        functools.partial(mixing_kernel, z),
        out_shape=jax.ShapeDtypeStruct((z.lat, z.rows, LANES), BF16),
        in_specs=[VMEM] * (1 + z.pieces),
        out_specs=VMEM,
        compiler_params=PARAMS,
        name="mixing",
    )(weights, *exchange(z, chunks))
    chunks = pl.pallas_call(
        functools.partial(balance_kernel, z),
        out_shape=chunk_shapes,
        in_specs=[VMEM] * (1 + z.var),
        out_specs=[VMEM] * z.pieces,
        compiler_params=PARAMS,
        name="balance",
    )(balance, blended, *spread_first(z, blended))
    return pl.pallas_call(
        functools.partial(synthesis_kernel, z),
        out_shape=jax.ShapeDtypeStruct(control.shape, BF16),
        in_specs=[VMEM] * (2 + z.pieces),
        out_specs=VMEM,
        scratch_shapes=[
            pltpu.VMEM((z.levels, z.lons + LANES), F32),
            pltpu.VMEM((2 * RADIX, 2 * z.levels, z.points), F32),
            pltpu.VMEM((z.lat, z.rows, LANES), BF16),
        ],
        compiler_params=PARAMS,
        name="synthesis",
    )(basis, twiddle, *exchange(z, list(chunks)))


def solution(mesh):
    placed = (
        P("var", "lat", None, None),
        P(),
        P(),
        P("var", None, None),
        P("var", None),
        P("var", None, None),
        P("var", None, None),
    )

    def run(control, row_order, row_length, vertical, amplitude, meridional, balance):
        lat_total, var_total = mesh.shape["lat"], mesh.shape["var"]
        assert control.shape[0] == var_total and control.shape[1] == lat_total
        z = Sizes(lat_total, var_total, control.shape[2], control.shape[3], amplitude.shape[1])
        return jax.shard_map(
            functools.partial(body, z),
            mesh=mesh,
            in_specs=placed,
            out_specs=P("var", "lat", None, None),
            check_vma=False,
        )(control, row_order, row_length, vertical, amplitude, meridional, balance)

    return run
```

```python
import functools

import jax
import jax.numpy as jnp
from jax import lax
from jax.experimental import pallas as pl
from jax.experimental.pallas import tpu as pltpu
from jax.sharding import PartitionSpec as P

RADIX = 4
LANES = 128
SUBLANES = 8
STRIP = 16
F32 = jnp.float32
BF16 = jnp.bfloat16

COS_POLY = (1, -19.7392044, 64.9391174, -85.4501419, 60.1676292, -25.9675999, 6.52865839)
SIN_POLY = (6.28318501, -41.3415909, 81.5999451, -76.6144714, 41.3428841, -12.4712439)

VMEM = pl.BlockSpec(memory_space=pltpu.VMEM)
HBM = pl.BlockSpec(memory_space=pltpu.HBM)
PARAMS = pltpu.CompilerParams(vmem_limit_bytes=32 * 1024 * 1024)
ALL_VMEM = pltpu.CompilerParams(vmem_limit_bytes=58 * 1024 * 1024)


def iota(shape, dim):
    return lax.broadcasted_iota(jnp.int32, shape, dim)


def horner(poly, x):
    total = jnp.full_like(x, poly[-1])
    for term in poly[-2::-1]:
        total = total * x + term
    return total


def cos_sin(turns):
    turns = turns - jnp.round(turns)
    square = turns * turns
    return horner(COS_POLY, square), horner(SIN_POLY, square) * turns


def ceil_div(a, b):
    return -(-a // b)


def round_up(a, b):
    return ceil_div(a, b) * b


def dot(a, b, contract=((1,), (0,))):
    return lax.dot_general(a, b, (contract, ((), ())), preferred_element_type=F32)


class Sizes:
    def __init__(self, lat_total, var_total, levels, lons, waves):
        self.lat, self.var, self.levels, self.lons, self.waves = lat_total, var_total, levels, lons, waves
        self.devices = lat_total * var_total
        self.points = lons // RADIX
        self.kaps = waves // RADIX
        self.rows = round_up(ceil_div(waves, self.devices), SUBLANES)
        assert self.kaps % self.rows == 0 and 2 * levels == LANES and lat_total <= LANES
        self.mixed = lat_total * self.rows
        self.heads = round_up(ceil_div(self.kaps, STRIP), SUBLANES)
        self.params = round_up(levels + lat_total, STRIP)


def own_length(order_ref, length_ref):
    slot = lax.axis_index("lat")
    row = order_ref[slot]
    return slot, row, length_ref[row]


def fetch(sources, targets, sems):
    copies = [pltpu.make_async_copy(s, t, sems.at[i]) for i, (s, t) in enumerate(zip(sources, targets))]
    for copy in copies:
        copy.start()
    return copies


def slot_matrix(z, order_ref, mer_ref):
    slot = iota((z.lat, z.lat), 0)
    row = jnp.zeros((z.lat, z.lat), jnp.int32)
    for t in range(z.lat):
        row = jnp.where(slot == t, order_ref[t], row)
    pick = (row == iota((z.lat, z.lat), 1)).astype(F32).astype(BF16)
    return dot(dot(pick, mer_ref[0]).astype(BF16), pick, ((1,), (1,)))


def analysis_kernel(z, *refs):
    given, outs, held, made = refs[:7], refs[7:11], refs[11:18], refs[18:22]
    sems, out_sems, field_ref, parts_ref, heads_ref, scale_ref = refs[22:]
    order_ref, length_ref, amp_ref, vert_ref, mer_ref, bal_ref, control_ref = held
    packet_ref, params_ref, basis_ref, twiddle_ref = made
    packet_out = outs[0]
    copies = fetch(given, held, sems)
    field_ref[:, z.lons :] = jnp.zeros((z.levels, LANES), F32)
    params_ref[...] = jnp.zeros(params_ref.shape, BF16)
    for copy in copies[:2]:
        copy.wait()
    slot, row, length = own_length(order_ref, length_ref)
    quarter = length // RADIX
    points = iota((1, z.points), 1)
    inside = points < quarter
    step = points.astype(F32) / jnp.full((1, z.points), quarter, jnp.int32).astype(F32)
    tail_cos, tail_sin = cos_sin(iota((STRIP, z.points), 0).astype(F32) * step)
    head_cos, head_sin = cos_sin(iota((z.heads, z.points), 0).astype(F32) * STRIP * step)
    heads_ref[: z.heads] = jnp.where(inside, head_cos, 0.0)
    heads_ref[z.heads :] = jnp.where(inside, head_sin, 0.0)
    for at in range(0, z.kaps, STRIP):
        head = at // STRIP
        head_cos, head_sin = heads_ref[head : head + 1], heads_ref[z.heads + head : z.heads + head + 1]
        basis_ref[at : at + STRIP, :] = (head_cos * tail_cos - head_sin * tail_sin).astype(BF16)
        basis_ref[z.kaps + at : z.kaps + at + STRIP, :] = (head_sin * tail_cos + head_cos * tail_sin).astype(BF16)
    tw_row = iota((2 * RADIX, z.points), 0)
    period = jnp.full((1, z.points), length, jnp.int32).astype(F32)
    tw_cos, tw_sin = cos_sin((tw_row % RADIX).astype(F32) * (points.astype(F32) / period))
    twiddle_ref[: 2 * RADIX] = jnp.where(tw_row < RADIX, tw_cos, tw_sin)
    twiddle_ref[2 * RADIX :] = jnp.broadcast_to(period, (SUBLANES, z.points))
    for copy in copies[2:6]:
        copy.wait()
    group = LANES // RADIX
    for r in range(RADIX):
        picked = iota((group, LANES), 1) == iota((group, LANES), 0) * RADIX + r
        for at in range(0, z.kaps, group):
            lanes = slice(at * RADIX, at * RADIX + LANES)
            amp = jnp.sum(jnp.where(picked, amp_ref[:, lanes], 0.0), axis=1, keepdims=True)
            wave = (at + iota((group, LANES), 0)) * RADIX + r
            weight = jnp.where(wave == 0, 1.0, 2.0) / period[:, :LANES]
            weight = jnp.where(wave <= (length - 1) // 2, weight, 0.0)
            scale_ref[r * z.kaps + at : r * z.kaps + at + group] = weight * amp
    params_ref[: z.levels] = jnp.concatenate([bal_ref[0], bal_ref[0]], axis=1)
    params_ref[z.levels : z.levels + z.lat, : z.lat] = slot_matrix(z, order_ref, mer_ref).astype(BF16)
    sent = fetch(made[1:], outs[1:], out_sems.at[pl.ds(RADIX, 3)])
    copies[6].wait()
    field_ref[:, : z.lons] = dot(vert_ref[0], control_ref[0, 0])
    starts = [quarter * j1 for j1 in range(1, RADIX)]
    bases = [pl.multiple_of(s // LANES * LANES, LANES) for s in starts]
    shifts = [(LANES - (s - b)) % LANES for s, b in zip(starts, bases)]
    lane = iota((STRIP, LANES), 1)
    for at in range(0, z.levels, STRIP):
        rows = slice(at, at + STRIP)

        def quarter_of(base, shift):
            wide = field_ref[rows, pl.ds(base, z.points + LANES)]
            tiles = [pltpu.roll(wide[:, c : c + LANES], shift, 1) for c in range(0, z.points + LANES, LANES)]
            keep = (lane < shift) | (shift == 0)
            return jnp.concatenate([jnp.where(keep, a, b) for a, b in zip(tiles, tiles[1:])], axis=1)

        first = field_ref[rows, : z.points]
        second, third, fourth = [quarter_of(b, s) for b, s in zip(bases, shifts)]
        even, odd = first + third, second + fourth
        real, imag = first - third, second - fourth
        cos1, cos2, cos3 = [twiddle_ref[r : r + 1, :] for r in (1, 2, 3)]
        sin1, sin2, sin3 = [twiddle_ref[RADIX + r : RADIX + r + 1, :] for r in (1, 2, 3)]
        turned = even - odd
        parts = (
            (even + odd, jnp.zeros((STRIP, z.points), F32)),
            (real * cos1 - imag * sin1, real * sin1 + imag * cos1),
            (turned * cos2, turned * sin2),
            (real * cos3 + imag * sin3, real * sin3 - imag * cos3),
        )
        for r, pair in enumerate(parts):
            for half, part in enumerate(pair):
                to = (2 * r + half) * z.levels + at
                parts_ref[to : to + STRIP, :] = part.astype(BF16)
    count = z.kaps // z.rows
    sign = jnp.where(iota((1, LANES), 1) < z.levels, -1.0, 1.0).astype(F32)
    for pair in range(0, RADIX, 2):
        product = dot(basis_ref[...], parts_ref[pair * LANES : (pair + 2) * LANES], ((1,), (1,)))
        for r in range(pair, pair + 2):
            lanes = slice((r - pair) * LANES, (r - pair + 1) * LANES)
            both = product[: z.kaps, lanes] + pltpu.roll(product[z.kaps :, lanes], z.levels, 1) * sign
            both = (both * scale_ref[r * z.kaps : (r + 1) * z.kaps]).reshape(count, z.rows, LANES)
            for i in range(count):
                packet_ref[r * count + i] = both[i].astype(BF16)
            part = pl.ds(r * count, count)
            sent += fetch((packet_ref.at[part],), (packet_out.at[part],), out_sems.at[pl.ds(r, 1)])
    if z.devices > RADIX * count:
        for i in range(RADIX * count, z.devices):
            packet_ref[i] = jnp.zeros((z.rows, LANES), BF16)
        part = pl.ds(RADIX * count, z.devices - RADIX * count)
        sent += fetch((packet_ref.at[part],), (packet_out.at[part],), out_sems.at[pl.ds(RADIX + 3, 1)])
    for copy in sent:
        copy.wait()


def matrices_kernel(z, *refs):
    *given, mix_ref, bal_ref, all_ref = refs
    own = lax.axis_index("var")
    for step, ref in enumerate(given):
        all_ref[(own + step) % z.var] = ref[...]
    size = z.mixed
    to_cols = (iota((z.lat, size), 0) == iota((z.lat, size), 1) // z.rows).astype(F32).astype(BF16)
    same = iota((size, size), 0) % z.rows == iota((size, size), 1) % z.rows
    halves = iota((LANES, LANES), 0) // z.levels == iota((LANES, LANES), 1) // z.levels
    for v in range(z.var):
        meridional = all_ref[v, z.levels :].astype(F32)[: z.lat, : z.lat].astype(BF16)
        slot_cols = dot(meridional, to_cols).astype(BF16)
        mix_ref[v] = jnp.where(same, dot(to_cols, slot_cols, ((0,), (0,))), 0.0).astype(BF16)
        if v > 0:
            balance = all_ref[v, : z.levels].astype(F32)
            balance = jnp.where(halves, jnp.concatenate([balance, balance], axis=0), 0.0)
            bal_ref[v - 1] = balance.T.astype(BF16)


def mixing_kernel(z, packet_ref, mix_ref, bal_ref, out_ref):
    stream = None
    for v in range(z.var):
        coeffs = packet_ref[v].astype(F32).reshape(z.mixed, LANES).astype(BF16)
        blended = dot(mix_ref[v], coeffs)
        if v == 0:
            stream = blended.astype(BF16)
        else:
            blended = blended + dot(stream, bal_ref[v - 1])
        blended = blended.reshape(z.lat, z.rows, LANES)
        for s in range(z.lat):
            out_ref[v, s] = blended[s].astype(BF16)


def synthesis_kernel(z, spectra_ref, basis_ref, twiddle_ref, out_ref, sems, field_ref, lhs_ref, parts_ref):
    period = twiddle_ref[2 * RADIX :, :LANES].astype(jnp.int32)
    length = jnp.max(period)
    used = z.waves // z.rows
    spectra = spectra_ref[:used].astype(F32).reshape(z.waves, LANES)
    at = iota((z.waves, LANES), 0)
    wave = at % z.kaps * RADIX + at // z.kaps
    spectra = jnp.where(wave <= (period[0:1] - 1) // 2, spectra, 0.0)
    sign = jnp.where(iota((1, LANES), 1) < z.levels, 1.0, -1.0).astype(F32)
    for r in range(RADIX):
        part = spectra[r * z.kaps : (r + 1) * z.kaps]
        part = jnp.concatenate([part * sign, pltpu.roll(part, z.levels, 1)], axis=0).T.astype(BF16)
        if r == 0:
            lhs_ref[: z.levels] = part[: z.levels]
        else:
            lhs_ref[(2 * r - 1) * z.levels : (2 * r + 1) * z.levels] = part
    parts_ref[...] = dot(lhs_ref[...], basis_ref[...])
    quarter = length // RADIX
    starts = [quarter * j1 for j1 in range(1, RADIX)]
    bases = [pl.multiple_of(s // LANES * LANES, LANES) for s in starts]
    shifts = [s - b for s, b in zip(starts, bases)]
    wide = z.points + LANES
    field_ref[:, wide:] = jnp.zeros((z.levels, z.lons + LANES - wide), BF16)
    lane = iota((STRIP, LANES), 1)
    zero = jnp.zeros((STRIP, LANES), F32)
    sent = []
    for at in range(0, z.levels, STRIP):
        rows = slice(at, at + STRIP)
        cos1, cos2, cos3 = [twiddle_ref[r : r + 1, :] for r in (1, 2, 3)]
        sin1, sin2, sin3 = [twiddle_ref[RADIX + r : RADIX + r + 1, :] for r in (1, 2, 3)]
        w0, re1, im1, re2, im2, re3, im3 = [
            parts_ref[i * z.levels + at : i * z.levels + at + STRIP] for i in range(2 * RADIX - 1)
        ]
        w2 = re2 * cos2 - im2 * sin2
        cross = (re1 * cos1 - im1 * sin1) + (re3 * cos3 - im3 * sin3)
        turn = (re1 * sin1 + im1 * cos1) - (re3 * sin3 + im3 * cos3)
        even, odd = w0 + w2, w0 - w2
        field_ref[rows, :wide] = jnp.concatenate([even + cross, zero], axis=1).astype(BF16)
        for base, shift, part in zip(bases, shifts, (odd - turn, even - cross, odd + turn)):
            tiles = [pltpu.roll(part[:, c : c + LANES], shift, 1) for c in range(0, z.points, LANES)]
            moved = [jnp.where(lane < shift, a, b) for a, b in zip([zero] + tiles, tiles + [zero])]
            moved[0] = moved[0] + field_ref[rows, pl.ds(base, LANES)].astype(F32)
            field_ref[rows, pl.ds(base, wide)] = jnp.concatenate(moved, axis=1).astype(BF16)
        sent += fetch(
            (field_ref.at[pl.ds(at, STRIP), pl.ds(0, z.lons)],),
            (out_ref.at[0, 0, pl.ds(at, STRIP)],),
            sems.at[pl.ds(at // STRIP, 1)],
        )
    for copy in sent:
        copy.wait()


def body(z, control, row_order, row_length, vertical, amplitude, meridional, balance):
    arguments = (row_order, row_length, amplitude, vertical, meridional, balance, control)
    made = (
        jax.ShapeDtypeStruct((z.devices, z.rows, LANES), BF16),
        jax.ShapeDtypeStruct((z.params, LANES), BF16),
        jax.ShapeDtypeStruct((2 * z.kaps, z.points), BF16),
        jax.ShapeDtypeStruct((2 * RADIX + SUBLANES, z.points), F32),
    )
    packets, params, basis, twiddle = pl.pallas_call(
        functools.partial(analysis_kernel, z),
        out_shape=made,
        in_specs=[HBM] * len(arguments),
        out_specs=(HBM,) * len(made),
        scratch_shapes=[
            *[pltpu.SMEM(x.shape, x.dtype) for x in arguments[:2]],
            *[pltpu.VMEM(x.shape, x.dtype) for x in arguments[2:]],
            *[pltpu.VMEM(x.shape, x.dtype) for x in made],
            pltpu.SemaphoreType.DMA((len(arguments),)),
            pltpu.SemaphoreType.DMA((RADIX + 4,)),
            pltpu.VMEM((z.levels, z.lons + LANES), F32),
            pltpu.VMEM((2 * RADIX * z.levels, z.points), BF16),
            pltpu.VMEM((2 * z.heads, z.points), F32),
            pltpu.VMEM((z.waves, LANES), F32),
        ],
        compiler_params=ALL_VMEM,
        name="analysis",
    )(*arguments)
    given = [params]
    for step in range(1, z.var):
        given.append(lax.ppermute(params, "var", [((i + step) % z.var, i) for i in range(z.var)]))
    packets = lax.all_to_all(packets, ("var", "lat"), 0, 0, tiled=True)
    mix, lift = pl.pallas_call(
        functools.partial(matrices_kernel, z),
        out_shape=(
            jax.ShapeDtypeStruct((z.var, z.mixed, z.mixed), BF16),
            jax.ShapeDtypeStruct((z.var - 1, LANES, LANES), BF16),
        ),
        in_specs=[VMEM] * z.var,
        out_specs=(VMEM, VMEM),
        scratch_shapes=[pltpu.VMEM((z.var, z.params, LANES), BF16)],
        compiler_params=PARAMS,
        cost_estimate=pl.CostEstimate(flops=10**8, bytes_accessed=10**6, transcendentals=0),
        name="matrices",
    )(*given)
    balanced = pl.pallas_call(
        functools.partial(mixing_kernel, z),
        out_shape=jax.ShapeDtypeStruct((z.var, z.lat, z.rows, LANES), BF16),
        in_specs=[VMEM] * 3,
        out_specs=VMEM,
        compiler_params=PARAMS,
        name="mixing",
    )(packets.reshape(z.var, z.lat, z.rows, LANES), mix, lift)
    balanced = balanced.reshape(z.devices, z.rows, LANES)
    balanced = lax.all_to_all(balanced, ("var", "lat"), 0, 0, tiled=True)
    return pl.pallas_call(
        functools.partial(synthesis_kernel, z),
        out_shape=jax.ShapeDtypeStruct(control.shape, BF16),
        in_specs=[VMEM] * 3,
        out_specs=HBM,
        scratch_shapes=[
            pltpu.SemaphoreType.DMA((z.levels // STRIP,)),
            pltpu.VMEM((z.levels, z.lons + LANES), BF16),
            pltpu.VMEM(((2 * RADIX - 1) * z.levels, 2 * z.kaps), BF16),
            pltpu.VMEM(((2 * RADIX - 1) * z.levels, z.points), F32),
        ],
        compiler_params=PARAMS,
        name="synthesis",
    )(balanced, basis, twiddle)


def solution(mesh):
    placed = (
        P("var", "lat", None, None),
        P(),
        P(),
        P("var", None, None),
        P("var", None),
        P("var", None, None),
        P("var", None, None),
    )

    def run(control, row_order, row_length, vertical, amplitude, meridional, balance):
        lat_total, var_total = mesh.shape["lat"], mesh.shape["var"]
        assert control.shape[0] == var_total and control.shape[1] == lat_total
        z = Sizes(lat_total, var_total, control.shape[2], control.shape[3], amplitude.shape[1])
        return jax.shard_map(
            functools.partial(body, z),
            mesh=mesh,
            in_specs=placed,
            out_specs=P("var", "lat", None, None),
            check_vma=False,
        )(control, row_order, row_length, vertical, amplitude, meridional, balance)

    return run
```

```python
import functools
import math

import jax
import jax.numpy as jnp
from jax import lax
from jax.experimental import pallas as pl
from jax.experimental.pallas import tpu as pltpu
from jax.sharding import PartitionSpec as P

RADIX = 4
LANES = 128
SUBLANES = 8
STRIP = 16
F32 = jnp.float32
BF16 = jnp.bfloat16

COS_POLY = (1, -19.7392044, 64.9391174, -85.4501419, 60.1676292, -25.9675999, 6.52865839)
SIN_POLY = (6.28318501, -41.3415909, 81.5999451, -76.6144714, 41.3428841, -12.4712439)

VMEM = pl.BlockSpec(memory_space=pltpu.VMEM)
HBM = pl.BlockSpec(memory_space=pltpu.HBM)
PARAMS = pltpu.CompilerParams(vmem_limit_bytes=32 * 1024 * 1024)
ALL_VMEM = pltpu.CompilerParams(vmem_limit_bytes=58 * 1024 * 1024)


def iota(shape, dim):
    return lax.broadcasted_iota(jnp.int32, shape, dim)


def horner(poly, x):
    total = jnp.full_like(x, poly[-1])
    for term in poly[-2::-1]:
        total = total * x + term
    return total


def cos_sin(turns):
    turns = turns - jnp.round(turns)
    square = turns * turns
    return horner(COS_POLY, square), horner(SIN_POLY, square) * turns


def ceil_div(a, b):
    return -(-a // b)


def round_up(a, b):
    return ceil_div(a, b) * b


def dot(a, b, contract=((1,), (0,))):
    return lax.dot_general(a, b, (contract, ((), ())), preferred_element_type=F32)


class Sizes:
    def __init__(self, lat_total, var_total, levels, lons, waves):
        self.lat, self.var, self.levels, self.lons, self.waves = lat_total, var_total, levels, lons, waves
        self.clans = math.gcd(var_total, 2)
        self.kin = var_total // self.clans
        self.devices = lat_total * self.kin
        self.points = lons // RADIX
        self.kaps = waves // RADIX
        self.rows = round_up(ceil_div(waves, self.devices), SUBLANES)
        assert self.kaps % self.rows == 0 and 2 * levels == LANES and lat_total <= LANES
        self.mixed = lat_total * self.rows
        self.heads = round_up(ceil_div(self.kaps, STRIP), SUBLANES)
        self.params = round_up(levels + lat_total, STRIP)


def own_length(order_ref, length_ref):
    slot = lax.axis_index("lat")
    row = order_ref[slot]
    return slot, row, length_ref[row]


def fetch(sources, targets, sems):
    copies = [pltpu.make_async_copy(s, t, sems.at[i]) for i, (s, t) in enumerate(zip(sources, targets))]
    for copy in copies:
        copy.start()
    return copies


def slot_matrix(z, order_ref, mer_ref):
    slot = iota((z.lat, z.lat), 0)
    row = jnp.zeros((z.lat, z.lat), jnp.int32)
    for t in range(z.lat):
        row = jnp.where(slot == t, order_ref[t], row)
    pick = (row == iota((z.lat, z.lat), 1)).astype(F32).astype(BF16)
    return dot(dot(pick, mer_ref[0]).astype(BF16), pick, ((1,), (1,)))


def analysis_kernel(z, *refs):
    given, outs, held, made = refs[:7], refs[7:11], refs[11:18], refs[18:22]
    sems, out_sems, field_ref, parts_ref, heads_ref, scale_ref = refs[22:]
    order_ref, length_ref, amp_ref, vert_ref, mer_ref, bal_ref, control_ref = held
    packet_ref, params_ref, basis_ref, twiddle_ref = made
    packet_out = outs[0]
    copies = fetch(given, held, sems)
    field_ref[:, z.lons :] = jnp.zeros((z.levels, LANES), F32)
    params_ref[...] = jnp.zeros(params_ref.shape, BF16)
    for copy in copies[:2]:
        copy.wait()
    slot, row, length = own_length(order_ref, length_ref)
    quarter = length // RADIX
    points = iota((1, z.points), 1)
    inside = points < quarter
    step = points.astype(F32) / jnp.full((1, z.points), quarter, jnp.int32).astype(F32)
    tail_cos, tail_sin = cos_sin(iota((STRIP, z.points), 0).astype(F32) * step)
    head_cos, head_sin = cos_sin(iota((z.heads, z.points), 0).astype(F32) * STRIP * step)
    heads_ref[: z.heads] = jnp.where(inside, head_cos, 0.0)
    heads_ref[z.heads :] = jnp.where(inside, head_sin, 0.0)
    for at in range(0, z.kaps, STRIP):
        head = at // STRIP
        head_cos, head_sin = heads_ref[head : head + 1], heads_ref[z.heads + head : z.heads + head + 1]
        basis_ref[at : at + STRIP, :] = (head_cos * tail_cos - head_sin * tail_sin).astype(BF16)
        basis_ref[z.kaps + at : z.kaps + at + STRIP, :] = (head_sin * tail_cos + head_cos * tail_sin).astype(BF16)
    tw_row = iota((2 * RADIX, z.points), 0)
    period = jnp.full((1, z.points), length, jnp.int32).astype(F32)
    tw_cos, tw_sin = cos_sin((tw_row % RADIX).astype(F32) * (points.astype(F32) / period))
    twiddle_ref[: 2 * RADIX] = jnp.where(tw_row < RADIX, tw_cos, tw_sin)
    twiddle_ref[2 * RADIX :] = jnp.broadcast_to(period, (SUBLANES, z.points))
    for copy in copies[2:6]:
        copy.wait()
    group = LANES // RADIX
    for r in range(RADIX):
        picked = iota((group, LANES), 1) == iota((group, LANES), 0) * RADIX + r
        for at in range(0, z.kaps, group):
            lanes = slice(at * RADIX, at * RADIX + LANES)
            amp = jnp.sum(jnp.where(picked, amp_ref[:, lanes], 0.0), axis=1, keepdims=True)
            wave = (at + iota((group, LANES), 0)) * RADIX + r
            weight = jnp.where(wave == 0, 1.0, 2.0) / period[:, :LANES]
            weight = jnp.where(wave <= (length - 1) // 2, weight, 0.0)
            scale_ref[r * z.kaps + at : r * z.kaps + at + group] = weight * amp
    params_ref[: z.levels] = jnp.concatenate([bal_ref[0], bal_ref[0]], axis=1)
    params_ref[z.levels : z.levels + z.lat, : z.lat] = slot_matrix(z, order_ref, mer_ref).astype(BF16)
    sent = fetch(made[1:], outs[1:], out_sems.at[pl.ds(RADIX, 3)])
    copies[6].wait()
    field_ref[:, : z.lons] = dot(vert_ref[0], control_ref[0, 0])
    starts = [quarter * j1 for j1 in range(1, RADIX)]
    bases = [pl.multiple_of(s // LANES * LANES, LANES) for s in starts]
    shifts = [(LANES - (s - b)) % LANES for s, b in zip(starts, bases)]
    lane = iota((STRIP, LANES), 1)
    for at in range(0, z.levels, STRIP):
        rows = slice(at, at + STRIP)

        def quarter_of(base, shift):
            wide = field_ref[rows, pl.ds(base, z.points + LANES)]
            tiles = [pltpu.roll(wide[:, c : c + LANES], shift, 1) for c in range(0, z.points + LANES, LANES)]
            keep = (lane < shift) | (shift == 0)
            return jnp.concatenate([jnp.where(keep, a, b) for a, b in zip(tiles, tiles[1:])], axis=1)

        first = field_ref[rows, : z.points]
        second, third, fourth = [quarter_of(b, s) for b, s in zip(bases, shifts)]
        even, odd = first + third, second + fourth
        real, imag = first - third, second - fourth
        cos1, cos2, cos3 = [twiddle_ref[r : r + 1, :] for r in (1, 2, 3)]
        sin1, sin2, sin3 = [twiddle_ref[RADIX + r : RADIX + r + 1, :] for r in (1, 2, 3)]
        turned = even - odd
        parts = (
            (even + odd, jnp.zeros((STRIP, z.points), F32)),
            (real * cos1 - imag * sin1, real * sin1 + imag * cos1),
            (turned * cos2, turned * sin2),
            (real * cos3 + imag * sin3, real * sin3 - imag * cos3),
        )
        for r, pair in enumerate(parts):
            for half, part in enumerate(pair):
                to = (2 * r + half) * z.levels + at
                parts_ref[to : to + STRIP, :] = part.astype(BF16)
    count = z.kaps // z.rows
    sign = jnp.where(iota((1, LANES), 1) < z.levels, -1.0, 1.0).astype(F32)
    for pair in range(0, RADIX, 2):
        product = dot(basis_ref[...], parts_ref[pair * LANES : (pair + 2) * LANES], ((1,), (1,)))
        for r in range(pair, pair + 2):
            lanes = slice((r - pair) * LANES, (r - pair + 1) * LANES)
            both = product[: z.kaps, lanes] + pltpu.roll(product[z.kaps :, lanes], z.levels, 1) * sign
            both = (both * scale_ref[r * z.kaps : (r + 1) * z.kaps]).reshape(count, z.rows, LANES)
            for i in range(count):
                packet_ref[r * count + i] = both[i].astype(BF16)
            part = pl.ds(r * count, count)
            sent += fetch((packet_ref.at[part],), (packet_out.at[part],), out_sems.at[pl.ds(r, 1)])
    if z.devices > RADIX * count:
        for i in range(RADIX * count, z.devices):
            packet_ref[i] = jnp.zeros((z.rows, LANES), BF16)
        part = pl.ds(RADIX * count, z.devices - RADIX * count)
        sent += fetch((packet_ref.at[part],), (packet_out.at[part],), out_sems.at[pl.ds(RADIX + 3, 1)])
    for copy in sent:
        copy.wait()


def matrices_kernel(z, *refs):
    *given, mix_ref, bal_ref, all_ref = refs
    own = lax.axis_index("var")
    for step, ref in enumerate(given):
        all_ref[(own // z.clans + step) % z.kin] = ref[...]
    size = z.mixed
    to_cols = (iota((z.lat, size), 0) == iota((z.lat, size), 1) // z.rows).astype(F32).astype(BF16)
    same = iota((size, size), 0) % z.rows == iota((size, size), 1) % z.rows
    halves = iota((LANES, LANES), 0) // z.levels == iota((LANES, LANES), 1) // z.levels
    for a in range(z.kin):
        meridional = all_ref[a, z.levels :].astype(F32)[: z.lat, : z.lat].astype(BF16)
        slot_cols = dot(meridional, to_cols).astype(BF16)
        mix_ref[a] = jnp.where(same, dot(to_cols, slot_cols, ((0,), (0,))), 0.0).astype(BF16)
        balance = all_ref[a, : z.levels].astype(F32)
        used = halves if a > 0 else halves & (own % z.clans > 0)
        balance = jnp.where(used, jnp.concatenate([balance, balance], axis=0), 0.0)
        bal_ref[a] = balance.T.astype(BF16)


def mixing_kernel(z, packet_ref, mix_ref, *out_refs):
    for a in range(z.kin):
        coeffs = packet_ref[a].astype(F32).reshape(z.mixed, LANES).astype(BF16)
        out_refs[a][...] = dot(mix_ref[a], coeffs).astype(BF16)


def balance_kernel(z, bal_ref, *refs):
    blended_refs, other_refs, out_ref = refs[: z.kin], refs[z.kin : -1], refs[-1]
    stream = blended_refs[0][...]
    for b, ref in enumerate(other_refs):
        stream = jnp.where(lax.axis_index("var") % z.clans == b + 1, ref[...], stream)
    for a in range(z.kin):
        balanced = blended_refs[a][...].astype(F32) + dot(stream, bal_ref[a])
        balanced = balanced.reshape(z.lat, z.rows, LANES)
        for s in range(z.lat):
            out_ref[a, s] = balanced[s].astype(BF16)


def synthesis_kernel(z, spectra_ref, basis_ref, twiddle_ref, out_ref, sems, field_ref, lhs_ref, parts_ref):
    period = twiddle_ref[2 * RADIX :, :LANES].astype(jnp.int32)
    length = jnp.max(period)
    used = z.waves // z.rows
    spectra = spectra_ref[:used].astype(F32).reshape(z.waves, LANES)
    at = iota((z.waves, LANES), 0)
    wave = at % z.kaps * RADIX + at // z.kaps
    spectra = jnp.where(wave <= (period[0:1] - 1) // 2, spectra, 0.0)
    sign = jnp.where(iota((1, LANES), 1) < z.levels, 1.0, -1.0).astype(F32)
    for r in range(RADIX):
        part = spectra[r * z.kaps : (r + 1) * z.kaps]
        part = jnp.concatenate([part * sign, pltpu.roll(part, z.levels, 1)], axis=0).T.astype(BF16)
        if r == 0:
            lhs_ref[: z.levels] = part[: z.levels]
        else:
            lhs_ref[(2 * r - 1) * z.levels : (2 * r + 1) * z.levels] = part
    parts_ref[...] = dot(lhs_ref[...], basis_ref[...])
    quarter = length // RADIX
    starts = [quarter * j1 for j1 in range(1, RADIX)]
    bases = [pl.multiple_of(s // LANES * LANES, LANES) for s in starts]
    shifts = [s - b for s, b in zip(starts, bases)]
    wide = z.points + LANES
    field_ref[:, wide:] = jnp.zeros((z.levels, z.lons + LANES - wide), BF16)
    lane = iota((STRIP, LANES), 1)
    zero = jnp.zeros((STRIP, LANES), F32)
    sent = []
    for at in range(0, z.levels, STRIP):
        rows = slice(at, at + STRIP)
        cos1, cos2, cos3 = [twiddle_ref[r : r + 1, :] for r in (1, 2, 3)]
        sin1, sin2, sin3 = [twiddle_ref[RADIX + r : RADIX + r + 1, :] for r in (1, 2, 3)]
        w0, re1, im1, re2, im2, re3, im3 = [
            parts_ref[i * z.levels + at : i * z.levels + at + STRIP] for i in range(2 * RADIX - 1)
        ]
        w2 = re2 * cos2 - im2 * sin2
        cross = (re1 * cos1 - im1 * sin1) + (re3 * cos3 - im3 * sin3)
        turn = (re1 * sin1 + im1 * cos1) - (re3 * sin3 + im3 * cos3)
        even, odd = w0 + w2, w0 - w2
        field_ref[rows, :wide] = jnp.concatenate([even + cross, zero], axis=1).astype(BF16)
        for base, shift, part in zip(bases, shifts, (odd - turn, even - cross, odd + turn)):
            tiles = [pltpu.roll(part[:, c : c + LANES], shift, 1) for c in range(0, z.points, LANES)]
            moved = [jnp.where(lane < shift, a, b) for a, b in zip([zero] + tiles, tiles + [zero])]
            moved[0] = moved[0] + field_ref[rows, pl.ds(base, LANES)].astype(F32)
            field_ref[rows, pl.ds(base, wide)] = jnp.concatenate(moved, axis=1).astype(BF16)
        sent += fetch(
            (field_ref.at[pl.ds(at, STRIP), pl.ds(0, z.lons)],),
            (out_ref.at[0, 0, pl.ds(at, STRIP)],),
            sems.at[pl.ds(at // STRIP, 1)],
        )
    for copy in sent:
        copy.wait()


def exchange(z, packets):
    clans = [
        [(a * z.clans + b) * z.lat + slot for a in range(z.kin) for slot in range(z.lat)] for b in range(z.clans)
    ]
    return lax.all_to_all(packets, ("var", "lat"), 0, 0, axis_index_groups=clans, tiled=True)


def body(z, control, row_order, row_length, vertical, amplitude, meridional, balance):
    arguments = (row_order, row_length, amplitude, vertical, meridional, balance, control)
    made = (
        jax.ShapeDtypeStruct((z.devices, z.rows, LANES), BF16),
        jax.ShapeDtypeStruct((z.params, LANES), BF16),
        jax.ShapeDtypeStruct((2 * z.kaps, z.points), BF16),
        jax.ShapeDtypeStruct((2 * RADIX + SUBLANES, z.points), F32),
    )
    packets, params, basis, twiddle = pl.pallas_call(
        functools.partial(analysis_kernel, z),
        out_shape=made,
        in_specs=[HBM] * len(arguments),
        out_specs=(HBM,) * len(made),
        scratch_shapes=[
            *[pltpu.SMEM(x.shape, x.dtype) for x in arguments[:2]],
            *[pltpu.VMEM(x.shape, x.dtype) for x in arguments[2:]],
            *[pltpu.VMEM(x.shape, x.dtype) for x in made],
            pltpu.SemaphoreType.DMA((len(arguments),)),
            pltpu.SemaphoreType.DMA((RADIX + 4,)),
            pltpu.VMEM((z.levels, z.lons + LANES), F32),
            pltpu.VMEM((2 * RADIX * z.levels, z.points), BF16),
            pltpu.VMEM((2 * z.heads, z.points), F32),
            pltpu.VMEM((z.waves, LANES), F32),
        ],
        compiler_params=ALL_VMEM,
        name="analysis",
    )(*arguments)
    given = [params]
    for step in range(z.clans, z.var, z.clans):
        given.append(lax.ppermute(params, "var", [((i + step) % z.var, i) for i in range(z.var)]))
    packets = exchange(z, packets)
    mix, lift = pl.pallas_call(
        functools.partial(matrices_kernel, z),
        out_shape=(
            jax.ShapeDtypeStruct((z.kin, z.mixed, z.mixed), BF16),
            jax.ShapeDtypeStruct((z.kin, LANES, LANES), BF16),
        ),
        in_specs=[VMEM] * z.kin,
        out_specs=(VMEM, VMEM),
        scratch_shapes=[pltpu.VMEM((z.kin, z.params, LANES), BF16)],
        compiler_params=PARAMS,
        cost_estimate=pl.CostEstimate(flops=10**8, bytes_accessed=10**6, transcendentals=0),
        name="matrices",
    )(*given)
    blended = pl.pallas_call(
        functools.partial(mixing_kernel, z),
        out_shape=[jax.ShapeDtypeStruct((z.mixed, LANES), BF16)] * z.kin,
        in_specs=[VMEM] * 2,
        out_specs=[VMEM] * z.kin,
        compiler_params=PARAMS,
        name="mixing",
    )(packets.reshape(z.kin, z.lat, z.rows, LANES), mix)
    streams = [
        lax.ppermute(blended[0], "var", [(v, v + b) for v in range(0, z.var, z.clans)]) for b in range(1, z.clans)
    ]
    balanced = pl.pallas_call(
        functools.partial(balance_kernel, z),
        out_shape=jax.ShapeDtypeStruct((z.kin, z.lat, z.rows, LANES), BF16),
        in_specs=[VMEM] * (1 + z.kin + len(streams)),
        out_specs=VMEM,
        compiler_params=PARAMS,
        name="balance",
    )(lift, *blended, *streams)
    balanced = exchange(z, balanced.reshape(z.devices, z.rows, LANES))
    return pl.pallas_call(
        functools.partial(synthesis_kernel, z),
        out_shape=jax.ShapeDtypeStruct(control.shape, BF16),
        in_specs=[VMEM] * 3,
        out_specs=HBM,
        scratch_shapes=[
            pltpu.SemaphoreType.DMA((z.levels // STRIP,)),
            pltpu.VMEM((z.levels, z.lons + LANES), BF16),
            pltpu.VMEM(((2 * RADIX - 1) * z.levels, 2 * z.kaps), BF16),
            pltpu.VMEM(((2 * RADIX - 1) * z.levels, z.points), F32),
        ],
        compiler_params=PARAMS,
        name="synthesis",
    )(balanced, basis, twiddle)


def solution(mesh):
    placed = (
        P("var", "lat", None, None),
        P(),
        P(),
        P("var", None, None),
        P("var", None),
        P("var", None, None),
        P("var", None, None),
    )

    def run(control, row_order, row_length, vertical, amplitude, meridional, balance):
        lat_total, var_total = mesh.shape["lat"], mesh.shape["var"]
        assert control.shape[0] == var_total and control.shape[1] == lat_total
        z = Sizes(lat_total, var_total, control.shape[2], control.shape[3], amplitude.shape[1])
        return jax.shard_map(
            functools.partial(body, z),
            mesh=mesh,
            in_specs=placed,
            out_specs=P("var", "lat", None, None),
            check_vma=False,
        )(control, row_order, row_length, vertical, amplitude, meridional, balance)

    return run
```

```python
import functools

import jax
import jax.numpy as jnp
from jax import lax
from jax.experimental import pallas as pl
from jax.experimental.pallas import tpu as pltpu
from jax.sharding import PartitionSpec as P

RADIX = 4
LANES = 128
SUBLANES = 8
STRIP = 16
F32 = jnp.float32
BF16 = jnp.bfloat16

COS_POLY = (1, -19.7392044, 64.9391174, -85.4501419, 60.1676292, -25.9675999, 6.52865839)
SIN_POLY = (6.28318501, -41.3415909, 81.5999451, -76.6144714, 41.3428841, -12.4712439)

VMEM = pl.BlockSpec(memory_space=pltpu.VMEM)
HBM = pl.BlockSpec(memory_space=pltpu.HBM)
PARAMS = pltpu.CompilerParams(vmem_limit_bytes=32 * 1024 * 1024)


def iota(shape, dim):
    return lax.broadcasted_iota(jnp.int32, shape, dim)


def horner(poly, x):
    total = jnp.full_like(x, poly[-1])
    for term in poly[-2::-1]:
        total = total * x + term
    return total


def cos_sin(turns):
    turns = turns - jnp.round(turns)
    square = turns * turns
    return horner(COS_POLY, square), horner(SIN_POLY, square) * turns


def ceil_div(a, b):
    return -(-a // b)


def round_up(a, b):
    return ceil_div(a, b) * b


def dot(a, b, contract=((1,), (0,))):
    return lax.dot_general(a, b, (contract, ((), ())), preferred_element_type=F32)


class Sizes:
    def __init__(self, lat_total, var_total, levels, lons, waves):
        self.lat, self.var, self.levels, self.lons, self.waves = lat_total, var_total, levels, lons, waves
        self.devices = lat_total * var_total
        self.points = lons // RADIX
        self.kaps = waves // RADIX
        self.rows = round_up(ceil_div(waves, self.devices), SUBLANES)
        assert self.kaps % self.rows == 0 and 2 * levels == LANES and lat_total <= LANES
        self.mixed = lat_total * self.rows
        self.heads = round_up(ceil_div(self.kaps, STRIP), SUBLANES)
        self.params = round_up(levels + lat_total, STRIP)


def own_length(order_ref, length_ref):
    slot = lax.axis_index("lat")
    row = order_ref[slot]
    return slot, row, length_ref[row]


def fetch(sources, targets, sems):
    copies = [pltpu.make_async_copy(s, t, sems.at[i]) for i, (s, t) in enumerate(zip(sources, targets))]
    for copy in copies:
        copy.start()
    return copies


def slot_matrix(z, order_ref, mer_ref):
    slot = iota((z.lat, z.lat), 0)
    row = jnp.zeros((z.lat, z.lat), jnp.int32)
    for t in range(z.lat):
        row = jnp.where(slot == t, order_ref[t], row)
    pick = (row == iota((z.lat, z.lat), 1)).astype(F32).astype(BF16)
    return dot(dot(pick, mer_ref[0]).astype(BF16), pick, ((1,), (1,)))


def analysis_kernel(z, *refs):
    given, made, held = refs[:7], refs[7:11], refs[11:18]
    sems, field_ref, parts_ref, heads_ref, scale_ref = refs[18:]
    order_ref, length_ref, amp_ref, vert_ref, mer_ref, bal_ref, control_ref = held
    packet_ref, params_ref, basis_ref, twiddle_ref = made
    copies = fetch(given, held, sems)
    field_ref[:, z.lons :] = jnp.zeros((z.levels, LANES), F32)
    params_ref[...] = jnp.zeros(params_ref.shape, BF16)
    for copy in copies[:2]:
        copy.wait()
    slot, row, length = own_length(order_ref, length_ref)
    quarter = length // RADIX
    points = iota((1, z.points), 1)
    inside = points < quarter
    step = points.astype(F32) / jnp.full((1, z.points), quarter, jnp.int32).astype(F32)
    tail_cos, tail_sin = cos_sin(iota((STRIP, z.points), 0).astype(F32) * step)
    head_cos, head_sin = cos_sin(iota((z.heads, z.points), 0).astype(F32) * STRIP * step)
    heads_ref[: z.heads] = jnp.where(inside, head_cos, 0.0)
    heads_ref[z.heads :] = jnp.where(inside, head_sin, 0.0)
    for at in range(0, z.kaps, STRIP):
        head = at // STRIP
        head_cos, head_sin = heads_ref[head : head + 1], heads_ref[z.heads + head : z.heads + head + 1]
        basis_ref[at : at + STRIP, :] = (head_cos * tail_cos - head_sin * tail_sin).astype(BF16)
        basis_ref[z.kaps + at : z.kaps + at + STRIP, :] = (head_sin * tail_cos + head_cos * tail_sin).astype(BF16)
    tw_row = iota((2 * RADIX, z.points), 0)
    period = jnp.full((1, z.points), length, jnp.int32).astype(F32)
    tw_cos, tw_sin = cos_sin((tw_row % RADIX).astype(F32) * (points.astype(F32) / period))
    twiddle_ref[: 2 * RADIX] = jnp.where(tw_row < RADIX, tw_cos, tw_sin)
    twiddle_ref[2 * RADIX :] = jnp.broadcast_to(period, (SUBLANES, z.points))
    for copy in copies[2:6]:
        copy.wait()
    group = LANES // RADIX
    for r in range(RADIX):
        picked = iota((group, LANES), 1) == iota((group, LANES), 0) * RADIX + r
        for at in range(0, z.kaps, group):
            lanes = slice(at * RADIX, at * RADIX + LANES)
            amp = jnp.sum(jnp.where(picked, amp_ref[:, lanes], 0.0), axis=1, keepdims=True)
            wave = (at + iota((group, LANES), 0)) * RADIX + r
            weight = jnp.where(wave == 0, 1.0, 2.0) / period[:, :LANES]
            weight = jnp.where(wave <= (length - 1) // 2, weight, 0.0)
            scale_ref[r * z.kaps + at : r * z.kaps + at + group] = weight * amp
    params_ref[: z.levels] = jnp.concatenate([bal_ref[0], bal_ref[0]], axis=1)
    params_ref[z.levels : z.levels + z.lat, : z.lat] = slot_matrix(z, order_ref, mer_ref).astype(BF16)
    copies[6].wait()
    field_ref[:, : z.lons] = dot(vert_ref[0], control_ref[0, 0])
    starts = [quarter * j1 for j1 in range(1, RADIX)]
    bases = [pl.multiple_of(s // LANES * LANES, LANES) for s in starts]
    shifts = [(LANES - (s - b)) % LANES for s, b in zip(starts, bases)]
    lane = iota((STRIP, LANES), 1)
    for at in range(0, z.levels, STRIP):
        rows = slice(at, at + STRIP)

        def quarter_of(base, shift):
            wide = field_ref[rows, pl.ds(base, z.points + LANES)]
            tiles = [pltpu.roll(wide[:, c : c + LANES], shift, 1) for c in range(0, z.points + LANES, LANES)]
            keep = (lane < shift) | (shift == 0)
            return jnp.concatenate([jnp.where(keep, a, b) for a, b in zip(tiles, tiles[1:])], axis=1)

        first = field_ref[rows, : z.points]
        second, third, fourth = [quarter_of(b, s) for b, s in zip(bases, shifts)]
        even, odd = first + third, second + fourth
        real, imag = first - third, second - fourth
        cos1, cos2, cos3 = [twiddle_ref[r : r + 1, :] for r in (1, 2, 3)]
        sin1, sin2, sin3 = [twiddle_ref[RADIX + r : RADIX + r + 1, :] for r in (1, 2, 3)]
        turned = even - odd
        parts = (
            (even + odd, jnp.zeros((STRIP, z.points), F32)),
            (real * cos1 - imag * sin1, real * sin1 + imag * cos1),
            (turned * cos2, turned * sin2),
            (real * cos3 + imag * sin3, real * sin3 - imag * cos3),
        )
        for r, pair in enumerate(parts):
            for half, part in enumerate(pair):
                to = (2 * r + half) * z.levels + at
                parts_ref[to : to + STRIP, :] = part.astype(BF16)
    count = z.kaps // z.rows
    sign = jnp.where(iota((1, LANES), 1) < z.levels, -1.0, 1.0).astype(F32)
    for pair in range(0, RADIX, 2):
        product = dot(basis_ref[...], parts_ref[pair * LANES : (pair + 2) * LANES], ((1,), (1,)))
        for r in range(pair, pair + 2):
            lanes = slice((r - pair) * LANES, (r - pair + 1) * LANES)
            both = product[: z.kaps, lanes] + pltpu.roll(product[z.kaps :, lanes], z.levels, 1) * sign
            both = (both * scale_ref[r * z.kaps : (r + 1) * z.kaps]).reshape(count, z.rows, LANES)
            for i in range(count):
                packet_ref[r * count + i] = both[i].astype(BF16)
    for i in range(RADIX * count, z.devices):
        packet_ref[i] = jnp.zeros((z.rows, LANES), BF16)


def matrices_kernel(z, *refs):
    *given, mix_ref, bal_ref, all_ref = refs
    own = lax.axis_index("var")
    for step, ref in enumerate(given):
        all_ref[(own + step) % z.var] = ref[...]
    size = z.mixed
    to_cols = (iota((z.lat, size), 0) == iota((z.lat, size), 1) // z.rows).astype(F32).astype(BF16)
    same = iota((size, size), 0) % z.rows == iota((size, size), 1) % z.rows
    halves = iota((LANES, LANES), 0) // z.levels == iota((LANES, LANES), 1) // z.levels
    for v in range(z.var):
        meridional = all_ref[v, z.levels :].astype(F32)[: z.lat, : z.lat].astype(BF16)
        slot_cols = dot(meridional, to_cols).astype(BF16)
        mix_ref[v] = jnp.where(same, dot(to_cols, slot_cols, ((0,), (0,))), 0.0).astype(BF16)
        if v > 0:
            balance = all_ref[v, : z.levels].astype(F32)
            balance = jnp.where(halves, jnp.concatenate([balance, balance], axis=0), 0.0)
            bal_ref[v - 1] = balance.T.astype(BF16)


def mixing_kernel(z, packet_ref, mix_ref, bal_ref, out_ref):
    stream = None
    for v in range(z.var):
        coeffs = packet_ref[v].astype(F32).reshape(z.mixed, LANES).astype(BF16)
        blended = dot(mix_ref[v], coeffs)
        if v == 0:
            stream = blended.astype(BF16)
        else:
            blended = blended + dot(stream, bal_ref[v - 1])
        blended = blended.reshape(z.lat, z.rows, LANES)
        for s in range(z.lat):
            out_ref[v, s] = blended[s].astype(BF16)


def synthesis_kernel(z, spectra_ref, basis_ref, twiddle_ref, out_ref, sems, field_ref, lhs_ref, parts_ref):
    period = twiddle_ref[2 * RADIX :, :LANES].astype(jnp.int32)
    length = jnp.max(period)
    used = z.waves // z.rows
    spectra = spectra_ref[:used].astype(F32).reshape(z.waves, LANES)
    at = iota((z.waves, LANES), 0)
    wave = at % z.kaps * RADIX + at // z.kaps
    spectra = jnp.where(wave <= (period[0:1] - 1) // 2, spectra, 0.0)
    sign = jnp.where(iota((1, LANES), 1) < z.levels, 1.0, -1.0).astype(F32)
    for r in range(RADIX):
        part = spectra[r * z.kaps : (r + 1) * z.kaps]
        part = jnp.concatenate([part * sign, pltpu.roll(part, z.levels, 1)], axis=0).T.astype(BF16)
        if r == 0:
            lhs_ref[: z.levels] = part[: z.levels]
        else:
            lhs_ref[(2 * r - 1) * z.levels : (2 * r + 1) * z.levels] = part
    parts_ref[...] = dot(lhs_ref[...], basis_ref[...])
    quarter = length // RADIX
    starts = [quarter * j1 for j1 in range(1, RADIX)]
    bases = [pl.multiple_of(s // LANES * LANES, LANES) for s in starts]
    shifts = [s - b for s, b in zip(starts, bases)]
    wide = z.points + LANES
    field_ref[:, wide:] = jnp.zeros((z.levels, z.lons + LANES - wide), BF16)
    lane = iota((STRIP, LANES), 1)
    zero = jnp.zeros((STRIP, LANES), F32)
    sent = []
    for at in range(0, z.levels, STRIP):
        rows = slice(at, at + STRIP)
        cos1, cos2, cos3 = [twiddle_ref[r : r + 1, :] for r in (1, 2, 3)]
        sin1, sin2, sin3 = [twiddle_ref[RADIX + r : RADIX + r + 1, :] for r in (1, 2, 3)]
        w0, re1, im1, re2, im2, re3, im3 = [
            parts_ref[i * z.levels + at : i * z.levels + at + STRIP] for i in range(2 * RADIX - 1)
        ]
        w2 = re2 * cos2 - im2 * sin2
        cross = (re1 * cos1 - im1 * sin1) + (re3 * cos3 - im3 * sin3)
        turn = (re1 * sin1 + im1 * cos1) - (re3 * sin3 + im3 * cos3)
        even, odd = w0 + w2, w0 - w2
        field_ref[rows, :wide] = jnp.concatenate([even + cross, zero], axis=1).astype(BF16)
        for base, shift, part in zip(bases, shifts, (odd - turn, even - cross, odd + turn)):
            tiles = [pltpu.roll(part[:, c : c + LANES], shift, 1) for c in range(0, z.points, LANES)]
            moved = [jnp.where(lane < shift, a, b) for a, b in zip([zero] + tiles, tiles + [zero])]
            moved[0] = moved[0] + field_ref[rows, pl.ds(base, LANES)].astype(F32)
            field_ref[rows, pl.ds(base, wide)] = jnp.concatenate(moved, axis=1).astype(BF16)
        sent += fetch(
            (field_ref.at[pl.ds(at, STRIP), pl.ds(0, z.lons)],),
            (out_ref.at[0, 0, pl.ds(at, STRIP)],),
            sems.at[pl.ds(at // STRIP, 1)],
        )
    for copy in sent:
        copy.wait()


def body(z, control, row_order, row_length, vertical, amplitude, meridional, balance):
    arguments = (row_order, row_length, amplitude, vertical, meridional, balance, control)
    made = (
        jax.ShapeDtypeStruct((z.devices, z.rows, LANES), BF16),
        jax.ShapeDtypeStruct((z.params, LANES), BF16),
        jax.ShapeDtypeStruct((2 * z.kaps, z.points), BF16),
        jax.ShapeDtypeStruct((2 * RADIX + SUBLANES, z.points), F32),
    )
    packets, params, basis, twiddle = pl.pallas_call(
        functools.partial(analysis_kernel, z),
        out_shape=made,
        in_specs=[HBM] * len(arguments),
        out_specs=(VMEM,) * len(made),
        scratch_shapes=[
            *[pltpu.SMEM(x.shape, x.dtype) for x in arguments[:2]],
            *[pltpu.VMEM(x.shape, x.dtype) for x in arguments[2:]],
            pltpu.SemaphoreType.DMA((len(arguments),)),
            pltpu.VMEM((z.levels, z.lons + LANES), F32),
            pltpu.VMEM((2 * RADIX * z.levels, z.points), BF16),
            pltpu.VMEM((2 * z.heads, z.points), F32),
            pltpu.VMEM((z.waves, LANES), F32),
        ],
        compiler_params=PARAMS,
        name="analysis",
    )(*[pltpu.with_memory_space_constraint(x, pltpu.HBM) for x in arguments])
    given = [params]
    for step in range(1, z.var):
        given.append(lax.ppermute(params, "var", [((i + step) % z.var, i) for i in range(z.var)]))
    packets = lax.all_to_all(packets, ("var", "lat"), 0, 0, tiled=True)
    mix, lift = pl.pallas_call(
        functools.partial(matrices_kernel, z),
        out_shape=(
            jax.ShapeDtypeStruct((z.var, z.mixed, z.mixed), BF16),
            jax.ShapeDtypeStruct((z.var - 1, LANES, LANES), BF16),
        ),
        in_specs=[VMEM] * z.var,
        out_specs=(VMEM, VMEM),
        scratch_shapes=[pltpu.VMEM((z.var, z.params, LANES), BF16)],
        compiler_params=PARAMS,
        cost_estimate=pl.CostEstimate(flops=10**8, bytes_accessed=10**6, transcendentals=0),
        name="matrices",
    )(*given)
    balanced = pl.pallas_call(
        functools.partial(mixing_kernel, z),
        out_shape=jax.ShapeDtypeStruct((z.var, z.lat, z.rows, LANES), BF16),
        in_specs=[VMEM] * 3,
        out_specs=VMEM,
        compiler_params=PARAMS,
        name="mixing",
    )(packets.reshape(z.var, z.lat, z.rows, LANES), mix, lift)
    balanced = balanced.reshape(z.devices, z.rows, LANES)
    balanced = lax.all_to_all(balanced, ("var", "lat"), 0, 0, tiled=True)
    return pl.pallas_call(
        functools.partial(synthesis_kernel, z),
        out_shape=jax.ShapeDtypeStruct(control.shape, BF16),
        in_specs=[VMEM] * 3,
        out_specs=HBM,
        scratch_shapes=[
            pltpu.SemaphoreType.DMA((z.levels // STRIP,)),
            pltpu.VMEM((z.levels, z.lons + LANES), BF16),
            pltpu.VMEM(((2 * RADIX - 1) * z.levels, 2 * z.kaps), BF16),
            pltpu.VMEM(((2 * RADIX - 1) * z.levels, z.points), F32),
        ],
        compiler_params=PARAMS,
        name="synthesis",
    )(balanced, basis, twiddle)


def solution(mesh):
    placed = (
        P("var", "lat", None, None),
        P(),
        P(),
        P("var", None, None),
        P("var", None),
        P("var", None, None),
        P("var", None, None),
    )

    def run(control, row_order, row_length, vertical, amplitude, meridional, balance):
        lat_total, var_total = mesh.shape["lat"], mesh.shape["var"]
        assert control.shape[0] == var_total and control.shape[1] == lat_total
        z = Sizes(lat_total, var_total, control.shape[2], control.shape[3], amplitude.shape[1])
        return jax.shard_map(
            functools.partial(body, z),
            mesh=mesh,
            in_specs=placed,
            out_specs=P("var", "lat", None, None),
            check_vma=False,
        )(control, row_order, row_length, vertical, amplitude, meridional, balance)

    return run
```

```python
import functools

import jax
import jax.numpy as jnp
from jax import lax
from jax.experimental import pallas as pl
from jax.experimental.pallas import tpu as pltpu
from jax.sharding import PartitionSpec as P

RADIX = 4
LANES = 128
SUBLANES = 8
STRIP = 16
F32 = jnp.float32
BF16 = jnp.bfloat16

COS_POLY = (1, -19.7392044, 64.9391174, -85.4501419, 60.1676292, -25.9675999, 6.52865839)
SIN_POLY = (6.28318501, -41.3415909, 81.5999451, -76.6144714, 41.3428841, -12.4712439)

VMEM = pl.BlockSpec(memory_space=pltpu.VMEM)
HBM = pl.BlockSpec(memory_space=pltpu.HBM)
PARAMS = pltpu.CompilerParams(vmem_limit_bytes=32 * 1024 * 1024)


def iota(shape, dim):
    return lax.broadcasted_iota(jnp.int32, shape, dim)


def horner(poly, x):
    total = jnp.full_like(x, poly[-1])
    for term in poly[-2::-1]:
        total = total * x + term
    return total


def cos_sin(turns):
    turns = turns - jnp.round(turns)
    square = turns * turns
    return horner(COS_POLY, square), horner(SIN_POLY, square) * turns


def repeat(count, step):
    lax.fori_loop(0, count, lambda i, none: step(i), None)


def rows_at(i, size):
    return pl.ds(pl.multiple_of(i * size, size), size)


def ceil_div(a, b):
    return -(-a // b)


def round_up(a, b):
    return ceil_div(a, b) * b


def dot(a, b, contract=((1,), (0,))):
    return lax.dot_general(a, b, (contract, ((), ())), preferred_element_type=F32)


class Sizes:
    def __init__(self, lat_total, var_total, levels, lons, waves):
        self.lat, self.var, self.levels, self.lons, self.waves = lat_total, var_total, levels, lons, waves
        self.devices = lat_total * var_total
        self.points = lons // RADIX
        self.kaps = waves // RADIX
        self.rows = round_up(ceil_div(waves, self.devices), SUBLANES)
        assert self.kaps % self.rows == 0 and 2 * levels == LANES and lat_total <= LANES
        self.mixed = lat_total * self.rows
        self.heads = round_up(ceil_div(self.kaps, STRIP), SUBLANES)
        self.params = round_up(levels + lat_total, STRIP)


def own_length(order_ref, length_ref):
    slot = lax.axis_index("lat")
    row = order_ref[slot]
    return slot, row, length_ref[row]


def fetch(sources, targets, sems):
    copies = [pltpu.make_async_copy(s, t, sems.at[i]) for i, (s, t) in enumerate(zip(sources, targets))]
    for copy in copies:
        copy.start()
    return copies


def slot_matrix(z, order_ref, mer_ref):
    slot = iota((z.lat, z.lat), 0)
    row = jnp.zeros((z.lat, z.lat), jnp.int32)
    for t in range(z.lat):
        row = jnp.where(slot == t, order_ref[t], row)
    pick = (row == iota((z.lat, z.lat), 1)).astype(F32).astype(BF16)
    return dot(dot(pick, mer_ref[0]).astype(BF16), pick, ((1,), (1,)))


def analysis_kernel(z, *refs):
    given, made, held = refs[:7], refs[7:11], refs[11:18]
    sems, field_ref, parts_ref, heads_ref, tails_ref, scale_ref, product_ref = refs[18:]
    order_ref, length_ref, amp_ref, vert_ref, mer_ref, bal_ref, control_ref = held
    packet_ref, params_ref, basis_ref, twiddle_ref = made
    copies = fetch(given, held, sems)
    field_ref[:, z.lons :] = jnp.zeros((z.levels, LANES), F32)
    params_ref[...] = jnp.zeros(params_ref.shape, BF16)
    for copy in copies[:2]:
        copy.wait()
    slot, row, length = own_length(order_ref, length_ref)
    quarter = length // RADIX
    points = iota((1, z.points), 1)
    inside = points < quarter
    step = points.astype(F32) / jnp.full((1, z.points), quarter, jnp.int32).astype(F32)
    tails_ref[:STRIP], tails_ref[STRIP:] = cos_sin(iota((STRIP, z.points), 0).astype(F32) * step)
    head_cos, head_sin = cos_sin(iota((z.heads, z.points), 0).astype(F32) * STRIP * step)
    heads_ref[: z.heads] = jnp.where(inside, head_cos, 0.0)
    heads_ref[z.heads :] = jnp.where(inside, head_sin, 0.0)

    def basis_strip(head):
        head_cos, head_sin = heads_ref[pl.ds(head, 1)], heads_ref[pl.ds(z.heads + head, 1)]
        tail_cos, tail_sin = tails_ref[:STRIP], tails_ref[STRIP:]
        basis_ref[rows_at(head, STRIP), :] = (head_cos * tail_cos - head_sin * tail_sin).astype(BF16)
        to = rows_at(z.kaps // STRIP + head, STRIP)
        basis_ref[to, :] = (head_sin * tail_cos + head_cos * tail_sin).astype(BF16)

    repeat(z.kaps // STRIP, basis_strip)
    tw_row = iota((2 * RADIX, z.points), 0)
    period = jnp.full((1, z.points), length, jnp.int32).astype(F32)
    tw_cos, tw_sin = cos_sin((tw_row % RADIX).astype(F32) * (points.astype(F32) / period))
    twiddle_ref[: 2 * RADIX] = jnp.where(tw_row < RADIX, tw_cos, tw_sin)
    twiddle_ref[2 * RADIX :] = jnp.broadcast_to(period, (SUBLANES, z.points))
    for copy in copies[2:6]:
        copy.wait()
    group = LANES // RADIX

    def scale_group(i):
        amps = amp_ref[:, pl.ds(pl.multiple_of(i * LANES, LANES), LANES)]
        for r in range(RADIX):
            picked = iota((group, LANES), 1) == iota((group, LANES), 0) * RADIX + r
            amp = jnp.sum(jnp.where(picked, amps, 0.0), axis=1, keepdims=True)
            wave = (i * group + iota((group, LANES), 0)) * RADIX + r
            weight = jnp.where(wave == 0, 1.0, 2.0) / period[:, :LANES]
            weight = jnp.where(wave <= (length - 1) // 2, weight, 0.0)
            scale_ref[rows_at(r * (z.kaps // group) + i, group)] = weight * amp

    repeat(z.kaps // group, scale_group)
    params_ref[: z.levels] = jnp.concatenate([bal_ref[0], bal_ref[0]], axis=1)
    params_ref[z.levels : z.levels + z.lat, : z.lat] = slot_matrix(z, order_ref, mer_ref).astype(BF16)
    copies[6].wait()
    field_ref[:, : z.lons] = dot(vert_ref[0], control_ref[0, 0])
    starts = [quarter * j1 for j1 in range(1, RADIX)]
    bases = [pl.multiple_of(s // LANES * LANES, LANES) for s in starts]
    shifts = [(LANES - (s - b)) % LANES for s, b in zip(starts, bases)]
    lane = iota((STRIP, LANES), 1)

    def quarters(strip):
        rows = rows_at(strip, STRIP)

        def quarter_of(base, shift):
            wide = field_ref[rows, pl.ds(base, z.points + LANES)]
            tiles = [pltpu.roll(wide[:, c : c + LANES], shift, 1) for c in range(0, z.points + LANES, LANES)]
            keep = (lane < shift) | (shift == 0)
            return jnp.concatenate([jnp.where(keep, a, b) for a, b in zip(tiles, tiles[1:])], axis=1)

        first = field_ref[rows, : z.points]
        second, third, fourth = [quarter_of(b, s) for b, s in zip(bases, shifts)]
        even, odd = first + third, second + fourth
        real, imag = first - third, second - fourth
        cos1, cos2, cos3 = [twiddle_ref[r : r + 1, :] for r in (1, 2, 3)]
        sin1, sin2, sin3 = [twiddle_ref[RADIX + r : RADIX + r + 1, :] for r in (1, 2, 3)]
        turned = even - odd
        parts = (
            (even + odd, jnp.zeros((STRIP, z.points), F32)),
            (real * cos1 - imag * sin1, real * sin1 + imag * cos1),
            (turned * cos2, turned * sin2),
            (real * cos3 + imag * sin3, real * sin3 - imag * cos3),
        )
        for r, pair in enumerate(parts):
            for half, part in enumerate(pair):
                to = rows_at((2 * r + half) * (z.levels // STRIP) + strip, STRIP)
                parts_ref[to, :] = part.astype(BF16)

    repeat(z.levels // STRIP, quarters)
    count = z.kaps // z.rows
    sign = jnp.where(iota((1, LANES), 1) < z.levels, -1.0, 1.0).astype(F32)
    product_ref[...] = dot(basis_ref[...], parts_ref[...], ((1,), (1,)))

    def coefficients(r):
        lanes = pl.ds(pl.multiple_of(r * LANES, LANES), LANES)
        both = product_ref[: z.kaps, lanes] + pltpu.roll(product_ref[z.kaps :, lanes], z.levels, 1) * sign
        both = (both * scale_ref[rows_at(r, z.kaps)]).reshape(count, z.rows, LANES)
        for i in range(count):
            packet_ref[r * count + i] = both[i].astype(BF16)

    repeat(RADIX, coefficients)
    if z.devices > RADIX * count:
        rest = z.devices - RADIX * count
        packet_ref[RADIX * count :] = jnp.zeros((rest, z.rows, LANES), BF16)


def matrices_kernel(z, *refs):
    *given, mix_ref, bal_ref, all_ref = refs
    own = lax.axis_index("var")
    for step, ref in enumerate(given):
        all_ref[(own + step) % z.var] = ref[...]
    size = z.mixed
    to_cols = (iota((z.lat, size), 0) == iota((z.lat, size), 1) // z.rows).astype(F32).astype(BF16)
    same = iota((size, size), 0) % z.rows == iota((size, size), 1) % z.rows
    halves = iota((LANES, LANES), 0) // z.levels == iota((LANES, LANES), 1) // z.levels
    for v in range(z.var):
        meridional = all_ref[v, z.levels :].astype(F32)[: z.lat, : z.lat].astype(BF16)
        slot_cols = dot(meridional, to_cols).astype(BF16)
        mix_ref[v] = jnp.where(same, dot(to_cols, slot_cols, ((0,), (0,))), 0.0).astype(BF16)
        if v > 0:
            balance = all_ref[v, : z.levels].astype(F32)
            balance = jnp.where(halves, jnp.concatenate([balance, balance], axis=0), 0.0)
            bal_ref[v - 1] = balance.T.astype(BF16)


def mixing_kernel(z, packet_ref, mix_ref, bal_ref, out_ref):
    stream = None
    for v in range(z.var):
        coeffs = packet_ref[v].astype(F32).reshape(z.mixed, LANES).astype(BF16)
        blended = dot(mix_ref[v], coeffs)
        if v == 0:
            stream = blended.astype(BF16)
        else:
            blended = blended + dot(stream, bal_ref[v - 1])
        blended = blended.reshape(z.lat, z.rows, LANES)
        for s in range(z.lat):
            out_ref[v, s] = blended[s].astype(BF16)


def synthesis_kernel(z, spectra_ref, basis_ref, twiddle_ref, out_ref, sems, field_ref, spectra_f32_ref, lhs_ref, parts_ref):
    period = twiddle_ref[2 * RADIX :, :LANES].astype(jnp.int32)
    length = jnp.max(period)
    used = z.waves // z.rows
    spectra = spectra_ref[:used].astype(F32).reshape(z.waves, LANES)
    at = iota((z.waves, LANES), 0)
    wave = at % z.kaps * RADIX + at // z.kaps
    spectra = jnp.where(wave <= (period[0:1] - 1) // 2, spectra, 0.0)
    sign = jnp.where(iota((1, LANES), 1) < z.levels, 1.0, -1.0).astype(F32)
    spectra_f32_ref[...] = spectra

    def operand(r):
        part = spectra_f32_ref[rows_at(r, z.kaps)]
        part = jnp.concatenate([part * sign, pltpu.roll(part, z.levels, 1)], axis=0).T
        lhs_ref[rows_at(r, LANES)] = part.astype(BF16)

    repeat(RADIX, operand)
    parts_ref[...] = dot(lhs_ref[...], basis_ref[...])
    quarter = length // RADIX
    starts = [quarter * j1 for j1 in range(1, RADIX)]
    bases = [pl.multiple_of(s // LANES * LANES, LANES) for s in starts]
    shifts = [s - b for s, b in zip(starts, bases)]
    wide = z.points + LANES
    field_ref[:, wide:] = jnp.zeros((z.levels, z.lons + LANES - wide), BF16)
    lane = iota((STRIP, LANES), 1)
    zero = jnp.zeros((STRIP, LANES), F32)

    def out_copy(strip):
        rows = rows_at(strip, STRIP)
        source = field_ref.at[rows, pl.ds(0, z.lons)]
        return pltpu.make_async_copy(source, out_ref.at[0, 0, rows], sems.at[strip])

    def quarters(strip):
        rows = rows_at(strip, STRIP)
        cos1, cos2, cos3 = [twiddle_ref[r : r + 1, :] for r in (1, 2, 3)]
        sin1, sin2, sin3 = [twiddle_ref[RADIX + r : RADIX + r + 1, :] for r in (1, 2, 3)]
        w0, _, re1, im1, re2, im2, re3, im3 = [
            parts_ref[rows_at(i * (z.levels // STRIP) + strip, STRIP)] for i in range(2 * RADIX)
        ]
        w2 = re2 * cos2 - im2 * sin2
        cross = (re1 * cos1 - im1 * sin1) + (re3 * cos3 - im3 * sin3)
        turn = (re1 * sin1 + im1 * cos1) - (re3 * sin3 + im3 * cos3)
        even, odd = w0 + w2, w0 - w2
        field_ref[rows, :wide] = jnp.concatenate([even + cross, zero], axis=1).astype(BF16)
        for base, shift, part in zip(bases, shifts, (odd - turn, even - cross, odd + turn)):
            tiles = [pltpu.roll(part[:, c : c + LANES], shift, 1) for c in range(0, z.points, LANES)]
            moved = [jnp.where(lane < shift, a, b) for a, b in zip([zero] + tiles, tiles + [zero])]
            moved[0] = moved[0] + field_ref[rows, pl.ds(base, LANES)].astype(F32)
            field_ref[rows, pl.ds(base, wide)] = jnp.concatenate(moved, axis=1).astype(BF16)
        out_copy(strip).start()

    repeat(z.levels // STRIP, quarters)
    repeat(z.levels // STRIP, lambda strip: out_copy(strip).wait())


def body(z, control, row_order, row_length, vertical, amplitude, meridional, balance):
    arguments = (row_order, row_length, amplitude, vertical, meridional, balance, control)
    made = (
        jax.ShapeDtypeStruct((z.devices, z.rows, LANES), BF16),
        jax.ShapeDtypeStruct((z.params, LANES), BF16),
        jax.ShapeDtypeStruct((2 * z.kaps, z.points), BF16),
        jax.ShapeDtypeStruct((2 * RADIX + SUBLANES, z.points), F32),
    )
    packets, params, basis, twiddle = pl.pallas_call(
        functools.partial(analysis_kernel, z),
        out_shape=made,
        in_specs=[HBM] * len(arguments),
        out_specs=(VMEM,) * len(made),
        scratch_shapes=[
            *[pltpu.SMEM(x.shape, x.dtype) for x in arguments[:2]],
            *[pltpu.VMEM(x.shape, x.dtype) for x in arguments[2:]],
            pltpu.SemaphoreType.DMA((len(arguments),)),
            pltpu.VMEM((z.levels, z.lons + LANES), F32),
            pltpu.VMEM((2 * RADIX * z.levels, z.points), BF16),
            pltpu.VMEM((2 * z.heads, z.points), F32),
            pltpu.VMEM((2 * STRIP, z.points), F32),
            pltpu.VMEM((z.waves, LANES), F32),
            pltpu.VMEM((2 * z.kaps, RADIX * LANES), F32),
        ],
        compiler_params=PARAMS,
        name="analysis",
    )(*[pltpu.with_memory_space_constraint(x, pltpu.HBM) for x in arguments])
    given = [params]
    for step in range(1, z.var):
        given.append(lax.ppermute(params, "var", [((i + step) % z.var, i) for i in range(z.var)]))
    packets = lax.all_to_all(packets, ("var", "lat"), 0, 0, tiled=True)
    mix, lift = pl.pallas_call(
        functools.partial(matrices_kernel, z),
        out_shape=(
            jax.ShapeDtypeStruct((z.var, z.mixed, z.mixed), BF16),
            jax.ShapeDtypeStruct((z.var - 1, LANES, LANES), BF16),
        ),
        in_specs=[VMEM] * z.var,
        out_specs=(VMEM, VMEM),
        scratch_shapes=[pltpu.VMEM((z.var, z.params, LANES), BF16)],
        compiler_params=PARAMS,
        cost_estimate=pl.CostEstimate(flops=10**8, bytes_accessed=10**6, transcendentals=0),
        name="matrices",
    )(*given)
    balanced = pl.pallas_call(
        functools.partial(mixing_kernel, z),
        out_shape=jax.ShapeDtypeStruct((z.var, z.lat, z.rows, LANES), BF16),
        in_specs=[VMEM] * 3,
        out_specs=VMEM,
        compiler_params=PARAMS,
        name="mixing",
    )(packets.reshape(z.var, z.lat, z.rows, LANES), mix, lift)
    balanced = balanced.reshape(z.devices, z.rows, LANES)
    balanced = lax.all_to_all(balanced, ("var", "lat"), 0, 0, tiled=True)
    return pl.pallas_call(
        functools.partial(synthesis_kernel, z),
        out_shape=jax.ShapeDtypeStruct(control.shape, BF16),
        in_specs=[VMEM] * 3,
        out_specs=HBM,
        scratch_shapes=[
            pltpu.SemaphoreType.DMA((z.levels // STRIP,)),
            pltpu.VMEM((z.levels, z.lons + LANES), BF16),
            pltpu.VMEM((z.waves, LANES), F32),
            pltpu.VMEM((2 * RADIX * z.levels, 2 * z.kaps), BF16),
            pltpu.VMEM((2 * RADIX * z.levels, z.points), F32),
        ],
        compiler_params=PARAMS,
        name="synthesis",
    )(balanced, basis, twiddle)


def solution(mesh):
    placed = (
        P("var", "lat", None, None),
        P(),
        P(),
        P("var", None, None),
        P("var", None),
        P("var", None, None),
        P("var", None, None),
    )

    def run(control, row_order, row_length, vertical, amplitude, meridional, balance):
        lat_total, var_total = mesh.shape["lat"], mesh.shape["var"]
        assert control.shape[0] == var_total and control.shape[1] == lat_total
        z = Sizes(lat_total, var_total, control.shape[2], control.shape[3], amplitude.shape[1])
        return jax.shard_map(
            functools.partial(body, z),
            mesh=mesh,
            in_specs=placed,
            out_specs=P("var", "lat", None, None),
            check_vma=False,
        )(control, row_order, row_length, vertical, amplitude, meridional, balance)

    return run
```

```python
import functools

import jax
import jax.numpy as jnp
from jax import lax
from jax.experimental import pallas as pl
from jax.experimental.pallas import tpu as pltpu
from jax.sharding import PartitionSpec as P

RADIX = 4
R_ORDER = (0, 2, 1, 3)
LANES = 128
SUBLANES = 8
STRIP = 16
F32 = jnp.float32
BF16 = jnp.bfloat16

COS_POLY = (1, -19.7392044, 64.9391174, -85.4501419, 60.1676292, -25.9675999, 6.52865839)
SIN_POLY = (6.28318501, -41.3415909, 81.5999451, -76.6144714, 41.3428841, -12.4712439)

VMEM = pl.BlockSpec(memory_space=pltpu.VMEM)
HBM = pl.BlockSpec(memory_space=pltpu.HBM)
PARAMS = pltpu.CompilerParams(vmem_limit_bytes=32 * 1024 * 1024)


def iota(shape, dim):
    return lax.broadcasted_iota(jnp.int32, shape, dim)


def horner(poly, x):
    total = jnp.full_like(x, poly[-1])
    for term in poly[-2::-1]:
        total = total * x + term
    return total


def cos_sin(turns):
    turns = turns - jnp.round(turns)
    square = turns * turns
    return horner(COS_POLY, square), horner(SIN_POLY, square) * turns


def ceil_div(a, b):
    return -(-a // b)


def round_up(a, b):
    return ceil_div(a, b) * b


def dot(a, b, contract=((1,), (0,))):
    return lax.dot_general(a, b, (contract, ((), ())), preferred_element_type=F32)


class Sizes:
    def __init__(self, lat_total, var_total, levels, lons, waves):
        self.lat, self.var, self.levels, self.lons, self.waves = lat_total, var_total, levels, lons, waves
        self.devices = lat_total * var_total
        self.points = lons // RADIX
        self.tiles = self.points // LANES
        self.kaps = waves // RADIX
        self.rows = round_up(ceil_div(waves, self.devices), SUBLANES)
        assert self.kaps % self.rows == 0 and self.points % LANES == 0 and 2 * levels == LANES and lat_total <= LANES
        self.mixed = lat_total * self.rows
        self.heads = round_up(ceil_div(self.kaps, STRIP), SUBLANES)
        self.params = round_up(levels + lat_total, STRIP)


def parts_row(z, r, half, at):
    return (2 * R_ORDER.index(r) + half) * z.levels + at


def own_length(order_ref, length_ref):
    slot = lax.axis_index("lat")
    row = order_ref[slot]
    return slot, row, length_ref[row]


def fetch(sources, targets, sems):
    copies = [pltpu.make_async_copy(s, t, sems.at[i]) for i, (s, t) in enumerate(zip(sources, targets))]
    for copy in copies:
        copy.start()
    return copies


def slot_matrix(z, order_ref, mer_ref):
    slot = iota((z.lat, z.lat), 0)
    row = jnp.zeros((z.lat, z.lat), jnp.int32)
    for t in range(z.lat):
        row = jnp.where(slot == t, order_ref[t], row)
    pick = (row == iota((z.lat, z.lat), 1)).astype(F32).astype(BF16)
    return dot(dot(pick, mer_ref[0]).astype(BF16), pick, ((1,), (1,)))


def tile(c):
    return slice(c * LANES, (c + 1) * LANES)


def analysis_kernel(z, *refs):
    given, made, held = refs[:7], refs[7:11], refs[11:18]
    sems, field_ref, parts_ref, heads_ref, tails_ref, scale_ref, diff_ref, product_ref = refs[18:]
    order_ref, length_ref, control_ref, vert_ref, amp_ref, mer_ref, bal_ref = held
    packet_ref, params_ref, basis_ref, twiddle_ref = made
    copies = fetch(given, held, sems)
    field_ref[:, z.lons :] = jnp.zeros((z.levels, LANES), F32)
    params_ref[...] = jnp.zeros(params_ref.shape, BF16)
    at = parts_row(z, 0, 1, 0)
    parts_ref[at : at + z.levels] = jnp.zeros((z.levels, z.points), BF16)
    for copy in copies[:2]:
        copy.wait()
    slot, row, length = own_length(order_ref, length_ref)
    quarter = length // RADIX
    period = jnp.full((1, LANES), length, jnp.int32).astype(F32)
    tail = iota((STRIP, LANES), 0).astype(F32)
    head = iota((z.heads, LANES), 0).astype(F32) * STRIP
    tw_row = iota((2 * RADIX, LANES), 0)
    tw_wave = jnp.where(tw_row < RADIX, tw_row, tw_row - RADIX).astype(F32)
    fraction = jnp.full((1, LANES), quarter, jnp.int32).astype(F32)
    for c in range(z.tiles):
        points = c * LANES + iota((1, LANES), 1)
        step = points.astype(F32) / fraction
        tails_ref[:STRIP, tile(c)], tails_ref[STRIP:, tile(c)] = cos_sin(tail * step)
        head_cos, head_sin = cos_sin(head * step)
        heads_ref[: z.heads, tile(c)] = jnp.where(points < quarter, head_cos, 0.0)
        heads_ref[z.heads :, tile(c)] = jnp.where(points < quarter, head_sin, 0.0)
        tw_cos, tw_sin = cos_sin(tw_wave * (points.astype(F32) / period))
        twiddle_ref[: 2 * RADIX, tile(c)] = jnp.where(tw_row < RADIX, tw_cos, tw_sin)
        twiddle_ref[2 * RADIX :, tile(c)] = jnp.broadcast_to(period, (SUBLANES, LANES))
    for copy in copies[2:]:
        copy.wait()
    field_ref[:, : z.lons] = dot(vert_ref[0], control_ref[0, 0])
    for c in range(z.tiles):
        tail_cos, tail_sin = tails_ref[:STRIP, tile(c)], tails_ref[STRIP:, tile(c)]
        for at in range(0, z.kaps, STRIP):
            i = at // STRIP
            head_cos, head_sin = heads_ref[i : i + 1, tile(c)], heads_ref[z.heads + i : z.heads + i + 1, tile(c)]
            basis_ref[at : at + STRIP, tile(c)] = (head_cos * tail_cos - head_sin * tail_sin).astype(BF16)
            to = slice(z.kaps + at, z.kaps + at + STRIP)
            basis_ref[to, tile(c)] = (head_sin * tail_cos + head_cos * tail_sin).astype(BF16)
    starts = [quarter * j1 for j1 in range(1, RADIX)]
    bases = [pl.multiple_of(s // LANES * LANES, LANES) for s in starts]
    shifts = [(LANES - (s - b)) % LANES for s, b in zip(starts, bases)]
    lane = iota((STRIP, LANES), 1)
    keeps = [(lane < shift) | (shift == 0) for shift in shifts]

    def put_part(r, half, at, c, value):
        to = parts_row(z, r, half, at)
        parts_ref[to : to + STRIP, tile(c)] = value.astype(BF16)

    for at in range(0, z.levels, STRIP):
        rows = slice(at, at + STRIP)

        def rolled(i, c):
            lanes = pl.ds(pl.multiple_of(bases[i] + c * LANES, LANES), LANES)
            return pltpu.roll(field_ref[rows, lanes], shifts[i], 1)

        before = [rolled(i, 0) for i in range(RADIX - 1)]
        for c in range(z.tiles):
            after = [rolled(i, c + 1) for i in range(RADIX - 1)]
            second, third, fourth = [jnp.where(k, a, b) for k, a, b in zip(keeps, before, after)]
            before = after
            first = field_ref[rows, tile(c)]
            even, odd = first + third, second + fourth
            diff_ref[rows, tile(c)] = first - third
            diff_ref[z.levels + at : z.levels + at + STRIP, tile(c)] = second - fourth
            put_part(0, 0, at, c, even + odd)
            turned = even - odd
            put_part(2, 0, at, c, turned * twiddle_ref[2:3, tile(c)])
            put_part(2, 1, at, c, turned * twiddle_ref[RADIX + 2 : RADIX + 3, tile(c)])
    wide = 2 * LANES
    product_ref[:, :wide] = dot(basis_ref[...], parts_ref[:wide], ((1,), (1,)))
    for at in range(0, z.levels, STRIP):
        for c in range(z.tiles):
            real = diff_ref[at : at + STRIP, tile(c)]
            imag = diff_ref[z.levels + at : z.levels + at + STRIP, tile(c)]
            cos1, cos3 = twiddle_ref[1:2, tile(c)], twiddle_ref[3:4, tile(c)]
            sin1, sin3 = [twiddle_ref[RADIX + r : RADIX + r + 1, tile(c)] for r in (1, 3)]
            put_part(1, 0, at, c, real * cos1 - imag * sin1)
            put_part(1, 1, at, c, real * sin1 + imag * cos1)
            put_part(3, 0, at, c, real * cos3 + imag * sin3)
            put_part(3, 1, at, c, real * sin3 - imag * cos3)
    product_ref[:, wide:] = dot(basis_ref[...], parts_ref[wide:], ((1,), (1,)))
    group = LANES // RADIX
    weights = 1.0 / period, 2.0 / period
    for r in range(RADIX):
        picked = iota((group, LANES), 1) == iota((group, LANES), 0) * RADIX + r
        for at in range(0, z.kaps, group):
            lanes = slice(at * RADIX, at * RADIX + LANES)
            amp = jnp.sum(jnp.where(picked, amp_ref[:, lanes], 0.0), axis=1, keepdims=True)
            wave = (at + iota((group, LANES), 0)) * RADIX + r
            weight = jnp.where(wave == 0, *weights) if at + r == 0 else weights[1]
            scale_ref[r * z.kaps + at : r * z.kaps + at + group] = jnp.where(
                wave <= (length - 1) // 2, weight * amp, 0.0
            )
    params_ref[: z.levels] = jnp.concatenate([bal_ref[0], bal_ref[0]], axis=1)
    params_ref[z.levels : z.levels + z.lat, : z.lat] = slot_matrix(z, order_ref, mer_ref).astype(BF16)
    count = z.kaps // z.rows
    sign = jnp.where(iota((1, LANES), 1) < z.levels, -1.0, 1.0).astype(F32)
    for r in R_ORDER:
        lanes = tile(R_ORDER.index(r))
        for i in range(count):
            rows = slice(i * z.rows, (i + 1) * z.rows)
            from_sin = product_ref[z.kaps + i * z.rows : z.kaps + (i + 1) * z.rows, lanes]
            both = product_ref[rows, lanes] + pltpu.roll(from_sin, z.levels, 1) * sign
            scale = scale_ref[r * z.kaps + i * z.rows : r * z.kaps + (i + 1) * z.rows]
            packet_ref[r * count + i] = (both * scale).astype(BF16)
    if z.devices > RADIX * count:
        packet_ref[RADIX * count :] = jnp.zeros((z.devices - RADIX * count, z.rows, LANES), BF16)


def matrices_kernel(z, *refs):
    *given, mix_ref, bal_ref, all_ref = refs
    own = lax.axis_index("var")
    for step, ref in enumerate(given):
        all_ref[(own + step) % z.var] = ref[...]
    size = z.mixed
    to_cols = (iota((z.lat, size), 0) == iota((z.lat, size), 1) // z.rows).astype(F32).astype(BF16)
    same = iota((size, size), 0) % z.rows == iota((size, size), 1) % z.rows
    halves = iota((LANES, LANES), 0) // z.levels == iota((LANES, LANES), 1) // z.levels
    for v in range(z.var):
        meridional = all_ref[v, z.levels :].astype(F32)[: z.lat, : z.lat].astype(BF16)
        slot_cols = dot(meridional, to_cols).astype(BF16)
        mix_ref[v] = jnp.where(same, dot(to_cols, slot_cols, ((0,), (0,))), 0.0).astype(BF16)
        if v > 0:
            balance = all_ref[v, : z.levels].astype(F32)
            balance = jnp.where(halves, jnp.concatenate([balance, balance], axis=0), 0.0)
            bal_ref[v - 1] = balance.T.astype(BF16)


def mixing_kernel(z, packet_ref, mix_ref, bal_ref, out_ref):
    stream = None
    for v in range(z.var):
        coeffs = packet_ref[v].astype(F32).reshape(z.mixed, LANES).astype(BF16)
        blended = dot(mix_ref[v], coeffs)
        if v == 0:
            stream = blended.astype(BF16)
        else:
            blended = blended + dot(stream, bal_ref[v - 1])
        blended = blended.reshape(z.lat, z.rows, LANES)
        for s in range(z.lat):
            out_ref[v, s] = blended[s].astype(BF16)


def synthesis_kernel(z, spectra_ref, basis_ref, twiddle_ref, out_ref, sems, field_ref, lhs_ref, parts_ref):
    period = twiddle_ref[2 * RADIX :, :LANES].astype(jnp.int32)
    length = jnp.max(period)
    kap = iota((z.kaps, LANES), 0)
    sign = jnp.where(iota((1, LANES), 1) < z.levels, 1.0, -1.0).astype(F32)
    count = z.kaps // z.rows
    half = z.levels // 2
    kinds = 2 * RADIX - 1
    for r in range(RADIX):
        part = spectra_ref[r * count : (r + 1) * count].astype(F32).reshape(z.kaps, LANES)
        part = jnp.where(kap * RADIX + r <= (period[0:1] - 1) // 2, part, 0.0)
        part = jnp.concatenate([part * sign, pltpu.roll(part, z.levels, 1)], axis=0).T.astype(BF16)
        for i in range(2):
            for kind in (2 * r - 1, 2 * r):
                if kind >= 0:
                    of = (kind + 1 - 2 * r) % 2 * z.levels if r else 0
                    to = (i * kinds + kind) * half
                    lhs_ref[to : to + half] = part[of + i * half : of + (i + 1) * half]
    quarter = length // RADIX
    starts = [quarter * j1 for j1 in range(1, RADIX)]
    bases = [pl.multiple_of(s // LANES * LANES, LANES) for s in starts]
    shifts = [s - b for s, b in zip(starts, bases)]
    wide = z.points + LANES
    field_ref[:, wide:] = jnp.zeros((z.levels, z.lons + LANES - wide), BF16)
    keep = [iota((STRIP, LANES), 1) < shift for shift in shifts]
    zero = jnp.zeros((STRIP, LANES), F32)
    for i in range(2):
        rows = slice(i * kinds * half, (i + 1) * kinds * half)
        parts_ref[rows] = dot(lhs_ref[rows], basis_ref[...])
    sent = []
    for at in range(0, z.levels, STRIP):
        rows = slice(at, at + STRIP)
        first = at // half * kinds * half + at % half
        quarters = [[], [], [], []]
        for c in range(z.tiles):
            cos1, cos2, cos3 = [twiddle_ref[r : r + 1, tile(c)] for r in (1, 2, 3)]
            sin1, sin2, sin3 = [twiddle_ref[RADIX + r : RADIX + r + 1, tile(c)] for r in (1, 2, 3)]
            w0, re1, im1, re2, im2, re3, im3 = [
                parts_ref[first + kind * half : first + kind * half + STRIP, tile(c)] for kind in range(kinds)
            ]
            w2 = re2 * cos2 - im2 * sin2
            cross = (re1 * cos1 - im1 * sin1) + (re3 * cos3 - im3 * sin3)
            turn = (re1 * sin1 + im1 * cos1) - (re3 * sin3 + im3 * cos3)
            even, odd = w0 + w2, w0 - w2
            field_ref[rows, tile(c)] = (even + cross).astype(BF16)
            for j1, part in ((1, odd - turn), (2, even - cross), (3, odd + turn)):
                quarters[j1].append(pltpu.roll(part, shifts[j1 - 1], 1))
        field_ref[rows, tile(z.tiles)] = zero.astype(BF16)
        for j1 in range(1, RADIX):
            pieces = zip([zero] + quarters[j1], quarters[j1] + [zero])
            for c, (left, right) in enumerate(pieces):
                lanes = pl.ds(pl.multiple_of(bases[j1 - 1] + c * LANES, LANES), LANES)
                piece = jnp.where(keep[j1 - 1], left, right)
                if c == 0:
                    piece = piece + field_ref[rows, lanes].astype(F32)
                field_ref[rows, lanes] = piece.astype(BF16)
        sent += fetch(
            (field_ref.at[pl.ds(at, STRIP), pl.ds(0, z.lons)],),
            (out_ref.at[0, 0, pl.ds(at, STRIP)],),
            sems.at[pl.ds(at // STRIP, 1)],
        )
    for copy in sent:
        copy.wait()


def body(z, control, row_order, row_length, vertical, amplitude, meridional, balance):
    arguments = (row_order, row_length, control, vertical, amplitude, meridional, balance)
    made = (
        jax.ShapeDtypeStruct((z.devices, z.rows, LANES), BF16),
        jax.ShapeDtypeStruct((z.params, LANES), BF16),
        jax.ShapeDtypeStruct((2 * z.kaps, z.points), BF16),
        jax.ShapeDtypeStruct((2 * RADIX + SUBLANES, z.points), F32),
    )
    packets, params, basis, twiddle = pl.pallas_call(
        functools.partial(analysis_kernel, z),
        out_shape=made,
        in_specs=[HBM] * len(arguments),
        out_specs=(VMEM,) * len(made),
        scratch_shapes=[
            *[pltpu.SMEM(x.shape, x.dtype) for x in arguments[:2]],
            *[pltpu.VMEM(x.shape, x.dtype) for x in arguments[2:]],
            pltpu.SemaphoreType.DMA((len(arguments),)),
            pltpu.VMEM((z.levels, z.lons + LANES), F32),
            pltpu.VMEM((2 * RADIX * z.levels, z.points), BF16),
            pltpu.VMEM((2 * z.heads, z.points), F32),
            pltpu.VMEM((2 * STRIP, z.points), F32),
            pltpu.VMEM((z.waves, LANES), F32),
            pltpu.VMEM((2 * z.levels, z.points), F32),
            pltpu.VMEM((2 * z.kaps, RADIX * LANES), F32),
        ],
        compiler_params=PARAMS,
        name="analysis",
    )(*[pltpu.with_memory_space_constraint(x, pltpu.HBM) for x in arguments])
    given = [params]
    for step in range(1, z.var):
        given.append(lax.ppermute(params, "var", [((i + step) % z.var, i) for i in range(z.var)]))
    packets = lax.all_to_all(packets, ("var", "lat"), 0, 0, tiled=True)
    mix, lift = pl.pallas_call(
        functools.partial(matrices_kernel, z),
        out_shape=(
            jax.ShapeDtypeStruct((z.var, z.mixed, z.mixed), BF16),
            jax.ShapeDtypeStruct((z.var - 1, LANES, LANES), BF16),
        ),
        in_specs=[VMEM] * z.var,
        out_specs=(VMEM, VMEM),
        scratch_shapes=[pltpu.VMEM((z.var, z.params, LANES), BF16)],
        compiler_params=PARAMS,
        cost_estimate=pl.CostEstimate(flops=10**8, bytes_accessed=10**6, transcendentals=0),
        name="matrices",
    )(*given)
    balanced = pl.pallas_call(
        functools.partial(mixing_kernel, z),
        out_shape=jax.ShapeDtypeStruct((z.var, z.lat, z.rows, LANES), BF16),
        in_specs=[VMEM] * 3,
        out_specs=VMEM,
        compiler_params=PARAMS,
        name="mixing",
    )(packets.reshape(z.var, z.lat, z.rows, LANES), mix, lift)
    balanced = balanced.reshape(z.devices, z.rows, LANES)
    balanced = lax.all_to_all(balanced, ("var", "lat"), 0, 0, tiled=True)
    return pl.pallas_call(
        functools.partial(synthesis_kernel, z),
        out_shape=jax.ShapeDtypeStruct(control.shape, BF16),
        in_specs=[VMEM] * 3,
        out_specs=HBM,
        scratch_shapes=[
            pltpu.SemaphoreType.DMA((z.levels // STRIP,)),
            pltpu.VMEM((z.levels, z.lons + LANES), BF16),
            pltpu.VMEM(((2 * RADIX - 1) * z.levels, 2 * z.kaps), BF16),
            pltpu.VMEM(((2 * RADIX - 1) * z.levels, z.points), F32),
        ],
        compiler_params=PARAMS,
        name="synthesis",
    )(balanced, basis, twiddle)


def solution(mesh):
    placed = (
        P("var", "lat", None, None),
        P(),
        P(),
        P("var", None, None),
        P("var", None),
        P("var", None, None),
        P("var", None, None),
    )

    def run(control, row_order, row_length, vertical, amplitude, meridional, balance):
        lat_total, var_total = mesh.shape["lat"], mesh.shape["var"]
        assert control.shape[0] == var_total and control.shape[1] == lat_total
        z = Sizes(lat_total, var_total, control.shape[2], control.shape[3], amplitude.shape[1])
        return jax.shard_map(
            functools.partial(body, z),
            mesh=mesh,
            in_specs=placed,
            out_specs=P("var", "lat", None, None),
            check_vma=False,
        )(control, row_order, row_length, vertical, amplitude, meridional, balance)

    return run
```

```python
import functools

import jax
import jax.numpy as jnp
from jax import lax
from jax.experimental import pallas as pl
from jax.experimental.pallas import tpu as pltpu
from jax.sharding import PartitionSpec as P

RADIX = 4
R_ORDER = (0, 2, 1, 3)
LANES = 128
SUBLANES = 8
STRIP = 16
F32 = jnp.float32
BF16 = jnp.bfloat16

COS_POLY = (1, -19.7392044, 64.9391174, -85.4501419, 60.1676292, -25.9675999, 6.52865839)
SIN_POLY = (6.28318501, -41.3415909, 81.5999451, -76.6144714, 41.3428841, -12.4712439)

VMEM = pl.BlockSpec(memory_space=pltpu.VMEM)
HBM = pl.BlockSpec(memory_space=pltpu.HBM)
PARAMS = pltpu.CompilerParams(vmem_limit_bytes=32 * 1024 * 1024)


def iota(shape, dim):
    return lax.broadcasted_iota(jnp.int32, shape, dim)


def horner(poly, x):
    total = jnp.full_like(x, poly[-1])
    for term in poly[-2::-1]:
        total = total * x + term
    return total


def cos_sin(turns):
    turns = turns - jnp.round(turns)
    square = turns * turns
    return horner(COS_POLY, square), horner(SIN_POLY, square) * turns


def ceil_div(a, b):
    return -(-a // b)


def round_up(a, b):
    return ceil_div(a, b) * b


def dot(a, b, contract=((1,), (0,))):
    return lax.dot_general(a, b, (contract, ((), ())), preferred_element_type=F32)


class Sizes:
    def __init__(self, lat_total, var_total, levels, lons, waves):
        self.lat, self.var, self.levels, self.lons, self.waves = lat_total, var_total, levels, lons, waves
        self.devices = lat_total * var_total
        self.points = lons // RADIX
        self.tiles = self.points // LANES
        self.kaps = waves // RADIX
        rows = round_up(ceil_div(waves, self.devices), SUBLANES)
        cut = round_up(rows // 2, STRIP) if rows >= 2 * SUBLANES else rows
        self.sets = [(0, cut)] + ([(cut * self.devices, rows - cut)] if rows > cut else [])
        assert all(self.kaps % size == 0 and first % size == 0 for first, size in self.sets)
        assert self.points % LANES == 0 and 2 * levels == LANES and lat_total <= LANES
        self.heads = round_up(ceil_div(self.kaps, STRIP), SUBLANES)
        self.params = round_up(levels + lat_total, STRIP)

    def chunks(self, first, size):
        return [divmod(row, self.kaps) for row in range(first, min(first + size * self.devices, self.waves), size)]


def parts_row(z, r, half, at):
    return (2 * R_ORDER.index(r) + half) * z.levels + at


def own_length(order_ref, length_ref):
    slot = lax.axis_index("lat")
    row = order_ref[slot]
    return slot, row, length_ref[row]


def fetch(sources, targets, sems):
    copies = [pltpu.make_async_copy(s, t, sems.at[i]) for i, (s, t) in enumerate(zip(sources, targets))]
    for copy in copies:
        copy.start()
    return copies


def slot_matrix(z, order_ref, mer_ref):
    slot = iota((z.lat, z.lat), 0)
    row = jnp.zeros((z.lat, z.lat), jnp.int32)
    for t in range(z.lat):
        row = jnp.where(slot == t, order_ref[t], row)
    pick = (row == iota((z.lat, z.lat), 1)).astype(F32).astype(BF16)
    return dot(dot(pick, mer_ref[0]).astype(BF16), pick, ((1,), (1,)))


def tile(c):
    return slice(c * LANES, (c + 1) * LANES)


def analysis_kernel(z, *refs):
    count = len(z.sets)
    given, packet_refs, refs = refs[:7], refs[7 : 7 + count], refs[7 + count :]
    made, held = refs[:3], refs[3:10]
    sems, field_ref, parts_ref, heads_ref, tails_ref, scale_ref, diff_ref, product_ref = refs[10:]
    order_ref, length_ref, control_ref, vert_ref, amp_ref, mer_ref, bal_ref = held
    params_ref, basis_ref, twiddle_ref = made
    copies = fetch(given, held, sems)
    field_ref[:, z.lons :] = jnp.zeros((z.levels, LANES), F32)
    params_ref[...] = jnp.zeros(params_ref.shape, BF16)
    at = parts_row(z, 0, 1, 0)
    parts_ref[at : at + z.levels] = jnp.zeros((z.levels, z.points), BF16)
    for copy in copies[:2]:
        copy.wait()
    slot, row, length = own_length(order_ref, length_ref)
    quarter = length // RADIX
    period = jnp.full((1, LANES), length, jnp.int32).astype(F32)
    tail = iota((STRIP, LANES), 0).astype(F32)
    head = iota((z.heads, LANES), 0).astype(F32) * STRIP
    tw_row = iota((2 * RADIX, LANES), 0)
    tw_wave = jnp.where(tw_row < RADIX, tw_row, tw_row - RADIX).astype(F32)
    fraction = jnp.full((1, LANES), quarter, jnp.int32).astype(F32)
    for c in range(z.tiles):
        points = c * LANES + iota((1, LANES), 1)
        step = points.astype(F32) / fraction
        tails_ref[:STRIP, tile(c)], tails_ref[STRIP:, tile(c)] = cos_sin(tail * step)
        head_cos, head_sin = cos_sin(head * step)
        heads_ref[: z.heads, tile(c)] = jnp.where(points < quarter, head_cos, 0.0)
        heads_ref[z.heads :, tile(c)] = jnp.where(points < quarter, head_sin, 0.0)
        tw_cos, tw_sin = cos_sin(tw_wave * (points.astype(F32) / period))
        twiddle_ref[: 2 * RADIX, tile(c)] = jnp.where(tw_row < RADIX, tw_cos, tw_sin)
        twiddle_ref[2 * RADIX :, tile(c)] = jnp.broadcast_to(period, (SUBLANES, LANES))
    for copy in copies[2:]:
        copy.wait()
    field_ref[:, : z.lons] = dot(vert_ref[0], control_ref[0, 0])
    for c in range(z.tiles):
        tail_cos, tail_sin = tails_ref[:STRIP, tile(c)], tails_ref[STRIP:, tile(c)]
        for at in range(0, z.kaps, STRIP):
            i = at // STRIP
            head_cos, head_sin = heads_ref[i : i + 1, tile(c)], heads_ref[z.heads + i : z.heads + i + 1, tile(c)]
            basis_ref[at : at + STRIP, tile(c)] = (head_cos * tail_cos - head_sin * tail_sin).astype(BF16)
            to = slice(z.kaps + at, z.kaps + at + STRIP)
            basis_ref[to, tile(c)] = (head_sin * tail_cos + head_cos * tail_sin).astype(BF16)
    starts = [quarter * j1 for j1 in range(1, RADIX)]
    bases = [pl.multiple_of(s // LANES * LANES, LANES) for s in starts]
    shifts = [(LANES - (s - b)) % LANES for s, b in zip(starts, bases)]
    lane = iota((STRIP, LANES), 1)
    keeps = [(lane < shift) | (shift == 0) for shift in shifts]

    def put_part(r, half, at, c, value):
        to = parts_row(z, r, half, at)
        parts_ref[to : to + STRIP, tile(c)] = value.astype(BF16)

    for at in range(0, z.levels, STRIP):
        rows = slice(at, at + STRIP)

        def rolled(i, c):
            lanes = pl.ds(pl.multiple_of(bases[i] + c * LANES, LANES), LANES)
            return pltpu.roll(field_ref[rows, lanes], shifts[i], 1)

        before = [rolled(i, 0) for i in range(RADIX - 1)]
        for c in range(z.tiles):
            after = [rolled(i, c + 1) for i in range(RADIX - 1)]
            second, third, fourth = [jnp.where(k, a, b) for k, a, b in zip(keeps, before, after)]
            before = after
            first = field_ref[rows, tile(c)]
            even, odd = first + third, second + fourth
            diff_ref[rows, tile(c)] = first - third
            diff_ref[z.levels + at : z.levels + at + STRIP, tile(c)] = second - fourth
            put_part(0, 0, at, c, even + odd)
            turned = even - odd
            put_part(2, 0, at, c, turned * twiddle_ref[2:3, tile(c)])
            put_part(2, 1, at, c, turned * twiddle_ref[RADIX + 2 : RADIX + 3, tile(c)])
    wide = 2 * LANES
    product_ref[:, :wide] = dot(basis_ref[...], parts_ref[:wide], ((1,), (1,)))
    for at in range(0, z.levels, STRIP):
        for c in range(z.tiles):
            real = diff_ref[at : at + STRIP, tile(c)]
            imag = diff_ref[z.levels + at : z.levels + at + STRIP, tile(c)]
            cos1, cos3 = twiddle_ref[1:2, tile(c)], twiddle_ref[3:4, tile(c)]
            sin1, sin3 = [twiddle_ref[RADIX + r : RADIX + r + 1, tile(c)] for r in (1, 3)]
            put_part(1, 0, at, c, real * cos1 - imag * sin1)
            put_part(1, 1, at, c, real * sin1 + imag * cos1)
            put_part(3, 0, at, c, real * cos3 + imag * sin3)
            put_part(3, 1, at, c, real * sin3 - imag * cos3)
    product_ref[:, wide:] = dot(basis_ref[...], parts_ref[wide:], ((1,), (1,)))
    group = LANES // RADIX
    weights = 1.0 / period, 2.0 / period
    for r in range(RADIX):
        picked = iota((group, LANES), 1) == iota((group, LANES), 0) * RADIX + r
        for at in range(0, z.kaps, group):
            lanes = slice(at * RADIX, at * RADIX + LANES)
            amp = jnp.sum(jnp.where(picked, amp_ref[:, lanes], 0.0), axis=1, keepdims=True)
            wave = (at + iota((group, LANES), 0)) * RADIX + r
            weight = jnp.where(wave == 0, *weights) if at + r == 0 else weights[1]
            scale_ref[r * z.kaps + at : r * z.kaps + at + group] = jnp.where(
                wave <= (length - 1) // 2, weight * amp, 0.0
            )
    params_ref[: z.levels] = jnp.concatenate([bal_ref[0], bal_ref[0]], axis=1)
    params_ref[z.levels : z.levels + z.lat, : z.lat] = slot_matrix(z, order_ref, mer_ref).astype(BF16)
    sign = jnp.where(iota((1, LANES), 1) < z.levels, -1.0, 1.0).astype(F32)
    for packet_ref, (first, size) in zip(packet_refs, z.sets):
        chunks = z.chunks(first, size)
        for i, (place, kap) in enumerate(chunks):
            from_sin = product_ref[z.kaps + kap : z.kaps + kap + size, tile(place)]
            both = product_ref[kap : kap + size, tile(place)] + pltpu.roll(from_sin, z.levels, 1) * sign
            scale_at = R_ORDER[place] * z.kaps + kap
            packet_ref[i] = (both * scale_ref[scale_at : scale_at + size]).astype(BF16)
        if len(chunks) < z.devices:
            packet_ref[len(chunks) :] = jnp.zeros((z.devices - len(chunks), size, LANES), BF16)


def matrices_kernel(z, *refs):
    given, mix_refs, (bal_ref, all_ref) = refs[: z.var], refs[z.var : -2], refs[-2:]
    own = lax.axis_index("var")
    for step, ref in enumerate(given):
        all_ref[(own + step) % z.var] = ref[...]
    halves = iota((LANES, LANES), 0) // z.levels == iota((LANES, LANES), 1) // z.levels
    for v in range(z.var):
        meridional = all_ref[v, z.levels :].astype(F32)[: z.lat, : z.lat].astype(BF16)
        for mix_ref, (_, rows) in zip(mix_refs, z.sets):
            size = z.lat * rows
            to_cols = (iota((z.lat, size), 0) == iota((z.lat, size), 1) // rows).astype(F32).astype(BF16)
            same = iota((size, size), 0) % rows == iota((size, size), 1) % rows
            slot_cols = dot(meridional, to_cols).astype(BF16)
            mix_ref[v] = jnp.where(same, dot(to_cols, slot_cols, ((0,), (0,))), 0.0).astype(BF16)
        if v > 0:
            balance = all_ref[v, : z.levels].astype(F32)
            balance = jnp.where(halves, jnp.concatenate([balance, balance], axis=0), 0.0)
            bal_ref[v - 1] = balance.T.astype(BF16)


def mixing_kernel(z, rows, packet_ref, mix_ref, bal_ref, out_ref):
    stream = None
    for v in range(z.var):
        coeffs = packet_ref[v].astype(F32).reshape(z.lat * rows, LANES).astype(BF16)
        blended = dot(mix_ref[v], coeffs)
        if v == 0:
            stream = blended.astype(BF16)
        else:
            blended = blended + dot(stream, bal_ref[v - 1])
        blended = blended.reshape(z.lat, rows, LANES)
        for s in range(z.lat):
            out_ref[v, s] = blended[s].astype(BF16)


def synthesis_kernel(z, *refs):
    spectra_refs, refs = refs[: len(z.sets)], refs[len(z.sets) :]
    basis_ref, twiddle_ref, out_ref, sems, field_ref, lhs_ref, parts_ref = refs
    period = twiddle_ref[2 * RADIX :, :LANES].astype(jnp.int32)
    length = jnp.max(period)
    kap = iota((z.kaps, LANES), 0)
    sign = jnp.where(iota((1, LANES), 1) < z.levels, 1.0, -1.0).astype(F32)
    half = z.levels // 2
    kinds = 2 * RADIX - 1
    for r in range(RADIX):
        pieces = []
        for spectra_ref, (first, size) in zip(spectra_refs, z.sets):
            mine = [i for i, (place, _) in enumerate(z.chunks(first, size)) if R_ORDER[place] == r]
            if mine:
                piece = spectra_ref[mine[0] : mine[-1] + 1].astype(F32)
                pieces.append(piece.reshape(len(mine) * size, LANES))
        part = jnp.concatenate(pieces, axis=0)
        part = jnp.where(kap * RADIX + r <= (period[0:1] - 1) // 2, part, 0.0)
        part = jnp.concatenate([part * sign, pltpu.roll(part, z.levels, 1)], axis=0).T.astype(BF16)
        for i in range(2):
            for kind in (2 * r - 1, 2 * r):
                if kind >= 0:
                    of = (kind + 1 - 2 * r) % 2 * z.levels if r else 0
                    to = (i * kinds + kind) * half
                    lhs_ref[to : to + half] = part[of + i * half : of + (i + 1) * half]
    quarter = length // RADIX
    starts = [quarter * j1 for j1 in range(1, RADIX)]
    bases = [pl.multiple_of(s // LANES * LANES, LANES) for s in starts]
    shifts = [s - b for s, b in zip(starts, bases)]
    wide = z.points + LANES
    field_ref[:, wide:] = jnp.zeros((z.levels, z.lons + LANES - wide), BF16)
    keep = [iota((STRIP, LANES), 1) < shift for shift in shifts]
    zero = jnp.zeros((STRIP, LANES), F32)
    for i in range(2):
        rows = slice(i * kinds * half, (i + 1) * kinds * half)
        parts_ref[rows] = dot(lhs_ref[rows], basis_ref[...])
    sent = []
    for at in range(0, z.levels, STRIP):
        rows = slice(at, at + STRIP)
        first = at // half * kinds * half + at % half
        quarters = [[], [], [], []]
        for c in range(z.tiles):
            cos1, cos2, cos3 = [twiddle_ref[r : r + 1, tile(c)] for r in (1, 2, 3)]
            sin1, sin2, sin3 = [twiddle_ref[RADIX + r : RADIX + r + 1, tile(c)] for r in (1, 2, 3)]
            w0, re1, im1, re2, im2, re3, im3 = [
                parts_ref[first + kind * half : first + kind * half + STRIP, tile(c)] for kind in range(kinds)
            ]
            w2 = re2 * cos2 - im2 * sin2
            cross = (re1 * cos1 - im1 * sin1) + (re3 * cos3 - im3 * sin3)
            turn = (re1 * sin1 + im1 * cos1) - (re3 * sin3 + im3 * cos3)
            even, odd = w0 + w2, w0 - w2
            field_ref[rows, tile(c)] = (even + cross).astype(BF16)
            for j1, part in ((1, odd - turn), (2, even - cross), (3, odd + turn)):
                quarters[j1].append(pltpu.roll(part, shifts[j1 - 1], 1))
        field_ref[rows, tile(z.tiles)] = zero.astype(BF16)
        for j1 in range(1, RADIX):
            pieces = zip([zero] + quarters[j1], quarters[j1] + [zero])
            for c, (left, right) in enumerate(pieces):
                lanes = pl.ds(pl.multiple_of(bases[j1 - 1] + c * LANES, LANES), LANES)
                piece = jnp.where(keep[j1 - 1], left, right)
                if c == 0:
                    piece = piece + field_ref[rows, lanes].astype(F32)
                field_ref[rows, lanes] = piece.astype(BF16)
        sent += fetch(
            (field_ref.at[pl.ds(at, STRIP), pl.ds(0, z.lons)],),
            (out_ref.at[0, 0, pl.ds(at, STRIP)],),
            sems.at[pl.ds(at // STRIP, 1)],
        )
    for copy in sent:
        copy.wait()


def body(z, control, row_order, row_length, vertical, amplitude, meridional, balance):
    arguments = (row_order, row_length, control, vertical, amplitude, meridional, balance)
    made = (
        *[jax.ShapeDtypeStruct((z.devices, rows, LANES), BF16) for _, rows in z.sets],
        jax.ShapeDtypeStruct((z.params, LANES), BF16),
        jax.ShapeDtypeStruct((2 * z.kaps, z.points), BF16),
        jax.ShapeDtypeStruct((2 * RADIX + SUBLANES, z.points), F32),
    )
    *packets, params, basis, twiddle = pl.pallas_call(
        functools.partial(analysis_kernel, z),
        out_shape=made,
        in_specs=[HBM] * len(arguments),
        out_specs=(VMEM,) * len(made),
        scratch_shapes=[
            *[pltpu.SMEM(x.shape, x.dtype) for x in arguments[:2]],
            *[pltpu.VMEM(x.shape, x.dtype) for x in arguments[2:]],
            pltpu.SemaphoreType.DMA((len(arguments),)),
            pltpu.VMEM((z.levels, z.lons + LANES), F32),
            pltpu.VMEM((2 * RADIX * z.levels, z.points), BF16),
            pltpu.VMEM((2 * z.heads, z.points), F32),
            pltpu.VMEM((2 * STRIP, z.points), F32),
            pltpu.VMEM((z.waves, LANES), F32),
            pltpu.VMEM((2 * z.levels, z.points), F32),
            pltpu.VMEM((2 * z.kaps, RADIX * LANES), F32),
        ],
        compiler_params=PARAMS,
        name="analysis",
    )(*[pltpu.with_memory_space_constraint(x, pltpu.HBM) for x in arguments])
    given = [params]
    for step in range(1, z.var):
        given.append(lax.ppermute(params, "var", [((i + step) % z.var, i) for i in range(z.var)]))
    packets = [lax.all_to_all(x, ("var", "lat"), 0, 0, tiled=True) for x in packets]
    *mixes, lift = pl.pallas_call(
        functools.partial(matrices_kernel, z),
        out_shape=(
            *[jax.ShapeDtypeStruct((z.var, z.lat * rows, z.lat * rows), BF16) for _, rows in z.sets],
            jax.ShapeDtypeStruct((z.var - 1, LANES, LANES), BF16),
        ),
        in_specs=[VMEM] * z.var,
        out_specs=(VMEM,) * (len(z.sets) + 1),
        scratch_shapes=[pltpu.VMEM((z.var, z.params, LANES), BF16)],
        compiler_params=PARAMS,
        cost_estimate=pl.CostEstimate(flops=10**8, bytes_accessed=10**6, transcendentals=0),
        name="matrices",
    )(*given)
    spectra = []
    for packet, mix, (_, rows) in zip(packets, mixes, z.sets):
        balanced = pl.pallas_call(
            functools.partial(mixing_kernel, z, rows),
            out_shape=jax.ShapeDtypeStruct((z.var, z.lat, rows, LANES), BF16),
            in_specs=[VMEM] * 3,
            out_specs=VMEM,
            compiler_params=PARAMS,
            name="mixing",
        )(packet.reshape(z.var, z.lat, rows, LANES), mix, lift)
        balanced = balanced.reshape(z.devices, rows, LANES)
        spectra.append(lax.all_to_all(balanced, ("var", "lat"), 0, 0, tiled=True))
    return pl.pallas_call(
        functools.partial(synthesis_kernel, z),
        out_shape=jax.ShapeDtypeStruct(control.shape, BF16),
        in_specs=[VMEM] * (2 + len(z.sets)),
        out_specs=HBM,
        scratch_shapes=[
            pltpu.SemaphoreType.DMA((z.levels // STRIP,)),
            pltpu.VMEM((z.levels, z.lons + LANES), BF16),
            pltpu.VMEM(((2 * RADIX - 1) * z.levels, 2 * z.kaps), BF16),
            pltpu.VMEM(((2 * RADIX - 1) * z.levels, z.points), F32),
        ],
        compiler_params=PARAMS,
        name="synthesis",
    )(*spectra, basis, twiddle)


def solution(mesh):
    placed = (
        P("var", "lat", None, None),
        P(),
        P(),
        P("var", None, None),
        P("var", None),
        P("var", None, None),
        P("var", None, None),
    )

    def run(control, row_order, row_length, vertical, amplitude, meridional, balance):
        lat_total, var_total = mesh.shape["lat"], mesh.shape["var"]
        assert control.shape[0] == var_total and control.shape[1] == lat_total
        z = Sizes(lat_total, var_total, control.shape[2], control.shape[3], amplitude.shape[1])
        return jax.shard_map(
            functools.partial(body, z),
            mesh=mesh,
            in_specs=placed,
            out_specs=P("var", "lat", None, None),
            check_vma=False,
        )(control, row_order, row_length, vertical, amplitude, meridional, balance)

    return run
```

```python
import functools

import jax
import jax.numpy as jnp
from jax import lax
from jax.experimental import pallas as pl
from jax.experimental.pallas import tpu as pltpu
from jax.sharding import PartitionSpec as P

RADIX = 4
R_ORDER = (0, 2, 1, 3)
LANES = 128
SUBLANES = 8
STRIP = 16
F32 = jnp.float32
BF16 = jnp.bfloat16

COS_POLY = (1, -19.7392044, 64.9391174, -85.4501419, 60.1676292, -25.9675999, 6.52865839)
SIN_POLY = (6.28318501, -41.3415909, 81.5999451, -76.6144714, 41.3428841, -12.4712439)

VMEM = pl.BlockSpec(memory_space=pltpu.VMEM)
HBM = pl.BlockSpec(memory_space=pltpu.HBM)
PARAMS = pltpu.CompilerParams(vmem_limit_bytes=32 * 1024 * 1024)


def iota(shape, dim):
    return lax.broadcasted_iota(jnp.int32, shape, dim)


def horner(poly, x):
    total = jnp.full_like(x, poly[-1])
    for term in poly[-2::-1]:
        total = total * x + term
    return total


def cos_sin(turns):
    turns = turns - jnp.round(turns)
    square = turns * turns
    return horner(COS_POLY, square), horner(SIN_POLY, square) * turns


def ceil_div(a, b):
    return -(-a // b)


def round_up(a, b):
    return ceil_div(a, b) * b


def dot(a, b, contract=((1,), (0,))):
    return lax.dot_general(a, b, (contract, ((), ())), preferred_element_type=F32)


class Sizes:
    def __init__(self, lat_total, var_total, levels, lons, waves):
        self.lat, self.var, self.levels, self.lons, self.waves = lat_total, var_total, levels, lons, waves
        self.devices = lat_total * var_total
        self.points = lons // RADIX
        self.tiles = self.points // LANES
        self.kaps = waves // RADIX
        self.rows = round_up(ceil_div(waves, self.devices), SUBLANES)
        assert self.kaps % self.rows == 0 and self.points % LANES == 0 and 2 * levels == LANES and lat_total <= LANES
        self.mixed = lat_total * self.rows
        self.sin = round_up(self.kaps, LANES)
        self.heads = round_up(ceil_div(self.kaps, STRIP), SUBLANES)
        self.params = round_up(levels + lat_total, STRIP)


def parts_row(z, r, half, at):
    return (2 * R_ORDER.index(r) + half) * z.levels + at


def own_length(order_ref, length_ref):
    slot = lax.axis_index("lat")
    row = order_ref[slot]
    return slot, row, length_ref[row]


def fetch(sources, targets, sems):
    copies = [pltpu.make_async_copy(s, t, sems.at[i]) for i, (s, t) in enumerate(zip(sources, targets))]
    for copy in copies:
        copy.start()
    return copies


def slot_matrix(z, order_ref, mer_ref):
    slot = iota((z.lat, z.lat), 0)
    row = jnp.zeros((z.lat, z.lat), jnp.int32)
    for t in range(z.lat):
        row = jnp.where(slot == t, order_ref[t], row)
    pick = (row == iota((z.lat, z.lat), 1)).astype(F32).astype(BF16)
    return dot(dot(pick, mer_ref[0]).astype(BF16), pick, ((1,), (1,)))


def tile(c):
    return slice(c * LANES, (c + 1) * LANES)


def analysis_kernel(z, *refs):
    given, made, held = refs[:7], refs[7:11], refs[11:18]
    sems, field_ref, parts_ref, heads_ref, tails_ref, scale_ref, diff_ref, product_ref = refs[18:]
    order_ref, length_ref, control_ref, vert_ref, amp_ref, mer_ref, bal_ref = held
    packet_ref, params_ref, basis_ref, twiddle_ref = made
    pieces = [pl.ds(at, STRIP) for at in range(0, z.levels, STRIP)]
    copies = fetch(
        [*given[:2], *[given[2].at[0, 0, piece] for piece in pieces], *given[3:]],
        [*held[:2], *[control_ref.at[0, 0, piece] for piece in pieces], *held[3:]],
        sems,
    )
    for at in (0, z.sin):
        basis_ref[at + z.kaps : at + z.sin] = jnp.zeros((z.sin - z.kaps, z.points), BF16)
    field_ref[:, z.lons :] = jnp.zeros((z.levels, LANES), F32)
    params_ref[...] = jnp.zeros(params_ref.shape, BF16)
    at = parts_row(z, 0, 1, 0)
    parts_ref[at : at + z.levels] = jnp.zeros((z.levels, z.points), BF16)
    for copy in copies[:2]:
        copy.wait()
    slot, row, length = own_length(order_ref, length_ref)
    quarter = length // RADIX
    period = jnp.full((1, LANES), length, jnp.int32).astype(F32)
    tail = iota((STRIP, LANES), 0).astype(F32)
    head = iota((z.heads, LANES), 0).astype(F32) * STRIP
    tw_row = iota((2 * RADIX, LANES), 0)
    tw_wave = jnp.where(tw_row < RADIX, tw_row, tw_row - RADIX).astype(F32)
    fraction = jnp.full((1, LANES), quarter, jnp.int32).astype(F32)
    for c in range(z.tiles):
        points = c * LANES + iota((1, LANES), 1)
        step = points.astype(F32) / fraction
        tails_ref[:STRIP, tile(c)], tails_ref[STRIP:, tile(c)] = cos_sin(tail * step)
        head_cos, head_sin = cos_sin(head * step)
        heads_ref[: z.heads, tile(c)] = jnp.where(points < quarter, head_cos, 0.0)
        heads_ref[z.heads :, tile(c)] = jnp.where(points < quarter, head_sin, 0.0)
        tw_cos, tw_sin = cos_sin(tw_wave * (points.astype(F32) / period))
        twiddle_ref[: 2 * RADIX, tile(c)] = jnp.where(tw_row < RADIX, tw_cos, tw_sin)
        twiddle_ref[2 * RADIX :, tile(c)] = jnp.broadcast_to(period, (SUBLANES, LANES))
    for copy in copies[2:]:
        copy.wait()
    field_ref[:, : z.lons] = dot(vert_ref[0], control_ref[0, 0])
    for c in range(z.tiles):
        tail_cos, tail_sin = tails_ref[:STRIP, tile(c)], tails_ref[STRIP:, tile(c)]
        for at in range(0, z.kaps, STRIP):
            i = at // STRIP
            head_cos, head_sin = heads_ref[i : i + 1, tile(c)], heads_ref[z.heads + i : z.heads + i + 1, tile(c)]
            basis_ref[at : at + STRIP, tile(c)] = (head_cos * tail_cos - head_sin * tail_sin).astype(BF16)
            to = slice(z.sin + at, z.sin + at + STRIP)
            basis_ref[to, tile(c)] = (head_sin * tail_cos + head_cos * tail_sin).astype(BF16)
    starts = [quarter * j1 for j1 in range(1, RADIX)]
    bases = [pl.multiple_of(s // LANES * LANES, LANES) for s in starts]
    shifts = [(LANES - (s - b)) % LANES for s, b in zip(starts, bases)]
    lane = iota((STRIP, LANES), 1)
    keeps = [(lane < shift) | (shift == 0) for shift in shifts]

    def put_part(r, half, at, c, value):
        to = parts_row(z, r, half, at)
        parts_ref[to : to + STRIP, tile(c)] = value.astype(BF16)

    for at in range(0, z.levels, STRIP):
        rows = slice(at, at + STRIP)

        def rolled(i, c):
            lanes = pl.ds(pl.multiple_of(bases[i] + c * LANES, LANES), LANES)
            return pltpu.roll(field_ref[rows, lanes], shifts[i], 1)

        before = [rolled(i, 0) for i in range(RADIX - 1)]
        for c in range(z.tiles):
            after = [rolled(i, c + 1) for i in range(RADIX - 1)]
            second, third, fourth = [jnp.where(k, a, b) for k, a, b in zip(keeps, before, after)]
            before = after
            first = field_ref[rows, tile(c)]
            even, odd = first + third, second + fourth
            diff_ref[rows, tile(c)] = first - third
            diff_ref[z.levels + at : z.levels + at + STRIP, tile(c)] = second - fourth
            put_part(0, 0, at, c, even + odd)
            turned = even - odd
            put_part(2, 0, at, c, turned * twiddle_ref[2:3, tile(c)])
            put_part(2, 1, at, c, turned * twiddle_ref[RADIX + 2 : RADIX + 3, tile(c)])
    wide = 2 * LANES
    basis = jnp.concatenate([basis_ref[: z.kaps], basis_ref[z.sin : z.sin + z.kaps]], axis=0)
    product_ref[:, :wide] = dot(basis, parts_ref[:wide], ((1,), (1,)))
    for at in range(0, z.levels, STRIP):
        for c in range(z.tiles):
            real = diff_ref[at : at + STRIP, tile(c)]
            imag = diff_ref[z.levels + at : z.levels + at + STRIP, tile(c)]
            cos1, cos3 = twiddle_ref[1:2, tile(c)], twiddle_ref[3:4, tile(c)]
            sin1, sin3 = [twiddle_ref[RADIX + r : RADIX + r + 1, tile(c)] for r in (1, 3)]
            put_part(1, 0, at, c, real * cos1 - imag * sin1)
            put_part(1, 1, at, c, real * sin1 + imag * cos1)
            put_part(3, 0, at, c, real * cos3 + imag * sin3)
            put_part(3, 1, at, c, real * sin3 - imag * cos3)
    product_ref[:, wide:] = dot(basis, parts_ref[wide:], ((1,), (1,)))
    group = LANES // RADIX
    weights = 1.0 / period, 2.0 / period
    for r in range(RADIX):
        picked = iota((group, LANES), 1) == iota((group, LANES), 0) * RADIX + r
        for at in range(0, z.kaps, group):
            lanes = slice(at * RADIX, at * RADIX + LANES)
            amp = jnp.sum(jnp.where(picked, amp_ref[:, lanes], 0.0), axis=1, keepdims=True)
            wave = (at + iota((group, LANES), 0)) * RADIX + r
            weight = jnp.where(wave == 0, *weights) if at + r == 0 else weights[1]
            scale_ref[r * z.kaps + at : r * z.kaps + at + group] = jnp.where(
                wave <= (length - 1) // 2, weight * amp, 0.0
            )
    params_ref[: z.levels] = jnp.concatenate([bal_ref[0], bal_ref[0]], axis=1)
    params_ref[z.levels : z.levels + z.lat, : z.lat] = slot_matrix(z, order_ref, mer_ref).astype(BF16)
    count = z.kaps // z.rows
    sign = jnp.where(iota((1, LANES), 1) < z.levels, -1.0, 1.0).astype(F32)
    for r in R_ORDER:
        lanes = tile(R_ORDER.index(r))
        for i in range(count):
            rows = slice(i * z.rows, (i + 1) * z.rows)
            from_sin = product_ref[z.kaps + i * z.rows : z.kaps + (i + 1) * z.rows, lanes]
            both = product_ref[rows, lanes] + pltpu.roll(from_sin, z.levels, 1) * sign
            scale = scale_ref[r * z.kaps + i * z.rows : r * z.kaps + (i + 1) * z.rows]
            packet_ref[r * count + i] = (both * scale).astype(BF16)
    if z.devices > RADIX * count:
        packet_ref[RADIX * count :] = jnp.zeros((z.devices - RADIX * count, z.rows, LANES), BF16)


def matrices_kernel(z, *refs):
    *given, mix_ref, bal_ref, all_ref = refs
    own = lax.axis_index("var")
    for step, ref in enumerate(given):
        all_ref[(own + step) % z.var] = ref[...]
    size = z.mixed
    to_cols = (iota((z.lat, size), 0) == iota((z.lat, size), 1) // z.rows).astype(F32).astype(BF16)
    same = iota((size, size), 0) % z.rows == iota((size, size), 1) % z.rows
    halves = iota((LANES, LANES), 0) // z.levels == iota((LANES, LANES), 1) // z.levels
    for v in range(z.var):
        meridional = all_ref[v, z.levels :].astype(F32)[: z.lat, : z.lat].astype(BF16)
        slot_cols = dot(meridional, to_cols).astype(BF16)
        mix_ref[v] = jnp.where(same, dot(to_cols, slot_cols, ((0,), (0,))), 0.0).astype(BF16)
        if v > 0:
            balance = all_ref[v, : z.levels].astype(F32)
            balance = jnp.where(halves, jnp.concatenate([balance, balance], axis=0), 0.0)
            bal_ref[v - 1] = balance.T.astype(BF16)


def mixing_kernel(z, packet_ref, mix_ref, bal_ref, out_ref):
    stream = None
    for v in range(z.var):
        coeffs = packet_ref[v].astype(F32).reshape(z.mixed, LANES).astype(BF16)
        blended = dot(mix_ref[v], coeffs)
        if v == 0:
            stream = blended.astype(BF16)
        else:
            blended = blended + dot(stream, bal_ref[v - 1])
        blended = blended.reshape(z.lat, z.rows, LANES)
        for s in range(z.lat):
            out_ref[v, s] = blended[s].astype(BF16)


def synthesis_kernel(z, spectra_ref, basis_ref, twiddle_ref, out_ref, sems, field_ref, lhs_ref, parts_ref):
    period = twiddle_ref[2 * RADIX :, :LANES].astype(jnp.int32)
    length = jnp.max(period)
    kap = iota((z.kaps, LANES), 0)
    count = z.kaps // z.rows
    half = z.levels // 2
    kinds = 2 * RADIX - 1
    for at in (0, z.sin):
        lhs_ref[:, at + z.kaps : at + z.sin] = jnp.zeros((2 * half * kinds, z.sin - z.kaps), BF16)
    for r in range(RADIX):
        part = spectra_ref[r * count : (r + 1) * count].astype(F32).reshape(z.kaps, LANES)
        part = jnp.where(kap * RADIX + r <= (period[0:1] - 1) // 2, part, 0.0)
        part = part.astype(BF16).T
        for i in range(2):
            from_cos = part[i * half : (i + 1) * half]
            from_sin = part[z.levels + i * half : z.levels + (i + 1) * half]
            pairs = [(from_cos, from_sin)] if r == 0 else [(from_cos, from_sin), (-from_sin, from_cos)]
            for kind, pair in zip((2 * r - 1, 2 * r) if r else (0,), pairs):
                to = slice((i * kinds + kind) * half, (i * kinds + kind + 1) * half)
                lhs_ref[to, : z.kaps] = pair[0]
                lhs_ref[to, z.sin : z.sin + z.kaps] = pair[1]
    quarter = length // RADIX
    starts = [quarter * j1 for j1 in range(1, RADIX)]
    bases = [pl.multiple_of(s // LANES * LANES, LANES) for s in starts]
    shifts = [s - b for s, b in zip(starts, bases)]
    wide = z.points + LANES
    field_ref[:, wide:] = jnp.zeros((z.levels, z.lons + LANES - wide), BF16)
    keep = [iota((STRIP, LANES), 1) < shift for shift in shifts]
    zero = jnp.zeros((STRIP, LANES), F32)
    for i in range(2):
        rows = slice(i * kinds * half, (i + 1) * kinds * half)
        parts_ref[rows] = dot(lhs_ref[rows], basis_ref[...])
    sent = []
    for at in range(0, z.levels, STRIP):
        rows = slice(at, at + STRIP)
        first = at // half * kinds * half + at % half
        quarters = [[], [], [], []]
        for c in range(z.tiles):
            cos1, cos2, cos3 = [twiddle_ref[r : r + 1, tile(c)] for r in (1, 2, 3)]
            sin1, sin2, sin3 = [twiddle_ref[RADIX + r : RADIX + r + 1, tile(c)] for r in (1, 2, 3)]
            w0, re1, im1, re2, im2, re3, im3 = [
                parts_ref[first + kind * half : first + kind * half + STRIP, tile(c)] for kind in range(kinds)
            ]
            w2 = re2 * cos2 - im2 * sin2
            cross = (re1 * cos1 - im1 * sin1) + (re3 * cos3 - im3 * sin3)
            turn = (re1 * sin1 + im1 * cos1) - (re3 * sin3 + im3 * cos3)
            even, odd = w0 + w2, w0 - w2
            field_ref[rows, tile(c)] = (even + cross).astype(BF16)
            for j1, part in ((1, odd - turn), (2, even - cross), (3, odd + turn)):
                quarters[j1].append(pltpu.roll(part, shifts[j1 - 1], 1))
        field_ref[rows, tile(z.tiles)] = zero.astype(BF16)
        for j1 in range(1, RADIX):
            pieces = zip([zero] + quarters[j1], quarters[j1] + [zero])
            for c, (left, right) in enumerate(pieces):
                lanes = pl.ds(pl.multiple_of(bases[j1 - 1] + c * LANES, LANES), LANES)
                piece = jnp.where(keep[j1 - 1], left, right)
                if c == 0:
                    piece = piece + field_ref[rows, lanes].astype(F32)
                field_ref[rows, lanes] = piece.astype(BF16)
        sent += fetch(
            (field_ref.at[pl.ds(at, STRIP), pl.ds(0, z.lons)],),
            (out_ref.at[0, 0, pl.ds(at, STRIP)],),
            sems.at[pl.ds(at // STRIP, 1)],
        )
    for copy in sent:
        copy.wait()


def body(z, control, row_order, row_length, vertical, amplitude, meridional, balance):
    arguments = (row_order, row_length, control, vertical, amplitude, meridional, balance)
    made = (
        jax.ShapeDtypeStruct((z.devices, z.rows, LANES), BF16),
        jax.ShapeDtypeStruct((z.params, LANES), BF16),
        jax.ShapeDtypeStruct((2 * z.sin, z.points), BF16),
        jax.ShapeDtypeStruct((2 * RADIX + SUBLANES, z.points), F32),
    )
    packets, params, basis, twiddle = pl.pallas_call(
        functools.partial(analysis_kernel, z),
        out_shape=made,
        in_specs=[HBM] * len(arguments),
        out_specs=(VMEM,) * len(made),
        scratch_shapes=[
            *[pltpu.SMEM(x.shape, x.dtype) for x in arguments[:2]],
            *[pltpu.VMEM(x.shape, x.dtype) for x in arguments[2:]],
            pltpu.SemaphoreType.DMA((len(arguments) - 1 + z.levels // STRIP,)),
            pltpu.VMEM((z.levels, z.lons + LANES), F32),
            pltpu.VMEM((2 * RADIX * z.levels, z.points), BF16),
            pltpu.VMEM((2 * z.heads, z.points), F32),
            pltpu.VMEM((2 * STRIP, z.points), F32),
            pltpu.VMEM((z.waves, LANES), F32),
            pltpu.VMEM((2 * z.levels, z.points), F32),
            pltpu.VMEM((2 * z.kaps, RADIX * LANES), F32),
        ],
        compiler_params=PARAMS,
        name="analysis",
    )(*[pltpu.with_memory_space_constraint(x, pltpu.HBM) for x in arguments])
    given = [params]
    for step in range(1, z.var):
        given.append(lax.ppermute(params, "var", [((i + step) % z.var, i) for i in range(z.var)]))
    packets = lax.all_to_all(packets, ("var", "lat"), 0, 0, tiled=True)
    mix, lift = pl.pallas_call(
        functools.partial(matrices_kernel, z),
        out_shape=(
            jax.ShapeDtypeStruct((z.var, z.mixed, z.mixed), BF16),
            jax.ShapeDtypeStruct((z.var - 1, LANES, LANES), BF16),
        ),
        in_specs=[VMEM] * z.var,
        out_specs=(VMEM, VMEM),
        scratch_shapes=[pltpu.VMEM((z.var, z.params, LANES), BF16)],
        compiler_params=PARAMS,
        cost_estimate=pl.CostEstimate(flops=10**8, bytes_accessed=10**6, transcendentals=0),
        name="matrices",
    )(*given)
    balanced = pl.pallas_call(
        functools.partial(mixing_kernel, z),
        out_shape=jax.ShapeDtypeStruct((z.var, z.lat, z.rows, LANES), BF16),
        in_specs=[VMEM] * 3,
        out_specs=VMEM,
        compiler_params=PARAMS,
        name="mixing",
    )(packets.reshape(z.var, z.lat, z.rows, LANES), mix, lift)
    balanced = balanced.reshape(z.devices, z.rows, LANES)
    balanced = lax.all_to_all(balanced, ("var", "lat"), 0, 0, tiled=True)
    return pl.pallas_call(
        functools.partial(synthesis_kernel, z),
        out_shape=jax.ShapeDtypeStruct(control.shape, BF16),
        in_specs=[VMEM] * 3,
        out_specs=HBM,
        scratch_shapes=[
            pltpu.SemaphoreType.DMA((z.levels // STRIP,)),
            pltpu.VMEM((z.levels, z.lons + LANES), BF16),
            pltpu.VMEM(((2 * RADIX - 1) * z.levels, 2 * z.sin), BF16),
            pltpu.VMEM(((2 * RADIX - 1) * z.levels, z.points), F32),
        ],
        compiler_params=PARAMS,
        name="synthesis",
    )(balanced, basis, twiddle)


def solution(mesh):
    placed = (
        P("var", "lat", None, None),
        P(),
        P(),
        P("var", None, None),
        P("var", None),
        P("var", None, None),
        P("var", None, None),
    )

    def run(control, row_order, row_length, vertical, amplitude, meridional, balance):
        lat_total, var_total = mesh.shape["lat"], mesh.shape["var"]
        assert control.shape[0] == var_total and control.shape[1] == lat_total
        z = Sizes(lat_total, var_total, control.shape[2], control.shape[3], amplitude.shape[1])
        return jax.shard_map(
            functools.partial(body, z),
            mesh=mesh,
            in_specs=placed,
            out_specs=P("var", "lat", None, None),
            check_vma=False,
        )(control, row_order, row_length, vertical, amplitude, meridional, balance)

    return run
```

```python
import functools

import jax
import jax.numpy as jnp
from jax import lax
from jax.experimental import pallas as pl
from jax.experimental.pallas import tpu as pltpu
from jax.sharding import PartitionSpec as P

RADIX = 4
R_ORDER = (0, 2, 1, 3)
LANES = 128
SUBLANES = 8
STRIP = 16
F32 = jnp.float32
BF16 = jnp.bfloat16

COS_POLY = (1, -19.7392044, 64.9391174, -85.4501419, 60.1676292, -25.9675999, 6.52865839)
SIN_POLY = (6.28318501, -41.3415909, 81.5999451, -76.6144714, 41.3428841, -12.4712439)

VMEM = pl.BlockSpec(memory_space=pltpu.VMEM)
HBM = pl.BlockSpec(memory_space=pltpu.HBM)
PARAMS = pltpu.CompilerParams(vmem_limit_bytes=32 * 1024 * 1024)


def iota(shape, dim):
    return lax.broadcasted_iota(jnp.int32, shape, dim)


def horner(poly, x):
    total = jnp.full_like(x, poly[-1])
    for term in poly[-2::-1]:
        total = total * x + term
    return total


def cos_sin(turns):
    turns = turns - jnp.round(turns)
    square = turns * turns
    return horner(COS_POLY, square), horner(SIN_POLY, square) * turns


def ceil_div(a, b):
    return -(-a // b)


def round_up(a, b):
    return ceil_div(a, b) * b


def dot(a, b, contract=((1,), (0,))):
    return lax.dot_general(a, b, (contract, ((), ())), preferred_element_type=F32)


class Sizes:
    def __init__(self, lat_total, var_total, levels, lons, waves):
        self.lat, self.var, self.levels, self.lons, self.waves = lat_total, var_total, levels, lons, waves
        self.devices = lat_total * var_total
        self.slots = [*range(0, lat_total, 2), *range(1, lat_total, 2)]
        self.points = lons // RADIX
        self.tiles = self.points // LANES
        self.kaps = waves // RADIX
        self.rows = round_up(ceil_div(waves, self.devices), SUBLANES)
        assert self.kaps % self.rows == 0 and self.points % LANES == 0 and 2 * levels == LANES and lat_total <= LANES
        self.mixed = lat_total * self.rows
        self.sin = round_up(self.kaps, LANES)
        self.heads = round_up(ceil_div(self.kaps, STRIP), SUBLANES)
        self.params = round_up(levels + lat_total, STRIP)


def parts_row(z, r, half, at):
    return (2 * R_ORDER.index(r) + half) * z.levels + at


def own_length(order_ref, length_ref):
    slot = lax.axis_index("lat")
    row = order_ref[slot]
    return slot, row, length_ref[row]


def fetch(sources, targets, sems):
    copies = [pltpu.make_async_copy(s, t, sems.at[i]) for i, (s, t) in enumerate(zip(sources, targets))]
    for copy in copies:
        copy.start()
    return copies


def slot_matrix(z, order_ref, mer_ref):
    slot = iota((z.lat, z.lat), 0)
    row = jnp.zeros((z.lat, z.lat), jnp.int32)
    for t in range(z.lat):
        row = jnp.where(slot == t, order_ref[z.slots[t]], row)
    pick = (row == iota((z.lat, z.lat), 1)).astype(F32).astype(BF16)
    return dot(dot(pick, mer_ref[0]).astype(BF16), pick, ((1,), (1,)))


def tile(c):
    return slice(c * LANES, (c + 1) * LANES)


def analysis_kernel(z, *refs):
    given, made, held = refs[:7], refs[7:11], refs[11:18]
    sems, field_ref, parts_ref, heads_ref, tails_ref, scale_ref, diff_ref, product_ref = refs[18:]
    order_ref, length_ref, control_ref, vert_ref, amp_ref, mer_ref, bal_ref = held
    packet_ref, params_ref, basis_ref, twiddle_ref = made
    copies = fetch(given, held, sems)
    for at in (0, z.sin):
        basis_ref[at + z.kaps : at + z.sin] = jnp.zeros((z.sin - z.kaps, z.points), BF16)
    field_ref[:, z.lons :] = jnp.zeros((z.levels, LANES), F32)
    params_ref[...] = jnp.zeros(params_ref.shape, BF16)
    at = parts_row(z, 0, 1, 0)
    parts_ref[at : at + z.levels] = jnp.zeros((z.levels, z.points), BF16)
    for copy in copies[:2]:
        copy.wait()
    slot, row, length = own_length(order_ref, length_ref)
    quarter = length // RADIX
    period = jnp.full((1, LANES), length, jnp.int32).astype(F32)
    tail = iota((STRIP, LANES), 0).astype(F32)
    head = iota((z.heads, LANES), 0).astype(F32) * STRIP
    tw_row = iota((2 * RADIX, LANES), 0)
    tw_wave = jnp.where(tw_row < RADIX, tw_row, tw_row - RADIX).astype(F32)
    fraction = jnp.full((1, LANES), quarter, jnp.int32).astype(F32)
    for c in range(z.tiles):
        points = c * LANES + iota((1, LANES), 1)
        step = points.astype(F32) / fraction
        tails_ref[:STRIP, tile(c)], tails_ref[STRIP:, tile(c)] = cos_sin(tail * step)
        head_cos, head_sin = cos_sin(head * step)
        heads_ref[: z.heads, tile(c)] = jnp.where(points < quarter, head_cos, 0.0)
        heads_ref[z.heads :, tile(c)] = jnp.where(points < quarter, head_sin, 0.0)
        tw_cos, tw_sin = cos_sin(tw_wave * (points.astype(F32) / period))
        twiddle_ref[: 2 * RADIX, tile(c)] = jnp.where(tw_row < RADIX, tw_cos, tw_sin)
        twiddle_ref[2 * RADIX :, tile(c)] = jnp.broadcast_to(period, (SUBLANES, LANES))
    for copy in copies[2:]:
        copy.wait()
    field_ref[:, : z.lons] = dot(vert_ref[0], control_ref[0, 0])
    for c in range(z.tiles):
        tail_cos, tail_sin = tails_ref[:STRIP, tile(c)], tails_ref[STRIP:, tile(c)]
        for at in range(0, z.kaps, STRIP):
            i = at // STRIP
            head_cos, head_sin = heads_ref[i : i + 1, tile(c)], heads_ref[z.heads + i : z.heads + i + 1, tile(c)]
            basis_ref[at : at + STRIP, tile(c)] = (head_cos * tail_cos - head_sin * tail_sin).astype(BF16)
            to = slice(z.sin + at, z.sin + at + STRIP)
            basis_ref[to, tile(c)] = (head_sin * tail_cos + head_cos * tail_sin).astype(BF16)
    starts = [quarter * j1 for j1 in range(1, RADIX)]
    bases = [pl.multiple_of(s // LANES * LANES, LANES) for s in starts]
    shifts = [(LANES - (s - b)) % LANES for s, b in zip(starts, bases)]
    lane = iota((STRIP, LANES), 1)
    keeps = [(lane < shift) | (shift == 0) for shift in shifts]

    def put_part(r, half, at, c, value):
        to = parts_row(z, r, half, at)
        parts_ref[to : to + STRIP, tile(c)] = value.astype(BF16)

    for at in range(0, z.levels, STRIP):
        rows = slice(at, at + STRIP)

        def rolled(i, c):
            lanes = pl.ds(pl.multiple_of(bases[i] + c * LANES, LANES), LANES)
            return pltpu.roll(field_ref[rows, lanes], shifts[i], 1)

        before = [rolled(i, 0) for i in range(RADIX - 1)]
        for c in range(z.tiles):
            after = [rolled(i, c + 1) for i in range(RADIX - 1)]
            second, third, fourth = [jnp.where(k, a, b) for k, a, b in zip(keeps, before, after)]
            before = after
            first = field_ref[rows, tile(c)]
            even, odd = first + third, second + fourth
            diff_ref[rows, tile(c)] = first - third
            diff_ref[z.levels + at : z.levels + at + STRIP, tile(c)] = second - fourth
            put_part(0, 0, at, c, even + odd)
            turned = even - odd
            put_part(2, 0, at, c, turned * twiddle_ref[2:3, tile(c)])
            put_part(2, 1, at, c, turned * twiddle_ref[RADIX + 2 : RADIX + 3, tile(c)])
    wide = 2 * LANES
    basis = jnp.concatenate([basis_ref[: z.kaps], basis_ref[z.sin : z.sin + z.kaps]], axis=0)
    product_ref[:, :wide] = dot(basis, parts_ref[:wide], ((1,), (1,)))
    for at in range(0, z.levels, STRIP):
        for c in range(z.tiles):
            real = diff_ref[at : at + STRIP, tile(c)]
            imag = diff_ref[z.levels + at : z.levels + at + STRIP, tile(c)]
            cos1, cos3 = twiddle_ref[1:2, tile(c)], twiddle_ref[3:4, tile(c)]
            sin1, sin3 = [twiddle_ref[RADIX + r : RADIX + r + 1, tile(c)] for r in (1, 3)]
            put_part(1, 0, at, c, real * cos1 - imag * sin1)
            put_part(1, 1, at, c, real * sin1 + imag * cos1)
            put_part(3, 0, at, c, real * cos3 + imag * sin3)
            put_part(3, 1, at, c, real * sin3 - imag * cos3)
    product_ref[:, wide:] = dot(basis, parts_ref[wide:], ((1,), (1,)))
    group = LANES // RADIX
    weights = 1.0 / period, 2.0 / period
    for r in range(RADIX):
        picked = iota((group, LANES), 1) == iota((group, LANES), 0) * RADIX + r
        for at in range(0, z.kaps, group):
            lanes = slice(at * RADIX, at * RADIX + LANES)
            amp = jnp.sum(jnp.where(picked, amp_ref[:, lanes], 0.0), axis=1, keepdims=True)
            wave = (at + iota((group, LANES), 0)) * RADIX + r
            weight = jnp.where(wave == 0, *weights) if at + r == 0 else weights[1]
            scale_ref[r * z.kaps + at : r * z.kaps + at + group] = jnp.where(
                wave <= (length - 1) // 2, weight * amp, 0.0
            )
    params_ref[: z.levels] = jnp.concatenate([bal_ref[0], bal_ref[0]], axis=1)
    params_ref[z.levels : z.levels + z.lat, : z.lat] = slot_matrix(z, order_ref, mer_ref).astype(BF16)
    count = z.kaps // z.rows
    sign = jnp.where(iota((1, LANES), 1) < z.levels, -1.0, 1.0).astype(F32)
    for r in R_ORDER:
        lanes = tile(R_ORDER.index(r))
        for i in range(count):
            rows = slice(i * z.rows, (i + 1) * z.rows)
            from_sin = product_ref[z.kaps + i * z.rows : z.kaps + (i + 1) * z.rows, lanes]
            both = product_ref[rows, lanes] + pltpu.roll(from_sin, z.levels, 1) * sign
            scale = scale_ref[r * z.kaps + i * z.rows : r * z.kaps + (i + 1) * z.rows]
            packet_ref[r * count + i] = (both * scale).astype(BF16)
    if z.devices > RADIX * count:
        packet_ref[RADIX * count :] = jnp.zeros((z.devices - RADIX * count, z.rows, LANES), BF16)


def matrices_kernel(z, *refs):
    *given, mix_ref, bal_ref, all_ref = refs
    own = lax.axis_index("var")
    for step, ref in enumerate(given):
        all_ref[(own + step) % z.var] = ref[...]
    size = z.mixed
    to_cols = (iota((z.lat, size), 0) == iota((z.lat, size), 1) // z.rows).astype(F32).astype(BF16)
    same = iota((size, size), 0) % z.rows == iota((size, size), 1) % z.rows
    halves = iota((LANES, LANES), 0) // z.levels == iota((LANES, LANES), 1) // z.levels
    for v in range(z.var):
        meridional = all_ref[v, z.levels :].astype(F32)[: z.lat, : z.lat].astype(BF16)
        slot_cols = dot(meridional, to_cols).astype(BF16)
        mix_ref[v] = jnp.where(same, dot(to_cols, slot_cols, ((0,), (0,))), 0.0).astype(BF16)
        if v > 0:
            balance = all_ref[v, : z.levels].astype(F32)
            balance = jnp.where(halves, jnp.concatenate([balance, balance], axis=0), 0.0)
            bal_ref[v - 1] = balance.T.astype(BF16)


def mixing_kernel(z, packet_ref, mix_ref, bal_ref, out_ref):
    stream = None
    for v in range(z.var):
        coeffs = packet_ref[v].astype(F32).reshape(z.mixed, LANES).astype(BF16)
        blended = dot(mix_ref[v], coeffs)
        if v == 0:
            stream = blended.astype(BF16)
        else:
            blended = blended + dot(stream, bal_ref[v - 1])
        blended = blended.reshape(z.lat, z.rows, LANES)
        for s in range(z.lat):
            out_ref[v, s] = blended[s].astype(BF16)


def synthesis_kernel(z, spectra_ref, basis_ref, twiddle_ref, out_ref, sems, field_ref, lhs_ref, parts_ref):
    period = twiddle_ref[2 * RADIX :, :LANES].astype(jnp.int32)
    length = jnp.max(period)
    kap = iota((z.kaps, LANES), 0)
    count = z.kaps // z.rows
    half = z.levels // 2
    kinds = 2 * RADIX - 1
    for at in (0, z.sin):
        lhs_ref[:, at + z.kaps : at + z.sin] = jnp.zeros((2 * half * kinds, z.sin - z.kaps), BF16)
    for r in range(RADIX):
        part = spectra_ref[r * count : (r + 1) * count].astype(F32).reshape(z.kaps, LANES)
        part = jnp.where(kap * RADIX + r <= (period[0:1] - 1) // 2, part, 0.0)
        part = part.astype(BF16).T
        for i in range(2):
            from_cos = part[i * half : (i + 1) * half]
            from_sin = part[z.levels + i * half : z.levels + (i + 1) * half]
            pairs = [(from_cos, from_sin)] if r == 0 else [(from_cos, from_sin), (-from_sin, from_cos)]
            for kind, pair in zip((2 * r - 1, 2 * r) if r else (0,), pairs):
                to = slice((i * kinds + kind) * half, (i * kinds + kind + 1) * half)
                lhs_ref[to, : z.kaps] = pair[0]
                lhs_ref[to, z.sin : z.sin + z.kaps] = pair[1]
    quarter = length // RADIX
    starts = [quarter * j1 for j1 in range(1, RADIX)]
    bases = [pl.multiple_of(s // LANES * LANES, LANES) for s in starts]
    shifts = [s - b for s, b in zip(starts, bases)]
    wide = z.points + LANES
    field_ref[:, wide:] = jnp.zeros((z.levels, z.lons + LANES - wide), BF16)
    keep = [iota((STRIP, LANES), 1) < shift for shift in shifts]
    zero = jnp.zeros((STRIP, LANES), F32)
    for i in range(2):
        rows = slice(i * kinds * half, (i + 1) * kinds * half)
        parts_ref[rows] = dot(lhs_ref[rows], basis_ref[...])
    sent = []
    for at in range(0, z.levels, STRIP):
        rows = slice(at, at + STRIP)
        first = at // half * kinds * half + at % half
        quarters = [[], [], [], []]
        for c in range(z.tiles):
            cos1, cos2, cos3 = [twiddle_ref[r : r + 1, tile(c)] for r in (1, 2, 3)]
            sin1, sin2, sin3 = [twiddle_ref[RADIX + r : RADIX + r + 1, tile(c)] for r in (1, 2, 3)]
            w0, re1, im1, re2, im2, re3, im3 = [
                parts_ref[first + kind * half : first + kind * half + STRIP, tile(c)] for kind in range(kinds)
            ]
            w2 = re2 * cos2 - im2 * sin2
            cross = (re1 * cos1 - im1 * sin1) + (re3 * cos3 - im3 * sin3)
            turn = (re1 * sin1 + im1 * cos1) - (re3 * sin3 + im3 * cos3)
            even, odd = w0 + w2, w0 - w2
            field_ref[rows, tile(c)] = (even + cross).astype(BF16)
            for j1, part in ((1, odd - turn), (2, even - cross), (3, odd + turn)):
                quarters[j1].append(pltpu.roll(part, shifts[j1 - 1], 1))
        field_ref[rows, tile(z.tiles)] = zero.astype(BF16)
        for j1 in range(1, RADIX):
            pieces = zip([zero] + quarters[j1], quarters[j1] + [zero])
            for c, (left, right) in enumerate(pieces):
                lanes = pl.ds(pl.multiple_of(bases[j1 - 1] + c * LANES, LANES), LANES)
                piece = jnp.where(keep[j1 - 1], left, right)
                if c == 0:
                    piece = piece + field_ref[rows, lanes].astype(F32)
                field_ref[rows, lanes] = piece.astype(BF16)
        sent += fetch(
            (field_ref.at[pl.ds(at, STRIP), pl.ds(0, z.lons)],),
            (out_ref.at[0, 0, pl.ds(at, STRIP)],),
            sems.at[pl.ds(at // STRIP, 1)],
        )
    for copy in sent:
        copy.wait()


def exchange(z, chunks):
    peers = [v * z.lat + slot for v in range(z.var) for slot in z.slots]
    return lax.all_to_all(chunks, ("var", "lat"), 0, 0, axis_index_groups=[peers], tiled=True)


def body(z, control, row_order, row_length, vertical, amplitude, meridional, balance):
    arguments = (row_order, row_length, control, vertical, amplitude, meridional, balance)
    made = (
        jax.ShapeDtypeStruct((z.devices, z.rows, LANES), BF16),
        jax.ShapeDtypeStruct((z.params, LANES), BF16),
        jax.ShapeDtypeStruct((2 * z.sin, z.points), BF16),
        jax.ShapeDtypeStruct((2 * RADIX + SUBLANES, z.points), F32),
    )
    packets, params, basis, twiddle = pl.pallas_call(
        functools.partial(analysis_kernel, z),
        out_shape=made,
        in_specs=[HBM] * len(arguments),
        out_specs=(VMEM,) * len(made),
        scratch_shapes=[
            *[pltpu.SMEM(x.shape, x.dtype) for x in arguments[:2]],
            *[pltpu.VMEM(x.shape, x.dtype) for x in arguments[2:]],
            pltpu.SemaphoreType.DMA((len(arguments),)),
            pltpu.VMEM((z.levels, z.lons + LANES), F32),
            pltpu.VMEM((2 * RADIX * z.levels, z.points), BF16),
            pltpu.VMEM((2 * z.heads, z.points), F32),
            pltpu.VMEM((2 * STRIP, z.points), F32),
            pltpu.VMEM((z.waves, LANES), F32),
            pltpu.VMEM((2 * z.levels, z.points), F32),
            pltpu.VMEM((2 * z.kaps, RADIX * LANES), F32),
        ],
        compiler_params=PARAMS,
        name="analysis",
    )(*[pltpu.with_memory_space_constraint(x, pltpu.HBM) for x in arguments])
    given = [params]
    for step in range(1, z.var):
        given.append(lax.ppermute(params, "var", [((i + step) % z.var, i) for i in range(z.var)]))
    packets = exchange(z, packets)
    mix, lift = pl.pallas_call(
        functools.partial(matrices_kernel, z),
        out_shape=(
            jax.ShapeDtypeStruct((z.var, z.mixed, z.mixed), BF16),
            jax.ShapeDtypeStruct((z.var - 1, LANES, LANES), BF16),
        ),
        in_specs=[VMEM] * z.var,
        out_specs=(VMEM, VMEM),
        scratch_shapes=[pltpu.VMEM((z.var, z.params, LANES), BF16)],
        compiler_params=PARAMS,
        cost_estimate=pl.CostEstimate(flops=10**8, bytes_accessed=10**6, transcendentals=0),
        name="matrices",
    )(*given)
    balanced = pl.pallas_call(
        functools.partial(mixing_kernel, z),
        out_shape=jax.ShapeDtypeStruct((z.var, z.lat, z.rows, LANES), BF16),
        in_specs=[VMEM] * 3,
        out_specs=VMEM,
        compiler_params=PARAMS,
        name="mixing",
    )(packets.reshape(z.var, z.lat, z.rows, LANES), mix, lift)
    balanced = balanced.reshape(z.devices, z.rows, LANES)
    balanced = exchange(z, balanced)
    return pl.pallas_call(
        functools.partial(synthesis_kernel, z),
        out_shape=jax.ShapeDtypeStruct(control.shape, BF16),
        in_specs=[VMEM] * 3,
        out_specs=HBM,
        scratch_shapes=[
            pltpu.SemaphoreType.DMA((z.levels // STRIP,)),
            pltpu.VMEM((z.levels, z.lons + LANES), BF16),
            pltpu.VMEM(((2 * RADIX - 1) * z.levels, 2 * z.sin), BF16),
            pltpu.VMEM(((2 * RADIX - 1) * z.levels, z.points), F32),
        ],
        compiler_params=PARAMS,
        name="synthesis",
    )(balanced, basis, twiddle)


def solution(mesh):
    placed = (
        P("var", "lat", None, None),
        P(),
        P(),
        P("var", None, None),
        P("var", None),
        P("var", None, None),
        P("var", None, None),
    )

    def run(control, row_order, row_length, vertical, amplitude, meridional, balance):
        lat_total, var_total = mesh.shape["lat"], mesh.shape["var"]
        assert control.shape[0] == var_total and control.shape[1] == lat_total
        z = Sizes(lat_total, var_total, control.shape[2], control.shape[3], amplitude.shape[1])
        return jax.shard_map(
            functools.partial(body, z),
            mesh=mesh,
            in_specs=placed,
            out_specs=P("var", "lat", None, None),
            check_vma=False,
        )(control, row_order, row_length, vertical, amplitude, meridional, balance)

    return run
```

```python
import functools
import math

import jax
import jax.numpy as jnp
from jax import lax
from jax.experimental import pallas as pl
from jax.experimental.pallas import tpu as pltpu
from jax.sharding import PartitionSpec as P

RADIX = 4
LANES = 128
SUBLANES = 8
STRIP = 16
F32 = jnp.float32
BF16 = jnp.bfloat16

COS_POLY = (1, -19.7392044, 64.9391174, -85.4501419, 60.1676292, -25.9675999, 6.52865839)
SIN_POLY = (6.28318501, -41.3415909, 81.5999451, -76.6144714, 41.3428841, -12.4712439)

VMEM = pl.BlockSpec(memory_space=pltpu.VMEM)
HBM = pl.BlockSpec(memory_space=pltpu.HBM)
PARAMS = pltpu.CompilerParams(vmem_limit_bytes=32 * 1024 * 1024)


def iota(shape, dim):
    return lax.broadcasted_iota(jnp.int32, shape, dim)


def horner(poly, x):
    total = jnp.full_like(x, poly[-1])
    for term in poly[-2::-1]:
        total = total * x + term
    return total


def cos_sin(turns):
    turns = turns - jnp.round(turns)
    square = turns * turns
    return horner(COS_POLY, square), horner(SIN_POLY, square) * turns


def ceil_div(a, b):
    return -(-a // b)


def round_up(a, b):
    return ceil_div(a, b) * b


def dot(a, b, contract=((1,), (0,))):
    return lax.dot_general(a, b, (contract, ((), ())), preferred_element_type=F32)


class Sizes:
    def __init__(self, lat_total, var_total, levels, lons, waves):
        self.lat, self.var, self.levels, self.lons, self.waves = lat_total, var_total, levels, lons, waves
        self.devices = lat_total * var_total
        self.points = lons // RADIX
        self.tiles = self.points // LANES
        self.block = math.gcd(self.tiles, 2)
        self.kaps = waves // RADIX
        self.rows = round_up(ceil_div(waves, self.devices), SUBLANES)
        assert self.kaps % self.rows == 0 and self.points % LANES == 0 and 2 * levels == LANES and lat_total <= LANES
        self.mixed = lat_total * self.rows
        self.sin = round_up(self.kaps, LANES)
        self.heads = round_up(ceil_div(self.kaps, STRIP), SUBLANES)
        self.params = round_up(levels + lat_total, STRIP)


def own_length(order_ref, length_ref):
    slot = lax.axis_index("lat")
    row = order_ref[slot]
    return slot, row, length_ref[row]


def fetch(sources, targets, sems):
    copies = [pltpu.make_async_copy(s, t, sems.at[i]) for i, (s, t) in enumerate(zip(sources, targets))]
    for copy in copies:
        copy.start()
    return copies


def slot_matrix(z, order_ref, mer_ref):
    slot = iota((z.lat, z.lat), 0)
    row = jnp.zeros((z.lat, z.lat), jnp.int32)
    for t in range(z.lat):
        row = jnp.where(slot == t, order_ref[t], row)
    pick = (row == iota((z.lat, z.lat), 1)).astype(F32).astype(BF16)
    return dot(dot(pick, mer_ref[0]).astype(BF16), pick, ((1,), (1,)))


def tile(c):
    return slice(c * LANES, (c + 1) * LANES)


def analysis_kernel(z, *refs):
    given, made, held = refs[:7], refs[7:11], refs[11:18]
    sems, field_ref, parts_ref, heads_ref, tails_ref, scale_ref, product_ref = refs[18:]
    order_ref, length_ref, control_ref, vert_ref, amp_ref, mer_ref, bal_ref = held
    packet_ref, params_ref, basis_ref, twiddle_ref = made
    copies = fetch(given, held, sems)
    for at in (0, z.sin):
        basis_ref[at + z.kaps : at + z.sin] = jnp.zeros((z.sin - z.kaps, z.points), BF16)
    field_ref[:, z.lons :] = jnp.zeros((z.levels, LANES), F32)
    params_ref[...] = jnp.zeros(params_ref.shape, BF16)
    parts_ref[z.levels : 2 * z.levels] = jnp.zeros((z.levels, z.points), BF16)
    for copy in copies[:2]:
        copy.wait()
    slot, row, length = own_length(order_ref, length_ref)
    quarter = length // RADIX
    period = jnp.full((1, LANES), length, jnp.int32).astype(F32)
    tail = iota((STRIP, LANES), 0).astype(F32)
    head = iota((z.heads, LANES), 0).astype(F32) * STRIP
    tw_row = iota((2 * RADIX, LANES), 0)
    tw_wave = jnp.where(tw_row < RADIX, tw_row, tw_row - RADIX).astype(F32)
    fraction = jnp.full((1, LANES), quarter, jnp.int32).astype(F32)
    for c in range(z.tiles):
        points = c * LANES + iota((1, LANES), 1)
        step = points.astype(F32) / fraction
        tails_ref[:STRIP, tile(c)], tails_ref[STRIP:, tile(c)] = cos_sin(tail * step)
        head_cos, head_sin = cos_sin(head * step)
        heads_ref[: z.heads, tile(c)] = jnp.where(points < quarter, head_cos, 0.0)
        heads_ref[z.heads :, tile(c)] = jnp.where(points < quarter, head_sin, 0.0)
        tw_cos, tw_sin = cos_sin(tw_wave * (points.astype(F32) / period))
        twiddle_ref[: 2 * RADIX, tile(c)] = jnp.where(tw_row < RADIX, tw_cos, tw_sin)
        twiddle_ref[2 * RADIX :, tile(c)] = jnp.broadcast_to(period, (SUBLANES, LANES))
    for copy in copies[2:]:
        copy.wait()
    field_ref[:, : z.lons] = dot(vert_ref[0], control_ref[0, 0])
    starts = [quarter * j1 for j1 in range(1, RADIX)]
    bases = [pl.multiple_of(s // LANES * LANES, LANES) for s in starts]
    shifts = [(LANES - (s - b)) % LANES for s, b in zip(starts, bases)]
    lane = iota((STRIP, LANES), 1)
    keeps = [(lane < shift) | (shift == 0) for shift in shifts]

    def rolled(i, at, c):
        lanes = pl.ds(pl.multiple_of(bases[i] + c * LANES, LANES), LANES)
        return pltpu.roll(field_ref[at : at + STRIP, lanes], shifts[i], 1)

    before = {}
    for block in range(0, z.tiles, z.block):
        for c in range(block, block + z.block):
            tail_cos, tail_sin = tails_ref[:STRIP, tile(c)], tails_ref[STRIP:, tile(c)]
            for at in range(0, z.kaps, STRIP):
                i = at // STRIP
                head_cos, head_sin = heads_ref[i : i + 1, tile(c)], heads_ref[z.heads + i : z.heads + i + 1, tile(c)]
                basis_ref[at : at + STRIP, tile(c)] = (head_cos * tail_cos - head_sin * tail_sin).astype(BF16)
                to = slice(z.sin + at, z.sin + at + STRIP)
                basis_ref[to, tile(c)] = (head_sin * tail_cos + head_cos * tail_sin).astype(BF16)
        for at in range(0, z.levels, STRIP):
            for c in range(block, block + z.block):
                if c == 0:
                    before[at] = [rolled(i, at, 0) for i in range(RADIX - 1)]
                after = [rolled(i, at, c + 1) for i in range(RADIX - 1)]
                second, third, fourth = [jnp.where(k, a, b) for k, a, b in zip(keeps, before[at], after)]
                before[at] = after
                first = field_ref[at : at + STRIP, tile(c)]
                even, odd = first + third, second + fourth
                real, imag, turned = first - third, second - fourth, even - odd
                cos1, cos2, cos3 = [twiddle_ref[r : r + 1, tile(c)] for r in (1, 2, 3)]
                sin1, sin2, sin3 = [twiddle_ref[RADIX + r : RADIX + r + 1, tile(c)] for r in (1, 2, 3)]
                parts = (
                    (even + odd,),
                    (real * cos1 - imag * sin1, real * sin1 + imag * cos1),
                    (turned * cos2, turned * sin2),
                    (real * cos3 + imag * sin3, real * sin3 - imag * cos3),
                )
                for r, pair in enumerate(parts):
                    for half, part in enumerate(pair):
                        to = (2 * r + half) * z.levels + at
                        parts_ref[to : to + STRIP, tile(c)] = part.astype(BF16)
        lanes = slice(block * LANES, (block + z.block) * LANES)
        basis = jnp.concatenate([basis_ref[: z.kaps, lanes], basis_ref[z.sin : z.sin + z.kaps, lanes]], axis=0)
        product = dot(basis, parts_ref[:, lanes], ((1,), (1,)))
        product_ref[...] = product if block == 0 else product_ref[...] + product
    group = LANES // RADIX
    weights = 1.0 / period, 2.0 / period
    for r in range(RADIX):
        picked = iota((group, LANES), 1) == iota((group, LANES), 0) * RADIX + r
        for at in range(0, z.kaps, group):
            lanes = slice(at * RADIX, at * RADIX + LANES)
            amp = jnp.sum(jnp.where(picked, amp_ref[:, lanes], 0.0), axis=1, keepdims=True)
            wave = (at + iota((group, LANES), 0)) * RADIX + r
            weight = jnp.where(wave == 0, *weights) if at + r == 0 else weights[1]
            scale_ref[r * z.kaps + at : r * z.kaps + at + group] = jnp.where(
                wave <= (length - 1) // 2, weight * amp, 0.0
            )
    params_ref[: z.levels] = jnp.concatenate([bal_ref[0], bal_ref[0]], axis=1)
    params_ref[z.levels : z.levels + z.lat, : z.lat] = slot_matrix(z, order_ref, mer_ref).astype(BF16)
    count = z.kaps // z.rows
    sign = jnp.where(iota((1, LANES), 1) < z.levels, -1.0, 1.0).astype(F32)
    for r in range(RADIX):
        lanes = tile(r)
        for i in range(count):
            rows = slice(i * z.rows, (i + 1) * z.rows)
            from_sin = product_ref[z.kaps + i * z.rows : z.kaps + (i + 1) * z.rows, lanes]
            both = product_ref[rows, lanes] + pltpu.roll(from_sin, z.levels, 1) * sign
            scale = scale_ref[r * z.kaps + i * z.rows : r * z.kaps + (i + 1) * z.rows]
            packet_ref[r * count + i] = (both * scale).astype(BF16)
    if z.devices > RADIX * count:
        packet_ref[RADIX * count :] = jnp.zeros((z.devices - RADIX * count, z.rows, LANES), BF16)


def matrices_kernel(z, *refs):
    *given, mix_ref, bal_ref, all_ref = refs
    own = lax.axis_index("var")
    for step, ref in enumerate(given):
        all_ref[(own + step) % z.var] = ref[...]
    size = z.mixed
    to_cols = (iota((z.lat, size), 0) == iota((z.lat, size), 1) // z.rows).astype(F32).astype(BF16)
    same = iota((size, size), 0) % z.rows == iota((size, size), 1) % z.rows
    halves = iota((LANES, LANES), 0) // z.levels == iota((LANES, LANES), 1) // z.levels
    for v in range(z.var):
        meridional = all_ref[v, z.levels :].astype(F32)[: z.lat, : z.lat].astype(BF16)
        slot_cols = dot(meridional, to_cols).astype(BF16)
        mix_ref[v] = jnp.where(same, dot(to_cols, slot_cols, ((0,), (0,))), 0.0).astype(BF16)
        if v > 0:
            balance = all_ref[v, : z.levels].astype(F32)
            balance = jnp.where(halves, jnp.concatenate([balance, balance], axis=0), 0.0)
            bal_ref[v - 1] = balance.T.astype(BF16)


def mixing_kernel(z, packet_ref, mix_ref, bal_ref, out_ref):
    stream = None
    for v in range(z.var):
        coeffs = packet_ref[v].astype(F32).reshape(z.mixed, LANES).astype(BF16)
        blended = dot(mix_ref[v], coeffs)
        if v == 0:
            stream = blended.astype(BF16)
        else:
            blended = blended + dot(stream, bal_ref[v - 1])
        blended = blended.reshape(z.lat, z.rows, LANES)
        for s in range(z.lat):
            out_ref[v, s] = blended[s].astype(BF16)


def synthesis_kernel(z, spectra_ref, basis_ref, twiddle_ref, out_ref, sems, field_ref, lhs_ref, parts_ref):
    period = twiddle_ref[2 * RADIX :, :LANES].astype(jnp.int32)
    length = jnp.max(period)
    kap = iota((z.kaps, LANES), 0)
    count = z.kaps // z.rows
    half = z.levels // 2
    kinds = 2 * RADIX - 1
    for at in (0, z.sin):
        lhs_ref[:, at + z.kaps : at + z.sin] = jnp.zeros((2 * half * kinds, z.sin - z.kaps), BF16)
    for r in range(RADIX):
        part = spectra_ref[r * count : (r + 1) * count].astype(F32).reshape(z.kaps, LANES)
        part = jnp.where(kap * RADIX + r <= (period[0:1] - 1) // 2, part, 0.0)
        part = part.astype(BF16).T
        for i in range(2):
            from_cos = part[i * half : (i + 1) * half]
            from_sin = part[z.levels + i * half : z.levels + (i + 1) * half]
            pairs = [(from_cos, from_sin)] if r == 0 else [(from_cos, from_sin), (-from_sin, from_cos)]
            for kind, pair in zip((2 * r - 1, 2 * r) if r else (0,), pairs):
                to = slice((i * kinds + kind) * half, (i * kinds + kind + 1) * half)
                lhs_ref[to, : z.kaps] = pair[0]
                lhs_ref[to, z.sin : z.sin + z.kaps] = pair[1]
    quarter = length // RADIX
    starts = [quarter * j1 for j1 in range(1, RADIX)]
    bases = [pl.multiple_of(s // LANES * LANES, LANES) for s in starts]
    shifts = [s - b for s, b in zip(starts, bases)]
    wide = z.points + LANES
    field_ref[:, wide:] = jnp.zeros((z.levels, z.lons + LANES - wide), BF16)
    keep = [iota((STRIP, LANES), 1) < shift for shift in shifts]
    zero = jnp.zeros((STRIP, LANES), F32)
    for i in range(2):
        rows = slice(i * kinds * half, (i + 1) * kinds * half)
        parts_ref[rows] = dot(lhs_ref[rows], basis_ref[...])
    sent = []
    for at in range(0, z.levels, STRIP):
        rows = slice(at, at + STRIP)
        first = at // half * kinds * half + at % half
        quarters = [[], [], [], []]
        for c in range(z.tiles):
            cos1, cos2, cos3 = [twiddle_ref[r : r + 1, tile(c)] for r in (1, 2, 3)]
            sin1, sin2, sin3 = [twiddle_ref[RADIX + r : RADIX + r + 1, tile(c)] for r in (1, 2, 3)]
            w0, re1, im1, re2, im2, re3, im3 = [
                parts_ref[first + kind * half : first + kind * half + STRIP, tile(c)] for kind in range(kinds)
            ]
            w2 = re2 * cos2 - im2 * sin2
            cross = (re1 * cos1 - im1 * sin1) + (re3 * cos3 - im3 * sin3)
            turn = (re1 * sin1 + im1 * cos1) - (re3 * sin3 + im3 * cos3)
            even, odd = w0 + w2, w0 - w2
            field_ref[rows, tile(c)] = (even + cross).astype(BF16)
            for j1, part in ((1, odd - turn), (2, even - cross), (3, odd + turn)):
                quarters[j1].append(pltpu.roll(part, shifts[j1 - 1], 1))
        field_ref[rows, tile(z.tiles)] = zero.astype(BF16)
        for j1 in range(1, RADIX):
            pieces = zip([zero] + quarters[j1], quarters[j1] + [zero])
            for c, (left, right) in enumerate(pieces):
                lanes = pl.ds(pl.multiple_of(bases[j1 - 1] + c * LANES, LANES), LANES)
                piece = jnp.where(keep[j1 - 1], left, right)
                if c == 0:
                    piece = piece + field_ref[rows, lanes].astype(F32)
                field_ref[rows, lanes] = piece.astype(BF16)
        sent += fetch(
            (field_ref.at[pl.ds(at, STRIP), pl.ds(0, z.lons)],),
            (out_ref.at[0, 0, pl.ds(at, STRIP)],),
            sems.at[pl.ds(at // STRIP, 1)],
        )
    for copy in sent:
        copy.wait()


def body(z, control, row_order, row_length, vertical, amplitude, meridional, balance):
    arguments = (row_order, row_length, control, vertical, amplitude, meridional, balance)
    made = (
        jax.ShapeDtypeStruct((z.devices, z.rows, LANES), BF16),
        jax.ShapeDtypeStruct((z.params, LANES), BF16),
        jax.ShapeDtypeStruct((2 * z.sin, z.points), BF16),
        jax.ShapeDtypeStruct((2 * RADIX + SUBLANES, z.points), F32),
    )
    packets, params, basis, twiddle = pl.pallas_call(
        functools.partial(analysis_kernel, z),
        out_shape=made,
        in_specs=[HBM] * len(arguments),
        out_specs=(VMEM,) * len(made),
        scratch_shapes=[
            *[pltpu.SMEM(x.shape, x.dtype) for x in arguments[:2]],
            *[pltpu.VMEM(x.shape, x.dtype) for x in arguments[2:]],
            pltpu.SemaphoreType.DMA((len(arguments),)),
            pltpu.VMEM((z.levels, z.lons + LANES), F32),
            pltpu.VMEM((2 * RADIX * z.levels, z.points), BF16),
            pltpu.VMEM((2 * z.heads, z.points), F32),
            pltpu.VMEM((2 * STRIP, z.points), F32),
            pltpu.VMEM((z.waves, LANES), F32),
            pltpu.VMEM((2 * z.kaps, RADIX * LANES), F32),
        ],
        compiler_params=PARAMS,
        name="analysis",
    )(*[pltpu.with_memory_space_constraint(x, pltpu.HBM) for x in arguments])
    given = [params]
    for step in range(1, z.var):
        given.append(lax.ppermute(params, "var", [((i + step) % z.var, i) for i in range(z.var)]))
    packets = lax.all_to_all(packets, ("var", "lat"), 0, 0, tiled=True)
    mix, lift = pl.pallas_call(
        functools.partial(matrices_kernel, z),
        out_shape=(
            jax.ShapeDtypeStruct((z.var, z.mixed, z.mixed), BF16),
            jax.ShapeDtypeStruct((z.var - 1, LANES, LANES), BF16),
        ),
        in_specs=[VMEM] * z.var,
        out_specs=(VMEM, VMEM),
        scratch_shapes=[pltpu.VMEM((z.var, z.params, LANES), BF16)],
        compiler_params=PARAMS,
        cost_estimate=pl.CostEstimate(flops=10**8, bytes_accessed=10**6, transcendentals=0),
        name="matrices",
    )(*given)
    balanced = pl.pallas_call(
        functools.partial(mixing_kernel, z),
        out_shape=jax.ShapeDtypeStruct((z.var, z.lat, z.rows, LANES), BF16),
        in_specs=[VMEM] * 3,
        out_specs=VMEM,
        compiler_params=PARAMS,
        name="mixing",
    )(packets.reshape(z.var, z.lat, z.rows, LANES), mix, lift)
    balanced = balanced.reshape(z.devices, z.rows, LANES)
    balanced = lax.all_to_all(balanced, ("var", "lat"), 0, 0, tiled=True)
    return pl.pallas_call(
        functools.partial(synthesis_kernel, z),
        out_shape=jax.ShapeDtypeStruct(control.shape, BF16),
        in_specs=[VMEM] * 3,
        out_specs=HBM,
        scratch_shapes=[
            pltpu.SemaphoreType.DMA((z.levels // STRIP,)),
            pltpu.VMEM((z.levels, z.lons + LANES), BF16),
            pltpu.VMEM(((2 * RADIX - 1) * z.levels, 2 * z.sin), BF16),
            pltpu.VMEM(((2 * RADIX - 1) * z.levels, z.points), F32),
        ],
        compiler_params=PARAMS,
        name="synthesis",
    )(balanced, basis, twiddle)


def solution(mesh):
    placed = (
        P("var", "lat", None, None),
        P(),
        P(),
        P("var", None, None),
        P("var", None),
        P("var", None, None),
        P("var", None, None),
    )

    def run(control, row_order, row_length, vertical, amplitude, meridional, balance):
        lat_total, var_total = mesh.shape["lat"], mesh.shape["var"]
        assert control.shape[0] == var_total and control.shape[1] == lat_total
        z = Sizes(lat_total, var_total, control.shape[2], control.shape[3], amplitude.shape[1])
        return jax.shard_map(
            functools.partial(body, z),
            mesh=mesh,
            in_specs=placed,
            out_specs=P("var", "lat", None, None),
            check_vma=False,
        )(control, row_order, row_length, vertical, amplitude, meridional, balance)

    return run
```

```python
import functools
import math

import jax
import jax.numpy as jnp
from jax import lax
from jax.experimental import pallas as pl
from jax.experimental.pallas import tpu as pltpu
from jax.sharding import PartitionSpec as P

RADIX = 4
LANES = 128
SUBLANES = 8
STRIP = 16
F32 = jnp.float32
BF16 = jnp.bfloat16

COS_POLY = (1, -19.7392044, 64.9391174, -85.4501419, 60.1676292, -25.9675999, 6.52865839)
SIN_POLY = (6.28318501, -41.3415909, 81.5999451, -76.6144714, 41.3428841, -12.4712439)

VMEM = pl.BlockSpec(memory_space=pltpu.VMEM)
HBM = pl.BlockSpec(memory_space=pltpu.HBM)
PARAMS = pltpu.CompilerParams(vmem_limit_bytes=32 * 1024 * 1024)


def iota(shape, dim):
    return lax.broadcasted_iota(jnp.int32, shape, dim)


def horner(poly, x):
    total = jnp.full_like(x, poly[-1])
    for term in poly[-2::-1]:
        total = total * x + term
    return total


def cos_sin(turns):
    turns = turns - jnp.round(turns)
    square = turns * turns
    return horner(COS_POLY, square), horner(SIN_POLY, square) * turns


def ceil_div(a, b):
    return -(-a // b)


def round_up(a, b):
    return ceil_div(a, b) * b


def dot(a, b, contract=((1,), (0,))):
    return lax.dot_general(a, b, (contract, ((), ())), preferred_element_type=F32)


class Sizes:
    def __init__(self, lat_total, var_total, levels, lons, waves):
        self.lat, self.var, self.levels, self.lons, self.waves = lat_total, var_total, levels, lons, waves
        self.devices = lat_total * var_total
        self.points = lons // RADIX
        self.tiles = self.points // LANES
        self.kinds = 2 * RADIX - 1
        self.block = math.gcd(self.tiles, 2)
        self.kaps = waves // RADIX
        self.rows = round_up(ceil_div(waves, self.devices), SUBLANES)
        assert self.kaps % self.rows == 0 and self.points % LANES == 0 and 2 * levels == LANES and lat_total <= LANES
        self.mixed = lat_total * self.rows
        self.sin = round_up(self.kaps, LANES)
        self.heads = round_up(ceil_div(self.kaps, STRIP), SUBLANES)
        self.params = round_up(levels + lat_total, STRIP)


def own_length(order_ref, length_ref):
    slot = lax.axis_index("lat")
    row = order_ref[slot]
    return slot, row, length_ref[row]


def fetch(sources, targets, sems):
    copies = [pltpu.make_async_copy(s, t, sems.at[i]) for i, (s, t) in enumerate(zip(sources, targets))]
    for copy in copies:
        copy.start()
    return copies


def slot_matrix(z, order_ref, mer_ref):
    slot = iota((z.lat, z.lat), 0)
    row = jnp.zeros((z.lat, z.lat), jnp.int32)
    for t in range(z.lat):
        row = jnp.where(slot == t, order_ref[t], row)
    pick = (row == iota((z.lat, z.lat), 1)).astype(F32).astype(BF16)
    return dot(dot(pick, mer_ref[0]).astype(BF16), pick, ((1,), (1,)))


def tile(c):
    return slice(c * LANES, (c + 1) * LANES)


def basis_tables(tails_ref, heads_ref, lanes, step, inside=True):
    heads = heads_ref.shape[0] // 2
    tails_ref[:STRIP, lanes], tails_ref[STRIP:, lanes] = cos_sin(iota((STRIP, LANES), 0).astype(F32) * step)
    cosine, sine = cos_sin(iota((heads, LANES), 0).astype(F32) * STRIP * step)
    heads_ref[:heads, lanes], heads_ref[heads:, lanes] = jnp.where(inside, cosine, 0.0), jnp.where(inside, sine, 0.0)


def basis_strip(tails_ref, heads_ref, lanes, i):
    heads = heads_ref.shape[0] // 2
    tail_cos, tail_sin = tails_ref[:STRIP, lanes], tails_ref[STRIP:, lanes]
    head_cos, head_sin = heads_ref[i : i + 1, lanes], heads_ref[heads + i : heads + i + 1, lanes]
    cosine = head_cos * tail_cos - head_sin * tail_sin
    sine = head_sin * tail_cos + head_cos * tail_sin
    return cosine.astype(BF16), sine.astype(BF16)


def analysis_kernel(z, *refs):
    given, made, held = refs[:7], refs[7:10], refs[10:17]
    sems, field_ref, parts_ref, heads_ref, tails_ref, basis_ref, scale_ref, product_ref = refs[17:]
    order_ref, length_ref, control_ref, vert_ref, amp_ref, mer_ref, bal_ref = held
    packet_ref, params_ref, twiddle_ref = made
    copies = fetch(given, held, sems)
    field_ref[:, z.lons :] = jnp.zeros((z.levels, LANES), F32)
    params_ref[...] = jnp.zeros(params_ref.shape, BF16)
    for copy in copies[:2]:
        copy.wait()
    slot, row, length = own_length(order_ref, length_ref)
    quarter = length // RADIX
    period = jnp.full((1, LANES), length, jnp.int32).astype(F32)
    fraction = jnp.full((1, LANES), quarter, jnp.int32).astype(F32)
    for c in range(z.sin // LANES):
        kap = (c * LANES + iota((1, LANES), 1)).astype(F32)
        basis_tables(tails_ref, heads_ref, tile(c), kap / fraction)
    tw_row = iota((2 * RADIX, LANES), 0)
    tw_wave = jnp.where(tw_row < RADIX, tw_row, tw_row - RADIX).astype(F32)
    for c in range(z.tiles):
        points = (c * LANES + iota((1, LANES), 1)).astype(F32)
        tw_cos, tw_sin = cos_sin(tw_wave * (points / period))
        twiddle_ref[: 2 * RADIX, tile(c)] = jnp.where(tw_row < RADIX, tw_cos, tw_sin)
        twiddle_ref[2 * RADIX :, tile(c)] = jnp.broadcast_to(period, (SUBLANES, LANES))
    for copy in copies[2:]:
        copy.wait()
    field_ref[:, : z.lons] = dot(vert_ref[0], control_ref[0, 0])
    starts = [quarter * j1 for j1 in range(1, RADIX)]
    bases = [pl.multiple_of(s // LANES * LANES, LANES) for s in starts]
    shifts = [(LANES - (s - b)) % LANES for s, b in zip(starts, bases)]
    lane = iota((STRIP, LANES), 1)
    keeps = [(lane < shift) | (shift == 0) for shift in shifts]

    def rolled(i, at, c):
        lanes = pl.ds(pl.multiple_of(bases[i] + c * LANES, LANES), LANES)
        return pltpu.roll(field_ref[at : at + STRIP, lanes], shifts[i], 1)

    before = {}
    for block in range(0, z.tiles, z.block):
        for i in range(block * LANES // STRIP, (block + z.block) * LANES // STRIP):
            for c in range(z.sin // LANES):
                cosine, sine = basis_strip(tails_ref, heads_ref, tile(c), i)
                basis_ref[i * STRIP : (i + 1) * STRIP, tile(c)] = cosine
                basis_ref[i * STRIP : (i + 1) * STRIP, tile(z.sin // LANES + c)] = sine
        for at in range(0, z.levels, STRIP):
            for c in range(block, block + z.block):
                if c == 0:
                    before[at] = [rolled(i, at, 0) for i in range(RADIX - 1)]
                after = [rolled(i, at, c + 1) for i in range(RADIX - 1)]
                quarters = [jnp.where(k, a, b) for k, a, b in zip(keeps, before[at], after)]
                before[at] = after
                inside = c * LANES + lane < quarter
                quarters = [jnp.where(inside, x, 0.0) for x in [field_ref[at : at + STRIP, tile(c)], *quarters]]
                first, second, third, fourth = quarters
                even, odd = first + third, second + fourth
                real, imag, turned = first - third, second - fourth, even - odd
                cos1, cos2, cos3 = [twiddle_ref[r : r + 1, tile(c)] for r in (1, 2, 3)]
                sin1, sin2, sin3 = [twiddle_ref[RADIX + r : RADIX + r + 1, tile(c)] for r in (1, 2, 3)]
                parts = (
                    even + odd,
                    *(real * cos1 - imag * sin1, real * sin1 + imag * cos1),
                    *(turned * cos2, turned * sin2),
                    *(real * cos3 + imag * sin3, real * sin3 - imag * cos3),
                )
                for kind, part in enumerate(parts):
                    to = kind * z.levels + at
                    parts_ref[to : to + STRIP, tile(c)] = part.astype(BF16)
        lanes = slice(block * LANES, (block + z.block) * LANES)
        product = dot(parts_ref[:, lanes], basis_ref[lanes])
        product_ref[...] = product if block == 0 else product_ref[...] + product
    group = LANES // RADIX
    weights = 1.0 / period, 2.0 / period
    for r in range(RADIX):
        picked = iota((group, LANES), 1) == iota((group, LANES), 0) * RADIX + r
        for at in range(0, z.kaps, group):
            lanes = slice(at * RADIX, at * RADIX + LANES)
            amp = jnp.sum(jnp.where(picked, amp_ref[:, lanes], 0.0), axis=1, keepdims=True)
            wave = (at + iota((group, LANES), 0)) * RADIX + r
            weight = jnp.where(wave == 0, *weights) if at + r == 0 else weights[1]
            scale_ref[r * z.kaps + at : r * z.kaps + at + group] = jnp.where(
                wave <= (length - 1) // 2, weight * amp, 0.0
            )
    params_ref[: z.levels] = jnp.concatenate([bal_ref[0], bal_ref[0]], axis=1)
    params_ref[z.levels : z.levels + z.lat, : z.lat] = slot_matrix(z, order_ref, mer_ref).astype(BF16)
    count = z.kaps // z.rows
    for r in range(RADIX):
        at = max(2 * r - 1, 0) * z.levels
        cosine, sine = product_ref[at : at + z.levels, : z.sin], product_ref[at : at + z.levels, z.sin :]
        if r > 0:
            at += z.levels
            cosine = cosine - product_ref[at : at + z.levels, z.sin :]
            sine = sine + product_ref[at : at + z.levels, : z.sin]
        both = jnp.concatenate([cosine, sine], axis=0).T
        for i in range(count):
            scale = scale_ref[r * z.kaps + i * z.rows : r * z.kaps + (i + 1) * z.rows]
            packet_ref[r * count + i] = (both[i * z.rows : (i + 1) * z.rows] * scale).astype(BF16)
    if z.devices > RADIX * count:
        packet_ref[RADIX * count :] = jnp.zeros((z.devices - RADIX * count, z.rows, LANES), BF16)


def matrices_kernel(z, *refs):
    *given, twiddle_ref, mix_ref, bal_ref, basis_ref, all_ref, heads_ref, tails_ref = refs
    own = lax.axis_index("var")
    for step, ref in enumerate(given):
        all_ref[(own + step) % z.var] = ref[...]
    size = z.mixed
    to_cols = (iota((z.lat, size), 0) == iota((z.lat, size), 1) // z.rows).astype(F32).astype(BF16)
    same = iota((size, size), 0) % z.rows == iota((size, size), 1) % z.rows
    halves = iota((LANES, LANES), 0) // z.levels == iota((LANES, LANES), 1) // z.levels
    for v in range(z.var):
        meridional = all_ref[v, z.levels :].astype(F32)[: z.lat, : z.lat].astype(BF16)
        slot_cols = dot(meridional, to_cols).astype(BF16)
        mix_ref[v] = jnp.where(same, dot(to_cols, slot_cols, ((0,), (0,))), 0.0).astype(BF16)
        if v > 0:
            balance = all_ref[v, : z.levels].astype(F32)
            balance = jnp.where(halves, jnp.concatenate([balance, balance], axis=0), 0.0)
            bal_ref[v - 1] = balance.T.astype(BF16)
    fraction = twiddle_ref[2 * RADIX : 2 * RADIX + 1, :LANES] * (1.0 / RADIX)
    for at in (0, z.sin):
        basis_ref[at + z.kaps : at + z.sin] = jnp.zeros((z.sin - z.kaps, z.points), BF16)
    for c in range(z.tiles):
        points = (c * LANES + iota((1, LANES), 1)).astype(F32)
        basis_tables(tails_ref, heads_ref, tile(c), points / fraction, points < fraction)
        for at in range(0, z.kaps, STRIP):
            cosine, sine = basis_strip(tails_ref, heads_ref, tile(c), at // STRIP)
            basis_ref[at : at + STRIP, tile(c)] = cosine
            basis_ref[z.sin + at : z.sin + at + STRIP, tile(c)] = sine


def mixing_kernel(z, packet_ref, mix_ref, bal_ref, out_ref):
    stream = None
    for v in range(z.var):
        coeffs = packet_ref[v].astype(F32).reshape(z.mixed, LANES).astype(BF16)
        blended = dot(mix_ref[v], coeffs)
        if v == 0:
            stream = blended.astype(BF16)
        else:
            blended = blended + dot(stream, bal_ref[v - 1])
        blended = blended.reshape(z.lat, z.rows, LANES)
        for s in range(z.lat):
            out_ref[v, s] = blended[s].astype(BF16)


def synthesis_kernel(z, spectra_ref, basis_ref, twiddle_ref, out_ref, sems, field_ref, lhs_ref, parts_ref):
    period = twiddle_ref[2 * RADIX :, :LANES].astype(jnp.int32)
    length = jnp.max(period)
    kap = iota((z.kaps, LANES), 0)
    count = z.kaps // z.rows
    half = z.levels // 2
    kinds = z.kinds
    for at in (0, z.sin):
        lhs_ref[:, at + z.kaps : at + z.sin] = jnp.zeros((2 * half * kinds, z.sin - z.kaps), BF16)
    for r in range(RADIX):
        part = spectra_ref[r * count : (r + 1) * count].astype(F32).reshape(z.kaps, LANES)
        part = jnp.where(kap * RADIX + r <= (period[0:1] - 1) // 2, part, 0.0)
        part = part.astype(BF16).T
        for i in range(2):
            from_cos = part[i * half : (i + 1) * half]
            from_sin = part[z.levels + i * half : z.levels + (i + 1) * half]
            pairs = [(from_cos, from_sin)] if r == 0 else [(from_cos, from_sin), (-from_sin, from_cos)]
            for kind, pair in zip((2 * r - 1, 2 * r) if r else (0,), pairs):
                to = slice((i * kinds + kind) * half, (i * kinds + kind + 1) * half)
                lhs_ref[to, : z.kaps] = pair[0]
                lhs_ref[to, z.sin : z.sin + z.kaps] = pair[1]
    quarter = length // RADIX
    starts = [quarter * j1 for j1 in range(1, RADIX)]
    bases = [pl.multiple_of(s // LANES * LANES, LANES) for s in starts]
    shifts = [s - b for s, b in zip(starts, bases)]
    wide = z.points + LANES
    field_ref[:, wide:] = jnp.zeros((z.levels, z.lons + LANES - wide), BF16)
    keep = [iota((STRIP, LANES), 1) < shift for shift in shifts]
    zero = jnp.zeros((STRIP, LANES), F32)
    for i in range(2):
        rows = slice(i * kinds * half, (i + 1) * kinds * half)
        parts_ref[rows] = dot(lhs_ref[rows], basis_ref[...])
    sent = []
    for at in range(0, z.levels, STRIP):
        rows = slice(at, at + STRIP)
        first = at // half * kinds * half + at % half
        quarters = [[], [], [], []]
        for c in range(z.tiles):
            cos1, cos2, cos3 = [twiddle_ref[r : r + 1, tile(c)] for r in (1, 2, 3)]
            sin1, sin2, sin3 = [twiddle_ref[RADIX + r : RADIX + r + 1, tile(c)] for r in (1, 2, 3)]
            w0, re1, im1, re2, im2, re3, im3 = [
                parts_ref[first + kind * half : first + kind * half + STRIP, tile(c)] for kind in range(kinds)
            ]
            w2 = re2 * cos2 - im2 * sin2
            cross = (re1 * cos1 - im1 * sin1) + (re3 * cos3 - im3 * sin3)
            turn = (re1 * sin1 + im1 * cos1) - (re3 * sin3 + im3 * cos3)
            even, odd = w0 + w2, w0 - w2
            field_ref[rows, tile(c)] = (even + cross).astype(BF16)
            for j1, part in ((1, odd - turn), (2, even - cross), (3, odd + turn)):
                quarters[j1].append(pltpu.roll(part, shifts[j1 - 1], 1))
        field_ref[rows, tile(z.tiles)] = zero.astype(BF16)
        for j1 in range(1, RADIX):
            pieces = zip([zero] + quarters[j1], quarters[j1] + [zero])
            for c, (left, right) in enumerate(pieces):
                lanes = pl.ds(pl.multiple_of(bases[j1 - 1] + c * LANES, LANES), LANES)
                piece = jnp.where(keep[j1 - 1], left, right)
                if c == 0:
                    piece = piece + field_ref[rows, lanes].astype(F32)
                field_ref[rows, lanes] = piece.astype(BF16)
        sent += fetch(
            (field_ref.at[pl.ds(at, STRIP), pl.ds(0, z.lons)],),
            (out_ref.at[0, 0, pl.ds(at, STRIP)],),
            sems.at[pl.ds(at // STRIP, 1)],
        )
    for copy in sent:
        copy.wait()


def body(z, control, row_order, row_length, vertical, amplitude, meridional, balance):
    arguments = (row_order, row_length, control, vertical, amplitude, meridional, balance)
    made = (
        jax.ShapeDtypeStruct((z.devices, z.rows, LANES), BF16),
        jax.ShapeDtypeStruct((z.params, LANES), BF16),
        jax.ShapeDtypeStruct((2 * RADIX + SUBLANES, z.points), F32),
    )
    packets, params, twiddle = pl.pallas_call(
        functools.partial(analysis_kernel, z),
        out_shape=made,
        in_specs=[HBM] * len(arguments),
        out_specs=(VMEM,) * len(made),
        scratch_shapes=[
            *[pltpu.SMEM(x.shape, x.dtype) for x in arguments[:2]],
            *[pltpu.VMEM(x.shape, x.dtype) for x in arguments[2:]],
            pltpu.SemaphoreType.DMA((len(arguments),)),
            pltpu.VMEM((z.levels, z.lons + LANES), F32),
            pltpu.VMEM((z.kinds * z.levels, z.points), BF16),
            pltpu.VMEM((2 * z.points // STRIP, z.sin), F32),
            pltpu.VMEM((2 * STRIP, z.sin), F32),
            pltpu.VMEM((z.points, 2 * z.sin), BF16),
            pltpu.VMEM((z.waves, LANES), F32),
            pltpu.VMEM((z.kinds * z.levels, 2 * z.sin), F32),
        ],
        compiler_params=PARAMS,
        name="analysis",
    )(*[pltpu.with_memory_space_constraint(x, pltpu.HBM) for x in arguments])
    given = [params]
    for step in range(1, z.var):
        given.append(lax.ppermute(params, "var", [((i + step) % z.var, i) for i in range(z.var)]))
    packets = lax.all_to_all(packets, ("var", "lat"), 0, 0, tiled=True)
    mix, lift, basis = pl.pallas_call(
        functools.partial(matrices_kernel, z),
        out_shape=(
            jax.ShapeDtypeStruct((z.var, z.mixed, z.mixed), BF16),
            jax.ShapeDtypeStruct((z.var - 1, LANES, LANES), BF16),
            jax.ShapeDtypeStruct((2 * z.sin, z.points), BF16),
        ),
        in_specs=[VMEM] * (z.var + 1),
        out_specs=(VMEM,) * 3,
        scratch_shapes=[
            pltpu.VMEM((z.var, z.params, LANES), BF16),
            pltpu.VMEM((2 * z.heads, z.points), F32),
            pltpu.VMEM((2 * STRIP, z.points), F32),
        ],
        compiler_params=PARAMS,
        cost_estimate=pl.CostEstimate(flops=10**8, bytes_accessed=10**6, transcendentals=0),
        name="matrices",
    )(*given, twiddle)
    balanced = pl.pallas_call(
        functools.partial(mixing_kernel, z),
        out_shape=jax.ShapeDtypeStruct((z.var, z.lat, z.rows, LANES), BF16),
        in_specs=[VMEM] * 3,
        out_specs=VMEM,
        compiler_params=PARAMS,
        name="mixing",
    )(packets.reshape(z.var, z.lat, z.rows, LANES), mix, lift)
    balanced = balanced.reshape(z.devices, z.rows, LANES)
    balanced = lax.all_to_all(balanced, ("var", "lat"), 0, 0, tiled=True)
    return pl.pallas_call(
        functools.partial(synthesis_kernel, z),
        out_shape=jax.ShapeDtypeStruct(control.shape, BF16),
        in_specs=[VMEM] * 3,
        out_specs=HBM,
        scratch_shapes=[
            pltpu.SemaphoreType.DMA((z.levels // STRIP,)),
            pltpu.VMEM((z.levels, z.lons + LANES), BF16),
            pltpu.VMEM((z.kinds * z.levels, 2 * z.sin), BF16),
            pltpu.VMEM((z.kinds * z.levels, z.points), F32),
        ],
        compiler_params=PARAMS,
        name="synthesis",
    )(balanced, basis, twiddle)


def solution(mesh):
    placed = (
        P("var", "lat", None, None),
        P(),
        P(),
        P("var", None, None),
        P("var", None),
        P("var", None, None),
        P("var", None, None),
    )

    def run(control, row_order, row_length, vertical, amplitude, meridional, balance):
        lat_total, var_total = mesh.shape["lat"], mesh.shape["var"]
        assert control.shape[0] == var_total and control.shape[1] == lat_total
        z = Sizes(lat_total, var_total, control.shape[2], control.shape[3], amplitude.shape[1])
        return jax.shard_map(
            functools.partial(body, z),
            mesh=mesh,
            in_specs=placed,
            out_specs=P("var", "lat", None, None),
            check_vma=False,
        )(control, row_order, row_length, vertical, amplitude, meridional, balance)

    return run
```

```python
import functools
import math

import jax
import jax.numpy as jnp
from jax import lax
from jax.experimental import pallas as pl
from jax.experimental.pallas import tpu as pltpu
from jax.sharding import PartitionSpec as P

RADIX = 4
LANES = 128
SUBLANES = 8
STRIP = 16
F32 = jnp.float32
BF16 = jnp.bfloat16

COS_POLY = (1, -19.7392044, 64.9391174, -85.4501419, 60.1676292, -25.9675999, 6.52865839)
SIN_POLY = (6.28318501, -41.3415909, 81.5999451, -76.6144714, 41.3428841, -12.4712439)

VMEM = pl.BlockSpec(memory_space=pltpu.VMEM)
HBM = pl.BlockSpec(memory_space=pltpu.HBM)
PARAMS = pltpu.CompilerParams(vmem_limit_bytes=32 * 1024 * 1024)


def iota(shape, dim):
    return lax.broadcasted_iota(jnp.int32, shape, dim)


def horner(poly, x):
    total = jnp.full_like(x, poly[-1])
    for term in poly[-2::-1]:
        total = total * x + term
    return total


def cos_sin(turns):
    turns = turns - jnp.round(turns)
    square = turns * turns
    return horner(COS_POLY, square), horner(SIN_POLY, square) * turns


def ceil_div(a, b):
    return -(-a // b)


def round_up(a, b):
    return ceil_div(a, b) * b


def dot(a, b, contract=((1,), (0,))):
    return lax.dot_general(a, b, (contract, ((), ())), preferred_element_type=F32)


class Sizes:
    def __init__(self, lat_total, var_total, levels, lons, waves):
        self.lat, self.var, self.levels, self.lons, self.waves = lat_total, var_total, levels, lons, waves
        self.devices = lat_total * var_total
        self.points = lons // RADIX
        self.tiles = self.points // LANES
        self.block = math.gcd(self.tiles, 2)
        self.kaps = waves // RADIX
        self.rows = round_up(ceil_div(waves, self.devices), SUBLANES)
        assert self.kaps % self.rows == 0 and self.points % LANES == 0 and 2 * levels == LANES and lat_total <= LANES
        self.mixed = lat_total * self.rows
        self.sin = round_up(self.kaps, LANES)
        self.heads = round_up(ceil_div(self.kaps, STRIP), SUBLANES)
        self.params = round_up(levels + lat_total, STRIP)


def own_length(order_ref, length_ref):
    slot = lax.axis_index("lat")
    row = order_ref[slot]
    return slot, row, length_ref[row]


def fetch(sources, targets, sems):
    copies = [pltpu.make_async_copy(s, t, sems.at[i]) for i, (s, t) in enumerate(zip(sources, targets))]
    for copy in copies:
        copy.start()
    return copies


def slot_matrix(z, order_ref, mer_ref):
    slot = iota((z.lat, z.lat), 0)
    row = jnp.zeros((z.lat, z.lat), jnp.int32)
    for t in range(z.lat):
        row = jnp.where(slot == t, order_ref[t], row)
    pick = (row == iota((z.lat, z.lat), 1)).astype(F32).astype(BF16)
    return dot(dot(pick, mer_ref[0]).astype(BF16), pick, ((1,), (1,)))


def tile(c):
    return slice(c * LANES, (c + 1) * LANES)


def tables_kernel(z, *refs):
    given, made, large, held = refs[:7], refs[7:11], refs[11:13], refs[13:18]
    sems, heads_ref, tails_ref = refs[18:]
    order_ref, length_ref, amp_ref, mer_ref, bal_ref = held
    params_ref, basis_ref, twiddle_ref, scale_ref = made
    copies = fetch(given, [*held, *large], sems)
    for at in (0, z.sin):
        basis_ref[at + z.kaps : at + z.sin] = jnp.zeros((z.sin - z.kaps, z.points), BF16)
    params_ref[...] = jnp.zeros(params_ref.shape, BF16)
    for copy in copies[:5]:
        copy.wait()
    slot, row, length = own_length(order_ref, length_ref)
    quarter = length // RADIX
    period = jnp.full((1, LANES), length, jnp.int32).astype(F32)
    tail = iota((STRIP, LANES), 0).astype(F32)
    head = iota((z.heads, LANES), 0).astype(F32) * STRIP
    tw_row = iota((2 * RADIX, LANES), 0)
    tw_wave = jnp.where(tw_row < RADIX, tw_row, tw_row - RADIX).astype(F32)
    fraction = jnp.full((1, LANES), quarter, jnp.int32).astype(F32)
    for c in range(z.tiles):
        points = c * LANES + iota((1, LANES), 1)
        step = points.astype(F32) / fraction
        tails_ref[:STRIP, tile(c)], tails_ref[STRIP:, tile(c)] = cos_sin(tail * step)
        head_cos, head_sin = cos_sin(head * step)
        heads_ref[: z.heads, tile(c)] = jnp.where(points < quarter, head_cos, 0.0)
        heads_ref[z.heads :, tile(c)] = jnp.where(points < quarter, head_sin, 0.0)
        tw_cos, tw_sin = cos_sin(tw_wave * (points.astype(F32) / period))
        twiddle_ref[: 2 * RADIX, tile(c)] = jnp.where(tw_row < RADIX, tw_cos, tw_sin)
        twiddle_ref[2 * RADIX :, tile(c)] = jnp.broadcast_to(period, (SUBLANES, LANES))
    for c in range(z.tiles):
        tail_cos, tail_sin = tails_ref[:STRIP, tile(c)], tails_ref[STRIP:, tile(c)]
        for at in range(0, z.kaps, STRIP):
            i = at // STRIP
            head_cos, head_sin = heads_ref[i : i + 1, tile(c)], heads_ref[z.heads + i : z.heads + i + 1, tile(c)]
            basis_ref[at : at + STRIP, tile(c)] = (head_cos * tail_cos - head_sin * tail_sin).astype(BF16)
            to = slice(z.sin + at, z.sin + at + STRIP)
            basis_ref[to, tile(c)] = (head_sin * tail_cos + head_cos * tail_sin).astype(BF16)
    group = LANES // RADIX
    weights = 1.0 / period, 2.0 / period
    for r in range(RADIX):
        picked = iota((group, LANES), 1) == iota((group, LANES), 0) * RADIX + r
        for at in range(0, z.kaps, group):
            lanes = slice(at * RADIX, at * RADIX + LANES)
            amp = jnp.sum(jnp.where(picked, amp_ref[:, lanes], 0.0), axis=1, keepdims=True)
            wave = (at + iota((group, LANES), 0)) * RADIX + r
            weight = jnp.where(wave == 0, *weights) if at + r == 0 else weights[1]
            scale_ref[r * z.kaps + at : r * z.kaps + at + group] = jnp.where(
                wave <= (length - 1) // 2, weight * amp, 0.0
            )
    params_ref[: z.levels] = jnp.concatenate([bal_ref[0], bal_ref[0]], axis=1)
    params_ref[z.levels : z.levels + z.lat, : z.lat] = slot_matrix(z, order_ref, mer_ref).astype(BF16)
    for copy in copies[5:]:
        copy.wait()


def analysis_kernel(z, control_ref, vert_ref, basis_ref, twiddle_ref, scale_ref, *refs):
    packet_ref, field_ref, parts_ref, product_ref = refs
    length = jnp.max(twiddle_ref[2 * RADIX :, :LANES].astype(jnp.int32))
    quarter = length // RADIX
    field_ref[:, z.lons :] = jnp.zeros((z.levels, LANES), F32)
    parts_ref[z.levels : 2 * z.levels] = jnp.zeros((z.levels, z.points), BF16)
    field_ref[:, : z.lons] = dot(vert_ref[0], control_ref[0, 0])
    starts = [quarter * j1 for j1 in range(1, RADIX)]
    bases = [pl.multiple_of(s // LANES * LANES, LANES) for s in starts]
    shifts = [(LANES - (s - b)) % LANES for s, b in zip(starts, bases)]
    lane = iota((STRIP, LANES), 1)
    keeps = [(lane < shift) | (shift == 0) for shift in shifts]

    def rolled(i, at, c):
        lanes = pl.ds(pl.multiple_of(bases[i] + c * LANES, LANES), LANES)
        return pltpu.roll(field_ref[at : at + STRIP, lanes], shifts[i], 1)

    before = {}
    for block in range(0, z.tiles, z.block):
        for at in range(0, z.levels, STRIP):
            for c in range(block, block + z.block):
                if c == 0:
                    before[at] = [rolled(i, at, 0) for i in range(RADIX - 1)]
                after = [rolled(i, at, c + 1) for i in range(RADIX - 1)]
                second, third, fourth = [jnp.where(k, a, b) for k, a, b in zip(keeps, before[at], after)]
                before[at] = after
                first = field_ref[at : at + STRIP, tile(c)]
                even, odd = first + third, second + fourth
                real, imag, turned = first - third, second - fourth, even - odd
                cos1, cos2, cos3 = [twiddle_ref[r : r + 1, tile(c)] for r in (1, 2, 3)]
                sin1, sin2, sin3 = [twiddle_ref[RADIX + r : RADIX + r + 1, tile(c)] for r in (1, 2, 3)]
                parts = (
                    (even + odd,),
                    (real * cos1 - imag * sin1, real * sin1 + imag * cos1),
                    (turned * cos2, turned * sin2),
                    (real * cos3 + imag * sin3, real * sin3 - imag * cos3),
                )
                for r, pair in enumerate(parts):
                    for half, part in enumerate(pair):
                        to = (2 * r + half) * z.levels + at
                        parts_ref[to : to + STRIP, tile(c)] = part.astype(BF16)
        lanes = slice(block * LANES, (block + z.block) * LANES)
        basis = jnp.concatenate([basis_ref[: z.kaps, lanes], basis_ref[z.sin : z.sin + z.kaps, lanes]], axis=0)
        product = dot(basis, parts_ref[:, lanes], ((1,), (1,)))
        product_ref[...] = product if block == 0 else product_ref[...] + product
    count = z.kaps // z.rows
    sign = jnp.where(iota((1, LANES), 1) < z.levels, -1.0, 1.0).astype(F32)
    for r in range(RADIX):
        lanes = tile(r)
        for i in range(count):
            rows = slice(i * z.rows, (i + 1) * z.rows)
            from_sin = product_ref[z.kaps + i * z.rows : z.kaps + (i + 1) * z.rows, lanes]
            both = product_ref[rows, lanes] + pltpu.roll(from_sin, z.levels, 1) * sign
            scale = scale_ref[r * z.kaps + i * z.rows : r * z.kaps + (i + 1) * z.rows]
            packet_ref[r * count + i] = (both * scale).astype(BF16)
    if z.devices > RADIX * count:
        packet_ref[RADIX * count :] = jnp.zeros((z.devices - RADIX * count, z.rows, LANES), BF16)


def matrices_kernel(z, *refs):
    *given, mix_ref, bal_ref, all_ref = refs
    own = lax.axis_index("var")
    for step, ref in enumerate(given):
        all_ref[(own + step) % z.var] = ref[...]
    size = z.mixed
    to_cols = (iota((z.lat, size), 0) == iota((z.lat, size), 1) // z.rows).astype(F32).astype(BF16)
    same = iota((size, size), 0) % z.rows == iota((size, size), 1) % z.rows
    halves = iota((LANES, LANES), 0) // z.levels == iota((LANES, LANES), 1) // z.levels
    for v in range(z.var):
        meridional = all_ref[v, z.levels :].astype(F32)[: z.lat, : z.lat].astype(BF16)
        slot_cols = dot(meridional, to_cols).astype(BF16)
        mix_ref[v] = jnp.where(same, dot(to_cols, slot_cols, ((0,), (0,))), 0.0).astype(BF16)
        if v > 0:
            balance = all_ref[v, : z.levels].astype(F32)
            balance = jnp.where(halves, jnp.concatenate([balance, balance], axis=0), 0.0)
            bal_ref[v - 1] = balance.T.astype(BF16)


def mixing_kernel(z, packet_ref, mix_ref, bal_ref, out_ref):
    stream = None
    for v in range(z.var):
        coeffs = packet_ref[v].astype(F32).reshape(z.mixed, LANES).astype(BF16)
        blended = dot(mix_ref[v], coeffs)
        if v == 0:
            stream = blended.astype(BF16)
        else:
            blended = blended + dot(stream, bal_ref[v - 1])
        blended = blended.reshape(z.lat, z.rows, LANES)
        for s in range(z.lat):
            out_ref[v, s] = blended[s].astype(BF16)


def synthesis_kernel(z, spectra_ref, basis_ref, twiddle_ref, out_ref, sems, field_ref, lhs_ref, parts_ref):
    period = twiddle_ref[2 * RADIX :, :LANES].astype(jnp.int32)
    length = jnp.max(period)
    kap = iota((z.kaps, LANES), 0)
    count = z.kaps // z.rows
    half = z.levels // 2
    kinds = 2 * RADIX - 1
    for at in (0, z.sin):
        lhs_ref[:, at + z.kaps : at + z.sin] = jnp.zeros((2 * half * kinds, z.sin - z.kaps), BF16)
    for r in range(RADIX):
        part = spectra_ref[r * count : (r + 1) * count].astype(F32).reshape(z.kaps, LANES)
        part = jnp.where(kap * RADIX + r <= (period[0:1] - 1) // 2, part, 0.0)
        part = part.astype(BF16).T
        for i in range(2):
            from_cos = part[i * half : (i + 1) * half]
            from_sin = part[z.levels + i * half : z.levels + (i + 1) * half]
            pairs = [(from_cos, from_sin)] if r == 0 else [(from_cos, from_sin), (-from_sin, from_cos)]
            for kind, pair in zip((2 * r - 1, 2 * r) if r else (0,), pairs):
                to = slice((i * kinds + kind) * half, (i * kinds + kind + 1) * half)
                lhs_ref[to, : z.kaps] = pair[0]
                lhs_ref[to, z.sin : z.sin + z.kaps] = pair[1]
    quarter = length // RADIX
    starts = [quarter * j1 for j1 in range(1, RADIX)]
    bases = [pl.multiple_of(s // LANES * LANES, LANES) for s in starts]
    shifts = [s - b for s, b in zip(starts, bases)]
    wide = z.points + LANES
    field_ref[:, wide:] = jnp.zeros((z.levels, z.lons + LANES - wide), BF16)
    keep = [iota((STRIP, LANES), 1) < shift for shift in shifts]
    zero = jnp.zeros((STRIP, LANES), F32)
    for i in range(2):
        rows = slice(i * kinds * half, (i + 1) * kinds * half)
        parts_ref[rows] = dot(lhs_ref[rows], basis_ref[...])
    sent = []
    for at in range(0, z.levels, STRIP):
        rows = slice(at, at + STRIP)
        first = at // half * kinds * half + at % half
        quarters = [[], [], [], []]
        for c in range(z.tiles):
            cos1, cos2, cos3 = [twiddle_ref[r : r + 1, tile(c)] for r in (1, 2, 3)]
            sin1, sin2, sin3 = [twiddle_ref[RADIX + r : RADIX + r + 1, tile(c)] for r in (1, 2, 3)]
            w0, re1, im1, re2, im2, re3, im3 = [
                parts_ref[first + kind * half : first + kind * half + STRIP, tile(c)] for kind in range(kinds)
            ]
            w2 = re2 * cos2 - im2 * sin2
            cross = (re1 * cos1 - im1 * sin1) + (re3 * cos3 - im3 * sin3)
            turn = (re1 * sin1 + im1 * cos1) - (re3 * sin3 + im3 * cos3)
            even, odd = w0 + w2, w0 - w2
            field_ref[rows, tile(c)] = (even + cross).astype(BF16)
            for j1, part in ((1, odd - turn), (2, even - cross), (3, odd + turn)):
                quarters[j1].append(pltpu.roll(part, shifts[j1 - 1], 1))
        field_ref[rows, tile(z.tiles)] = zero.astype(BF16)
        for j1 in range(1, RADIX):
            pieces = zip([zero] + quarters[j1], quarters[j1] + [zero])
            for c, (left, right) in enumerate(pieces):
                lanes = pl.ds(pl.multiple_of(bases[j1 - 1] + c * LANES, LANES), LANES)
                piece = jnp.where(keep[j1 - 1], left, right)
                if c == 0:
                    piece = piece + field_ref[rows, lanes].astype(F32)
                field_ref[rows, lanes] = piece.astype(BF16)
        sent += fetch(
            (field_ref.at[pl.ds(at, STRIP), pl.ds(0, z.lons)],),
            (out_ref.at[0, 0, pl.ds(at, STRIP)],),
            sems.at[pl.ds(at // STRIP, 1)],
        )
    for copy in sent:
        copy.wait()


def body(z, control, row_order, row_length, vertical, amplitude, meridional, balance):
    small = (row_order, row_length, amplitude, meridional, balance)
    large = (control, vertical)
    params, basis, twiddle, scale, *large = pl.pallas_call(
        functools.partial(tables_kernel, z),
        out_shape=(
            jax.ShapeDtypeStruct((z.params, LANES), BF16),
            jax.ShapeDtypeStruct((2 * z.sin, z.points), BF16),
            jax.ShapeDtypeStruct((2 * RADIX + SUBLANES, z.points), F32),
            jax.ShapeDtypeStruct((z.waves, LANES), F32),
            *[jax.ShapeDtypeStruct(x.shape, x.dtype) for x in large],
        ),
        in_specs=[HBM] * (len(small) + len(large)),
        out_specs=(VMEM,) * (4 + len(large)),
        scratch_shapes=[
            *[pltpu.SMEM(x.shape, x.dtype) for x in small[:2]],
            *[pltpu.VMEM(x.shape, x.dtype) for x in small[2:]],
            pltpu.SemaphoreType.DMA((len(small) + len(large),)),
            pltpu.VMEM((2 * z.heads, z.points), F32),
            pltpu.VMEM((2 * STRIP, z.points), F32),
        ],
        compiler_params=PARAMS,
        cost_estimate=pl.CostEstimate(flops=10**8, bytes_accessed=10**6, transcendentals=0),
        name="tables",
    )(*[pltpu.with_memory_space_constraint(x, pltpu.HBM) for x in (*small, *large)])
    packets = pl.pallas_call(
        functools.partial(analysis_kernel, z),
        out_shape=jax.ShapeDtypeStruct((z.devices, z.rows, LANES), BF16),
        in_specs=[VMEM] * 5,
        out_specs=VMEM,
        scratch_shapes=[
            pltpu.VMEM((z.levels, z.lons + LANES), F32),
            pltpu.VMEM((2 * RADIX * z.levels, z.points), BF16),
            pltpu.VMEM((2 * z.kaps, RADIX * LANES), F32),
        ],
        compiler_params=PARAMS,
        name="analysis",
    )(*large, basis, twiddle, scale)
    given = [params]
    for step in range(1, z.var):
        given.append(lax.ppermute(params, "var", [((i + step) % z.var, i) for i in range(z.var)]))
    packets = lax.all_to_all(packets, ("var", "lat"), 0, 0, tiled=True)
    mix, lift = pl.pallas_call(
        functools.partial(matrices_kernel, z),
        out_shape=(
            jax.ShapeDtypeStruct((z.var, z.mixed, z.mixed), BF16),
            jax.ShapeDtypeStruct((z.var - 1, LANES, LANES), BF16),
        ),
        in_specs=[VMEM] * z.var,
        out_specs=(VMEM, VMEM),
        scratch_shapes=[pltpu.VMEM((z.var, z.params, LANES), BF16)],
        compiler_params=PARAMS,
        cost_estimate=pl.CostEstimate(flops=10**8, bytes_accessed=10**6, transcendentals=0),
        name="matrices",
    )(*given)
    balanced = pl.pallas_call(
        functools.partial(mixing_kernel, z),
        out_shape=jax.ShapeDtypeStruct((z.var, z.lat, z.rows, LANES), BF16),
        in_specs=[VMEM] * 3,
        out_specs=VMEM,
        compiler_params=PARAMS,
        name="mixing",
    )(packets.reshape(z.var, z.lat, z.rows, LANES), mix, lift)
    balanced = balanced.reshape(z.devices, z.rows, LANES)
    balanced = lax.all_to_all(balanced, ("var", "lat"), 0, 0, tiled=True)
    return pl.pallas_call(
        functools.partial(synthesis_kernel, z),
        out_shape=jax.ShapeDtypeStruct(control.shape, BF16),
        in_specs=[VMEM] * 3,
        out_specs=HBM,
        scratch_shapes=[
            pltpu.SemaphoreType.DMA((z.levels // STRIP,)),
            pltpu.VMEM((z.levels, z.lons + LANES), BF16),
            pltpu.VMEM(((2 * RADIX - 1) * z.levels, 2 * z.sin), BF16),
            pltpu.VMEM(((2 * RADIX - 1) * z.levels, z.points), F32),
        ],
        compiler_params=PARAMS,
        name="synthesis",
    )(balanced, basis, twiddle)


def solution(mesh):
    placed = (
        P("var", "lat", None, None),
        P(),
        P(),
        P("var", None, None),
        P("var", None),
        P("var", None, None),
        P("var", None, None),
    )

    def run(control, row_order, row_length, vertical, amplitude, meridional, balance):
        lat_total, var_total = mesh.shape["lat"], mesh.shape["var"]
        assert control.shape[0] == var_total and control.shape[1] == lat_total
        z = Sizes(lat_total, var_total, control.shape[2], control.shape[3], amplitude.shape[1])
        return jax.shard_map(
            functools.partial(body, z),
            mesh=mesh,
            in_specs=placed,
            out_specs=P("var", "lat", None, None),
            check_vma=False,
        )(control, row_order, row_length, vertical, amplitude, meridional, balance)

    return run
```

```python
import functools
import math

import jax
import jax.numpy as jnp
from jax import lax
from jax.experimental import pallas as pl
from jax.experimental.pallas import tpu as pltpu
from jax.sharding import PartitionSpec as P

RADIX = 4
LANES = 128
SUBLANES = 8
STRIP = 16
F32 = jnp.float32
BF16 = jnp.bfloat16

COS_POLY = (1, -19.7392044, 64.9391174, -85.4501419, 60.1676292, -25.9675999, 6.52865839)
SIN_POLY = (6.28318501, -41.3415909, 81.5999451, -76.6144714, 41.3428841, -12.4712439)

VMEM = pl.BlockSpec(memory_space=pltpu.VMEM)
HBM = pl.BlockSpec(memory_space=pltpu.HBM)
PARAMS = pltpu.CompilerParams(vmem_limit_bytes=32 * 1024 * 1024)


def iota(shape, dim):
    return lax.broadcasted_iota(jnp.int32, shape, dim)


def horner(poly, x):
    total = jnp.full_like(x, poly[-1])
    for term in poly[-2::-1]:
        total = total * x + term
    return total


def cos_sin(turns):
    turns = turns - jnp.round(turns)
    square = turns * turns
    return horner(COS_POLY, square), horner(SIN_POLY, square) * turns


def ceil_div(a, b):
    return -(-a // b)


def round_up(a, b):
    return ceil_div(a, b) * b


def dot(a, b, contract=((1,), (0,))):
    return lax.dot_general(a, b, (contract, ((), ())), preferred_element_type=F32)


class Sizes:
    def __init__(self, lat_total, var_total, levels, lons, waves):
        self.lat, self.var, self.levels, self.lons, self.waves = lat_total, var_total, levels, lons, waves
        self.devices = lat_total * var_total
        self.points = lons // RADIX
        self.tiles = self.points // LANES
        self.block = math.gcd(self.tiles, 2)
        self.kaps = waves // RADIX
        self.rows = round_up(ceil_div(waves, self.devices), SUBLANES)
        assert self.kaps % self.rows == 0 and self.points % LANES == 0 and 2 * levels == LANES and lat_total <= LANES
        self.mixed = lat_total * self.rows
        self.sin = round_up(self.kaps, LANES)
        self.heads = round_up(ceil_div(self.kaps, STRIP), SUBLANES)
        self.params = round_up(levels + lat_total, STRIP)


def own_length(order_ref, length_ref):
    slot = lax.axis_index("lat")
    row = order_ref[slot]
    return slot, row, length_ref[row]


def fetch(sources, targets, sems):
    copies = [pltpu.make_async_copy(s, t, sems.at[i]) for i, (s, t) in enumerate(zip(sources, targets))]
    for copy in copies:
        copy.start()
    return copies


def slot_matrix(z, order_ref, mer_ref):
    slot = iota((z.lat, z.lat), 0)
    row = jnp.zeros((z.lat, z.lat), jnp.int32)
    for t in range(z.lat):
        row = jnp.where(slot == t, order_ref[t], row)
    pick = (row == iota((z.lat, z.lat), 1)).astype(F32).astype(BF16)
    return dot(dot(pick, mer_ref[0]).astype(BF16), pick, ((1,), (1,)))


def tile(c):
    return slice(c * LANES, (c + 1) * LANES)


def tables_kernel(z, *refs):
    given, made, held = refs[:7], refs[7:12], refs[12:19]
    sems, heads_ref, tails_ref = refs[19:]
    order_ref, length_ref, amp_ref, mer_ref, bal_ref, control_ref, vert_ref = held
    params_ref, basis_ref, twiddle_ref, scale_ref, field_ref = made
    copies = fetch(given, held, sems)
    field_ref[:, z.lons :] = jnp.zeros((z.levels, LANES), F32)
    for at in (0, z.sin):
        basis_ref[at + z.kaps : at + z.sin] = jnp.zeros((z.sin - z.kaps, z.points), BF16)
    params_ref[...] = jnp.zeros(params_ref.shape, BF16)
    for copy in copies[:5]:
        copy.wait()
    slot, row, length = own_length(order_ref, length_ref)
    quarter = length // RADIX
    period = jnp.full((1, LANES), length, jnp.int32).astype(F32)
    tail = iota((STRIP, LANES), 0).astype(F32)
    head = iota((z.heads, LANES), 0).astype(F32) * STRIP
    tw_row = iota((2 * RADIX, LANES), 0)
    tw_wave = jnp.where(tw_row < RADIX, tw_row, tw_row - RADIX).astype(F32)
    fraction = jnp.full((1, LANES), quarter, jnp.int32).astype(F32)
    for c in range(z.tiles):
        points = c * LANES + iota((1, LANES), 1)
        step = points.astype(F32) / fraction
        tails_ref[:STRIP, tile(c)], tails_ref[STRIP:, tile(c)] = cos_sin(tail * step)
        head_cos, head_sin = cos_sin(head * step)
        heads_ref[: z.heads, tile(c)] = jnp.where(points < quarter, head_cos, 0.0)
        heads_ref[z.heads :, tile(c)] = jnp.where(points < quarter, head_sin, 0.0)
        tw_cos, tw_sin = cos_sin(tw_wave * (points.astype(F32) / period))
        twiddle_ref[: 2 * RADIX, tile(c)] = jnp.where(tw_row < RADIX, tw_cos, tw_sin)
        twiddle_ref[2 * RADIX :, tile(c)] = jnp.broadcast_to(period, (SUBLANES, LANES))
    for copy in copies[5:]:
        copy.wait()
    field_ref[:, : z.lons] = dot(vert_ref[0], control_ref[0, 0])
    for c in range(z.tiles):
        tail_cos, tail_sin = tails_ref[:STRIP, tile(c)], tails_ref[STRIP:, tile(c)]
        for at in range(0, z.kaps, STRIP):
            i = at // STRIP
            head_cos, head_sin = heads_ref[i : i + 1, tile(c)], heads_ref[z.heads + i : z.heads + i + 1, tile(c)]
            basis_ref[at : at + STRIP, tile(c)] = (head_cos * tail_cos - head_sin * tail_sin).astype(BF16)
            to = slice(z.sin + at, z.sin + at + STRIP)
            basis_ref[to, tile(c)] = (head_sin * tail_cos + head_cos * tail_sin).astype(BF16)
    group = LANES // RADIX
    weights = 1.0 / period, 2.0 / period
    for r in range(RADIX):
        picked = iota((group, LANES), 1) == iota((group, LANES), 0) * RADIX + r
        for at in range(0, z.kaps, group):
            lanes = slice(at * RADIX, at * RADIX + LANES)
            amp = jnp.sum(jnp.where(picked, amp_ref[:, lanes], 0.0), axis=1, keepdims=True)
            wave = (at + iota((group, LANES), 0)) * RADIX + r
            weight = jnp.where(wave == 0, *weights) if at + r == 0 else weights[1]
            scale_ref[r * z.kaps + at : r * z.kaps + at + group] = jnp.where(
                wave <= (length - 1) // 2, weight * amp, 0.0
            )
    params_ref[: z.levels] = jnp.concatenate([bal_ref[0], bal_ref[0]], axis=1)
    params_ref[z.levels : z.levels + z.lat, : z.lat] = slot_matrix(z, order_ref, mer_ref).astype(BF16)


def analysis_kernel(z, field_ref, basis_ref, twiddle_ref, scale_ref, packet_ref, parts_ref, product_ref):
    length = jnp.max(twiddle_ref[2 * RADIX :, :LANES].astype(jnp.int32))
    quarter = length // RADIX
    parts_ref[z.levels : 2 * z.levels] = jnp.zeros((z.levels, z.points), BF16)
    starts = [quarter * j1 for j1 in range(1, RADIX)]
    bases = [pl.multiple_of(s // LANES * LANES, LANES) for s in starts]
    shifts = [(LANES - (s - b)) % LANES for s, b in zip(starts, bases)]
    lane = iota((STRIP, LANES), 1)
    keeps = [(lane < shift) | (shift == 0) for shift in shifts]

    def rolled(i, at, c):
        lanes = pl.ds(pl.multiple_of(bases[i] + c * LANES, LANES), LANES)
        return pltpu.roll(field_ref[at : at + STRIP, lanes], shifts[i], 1)

    before = {}
    for block in range(0, z.tiles, z.block):
        for at in range(0, z.levels, STRIP):
            for c in range(block, block + z.block):
                if c == 0:
                    before[at] = [rolled(i, at, 0) for i in range(RADIX - 1)]
                after = [rolled(i, at, c + 1) for i in range(RADIX - 1)]
                second, third, fourth = [jnp.where(k, a, b) for k, a, b in zip(keeps, before[at], after)]
                before[at] = after
                first = field_ref[at : at + STRIP, tile(c)]
                even, odd = first + third, second + fourth
                real, imag, turned = first - third, second - fourth, even - odd
                cos1, cos2, cos3 = [twiddle_ref[r : r + 1, tile(c)] for r in (1, 2, 3)]
                sin1, sin2, sin3 = [twiddle_ref[RADIX + r : RADIX + r + 1, tile(c)] for r in (1, 2, 3)]
                parts = (
                    (even + odd,),
                    (real * cos1 - imag * sin1, real * sin1 + imag * cos1),
                    (turned * cos2, turned * sin2),
                    (real * cos3 + imag * sin3, real * sin3 - imag * cos3),
                )
                for r, pair in enumerate(parts):
                    for half, part in enumerate(pair):
                        to = (2 * r + half) * z.levels + at
                        parts_ref[to : to + STRIP, tile(c)] = part.astype(BF16)
        lanes = slice(block * LANES, (block + z.block) * LANES)
        basis = jnp.concatenate([basis_ref[: z.kaps, lanes], basis_ref[z.sin : z.sin + z.kaps, lanes]], axis=0)
        product = dot(basis, parts_ref[:, lanes], ((1,), (1,)))
        product_ref[...] = product if block == 0 else product_ref[...] + product
    count = z.kaps // z.rows
    sign = jnp.where(iota((1, LANES), 1) < z.levels, -1.0, 1.0).astype(F32)
    for r in range(RADIX):
        lanes = tile(r)
        for i in range(count):
            rows = slice(i * z.rows, (i + 1) * z.rows)
            from_sin = product_ref[z.kaps + i * z.rows : z.kaps + (i + 1) * z.rows, lanes]
            both = product_ref[rows, lanes] + pltpu.roll(from_sin, z.levels, 1) * sign
            scale = scale_ref[r * z.kaps + i * z.rows : r * z.kaps + (i + 1) * z.rows]
            packet_ref[r * count + i] = (both * scale).astype(BF16)
    if z.devices > RADIX * count:
        packet_ref[RADIX * count :] = jnp.zeros((z.devices - RADIX * count, z.rows, LANES), BF16)


def matrices_kernel(z, *refs):
    *given, mix_ref, bal_ref, all_ref = refs
    own = lax.axis_index("var")
    for step, ref in enumerate(given):
        all_ref[(own + step) % z.var] = ref[...]
    size = z.mixed
    to_cols = (iota((z.lat, size), 0) == iota((z.lat, size), 1) // z.rows).astype(F32).astype(BF16)
    same = iota((size, size), 0) % z.rows == iota((size, size), 1) % z.rows
    halves = iota((LANES, LANES), 0) // z.levels == iota((LANES, LANES), 1) // z.levels
    for v in range(z.var):
        meridional = all_ref[v, z.levels :].astype(F32)[: z.lat, : z.lat].astype(BF16)
        slot_cols = dot(meridional, to_cols).astype(BF16)
        mix_ref[v] = jnp.where(same, dot(to_cols, slot_cols, ((0,), (0,))), 0.0).astype(BF16)
        if v > 0:
            balance = all_ref[v, : z.levels].astype(F32)
            balance = jnp.where(halves, jnp.concatenate([balance, balance], axis=0), 0.0)
            bal_ref[v - 1] = balance.T.astype(BF16)


def mixing_kernel(z, packet_ref, mix_ref, bal_ref, out_ref):
    stream = None
    for v in range(z.var):
        coeffs = packet_ref[v].astype(F32).reshape(z.mixed, LANES).astype(BF16)
        blended = dot(mix_ref[v], coeffs)
        if v == 0:
            stream = blended.astype(BF16)
        else:
            blended = blended + dot(stream, bal_ref[v - 1])
        blended = blended.reshape(z.lat, z.rows, LANES)
        for s in range(z.lat):
            out_ref[v, s] = blended[s].astype(BF16)


def synthesis_kernel(z, spectra_ref, basis_ref, twiddle_ref, out_ref, sems, field_ref, lhs_ref, parts_ref):
    period = twiddle_ref[2 * RADIX :, :LANES].astype(jnp.int32)
    length = jnp.max(period)
    kap = iota((z.kaps, LANES), 0)
    count = z.kaps // z.rows
    half = z.levels // 2
    kinds = 2 * RADIX - 1
    for at in (0, z.sin):
        lhs_ref[:, at + z.kaps : at + z.sin] = jnp.zeros((2 * half * kinds, z.sin - z.kaps), BF16)
    for r in range(RADIX):
        part = spectra_ref[r * count : (r + 1) * count].astype(F32).reshape(z.kaps, LANES)
        part = jnp.where(kap * RADIX + r <= (period[0:1] - 1) // 2, part, 0.0)
        part = part.astype(BF16).T
        for i in range(2):
            from_cos = part[i * half : (i + 1) * half]
            from_sin = part[z.levels + i * half : z.levels + (i + 1) * half]
            pairs = [(from_cos, from_sin)] if r == 0 else [(from_cos, from_sin), (-from_sin, from_cos)]
            for kind, pair in zip((2 * r - 1, 2 * r) if r else (0,), pairs):
                to = slice((i * kinds + kind) * half, (i * kinds + kind + 1) * half)
                lhs_ref[to, : z.kaps] = pair[0]
                lhs_ref[to, z.sin : z.sin + z.kaps] = pair[1]
    quarter = length // RADIX
    starts = [quarter * j1 for j1 in range(1, RADIX)]
    bases = [pl.multiple_of(s // LANES * LANES, LANES) for s in starts]
    shifts = [s - b for s, b in zip(starts, bases)]
    wide = z.points + LANES
    field_ref[:, wide:] = jnp.zeros((z.levels, z.lons + LANES - wide), BF16)
    keep = [iota((STRIP, LANES), 1) < shift for shift in shifts]
    zero = jnp.zeros((STRIP, LANES), F32)
    for i in range(2):
        rows = slice(i * kinds * half, (i + 1) * kinds * half)
        parts_ref[rows] = dot(lhs_ref[rows], basis_ref[...])
    sent = []
    for at in range(0, z.levels, STRIP):
        rows = slice(at, at + STRIP)
        first = at // half * kinds * half + at % half
        quarters = [[], [], [], []]
        for c in range(z.tiles):
            cos1, cos2, cos3 = [twiddle_ref[r : r + 1, tile(c)] for r in (1, 2, 3)]
            sin1, sin2, sin3 = [twiddle_ref[RADIX + r : RADIX + r + 1, tile(c)] for r in (1, 2, 3)]
            w0, re1, im1, re2, im2, re3, im3 = [
                parts_ref[first + kind * half : first + kind * half + STRIP, tile(c)] for kind in range(kinds)
            ]
            w2 = re2 * cos2 - im2 * sin2
            cross = (re1 * cos1 - im1 * sin1) + (re3 * cos3 - im3 * sin3)
            turn = (re1 * sin1 + im1 * cos1) - (re3 * sin3 + im3 * cos3)
            even, odd = w0 + w2, w0 - w2
            field_ref[rows, tile(c)] = (even + cross).astype(BF16)
            for j1, part in ((1, odd - turn), (2, even - cross), (3, odd + turn)):
                quarters[j1].append(pltpu.roll(part, shifts[j1 - 1], 1))
        field_ref[rows, tile(z.tiles)] = zero.astype(BF16)
        for j1 in range(1, RADIX):
            pieces = zip([zero] + quarters[j1], quarters[j1] + [zero])
            for c, (left, right) in enumerate(pieces):
                lanes = pl.ds(pl.multiple_of(bases[j1 - 1] + c * LANES, LANES), LANES)
                piece = jnp.where(keep[j1 - 1], left, right)
                if c == 0:
                    piece = piece + field_ref[rows, lanes].astype(F32)
                field_ref[rows, lanes] = piece.astype(BF16)
        sent += fetch(
            (field_ref.at[pl.ds(at, STRIP), pl.ds(0, z.lons)],),
            (out_ref.at[0, 0, pl.ds(at, STRIP)],),
            sems.at[pl.ds(at // STRIP, 1)],
        )
    for copy in sent:
        copy.wait()


def body(z, control, row_order, row_length, vertical, amplitude, meridional, balance):
    arguments = (row_order, row_length, amplitude, meridional, balance, control, vertical)
    params, basis, twiddle, scale, levels = pl.pallas_call(
        functools.partial(tables_kernel, z),
        out_shape=(
            jax.ShapeDtypeStruct((z.params, LANES), BF16),
            jax.ShapeDtypeStruct((2 * z.sin, z.points), BF16),
            jax.ShapeDtypeStruct((2 * RADIX + SUBLANES, z.points), F32),
            jax.ShapeDtypeStruct((z.waves, LANES), F32),
            jax.ShapeDtypeStruct((z.levels, z.lons + LANES), F32),
        ),
        in_specs=[HBM] * len(arguments),
        out_specs=(VMEM,) * 5,
        scratch_shapes=[
            *[pltpu.SMEM(x.shape, x.dtype) for x in arguments[:2]],
            *[pltpu.VMEM(x.shape, x.dtype) for x in arguments[2:]],
            pltpu.SemaphoreType.DMA((len(arguments),)),
            pltpu.VMEM((2 * z.heads, z.points), F32),
            pltpu.VMEM((2 * STRIP, z.points), F32),
        ],
        compiler_params=PARAMS,
        cost_estimate=pl.CostEstimate(flops=10**8, bytes_accessed=10**6, transcendentals=0),
        name="tables",
    )(*[pltpu.with_memory_space_constraint(x, pltpu.HBM) for x in arguments])
    packets = pl.pallas_call(
        functools.partial(analysis_kernel, z),
        out_shape=jax.ShapeDtypeStruct((z.devices, z.rows, LANES), BF16),
        in_specs=[VMEM] * 4,
        out_specs=VMEM,
        scratch_shapes=[
            pltpu.VMEM((2 * RADIX * z.levels, z.points), BF16),
            pltpu.VMEM((2 * z.kaps, RADIX * LANES), F32),
        ],
        compiler_params=PARAMS,
        name="analysis",
    )(levels, basis, twiddle, scale)
    given = [params]
    for step in range(1, z.var):
        given.append(lax.ppermute(params, "var", [((i + step) % z.var, i) for i in range(z.var)]))
    packets = lax.all_to_all(packets, ("var", "lat"), 0, 0, tiled=True)
    mix, lift = pl.pallas_call(
        functools.partial(matrices_kernel, z),
        out_shape=(
            jax.ShapeDtypeStruct((z.var, z.mixed, z.mixed), BF16),
            jax.ShapeDtypeStruct((z.var - 1, LANES, LANES), BF16),
        ),
        in_specs=[VMEM] * z.var,
        out_specs=(VMEM, VMEM),
        scratch_shapes=[pltpu.VMEM((z.var, z.params, LANES), BF16)],
        compiler_params=PARAMS,
        cost_estimate=pl.CostEstimate(flops=10**8, bytes_accessed=10**6, transcendentals=0),
        name="matrices",
    )(*given)
    balanced = pl.pallas_call(
        functools.partial(mixing_kernel, z),
        out_shape=jax.ShapeDtypeStruct((z.var, z.lat, z.rows, LANES), BF16),
        in_specs=[VMEM] * 3,
        out_specs=VMEM,
        compiler_params=PARAMS,
        name="mixing",
    )(packets.reshape(z.var, z.lat, z.rows, LANES), mix, lift)
    balanced = balanced.reshape(z.devices, z.rows, LANES)
    balanced = lax.all_to_all(balanced, ("var", "lat"), 0, 0, tiled=True)
    return pl.pallas_call(
        functools.partial(synthesis_kernel, z),
        out_shape=jax.ShapeDtypeStruct(control.shape, BF16),
        in_specs=[VMEM] * 3,
        out_specs=HBM,
        scratch_shapes=[
            pltpu.SemaphoreType.DMA((z.levels // STRIP,)),
            pltpu.VMEM((z.levels, z.lons + LANES), BF16),
            pltpu.VMEM(((2 * RADIX - 1) * z.levels, 2 * z.sin), BF16),
            pltpu.VMEM(((2 * RADIX - 1) * z.levels, z.points), F32),
        ],
        compiler_params=PARAMS,
        name="synthesis",
    )(balanced, basis, twiddle)


def solution(mesh):
    placed = (
        P("var", "lat", None, None),
        P(),
        P(),
        P("var", None, None),
        P("var", None),
        P("var", None, None),
        P("var", None, None),
    )

    def run(control, row_order, row_length, vertical, amplitude, meridional, balance):
        lat_total, var_total = mesh.shape["lat"], mesh.shape["var"]
        assert control.shape[0] == var_total and control.shape[1] == lat_total
        z = Sizes(lat_total, var_total, control.shape[2], control.shape[3], amplitude.shape[1])
        return jax.shard_map(
            functools.partial(body, z),
            mesh=mesh,
            in_specs=placed,
            out_specs=P("var", "lat", None, None),
            check_vma=False,
        )(control, row_order, row_length, vertical, amplitude, meridional, balance)

    return run
```

```python
import functools
import math

import jax
import jax.numpy as jnp
from jax import lax
from jax.experimental import pallas as pl
from jax.experimental.pallas import tpu as pltpu
from jax.sharding import PartitionSpec as P

RADIX = 4
LANES = 128
SUBLANES = 8
STRIP = 16
F32 = jnp.float32
BF16 = jnp.bfloat16

COS_POLY = (1, -19.7392044, 64.9391174, -85.4501419, 60.1676292, -25.9675999, 6.52865839)
SIN_POLY = (6.28318501, -41.3415909, 81.5999451, -76.6144714, 41.3428841, -12.4712439)

VMEM = pl.BlockSpec(memory_space=pltpu.VMEM)
HBM = pl.BlockSpec(memory_space=pltpu.HBM)
PARAMS = pltpu.CompilerParams(vmem_limit_bytes=32 * 1024 * 1024)


def iota(shape, dim):
    return lax.broadcasted_iota(jnp.int32, shape, dim)


def horner(poly, x):
    total = jnp.full_like(x, poly[-1])
    for term in poly[-2::-1]:
        total = total * x + term
    return total


def cos_sin(turns):
    turns = turns - jnp.round(turns)
    square = turns * turns
    return horner(COS_POLY, square), horner(SIN_POLY, square) * turns


def ceil_div(a, b):
    return -(-a // b)


def round_up(a, b):
    return ceil_div(a, b) * b


def dot(a, b, contract=((1,), (0,))):
    return lax.dot_general(a, b, (contract, ((), ())), preferred_element_type=F32)


class Sizes:
    def __init__(self, lat_total, var_total, levels, lons, waves):
        self.lat, self.var, self.levels, self.lons, self.waves = lat_total, var_total, levels, lons, waves
        self.devices = lat_total * var_total
        self.points = lons // RADIX
        self.tiles = self.points // LANES
        self.block = math.gcd(self.tiles, 2)
        self.kaps = waves // RADIX
        self.rows = round_up(ceil_div(waves, self.devices), SUBLANES)
        assert self.kaps % self.rows == 0 and self.points % LANES == 0 and 2 * levels == LANES and lat_total <= LANES
        self.mixed = lat_total * self.rows
        self.sin = round_up(self.kaps, LANES)
        self.heads = round_up(ceil_div(self.kaps, STRIP), SUBLANES)
        self.params = round_up(levels + lat_total, STRIP)


def own_length(order_ref, length_ref):
    slot = lax.axis_index("lat")
    row = order_ref[slot]
    return slot, row, length_ref[row]


def fetch(sources, targets, sems):
    copies = [pltpu.make_async_copy(s, t, sems.at[i]) for i, (s, t) in enumerate(zip(sources, targets))]
    for copy in copies:
        copy.start()
    return copies


def slot_matrix(z, order_ref, mer_ref):
    slot = iota((z.lat, z.lat), 0)
    row = jnp.zeros((z.lat, z.lat), jnp.int32)
    for t in range(z.lat):
        row = jnp.where(slot == t, order_ref[t], row)
    pick = (row == iota((z.lat, z.lat), 1)).astype(F32).astype(BF16)
    return dot(dot(pick, mer_ref[0]).astype(BF16), pick, ((1,), (1,)))


def lanes_below(bound):
    lane = iota((STRIP, LANES), 1).astype(F32).astype(BF16)
    return lane < jnp.full((STRIP, LANES), bound, jnp.int32).astype(F32).astype(BF16)


def tile(c):
    return slice(c * LANES, (c + 1) * LANES)


def analysis_kernel(z, *refs):
    given, made, held = refs[:7], refs[7:11], refs[11:18]
    sems, field_ref, quarters_ref, parts_ref, heads_ref, tails_ref, scale_ref, product_ref = refs[18:]
    order_ref, length_ref, control_ref, vert_ref, amp_ref, mer_ref, bal_ref = held
    packet_ref, params_ref, basis_ref, twiddle_ref = made
    control_ref[:, z.lons :] = jnp.zeros((z.levels, LANES), BF16)
    targets = [control_ref.at[:, pl.ds(0, z.lons)] if ref is control_ref else ref for ref in held]
    copies = fetch([*given[:2], given[2].at[0, 0], *given[3:]], targets, sems)
    for at in (0, z.sin):
        basis_ref[at + z.kaps : at + z.sin] = jnp.zeros((z.sin - z.kaps, z.points), BF16)
    params_ref[...] = jnp.zeros(params_ref.shape, BF16)
    parts_ref[z.levels : 2 * z.levels] = jnp.zeros((z.levels, z.points), BF16)
    for copy in copies[:2]:
        copy.wait()
    slot, row, length = own_length(order_ref, length_ref)
    quarter = length // RADIX
    period = jnp.full((1, LANES), length, jnp.int32).astype(F32)
    tail = iota((STRIP, LANES), 0).astype(F32)
    head = iota((z.heads, LANES), 0).astype(F32) * STRIP
    tw_row = iota((2 * RADIX, LANES), 0)
    tw_wave = jnp.where(tw_row < RADIX, tw_row, tw_row - RADIX).astype(F32)
    fraction = jnp.full((1, LANES), quarter, jnp.int32).astype(F32)
    for c in range(z.tiles):
        points = c * LANES + iota((1, LANES), 1)
        step = points.astype(F32) / fraction
        tails_ref[:STRIP, tile(c)], tails_ref[STRIP:, tile(c)] = cos_sin(tail * step)
        head_cos, head_sin = cos_sin(head * step)
        heads_ref[: z.heads, tile(c)] = jnp.where(points < quarter, head_cos, 0.0)
        heads_ref[z.heads :, tile(c)] = jnp.where(points < quarter, head_sin, 0.0)
        tw_cos, tw_sin = cos_sin(tw_wave * (points.astype(F32) / period))
        twiddle_ref[: 2 * RADIX, tile(c)] = jnp.where(tw_row < RADIX, tw_cos, tw_sin)
        twiddle_ref[2 * RADIX :, tile(c)] = jnp.broadcast_to(period, (SUBLANES, LANES))
    for copy in copies[2:]:
        copy.wait()
    starts = [quarter * j1 for j1 in range(1, RADIX)]
    bases = [pl.multiple_of(s // LANES * LANES, LANES) for s in starts]
    shifts = [(LANES - (s - b)) % LANES for s, b in zip(starts, bases)]
    keeps = [lanes_below(jnp.where(shift == 0, LANES, shift)) for shift in shifts]

    def rolled(i, at, c):
        lanes = pl.ds(pl.multiple_of(bases[i] + c * LANES, LANES), LANES)
        return pltpu.roll(control_ref[at : at + STRIP, lanes], shifts[i], 1)

    before = {}
    for block in range(0, z.tiles, z.block):
        for c in range(block, block + z.block):
            tail_cos, tail_sin = tails_ref[:STRIP, tile(c)], tails_ref[STRIP:, tile(c)]
            for at in range(0, z.kaps, STRIP):
                i = at // STRIP
                head_cos, head_sin = heads_ref[i : i + 1, tile(c)], heads_ref[z.heads + i : z.heads + i + 1, tile(c)]
                basis_ref[at : at + STRIP, tile(c)] = (head_cos * tail_cos - head_sin * tail_sin).astype(BF16)
                to = slice(z.sin + at, z.sin + at + STRIP)
                basis_ref[to, tile(c)] = (head_sin * tail_cos + head_cos * tail_sin).astype(BF16)
        lanes = slice(block * LANES, (block + z.block) * LANES)
        for at in range(0, z.levels, STRIP):
            for c in range(block, block + z.block):
                if c == 0:
                    before[at] = [rolled(i, at, 0) for i in range(RADIX - 1)]
                after = [rolled(i, at, c + 1) for i in range(RADIX - 1)]
                for i in range(RADIX - 1):
                    quarters_ref[i, at : at + STRIP, tile(c)] = jnp.where(keeps[i], before[at][i], after[i])
                before[at] = after
        field_ref[0, :, lanes] = dot(vert_ref[0], control_ref[:, lanes])
        for i in range(RADIX - 1):
            field_ref[i + 1, :, lanes] = dot(vert_ref[0], quarters_ref[i, :, lanes])
        for at in range(0, z.levels, STRIP):
            for c in range(block, block + z.block):
                first, second, third, fourth = [field_ref[i, at : at + STRIP, tile(c)] for i in range(RADIX)]
                even, odd = first + third, second + fourth
                real, imag, turned = first - third, second - fourth, even - odd
                cos1, cos2, cos3 = [twiddle_ref[r : r + 1, tile(c)] for r in (1, 2, 3)]
                sin1, sin2, sin3 = [twiddle_ref[RADIX + r : RADIX + r + 1, tile(c)] for r in (1, 2, 3)]
                parts = (
                    (even + odd,),
                    (real * cos1 - imag * sin1, real * sin1 + imag * cos1),
                    (turned * cos2, turned * sin2),
                    (real * cos3 + imag * sin3, real * sin3 - imag * cos3),
                )
                for r, pair in enumerate(parts):
                    for half, part in enumerate(pair):
                        to = (2 * r + half) * z.levels + at
                        parts_ref[to : to + STRIP, tile(c)] = part.astype(BF16)
        basis = jnp.concatenate([basis_ref[: z.kaps, lanes], basis_ref[z.sin : z.sin + z.kaps, lanes]], axis=0)
        product = dot(basis, parts_ref[:, lanes], ((1,), (1,)))
        product_ref[...] = product if block == 0 else product_ref[...] + product
    group = LANES // RADIX
    weights = 1.0 / period, 2.0 / period
    for r in range(RADIX):
        picked = iota((group, LANES), 1) == iota((group, LANES), 0) * RADIX + r
        for at in range(0, z.kaps, group):
            lanes = slice(at * RADIX, at * RADIX + LANES)
            amp = jnp.sum(jnp.where(picked, amp_ref[:, lanes], 0.0), axis=1, keepdims=True)
            wave = (at + iota((group, LANES), 0)) * RADIX + r
            weight = jnp.where(wave == 0, *weights) if at + r == 0 else weights[1]
            scale_ref[r * z.kaps + at : r * z.kaps + at + group] = jnp.where(
                wave <= (length - 1) // 2, weight * amp, 0.0
            )
    params_ref[: z.levels] = jnp.concatenate([bal_ref[0], bal_ref[0]], axis=1)
    params_ref[z.levels : z.levels + z.lat, : z.lat] = slot_matrix(z, order_ref, mer_ref).astype(BF16)
    count = z.kaps // z.rows
    sign = jnp.where(iota((1, LANES), 1) < z.levels, -1.0, 1.0).astype(F32)
    for r in range(RADIX):
        lanes = tile(r)
        for i in range(count):
            rows = slice(i * z.rows, (i + 1) * z.rows)
            from_sin = product_ref[z.kaps + i * z.rows : z.kaps + (i + 1) * z.rows, lanes]
            both = product_ref[rows, lanes] + pltpu.roll(from_sin, z.levels, 1) * sign
            scale = scale_ref[r * z.kaps + i * z.rows : r * z.kaps + (i + 1) * z.rows]
            packet_ref[r * count + i] = (both * scale).astype(BF16)
    if z.devices > RADIX * count:
        packet_ref[RADIX * count :] = jnp.zeros((z.devices - RADIX * count, z.rows, LANES), BF16)


def matrices_kernel(z, *refs):
    *given, mix_ref, bal_ref, all_ref = refs
    own = lax.axis_index("var")
    for step, ref in enumerate(given):
        all_ref[(own + step) % z.var] = ref[...]
    size = z.mixed
    to_cols = (iota((z.lat, size), 0) == iota((z.lat, size), 1) // z.rows).astype(F32).astype(BF16)
    same = iota((size, size), 0) % z.rows == iota((size, size), 1) % z.rows
    halves = iota((LANES, LANES), 0) // z.levels == iota((LANES, LANES), 1) // z.levels
    for v in range(z.var):
        meridional = all_ref[v, z.levels :].astype(F32)[: z.lat, : z.lat].astype(BF16)
        slot_cols = dot(meridional, to_cols).astype(BF16)
        mix_ref[v] = jnp.where(same, dot(to_cols, slot_cols, ((0,), (0,))), 0.0).astype(BF16)
        if v > 0:
            balance = all_ref[v, : z.levels].astype(F32)
            balance = jnp.where(halves, jnp.concatenate([balance, balance], axis=0), 0.0)
            bal_ref[v - 1] = balance.T.astype(BF16)


def mixing_kernel(z, packet_ref, mix_ref, bal_ref, out_ref):
    stream = None
    for v in range(z.var):
        coeffs = packet_ref[v].astype(F32).reshape(z.mixed, LANES).astype(BF16)
        blended = dot(mix_ref[v], coeffs)
        if v == 0:
            stream = blended.astype(BF16)
        else:
            blended = blended + dot(stream, bal_ref[v - 1])
        blended = blended.reshape(z.lat, z.rows, LANES)
        for s in range(z.lat):
            out_ref[v, s] = blended[s].astype(BF16)


def synthesis_kernel(z, spectra_ref, basis_ref, twiddle_ref, out_ref, sems, field_ref, lhs_ref, parts_ref):
    period = twiddle_ref[2 * RADIX :, :LANES].astype(jnp.int32)
    length = jnp.max(period)
    kap = iota((z.kaps, LANES), 0)
    count = z.kaps // z.rows
    half = z.levels // 2
    kinds = 2 * RADIX - 1
    for at in (0, z.sin):
        lhs_ref[:, at + z.kaps : at + z.sin] = jnp.zeros((2 * half * kinds, z.sin - z.kaps), BF16)
    for r in range(RADIX):
        part = spectra_ref[r * count : (r + 1) * count].astype(F32).reshape(z.kaps, LANES)
        part = jnp.where(kap * RADIX + r <= (period[0:1] - 1) // 2, part, 0.0)
        part = part.astype(BF16).T
        for i in range(2):
            from_cos = part[i * half : (i + 1) * half]
            from_sin = part[z.levels + i * half : z.levels + (i + 1) * half]
            pairs = [(from_cos, from_sin)] if r == 0 else [(from_cos, from_sin), (-from_sin, from_cos)]
            for kind, pair in zip((2 * r - 1, 2 * r) if r else (0,), pairs):
                to = slice((i * kinds + kind) * half, (i * kinds + kind + 1) * half)
                lhs_ref[to, : z.kaps] = pair[0]
                lhs_ref[to, z.sin : z.sin + z.kaps] = pair[1]
    quarter = length // RADIX
    starts = [quarter * j1 for j1 in range(1, RADIX)]
    bases = [pl.multiple_of(s // LANES * LANES, LANES) for s in starts]
    shifts = [s - b for s, b in zip(starts, bases)]
    wide = z.points + LANES
    field_ref[:, wide:] = jnp.zeros((z.levels, z.lons + LANES - wide), BF16)
    keep = [lanes_below(shift) for shift in shifts]
    zero = jnp.zeros((STRIP, LANES), BF16)
    for i in range(2):
        rows = slice(i * kinds * half, (i + 1) * kinds * half)
        parts_ref[rows] = dot(lhs_ref[rows], basis_ref[...])
    sent = []
    for at in range(0, z.levels, STRIP):
        rows = slice(at, at + STRIP)
        first = at // half * kinds * half + at % half
        quarters = [[], [], [], []]
        for c in range(z.tiles):
            cos1, cos2, cos3 = [twiddle_ref[r : r + 1, tile(c)] for r in (1, 2, 3)]
            sin1, sin2, sin3 = [twiddle_ref[RADIX + r : RADIX + r + 1, tile(c)] for r in (1, 2, 3)]
            w0, re1, im1, re2, im2, re3, im3 = [
                parts_ref[first + kind * half : first + kind * half + STRIP, tile(c)] for kind in range(kinds)
            ]
            w2 = re2 * cos2 - im2 * sin2
            cross = (re1 * cos1 - im1 * sin1) + (re3 * cos3 - im3 * sin3)
            turn = (re1 * sin1 + im1 * cos1) - (re3 * sin3 + im3 * cos3)
            even, odd = w0 + w2, w0 - w2
            field_ref[rows, tile(c)] = (even + cross).astype(BF16)
            for j1, part in ((1, odd - turn), (2, even - cross), (3, odd + turn)):
                quarters[j1].append(pltpu.roll(part.astype(BF16), shifts[j1 - 1], 1))
        field_ref[rows, tile(z.tiles)] = zero
        for j1 in range(1, RADIX):
            pieces = zip([zero] + quarters[j1], quarters[j1] + [zero])
            for c, (left, right) in enumerate(pieces):
                lanes = pl.ds(pl.multiple_of(bases[j1 - 1] + c * LANES, LANES), LANES)
                piece = jnp.where(keep[j1 - 1], left, right)
                if c == 0:
                    piece = piece + field_ref[rows, lanes]
                field_ref[rows, lanes] = piece
        sent += fetch(
            (field_ref.at[pl.ds(at, STRIP), pl.ds(0, z.lons)],),
            (out_ref.at[0, 0, pl.ds(at, STRIP)],),
            sems.at[pl.ds(at // STRIP, 1)],
        )
    for copy in sent:
        copy.wait()


def body(z, control, row_order, row_length, vertical, amplitude, meridional, balance):
    arguments = (row_order, row_length, control, vertical, amplitude, meridional, balance)
    made = (
        jax.ShapeDtypeStruct((z.devices, z.rows, LANES), BF16),
        jax.ShapeDtypeStruct((z.params, LANES), BF16),
        jax.ShapeDtypeStruct((2 * z.sin, z.points), BF16),
        jax.ShapeDtypeStruct((2 * RADIX + SUBLANES, z.points), F32),
    )
    packets, params, basis, twiddle = pl.pallas_call(
        functools.partial(analysis_kernel, z),
        out_shape=made,
        in_specs=[HBM] * len(arguments),
        out_specs=(VMEM,) * len(made),
        scratch_shapes=[
            *[pltpu.SMEM(x.shape, x.dtype) for x in arguments[:2]],
            pltpu.VMEM((z.levels, z.lons + LANES), BF16),
            *[pltpu.VMEM(x.shape, x.dtype) for x in arguments[3:]],
            pltpu.SemaphoreType.DMA((len(arguments),)),
            pltpu.VMEM((RADIX, z.levels, z.points), F32),
            pltpu.VMEM((RADIX - 1, z.levels, z.points), BF16),
            pltpu.VMEM((2 * RADIX * z.levels, z.points), BF16),
            pltpu.VMEM((2 * z.heads, z.points), F32),
            pltpu.VMEM((2 * STRIP, z.points), F32),
            pltpu.VMEM((z.waves, LANES), F32),
            pltpu.VMEM((2 * z.kaps, RADIX * LANES), F32),
        ],
        compiler_params=PARAMS,
        name="analysis",
    )(*[pltpu.with_memory_space_constraint(x, pltpu.HBM) for x in arguments])
    given = [params]
    for step in range(1, z.var):
        given.append(lax.ppermute(params, "var", [((i + step) % z.var, i) for i in range(z.var)]))
    packets = lax.all_to_all(packets, ("var", "lat"), 0, 0, tiled=True)
    mix, lift = pl.pallas_call(
        functools.partial(matrices_kernel, z),
        out_shape=(
            jax.ShapeDtypeStruct((z.var, z.mixed, z.mixed), BF16),
            jax.ShapeDtypeStruct((z.var - 1, LANES, LANES), BF16),
        ),
        in_specs=[VMEM] * z.var,
        out_specs=(VMEM, VMEM),
        scratch_shapes=[pltpu.VMEM((z.var, z.params, LANES), BF16)],
        compiler_params=PARAMS,
        cost_estimate=pl.CostEstimate(flops=10**8, bytes_accessed=10**6, transcendentals=0),
        name="matrices",
    )(*given)
    balanced = pl.pallas_call(
        functools.partial(mixing_kernel, z),
        out_shape=jax.ShapeDtypeStruct((z.var, z.lat, z.rows, LANES), BF16),
        in_specs=[VMEM] * 3,
        out_specs=VMEM,
        compiler_params=PARAMS,
        name="mixing",
    )(packets.reshape(z.var, z.lat, z.rows, LANES), mix, lift)
    balanced = balanced.reshape(z.devices, z.rows, LANES)
    balanced = lax.all_to_all(balanced, ("var", "lat"), 0, 0, tiled=True)
    return pl.pallas_call(
        functools.partial(synthesis_kernel, z),
        out_shape=jax.ShapeDtypeStruct(control.shape, BF16),
        in_specs=[VMEM] * 3,
        out_specs=HBM,
        scratch_shapes=[
            pltpu.SemaphoreType.DMA((z.levels // STRIP,)),
            pltpu.VMEM((z.levels, z.lons + LANES), BF16),
            pltpu.VMEM(((2 * RADIX - 1) * z.levels, 2 * z.sin), BF16),
            pltpu.VMEM(((2 * RADIX - 1) * z.levels, z.points), F32),
        ],
        compiler_params=PARAMS,
        name="synthesis",
    )(balanced, basis, twiddle)


def solution(mesh):
    placed = (
        P("var", "lat", None, None),
        P(),
        P(),
        P("var", None, None),
        P("var", None),
        P("var", None, None),
        P("var", None, None),
    )

    def run(control, row_order, row_length, vertical, amplitude, meridional, balance):
        lat_total, var_total = mesh.shape["lat"], mesh.shape["var"]
        assert control.shape[0] == var_total and control.shape[1] == lat_total
        z = Sizes(lat_total, var_total, control.shape[2], control.shape[3], amplitude.shape[1])
        return jax.shard_map(
            functools.partial(body, z),
            mesh=mesh,
            in_specs=placed,
            out_specs=P("var", "lat", None, None),
            check_vma=False,
        )(control, row_order, row_length, vertical, amplitude, meridional, balance)

    return run
```

```python
import functools
import math

import jax
import jax.numpy as jnp
from jax import lax
from jax.experimental import pallas as pl
from jax.experimental.pallas import tpu as pltpu
from jax.sharding import PartitionSpec as P

RADIX = 4
LANES = 128
SUBLANES = 8
STRIP = 16
PIECES = 3
F32 = jnp.float32
BF16 = jnp.bfloat16

COS_POLY = (1, -19.7392044, 64.9391174, -85.4501419, 60.1676292, -25.9675999, 6.52865839)
SIN_POLY = (6.28318501, -41.3415909, 81.5999451, -76.6144714, 41.3428841, -12.4712439)

VMEM = pl.BlockSpec(memory_space=pltpu.VMEM)
HBM = pl.BlockSpec(memory_space=pltpu.HBM)
PARAMS = pltpu.CompilerParams(vmem_limit_bytes=32 * 1024 * 1024)


def iota(shape, dim):
    return lax.broadcasted_iota(jnp.int32, shape, dim)


def horner(poly, x):
    total = jnp.full_like(x, poly[-1])
    for term in poly[-2::-1]:
        total = total * x + term
    return total


def cos_sin(turns):
    turns = turns - jnp.round(turns)
    square = turns * turns
    return horner(COS_POLY, square), horner(SIN_POLY, square) * turns


def ceil_div(a, b):
    return -(-a // b)


def round_up(a, b):
    return ceil_div(a, b) * b


def dot(a, b, contract=((1,), (0,))):
    return lax.dot_general(a, b, (contract, ((), ())), preferred_element_type=F32)


class Sizes:
    def __init__(self, lat_total, var_total, levels, lons, waves):
        self.lat, self.var, self.levels, self.lons, self.waves = lat_total, var_total, levels, lons, waves
        self.devices = lat_total * var_total
        self.points = lons // RADIX
        self.tiles = self.points // LANES
        self.block = math.gcd(self.tiles, 2)
        self.kaps = waves // RADIX
        self.rows = round_up(ceil_div(waves, self.devices), SUBLANES)
        assert self.kaps % self.rows == 0 and lons % (PIECES * LANES) == 0 and self.points % LANES == 0 and 2 * levels == LANES and lat_total <= LANES
        self.mixed = lat_total * self.rows
        self.sin = round_up(self.kaps, LANES)
        self.heads = round_up(ceil_div(self.kaps, STRIP), SUBLANES)
        self.params = round_up(levels + lat_total, STRIP)


def own_length(order_ref, length_ref):
    slot = lax.axis_index("lat")
    row = order_ref[slot]
    return slot, row, length_ref[row]


def fetch(sources, targets, sems):
    copies = [pltpu.make_async_copy(s, t, sems.at[i]) for i, (s, t) in enumerate(zip(sources, targets))]
    for copy in copies:
        copy.start()
    return copies


def slot_matrix(z, order_ref, mer_ref):
    slot = iota((z.lat, z.lat), 0)
    row = jnp.zeros((z.lat, z.lat), jnp.int32)
    for t in range(z.lat):
        row = jnp.where(slot == t, order_ref[t], row)
    pick = (row == iota((z.lat, z.lat), 1)).astype(F32).astype(BF16)
    return dot(dot(pick, mer_ref[0]).astype(BF16), pick, ((1,), (1,)))


def tile(c):
    return slice(c * LANES, (c + 1) * LANES)


def analysis_kernel(z, *refs):
    given, made, held = refs[:7], refs[7:11], refs[11:18]
    sems, field_ref, parts_ref, heads_ref, tails_ref, scale_ref, product_ref = refs[18:]
    order_ref, length_ref, control_ref, vert_ref, amp_ref, mer_ref, bal_ref = held
    packet_ref, params_ref, basis_ref, twiddle_ref = made
    pieces = [pl.ds(at, z.lons // PIECES) for at in range(0, z.lons, z.lons // PIECES)]
    levels = pl.ds(0, z.levels)
    copies = fetch(
        [*given[:2], *[given[2].at[0, 0, levels, piece] for piece in pieces], *given[3:]],
        [*held[:2], *[control_ref.at[0, 0, levels, piece] for piece in pieces], *held[3:]],
        sems,
    )
    for at in (0, z.sin):
        basis_ref[at + z.kaps : at + z.sin] = jnp.zeros((z.sin - z.kaps, z.points), BF16)
    field_ref[:, z.lons :] = jnp.zeros((z.levels, LANES), F32)
    params_ref[...] = jnp.zeros(params_ref.shape, BF16)
    parts_ref[z.levels : 2 * z.levels] = jnp.zeros((z.levels, z.points), BF16)
    for copy in copies[:2]:
        copy.wait()
    slot, row, length = own_length(order_ref, length_ref)
    quarter = length // RADIX
    period = jnp.full((1, LANES), length, jnp.int32).astype(F32)
    tail = iota((STRIP, LANES), 0).astype(F32)
    head = iota((z.heads, LANES), 0).astype(F32) * STRIP
    tw_row = iota((2 * RADIX, LANES), 0)
    tw_wave = jnp.where(tw_row < RADIX, tw_row, tw_row - RADIX).astype(F32)
    fraction = jnp.full((1, LANES), quarter, jnp.int32).astype(F32)
    for c in range(z.tiles):
        points = c * LANES + iota((1, LANES), 1)
        step = points.astype(F32) / fraction
        tails_ref[:STRIP, tile(c)], tails_ref[STRIP:, tile(c)] = cos_sin(tail * step)
        head_cos, head_sin = cos_sin(head * step)
        heads_ref[: z.heads, tile(c)] = jnp.where(points < quarter, head_cos, 0.0)
        heads_ref[z.heads :, tile(c)] = jnp.where(points < quarter, head_sin, 0.0)
        tw_cos, tw_sin = cos_sin(tw_wave * (points.astype(F32) / period))
        twiddle_ref[: 2 * RADIX, tile(c)] = jnp.where(tw_row < RADIX, tw_cos, tw_sin)
        twiddle_ref[2 * RADIX :, tile(c)] = jnp.broadcast_to(period, (SUBLANES, LANES))
    for copy in copies[2 + PIECES :]:
        copy.wait()
    for piece, copy in zip(pieces, copies[2:]):
        copy.wait()
        field_ref[:, piece] = dot(vert_ref[0], control_ref[0, 0, :, piece])
    starts = [quarter * j1 for j1 in range(1, RADIX)]
    bases = [pl.multiple_of(s // LANES * LANES, LANES) for s in starts]
    shifts = [(LANES - (s - b)) % LANES for s, b in zip(starts, bases)]
    lane = iota((STRIP, LANES), 1)
    keeps = [(lane < shift) | (shift == 0) for shift in shifts]

    def rolled(i, at, c):
        lanes = pl.ds(pl.multiple_of(bases[i] + c * LANES, LANES), LANES)
        return pltpu.roll(field_ref[at : at + STRIP, lanes], shifts[i], 1)

    before = {}
    for block in range(0, z.tiles, z.block):
        for c in range(block, block + z.block):
            tail_cos, tail_sin = tails_ref[:STRIP, tile(c)], tails_ref[STRIP:, tile(c)]
            for at in range(0, z.kaps, STRIP):
                i = at // STRIP
                head_cos, head_sin = heads_ref[i : i + 1, tile(c)], heads_ref[z.heads + i : z.heads + i + 1, tile(c)]
                basis_ref[at : at + STRIP, tile(c)] = (head_cos * tail_cos - head_sin * tail_sin).astype(BF16)
                to = slice(z.sin + at, z.sin + at + STRIP)
                basis_ref[to, tile(c)] = (head_sin * tail_cos + head_cos * tail_sin).astype(BF16)
        for at in range(0, z.levels, STRIP):
            for c in range(block, block + z.block):
                if c == 0:
                    before[at] = [rolled(i, at, 0) for i in range(RADIX - 1)]
                after = [rolled(i, at, c + 1) for i in range(RADIX - 1)]
                second, third, fourth = [jnp.where(k, a, b) for k, a, b in zip(keeps, before[at], after)]
                before[at] = after
                first = field_ref[at : at + STRIP, tile(c)]
                even, odd = first + third, second + fourth
                real, imag, turned = first - third, second - fourth, even - odd
                cos1, cos2, cos3 = [twiddle_ref[r : r + 1, tile(c)] for r in (1, 2, 3)]
                sin1, sin2, sin3 = [twiddle_ref[RADIX + r : RADIX + r + 1, tile(c)] for r in (1, 2, 3)]
                parts = (
                    (even + odd,),
                    (real * cos1 - imag * sin1, real * sin1 + imag * cos1),
                    (turned * cos2, turned * sin2),
                    (real * cos3 + imag * sin3, real * sin3 - imag * cos3),
                )
                for r, pair in enumerate(parts):
                    for half, part in enumerate(pair):
                        to = (2 * r + half) * z.levels + at
                        parts_ref[to : to + STRIP, tile(c)] = part.astype(BF16)
        lanes = slice(block * LANES, (block + z.block) * LANES)
        basis = jnp.concatenate([basis_ref[: z.kaps, lanes], basis_ref[z.sin : z.sin + z.kaps, lanes]], axis=0)
        for pair in range(0, RADIX, 2):
            rows = slice(pair * LANES, (pair + 2) * LANES)
            product = dot(basis, parts_ref[rows, lanes], ((1,), (1,)))
            product_ref[:, rows] = product if block == 0 else product_ref[:, rows] + product
    group = LANES // RADIX
    weights = 1.0 / period, 2.0 / period
    for r in range(RADIX):
        picked = iota((group, LANES), 1) == iota((group, LANES), 0) * RADIX + r
        for at in range(0, z.kaps, group):
            lanes = slice(at * RADIX, at * RADIX + LANES)
            amp = jnp.sum(jnp.where(picked, amp_ref[:, lanes], 0.0), axis=1, keepdims=True)
            wave = (at + iota((group, LANES), 0)) * RADIX + r
            weight = jnp.where(wave == 0, *weights) if at + r == 0 else weights[1]
            scale_ref[r * z.kaps + at : r * z.kaps + at + group] = jnp.where(
                wave <= (length - 1) // 2, weight * amp, 0.0
            )
    params_ref[: z.levels] = jnp.concatenate([bal_ref[0], bal_ref[0]], axis=1)
    params_ref[z.levels : z.levels + z.lat, : z.lat] = slot_matrix(z, order_ref, mer_ref).astype(BF16)
    count = z.kaps // z.rows
    sign = jnp.where(iota((1, LANES), 1) < z.levels, -1.0, 1.0).astype(F32)
    for r in range(RADIX):
        lanes = tile(r)
        for i in range(count):
            rows = slice(i * z.rows, (i + 1) * z.rows)
            from_sin = product_ref[z.kaps + i * z.rows : z.kaps + (i + 1) * z.rows, lanes]
            both = product_ref[rows, lanes] + pltpu.roll(from_sin, z.levels, 1) * sign
            scale = scale_ref[r * z.kaps + i * z.rows : r * z.kaps + (i + 1) * z.rows]
            packet_ref[r * count + i] = (both * scale).astype(BF16)
    if z.devices > RADIX * count:
        packet_ref[RADIX * count :] = jnp.zeros((z.devices - RADIX * count, z.rows, LANES), BF16)


def matrices_kernel(z, *refs):
    *given, mix_ref, bal_ref, all_ref = refs
    own = lax.axis_index("var")
    for step, ref in enumerate(given):
        all_ref[(own + step) % z.var] = ref[...]
    size = z.mixed
    to_cols = (iota((z.lat, size), 0) == iota((z.lat, size), 1) // z.rows).astype(F32).astype(BF16)
    same = iota((size, size), 0) % z.rows == iota((size, size), 1) % z.rows
    halves = iota((LANES, LANES), 0) // z.levels == iota((LANES, LANES), 1) // z.levels
    for v in range(z.var):
        meridional = all_ref[v, z.levels :].astype(F32)[: z.lat, : z.lat].astype(BF16)
        slot_cols = dot(meridional, to_cols).astype(BF16)
        mix_ref[v] = jnp.where(same, dot(to_cols, slot_cols, ((0,), (0,))), 0.0).astype(BF16)
        if v > 0:
            balance = all_ref[v, : z.levels].astype(F32)
            balance = jnp.where(halves, jnp.concatenate([balance, balance], axis=0), 0.0)
            bal_ref[v - 1] = balance.T.astype(BF16)


def mixing_kernel(z, packet_ref, mix_ref, bal_ref, out_ref):
    stream = None
    for v in range(z.var):
        coeffs = packet_ref[v].astype(F32).reshape(z.mixed, LANES).astype(BF16)
        blended = dot(mix_ref[v], coeffs)
        if v == 0:
            stream = blended.astype(BF16)
        else:
            blended = blended + dot(stream, bal_ref[v - 1])
        blended = blended.reshape(z.lat, z.rows, LANES)
        for s in range(z.lat):
            out_ref[v, s] = blended[s].astype(BF16)


def synthesis_kernel(z, spectra_ref, basis_ref, twiddle_ref, out_ref, sems, field_ref, lhs_ref, parts_ref):
    period = twiddle_ref[2 * RADIX :, :LANES].astype(jnp.int32)
    length = jnp.max(period)
    kap = iota((z.kaps, LANES), 0)
    count = z.kaps // z.rows
    half = z.levels // 2
    kinds = 2 * RADIX - 1
    for at in (0, z.sin):
        lhs_ref[:, at + z.kaps : at + z.sin] = jnp.zeros((2 * half * kinds, z.sin - z.kaps), BF16)
    for r in range(RADIX):
        part = spectra_ref[r * count : (r + 1) * count].astype(F32).reshape(z.kaps, LANES)
        part = jnp.where(kap * RADIX + r <= (period[0:1] - 1) // 2, part, 0.0)
        part = part.astype(BF16).T
        for i in range(2):
            from_cos = part[i * half : (i + 1) * half]
            from_sin = part[z.levels + i * half : z.levels + (i + 1) * half]
            pairs = [(from_cos, from_sin)] if r == 0 else [(from_cos, from_sin), (-from_sin, from_cos)]
            for kind, pair in zip((2 * r - 1, 2 * r) if r else (0,), pairs):
                to = slice((i * kinds + kind) * half, (i * kinds + kind + 1) * half)
                lhs_ref[to, : z.kaps] = pair[0]
                lhs_ref[to, z.sin : z.sin + z.kaps] = pair[1]
    quarter = length // RADIX
    starts = [quarter * j1 for j1 in range(1, RADIX)]
    bases = [pl.multiple_of(s // LANES * LANES, LANES) for s in starts]
    shifts = [s - b for s, b in zip(starts, bases)]
    wide = z.points + LANES
    field_ref[:, wide:] = jnp.zeros((z.levels, z.lons + LANES - wide), BF16)
    keep = [iota((STRIP, LANES), 1) < shift for shift in shifts]
    zero = jnp.zeros((STRIP, LANES), F32)
    for i in range(2):
        rows = slice(i * kinds * half, (i + 1) * kinds * half)
        parts_ref[rows] = dot(lhs_ref[rows], basis_ref[...])
    sent = []
    for at in range(0, z.levels, STRIP):
        rows = slice(at, at + STRIP)
        first = at // half * kinds * half + at % half
        quarters = [[], [], [], []]
        for c in range(z.tiles):
            cos1, cos2, cos3 = [twiddle_ref[r : r + 1, tile(c)] for r in (1, 2, 3)]
            sin1, sin2, sin3 = [twiddle_ref[RADIX + r : RADIX + r + 1, tile(c)] for r in (1, 2, 3)]
            w0, re1, im1, re2, im2, re3, im3 = [
                parts_ref[first + kind * half : first + kind * half + STRIP, tile(c)] for kind in range(kinds)
            ]
            w2 = re2 * cos2 - im2 * sin2
            cross = (re1 * cos1 - im1 * sin1) + (re3 * cos3 - im3 * sin3)
            turn = (re1 * sin1 + im1 * cos1) - (re3 * sin3 + im3 * cos3)
            even, odd = w0 + w2, w0 - w2
            field_ref[rows, tile(c)] = (even + cross).astype(BF16)
            for j1, part in ((1, odd - turn), (2, even - cross), (3, odd + turn)):
                quarters[j1].append(pltpu.roll(part, shifts[j1 - 1], 1))
        field_ref[rows, tile(z.tiles)] = zero.astype(BF16)
        for j1 in range(1, RADIX):
            pieces = zip([zero] + quarters[j1], quarters[j1] + [zero])
            for c, (left, right) in enumerate(pieces):
                lanes = pl.ds(pl.multiple_of(bases[j1 - 1] + c * LANES, LANES), LANES)
                piece = jnp.where(keep[j1 - 1], left, right)
                if c == 0:
                    piece = piece + field_ref[rows, lanes].astype(F32)
                field_ref[rows, lanes] = piece.astype(BF16)
        sent += fetch(
            (field_ref.at[pl.ds(at, STRIP), pl.ds(0, z.lons)],),
            (out_ref.at[0, 0, pl.ds(at, STRIP)],),
            sems.at[pl.ds(at // STRIP, 1)],
        )
    for copy in sent:
        copy.wait()


def body(z, control, row_order, row_length, vertical, amplitude, meridional, balance):
    arguments = (row_order, row_length, control, vertical, amplitude, meridional, balance)
    made = (
        jax.ShapeDtypeStruct((z.devices, z.rows, LANES), BF16),
        jax.ShapeDtypeStruct((z.params, LANES), BF16),
        jax.ShapeDtypeStruct((2 * z.sin, z.points), BF16),
        jax.ShapeDtypeStruct((2 * RADIX + SUBLANES, z.points), F32),
    )
    packets, params, basis, twiddle = pl.pallas_call(
        functools.partial(analysis_kernel, z),
        out_shape=made,
        in_specs=[HBM] * len(arguments),
        out_specs=(VMEM,) * len(made),
        scratch_shapes=[
            *[pltpu.SMEM(x.shape, x.dtype) for x in arguments[:2]],
            *[pltpu.VMEM(x.shape, x.dtype) for x in arguments[2:]],
            pltpu.SemaphoreType.DMA((len(arguments) - 1 + PIECES,)),
            pltpu.VMEM((z.levels, z.lons + LANES), F32),
            pltpu.VMEM((2 * RADIX * z.levels, z.points), BF16),
            pltpu.VMEM((2 * z.heads, z.points), F32),
            pltpu.VMEM((2 * STRIP, z.points), F32),
            pltpu.VMEM((z.waves, LANES), F32),
            pltpu.VMEM((2 * z.kaps, RADIX * LANES), F32),
        ],
        compiler_params=PARAMS,
        name="analysis",
    )(*[pltpu.with_memory_space_constraint(x, pltpu.HBM) for x in arguments])
    given = [params]
    for step in range(1, z.var):
        given.append(lax.ppermute(params, "var", [((i + step) % z.var, i) for i in range(z.var)]))
    packets = lax.all_to_all(packets, ("var", "lat"), 0, 0, tiled=True)
    mix, lift = pl.pallas_call(
        functools.partial(matrices_kernel, z),
        out_shape=(
            jax.ShapeDtypeStruct((z.var, z.mixed, z.mixed), BF16),
            jax.ShapeDtypeStruct((z.var - 1, LANES, LANES), BF16),
        ),
        in_specs=[VMEM] * z.var,
        out_specs=(VMEM, VMEM),
        scratch_shapes=[pltpu.VMEM((z.var, z.params, LANES), BF16)],
        compiler_params=PARAMS,
        cost_estimate=pl.CostEstimate(flops=10**8, bytes_accessed=10**6, transcendentals=0),
        name="matrices",
    )(*given)
    balanced = pl.pallas_call(
        functools.partial(mixing_kernel, z),
        out_shape=jax.ShapeDtypeStruct((z.var, z.lat, z.rows, LANES), BF16),
        in_specs=[VMEM] * 3,
        out_specs=VMEM,
        compiler_params=PARAMS,
        name="mixing",
    )(packets.reshape(z.var, z.lat, z.rows, LANES), mix, lift)
    balanced = balanced.reshape(z.devices, z.rows, LANES)
    balanced = lax.all_to_all(balanced, ("var", "lat"), 0, 0, tiled=True)
    return pl.pallas_call(
        functools.partial(synthesis_kernel, z),
        out_shape=jax.ShapeDtypeStruct(control.shape, BF16),
        in_specs=[VMEM] * 3,
        out_specs=HBM,
        scratch_shapes=[
            pltpu.SemaphoreType.DMA((z.levels // STRIP,)),
            pltpu.VMEM((z.levels, z.lons + LANES), BF16),
            pltpu.VMEM(((2 * RADIX - 1) * z.levels, 2 * z.sin), BF16),
            pltpu.VMEM(((2 * RADIX - 1) * z.levels, z.points), F32),
        ],
        compiler_params=PARAMS,
        name="synthesis",
    )(balanced, basis, twiddle)


def solution(mesh):
    placed = (
        P("var", "lat", None, None),
        P(),
        P(),
        P("var", None, None),
        P("var", None),
        P("var", None, None),
        P("var", None, None),
    )

    def run(control, row_order, row_length, vertical, amplitude, meridional, balance):
        lat_total, var_total = mesh.shape["lat"], mesh.shape["var"]
        assert control.shape[0] == var_total and control.shape[1] == lat_total
        z = Sizes(lat_total, var_total, control.shape[2], control.shape[3], amplitude.shape[1])
        return jax.shard_map(
            functools.partial(body, z),
            mesh=mesh,
            in_specs=placed,
            out_specs=P("var", "lat", None, None),
            check_vma=False,
        )(control, row_order, row_length, vertical, amplitude, meridional, balance)

    return run
```

```python
import functools

import jax
import jax.numpy as jnp
from jax import lax
from jax.experimental import pallas as pl
from jax.experimental.pallas import tpu as pltpu
from jax.sharding import PartitionSpec as P

RADIX = 4
LANES = 128
SUBLANES = 8
STRIP = 16
F32 = jnp.float32
BF16 = jnp.bfloat16

COS_POLY = (1, -19.7392044, 64.9391174, -85.4501419, 60.1676292, -25.9675999, 6.52865839)
SIN_POLY = (6.28318501, -41.3415909, 81.5999451, -76.6144714, 41.3428841, -12.4712439)

VMEM = pl.BlockSpec(memory_space=pltpu.VMEM)
HBM = pl.BlockSpec(memory_space=pltpu.HBM)
PARAMS = pltpu.CompilerParams(vmem_limit_bytes=32 * 1024 * 1024)


def iota(shape, dim):
    return lax.broadcasted_iota(jnp.int32, shape, dim)


def horner(poly, x):
    total = jnp.full_like(x, poly[-1])
    for term in poly[-2::-1]:
        total = total * x + term
    return total


def cos_sin(turns):
    turns = turns - jnp.round(turns)
    square = turns * turns
    return horner(COS_POLY, square), horner(SIN_POLY, square) * turns


def ceil_div(a, b):
    return -(-a // b)


def round_up(a, b):
    return ceil_div(a, b) * b


def dot(a, b, contract=((1,), (0,))):
    return lax.dot_general(a, b, (contract, ((), ())), preferred_element_type=F32)


class Sizes:
    def __init__(self, lat_total, var_total, levels, lons, waves):
        self.lat, self.var, self.levels, self.lons, self.waves = lat_total, var_total, levels, lons, waves
        self.devices = lat_total * var_total
        self.points = lons // RADIX
        self.tiles = self.points // LANES
        self.kaps = waves // RADIX
        self.rows = round_up(ceil_div(waves, self.devices), SUBLANES)
        assert self.kaps % self.rows == 0 and self.points % LANES == 0 and 2 * levels == LANES and lat_total <= LANES
        self.mixed = lat_total * self.rows
        self.sin = round_up(self.kaps, LANES)
        self.heads = round_up(ceil_div(self.kaps, STRIP), SUBLANES)
        self.params = round_up(levels + lat_total, STRIP)


def own_length(order_ref, length_ref):
    slot = lax.axis_index("lat")
    row = order_ref[slot]
    return slot, row, length_ref[row]


def fetch(sources, targets, sems):
    copies = [pltpu.make_async_copy(s, t, sems.at[i]) for i, (s, t) in enumerate(zip(sources, targets))]
    for copy in copies:
        copy.start()
    return copies


def slot_matrix(z, order_ref, mer_ref):
    slot = iota((z.lat, z.lat), 0)
    row = jnp.zeros((z.lat, z.lat), jnp.int32)
    for t in range(z.lat):
        row = jnp.where(slot == t, order_ref[t], row)
    pick = (row == iota((z.lat, z.lat), 1)).astype(F32).astype(BF16)
    return dot(dot(pick, mer_ref[0]).astype(BF16), pick, ((1,), (1,)))


def tile(c):
    return slice(c * LANES, (c + 1) * LANES)


def analysis_kernel(z, *refs):
    given, made, held = refs[:7], refs[7:11], refs[11:18]
    sems, field_ref, parts_ref, heads_ref, tails_ref, scale_ref, product_ref = refs[18:]
    control_ref, vert_ref, order_ref, length_ref, amp_ref, mer_ref, bal_ref = held
    packet_ref, params_ref, basis_ref, twiddle_ref = made
    copies = fetch(given, held, sems)
    for at in (0, z.sin):
        basis_ref[at + z.kaps : at + z.sin] = jnp.zeros((z.sin - z.kaps, z.points), BF16)
    field_ref[:, z.lons :] = jnp.zeros((z.levels, LANES), F32)
    params_ref[...] = jnp.zeros(params_ref.shape, BF16)
    parts_ref[z.levels : 2 * z.levels] = jnp.zeros((z.levels, z.points), BF16)
    for copy in copies[2:4]:
        copy.wait()
    slot, row, length = own_length(order_ref, length_ref)
    quarter = length // RADIX
    period = jnp.full((1, LANES), length, jnp.int32).astype(F32)
    tail = iota((STRIP, LANES), 0).astype(F32)
    head = iota((z.heads, LANES), 0).astype(F32) * STRIP
    tw_row = iota((2 * RADIX, LANES), 0)
    tw_wave = jnp.where(tw_row < RADIX, tw_row, tw_row - RADIX).astype(F32)
    fraction = jnp.full((1, LANES), quarter, jnp.int32).astype(F32)
    for c in range(z.tiles):
        points = c * LANES + iota((1, LANES), 1)
        step = points.astype(F32) / fraction
        tails_ref[:STRIP, tile(c)], tails_ref[STRIP:, tile(c)] = cos_sin(tail * step)
        head_cos, head_sin = cos_sin(head * step)
        heads_ref[: z.heads, tile(c)] = jnp.where(points < quarter, head_cos, 0.0)
        heads_ref[z.heads :, tile(c)] = jnp.where(points < quarter, head_sin, 0.0)
        tw_cos, tw_sin = cos_sin(tw_wave * (points.astype(F32) / period))
        twiddle_ref[: 2 * RADIX, tile(c)] = jnp.where(tw_row < RADIX, tw_cos, tw_sin)
        twiddle_ref[2 * RADIX :, tile(c)] = jnp.broadcast_to(period, (SUBLANES, LANES))
    for copy in [*copies[:2], *copies[4:]]:
        copy.wait()
    field_ref[:, : z.lons] = dot(vert_ref[0], control_ref[0, 0])
    starts = [quarter * j1 for j1 in range(1, RADIX)]
    bases = [pl.multiple_of(s // LANES * LANES, LANES) for s in starts]
    shifts = [(LANES - (s - b)) % LANES for s, b in zip(starts, bases)]
    lane = iota((STRIP, LANES), 1)
    keeps = [(lane < shift) | (shift == 0) for shift in shifts]

    def rolled(i, at, c):
        lanes = pl.ds(pl.multiple_of(bases[i] + c * LANES, LANES), LANES)
        return pltpu.roll(field_ref[at : at + STRIP, lanes], shifts[i], 1)

    before = {}
    for c in range(z.tiles):
        tail_cos, tail_sin = tails_ref[:STRIP, tile(c)], tails_ref[STRIP:, tile(c)]
        for at in range(0, z.kaps, STRIP):
            i = at // STRIP
            head_cos, head_sin = heads_ref[i : i + 1, tile(c)], heads_ref[z.heads + i : z.heads + i + 1, tile(c)]
            basis_ref[at : at + STRIP, tile(c)] = (head_cos * tail_cos - head_sin * tail_sin).astype(BF16)
            to = slice(z.sin + at, z.sin + at + STRIP)
            basis_ref[to, tile(c)] = (head_sin * tail_cos + head_cos * tail_sin).astype(BF16)
    for at in range(0, z.levels, STRIP):
        for c in range(z.tiles):
            if c == 0:
                before[at] = [rolled(i, at, 0) for i in range(RADIX - 1)]
            after = [rolled(i, at, c + 1) for i in range(RADIX - 1)]
            second, third, fourth = [jnp.where(k, a, b) for k, a, b in zip(keeps, before[at], after)]
            before[at] = after
            first = field_ref[at : at + STRIP, tile(c)]
            even, odd = first + third, second + fourth
            real, imag, turned = first - third, second - fourth, even - odd
            cos1, cos2, cos3 = [twiddle_ref[r : r + 1, tile(c)] for r in (1, 2, 3)]
            sin1, sin2, sin3 = [twiddle_ref[RADIX + r : RADIX + r + 1, tile(c)] for r in (1, 2, 3)]
            parts = (
                (even + odd,),
                (real * cos1 - imag * sin1, real * sin1 + imag * cos1),
                (turned * cos2, turned * sin2),
                (real * cos3 + imag * sin3, real * sin3 - imag * cos3),
            )
            for r, pair in enumerate(parts):
                for half, part in enumerate(pair):
                    to = (2 * r + half) * z.levels + at
                    parts_ref[to : to + STRIP, tile(c)] = part.astype(BF16)
    basis = jnp.concatenate([basis_ref[: z.kaps], basis_ref[z.sin : z.sin + z.kaps]], axis=0)
    product_ref[...] = dot(basis, parts_ref[...], ((1,), (1,)))
    group = LANES // RADIX
    weights = 1.0 / period, 2.0 / period
    for r in range(RADIX):
        picked = iota((group, LANES), 1) == iota((group, LANES), 0) * RADIX + r
        for at in range(0, z.kaps, group):
            lanes = slice(at * RADIX, at * RADIX + LANES)
            amp = jnp.sum(jnp.where(picked, amp_ref[:, lanes], 0.0), axis=1, keepdims=True)
            wave = (at + iota((group, LANES), 0)) * RADIX + r
            weight = jnp.where(wave == 0, *weights) if at + r == 0 else weights[1]
            scale_ref[r * z.kaps + at : r * z.kaps + at + group] = jnp.where(
                wave <= (length - 1) // 2, weight * amp, 0.0
            )
    params_ref[: z.levels] = jnp.concatenate([bal_ref[0], bal_ref[0]], axis=1)
    params_ref[z.levels : z.levels + z.lat, : z.lat] = slot_matrix(z, order_ref, mer_ref).astype(BF16)
    count = z.kaps // z.rows
    sign = jnp.where(iota((1, LANES), 1) < z.levels, -1.0, 1.0).astype(F32)
    for r in range(RADIX):
        lanes = tile(r)
        for i in range(count):
            rows = slice(i * z.rows, (i + 1) * z.rows)
            from_sin = product_ref[z.kaps + i * z.rows : z.kaps + (i + 1) * z.rows, lanes]
            both = product_ref[rows, lanes] + pltpu.roll(from_sin, z.levels, 1) * sign
            scale = scale_ref[r * z.kaps + i * z.rows : r * z.kaps + (i + 1) * z.rows]
            packet_ref[r * count + i] = (both * scale).astype(BF16)
    if z.devices > RADIX * count:
        packet_ref[RADIX * count :] = jnp.zeros((z.devices - RADIX * count, z.rows, LANES), BF16)


def matrices_kernel(z, *refs):
    *given, mix_ref, bal_ref, all_ref = refs
    own = lax.axis_index("var")
    for step, ref in enumerate(given):
        all_ref[(own + step) % z.var] = ref[...]
    size = z.mixed
    to_cols = (iota((z.lat, size), 0) == iota((z.lat, size), 1) // z.rows).astype(F32).astype(BF16)
    same = iota((size, size), 0) % z.rows == iota((size, size), 1) % z.rows
    halves = iota((LANES, LANES), 0) // z.levels == iota((LANES, LANES), 1) // z.levels
    for v in range(z.var):
        meridional = all_ref[v, z.levels :].astype(F32)[: z.lat, : z.lat].astype(BF16)
        slot_cols = dot(meridional, to_cols).astype(BF16)
        mix_ref[v] = jnp.where(same, dot(to_cols, slot_cols, ((0,), (0,))), 0.0).astype(BF16)
        if v > 0:
            balance = all_ref[v, : z.levels].astype(F32)
            balance = jnp.where(halves, jnp.concatenate([balance, balance], axis=0), 0.0)
            bal_ref[v - 1] = balance.T.astype(BF16)


def mixing_kernel(z, packet_ref, mix_ref, bal_ref, out_ref):
    stream = None
    for v in range(z.var):
        coeffs = packet_ref[v].astype(F32).reshape(z.mixed, LANES).astype(BF16)
        blended = dot(mix_ref[v], coeffs)
        if v == 0:
            stream = blended.astype(BF16)
        else:
            blended = blended + dot(stream, bal_ref[v - 1])
        blended = blended.reshape(z.lat, z.rows, LANES)
        for s in range(z.lat):
            out_ref[v, s] = blended[s].astype(BF16)


def synthesis_kernel(z, spectra_ref, basis_ref, twiddle_ref, out_ref, sems, field_ref, lhs_ref, parts_ref):
    period = twiddle_ref[2 * RADIX :, :LANES].astype(jnp.int32)
    length = jnp.max(period)
    kap = iota((z.kaps, LANES), 0)
    count = z.kaps // z.rows
    half = z.levels // 2
    kinds = 2 * RADIX - 1
    for at in (0, z.sin):
        lhs_ref[:, at + z.kaps : at + z.sin] = jnp.zeros((2 * half * kinds, z.sin - z.kaps), BF16)
    for r in range(RADIX):
        part = spectra_ref[r * count : (r + 1) * count].astype(F32).reshape(z.kaps, LANES)
        part = jnp.where(kap * RADIX + r <= (period[0:1] - 1) // 2, part, 0.0)
        part = part.astype(BF16).T
        for i in range(2):
            from_cos = part[i * half : (i + 1) * half]
            from_sin = part[z.levels + i * half : z.levels + (i + 1) * half]
            pairs = [(from_cos, from_sin)] if r == 0 else [(from_cos, from_sin), (-from_sin, from_cos)]
            for kind, pair in zip((2 * r - 1, 2 * r) if r else (0,), pairs):
                to = slice((i * kinds + kind) * half, (i * kinds + kind + 1) * half)
                lhs_ref[to, : z.kaps] = pair[0]
                lhs_ref[to, z.sin : z.sin + z.kaps] = pair[1]
    quarter = length // RADIX
    starts = [quarter * j1 for j1 in range(1, RADIX)]
    bases = [pl.multiple_of(s // LANES * LANES, LANES) for s in starts]
    shifts = [s - b for s, b in zip(starts, bases)]
    wide = z.points + LANES
    field_ref[:, wide:] = jnp.zeros((z.levels, z.lons + LANES - wide), BF16)
    keep = [iota((STRIP, LANES), 1) < shift for shift in shifts]
    zero = jnp.zeros((STRIP, LANES), F32)
    for i in range(2):
        rows = slice(i * kinds * half, (i + 1) * kinds * half)
        parts_ref[rows] = dot(lhs_ref[rows], basis_ref[...])
    sent = []
    for at in range(0, z.levels, STRIP):
        rows = slice(at, at + STRIP)
        first = at // half * kinds * half + at % half
        quarters = [[], [], [], []]
        for c in range(z.tiles):
            cos1, cos2, cos3 = [twiddle_ref[r : r + 1, tile(c)] for r in (1, 2, 3)]
            sin1, sin2, sin3 = [twiddle_ref[RADIX + r : RADIX + r + 1, tile(c)] for r in (1, 2, 3)]
            w0, re1, im1, re2, im2, re3, im3 = [
                parts_ref[first + kind * half : first + kind * half + STRIP, tile(c)] for kind in range(kinds)
            ]
            w2 = re2 * cos2 - im2 * sin2
            cross = (re1 * cos1 - im1 * sin1) + (re3 * cos3 - im3 * sin3)
            turn = (re1 * sin1 + im1 * cos1) - (re3 * sin3 + im3 * cos3)
            even, odd = w0 + w2, w0 - w2
            field_ref[rows, tile(c)] = (even + cross).astype(BF16)
            for j1, part in ((1, odd - turn), (2, even - cross), (3, odd + turn)):
                quarters[j1].append(pltpu.roll(part, shifts[j1 - 1], 1))
        field_ref[rows, tile(z.tiles)] = zero.astype(BF16)
        for j1 in range(1, RADIX):
            pieces = zip([zero] + quarters[j1], quarters[j1] + [zero])
            for c, (left, right) in enumerate(pieces):
                lanes = pl.ds(pl.multiple_of(bases[j1 - 1] + c * LANES, LANES), LANES)
                piece = jnp.where(keep[j1 - 1], left, right)
                if c == 0:
                    piece = piece + field_ref[rows, lanes].astype(F32)
                field_ref[rows, lanes] = piece.astype(BF16)
        sent += fetch(
            (field_ref.at[pl.ds(at, STRIP), pl.ds(0, z.lons)],),
            (out_ref.at[0, 0, pl.ds(at, STRIP)],),
            sems.at[pl.ds(at // STRIP, 1)],
        )
    for copy in sent:
        copy.wait()


def body(z, control, row_order, row_length, vertical, amplitude, meridional, balance):
    arguments = (control, vertical, row_order, row_length, amplitude, meridional, balance)
    made = (
        jax.ShapeDtypeStruct((z.devices, z.rows, LANES), BF16),
        jax.ShapeDtypeStruct((z.params, LANES), BF16),
        jax.ShapeDtypeStruct((2 * z.sin, z.points), BF16),
        jax.ShapeDtypeStruct((2 * RADIX + SUBLANES, z.points), F32),
    )
    packets, params, basis, twiddle = pl.pallas_call(
        functools.partial(analysis_kernel, z),
        out_shape=made,
        in_specs=[HBM] * len(arguments),
        out_specs=(VMEM,) * len(made),
        scratch_shapes=[
            *[(pltpu.SMEM if x.ndim == 1 else pltpu.VMEM)(x.shape, x.dtype) for x in arguments],
            pltpu.SemaphoreType.DMA((len(arguments),)),
            pltpu.VMEM((z.levels, z.lons + LANES), F32),
            pltpu.VMEM((2 * RADIX * z.levels, z.points), BF16),
            pltpu.VMEM((2 * z.heads, z.points), F32),
            pltpu.VMEM((2 * STRIP, z.points), F32),
            pltpu.VMEM((z.waves, LANES), F32),
            pltpu.VMEM((2 * z.kaps, RADIX * LANES), F32),
        ],
        compiler_params=PARAMS,
        name="analysis",
    )(*[pltpu.with_memory_space_constraint(x, pltpu.HBM) for x in arguments])
    given = [params]
    for step in range(1, z.var):
        given.append(lax.ppermute(params, "var", [((i + step) % z.var, i) for i in range(z.var)]))
    packets = lax.all_to_all(packets, ("var", "lat"), 0, 0, tiled=True)
    mix, lift = pl.pallas_call(
        functools.partial(matrices_kernel, z),
        out_shape=(
            jax.ShapeDtypeStruct((z.var, z.mixed, z.mixed), BF16),
            jax.ShapeDtypeStruct((z.var - 1, LANES, LANES), BF16),
        ),
        in_specs=[VMEM] * z.var,
        out_specs=(VMEM, VMEM),
        scratch_shapes=[pltpu.VMEM((z.var, z.params, LANES), BF16)],
        compiler_params=PARAMS,
        cost_estimate=pl.CostEstimate(flops=10**8, bytes_accessed=10**6, transcendentals=0),
        name="matrices",
    )(*given)
    balanced = pl.pallas_call(
        functools.partial(mixing_kernel, z),
        out_shape=jax.ShapeDtypeStruct((z.var, z.lat, z.rows, LANES), BF16),
        in_specs=[VMEM] * 3,
        out_specs=VMEM,
        compiler_params=PARAMS,
        name="mixing",
    )(packets.reshape(z.var, z.lat, z.rows, LANES), mix, lift)
    balanced = balanced.reshape(z.devices, z.rows, LANES)
    balanced = lax.all_to_all(balanced, ("var", "lat"), 0, 0, tiled=True)
    return pl.pallas_call(
        functools.partial(synthesis_kernel, z),
        out_shape=jax.ShapeDtypeStruct(control.shape, BF16),
        in_specs=[VMEM] * 3,
        out_specs=HBM,
        scratch_shapes=[
            pltpu.SemaphoreType.DMA((z.levels // STRIP,)),
            pltpu.VMEM((z.levels, z.lons + LANES), BF16),
            pltpu.VMEM(((2 * RADIX - 1) * z.levels, 2 * z.sin), BF16),
            pltpu.VMEM(((2 * RADIX - 1) * z.levels, z.points), F32),
        ],
        compiler_params=PARAMS,
        name="synthesis",
    )(balanced, basis, twiddle)


def solution(mesh):
    placed = (
        P("var", "lat", None, None),
        P(),
        P(),
        P("var", None, None),
        P("var", None),
        P("var", None, None),
        P("var", None, None),
    )

    def run(control, row_order, row_length, vertical, amplitude, meridional, balance):
        lat_total, var_total = mesh.shape["lat"], mesh.shape["var"]
        assert control.shape[0] == var_total and control.shape[1] == lat_total
        z = Sizes(lat_total, var_total, control.shape[2], control.shape[3], amplitude.shape[1])
        return jax.shard_map(
            functools.partial(body, z),
            mesh=mesh,
            in_specs=placed,
            out_specs=P("var", "lat", None, None),
            check_vma=False,
        )(control, row_order, row_length, vertical, amplitude, meridional, balance)

    return run
```

```python
import functools
import math

import jax
import jax.numpy as jnp
from jax import lax
from jax.experimental import pallas as pl
from jax.experimental.pallas import tpu as pltpu
from jax.sharding import PartitionSpec as P

RADIX = 4
LANES = 128
SUBLANES = 8
STRIP = 16
F32 = jnp.float32
BF16 = jnp.bfloat16

COS_POLY = (1, -19.7392044, 64.9391174, -85.4501419, 60.1676292, -25.9675999, 6.52865839)
SIN_POLY = (6.28318501, -41.3415909, 81.5999451, -76.6144714, 41.3428841, -12.4712439)

VMEM = pl.BlockSpec(memory_space=pltpu.VMEM)
HBM = pl.BlockSpec(memory_space=pltpu.HBM)
PARAMS = pltpu.CompilerParams(vmem_limit_bytes=32 * 1024 * 1024)


def iota(shape, dim):
    return lax.broadcasted_iota(jnp.int32, shape, dim)


def horner(poly, x):
    total = jnp.full_like(x, poly[-1])
    for term in poly[-2::-1]:
        total = total * x + term
    return total


def cos_sin(turns):
    turns = turns - jnp.round(turns)
    square = turns * turns
    return horner(COS_POLY, square), horner(SIN_POLY, square) * turns


def ceil_div(a, b):
    return -(-a // b)


def round_up(a, b):
    return ceil_div(a, b) * b


def dot(a, b, contract=((1,), (0,))):
    return lax.dot_general(a, b, (contract, ((), ())), preferred_element_type=F32)


class Sizes:
    def __init__(self, lat_total, var_total, levels, lons, waves):
        self.lat, self.var, self.levels, self.lons, self.waves = lat_total, var_total, levels, lons, waves
        self.devices = lat_total * var_total
        self.points = lons // RADIX
        self.tiles = self.points // LANES
        self.block = math.gcd(self.tiles, 2)
        self.kaps = waves // RADIX
        self.rows = round_up(ceil_div(waves, self.devices), SUBLANES)
        assert self.kaps % self.rows == 0 and self.points % LANES == 0 and 2 * levels == LANES and lat_total <= LANES
        self.mixed = lat_total * self.rows
        self.sin = round_up(self.kaps, LANES)
        self.heads = round_up(ceil_div(self.kaps, STRIP), SUBLANES)


def own_length(order_ref, length_ref):
    slot = lax.axis_index("lat")
    row = order_ref[slot]
    return slot, row, length_ref[row]


def fetch(sources, targets, sems):
    copies = [pltpu.make_async_copy(s, t, sems.at[i]) for i, (s, t) in enumerate(zip(sources, targets))]
    for copy in copies:
        copy.start()
    return copies


def slot_picks(z, order_ref):
    slot = iota((z.lat, z.lat), 0)
    row = jnp.zeros((z.lat, z.lat), jnp.int32)
    for t in range(z.lat):
        row = jnp.where(slot == t, order_ref[t], row)
    return (row == iota((z.lat, z.lat), 1)).astype(F32).astype(BF16)


def tile(c):
    return slice(c * LANES, (c + 1) * LANES)


def analysis_kernel(z, *refs):
    given, made, held = refs[:5], refs[5:8], refs[8:13]
    sems, field_ref, parts_ref, heads_ref, tails_ref, scale_ref, product_ref = refs[13:]
    order_ref, length_ref, control_ref, vert_ref, amp_ref = held
    packet_ref, basis_ref, twiddle_ref = made
    copies = fetch(given, held, sems)
    for at in (0, z.sin):
        basis_ref[at + z.kaps : at + z.sin] = jnp.zeros((z.sin - z.kaps, z.points), BF16)
    field_ref[:, z.lons :] = jnp.zeros((z.levels, LANES), F32)
    parts_ref[z.levels : 2 * z.levels] = jnp.zeros((z.levels, z.points), BF16)
    for copy in copies[:2]:
        copy.wait()
    slot, row, length = own_length(order_ref, length_ref)
    quarter = length // RADIX
    period = jnp.full((1, LANES), length, jnp.int32).astype(F32)
    tail = iota((STRIP, LANES), 0).astype(F32)
    head = iota((z.heads, LANES), 0).astype(F32) * STRIP
    tw_row = iota((2 * RADIX, LANES), 0)
    tw_wave = jnp.where(tw_row < RADIX, tw_row, tw_row - RADIX).astype(F32)
    fraction = jnp.full((1, LANES), quarter, jnp.int32).astype(F32)
    for c in range(z.tiles):
        points = c * LANES + iota((1, LANES), 1)
        step = points.astype(F32) / fraction
        tails_ref[:STRIP, tile(c)], tails_ref[STRIP:, tile(c)] = cos_sin(tail * step)
        head_cos, head_sin = cos_sin(head * step)
        heads_ref[: z.heads, tile(c)] = jnp.where(points < quarter, head_cos, 0.0)
        heads_ref[z.heads :, tile(c)] = jnp.where(points < quarter, head_sin, 0.0)
        tw_cos, tw_sin = cos_sin(tw_wave * (points.astype(F32) / period))
        twiddle_ref[: 2 * RADIX, tile(c)] = jnp.where(tw_row < RADIX, tw_cos, tw_sin)
        twiddle_ref[2 * RADIX :, tile(c)] = jnp.broadcast_to(period, (SUBLANES, LANES))
    for copy in copies[2:]:
        copy.wait()
    field_ref[:, : z.lons] = dot(vert_ref[0], control_ref[0, 0])
    starts = [quarter * j1 for j1 in range(1, RADIX)]
    bases = [pl.multiple_of(s // LANES * LANES, LANES) for s in starts]
    shifts = [(LANES - (s - b)) % LANES for s, b in zip(starts, bases)]
    lane = iota((STRIP, LANES), 1)
    keeps = [(lane < shift) | (shift == 0) for shift in shifts]

    def rolled(i, at, c):
        lanes = pl.ds(pl.multiple_of(bases[i] + c * LANES, LANES), LANES)
        return pltpu.roll(field_ref[at : at + STRIP, lanes], shifts[i], 1)

    before = {}
    for block in range(0, z.tiles, z.block):
        for c in range(block, block + z.block):
            tail_cos, tail_sin = tails_ref[:STRIP, tile(c)], tails_ref[STRIP:, tile(c)]
            for at in range(0, z.kaps, STRIP):
                i = at // STRIP
                head_cos, head_sin = heads_ref[i : i + 1, tile(c)], heads_ref[z.heads + i : z.heads + i + 1, tile(c)]
                basis_ref[at : at + STRIP, tile(c)] = (head_cos * tail_cos - head_sin * tail_sin).astype(BF16)
                to = slice(z.sin + at, z.sin + at + STRIP)
                basis_ref[to, tile(c)] = (head_sin * tail_cos + head_cos * tail_sin).astype(BF16)
        for at in range(0, z.levels, STRIP):
            for c in range(block, block + z.block):
                if c == 0:
                    before[at] = [rolled(i, at, 0) for i in range(RADIX - 1)]
                after = [rolled(i, at, c + 1) for i in range(RADIX - 1)]
                second, third, fourth = [jnp.where(k, a, b) for k, a, b in zip(keeps, before[at], after)]
                before[at] = after
                first = field_ref[at : at + STRIP, tile(c)]
                even, odd = first + third, second + fourth
                real, imag, turned = first - third, second - fourth, even - odd
                cos1, cos2, cos3 = [twiddle_ref[r : r + 1, tile(c)] for r in (1, 2, 3)]
                sin1, sin2, sin3 = [twiddle_ref[RADIX + r : RADIX + r + 1, tile(c)] for r in (1, 2, 3)]
                parts = (
                    (even + odd,),
                    (real * cos1 - imag * sin1, real * sin1 + imag * cos1),
                    (turned * cos2, turned * sin2),
                    (real * cos3 + imag * sin3, real * sin3 - imag * cos3),
                )
                for r, pair in enumerate(parts):
                    for half, part in enumerate(pair):
                        to = (2 * r + half) * z.levels + at
                        parts_ref[to : to + STRIP, tile(c)] = part.astype(BF16)
        lanes = slice(block * LANES, (block + z.block) * LANES)
        basis = jnp.concatenate([basis_ref[: z.kaps, lanes], basis_ref[z.sin : z.sin + z.kaps, lanes]], axis=0)
        product = dot(basis, parts_ref[:, lanes], ((1,), (1,)))
        product_ref[...] = product if block == 0 else product_ref[...] + product
    group = LANES // RADIX
    weights = 1.0 / period, 2.0 / period
    for r in range(RADIX):
        picked = iota((group, LANES), 1) == iota((group, LANES), 0) * RADIX + r
        for at in range(0, z.kaps, group):
            lanes = slice(at * RADIX, at * RADIX + LANES)
            amp = jnp.sum(jnp.where(picked, amp_ref[:, lanes], 0.0), axis=1, keepdims=True)
            wave = (at + iota((group, LANES), 0)) * RADIX + r
            weight = jnp.where(wave == 0, *weights) if at + r == 0 else weights[1]
            scale_ref[r * z.kaps + at : r * z.kaps + at + group] = jnp.where(
                wave <= (length - 1) // 2, weight * amp, 0.0
            )
    count = z.kaps // z.rows
    sign = jnp.where(iota((1, LANES), 1) < z.levels, -1.0, 1.0).astype(F32)
    for r in range(RADIX):
        lanes = tile(r)
        for i in range(count):
            rows = slice(i * z.rows, (i + 1) * z.rows)
            from_sin = product_ref[z.kaps + i * z.rows : z.kaps + (i + 1) * z.rows, lanes]
            both = product_ref[rows, lanes] + pltpu.roll(from_sin, z.levels, 1) * sign
            scale = scale_ref[r * z.kaps + i * z.rows : r * z.kaps + (i + 1) * z.rows]
            packet_ref[r * count + i] = (both * scale).astype(BF16)
    if z.devices > RADIX * count:
        packet_ref[RADIX * count :] = jnp.zeros((z.devices - RADIX * count, z.rows, LANES), BF16)


def matrices_kernel(z, *refs):
    given, (mix_ref, bal_ref), held, sems = refs[:3], refs[3:5], refs[5:8], refs[8]
    order_ref, mer_ref, all_bal_ref = held
    copies = fetch(given, held, sems)
    size = z.mixed
    to_cols = (iota((z.lat, size), 0) == iota((z.lat, size), 1) // z.rows).astype(F32).astype(BF16)
    same = iota((size, size), 0) % z.rows == iota((size, size), 1) % z.rows
    halves = iota((LANES, LANES), 0) // z.levels == iota((LANES, LANES), 1) // z.levels
    for copy in copies:
        copy.wait()
    for v in range(1, z.var):
        balance = all_bal_ref[v].astype(F32)
        balance = jnp.concatenate([balance, balance], axis=1)
        balance = jnp.where(halves, jnp.concatenate([balance, balance], axis=0), 0.0)
        bal_ref[v - 1] = balance.T.astype(BF16)
    to_cols = dot(slot_picks(z, order_ref), to_cols, ((0,), (0,))).astype(BF16)
    for v in range(z.var):
        slot_cols = dot(mer_ref[v], to_cols).astype(BF16)
        mix_ref[v] = jnp.where(same, dot(to_cols, slot_cols, ((0,), (0,))), 0.0).astype(BF16)


def mixing_kernel(z, packet_ref, mix_ref, bal_ref, out_ref):
    stream = None
    for v in range(z.var):
        coeffs = packet_ref[v].astype(F32).reshape(z.mixed, LANES).astype(BF16)
        blended = dot(mix_ref[v], coeffs)
        if v == 0:
            stream = blended.astype(BF16)
        else:
            blended = blended + dot(stream, bal_ref[v - 1])
        blended = blended.reshape(z.lat, z.rows, LANES)
        for s in range(z.lat):
            out_ref[v, s] = blended[s].astype(BF16)


def synthesis_kernel(z, spectra_ref, basis_ref, twiddle_ref, out_ref, sems, field_ref, lhs_ref, parts_ref):
    period = twiddle_ref[2 * RADIX :, :LANES].astype(jnp.int32)
    length = jnp.max(period)
    kap = iota((z.kaps, LANES), 0)
    count = z.kaps // z.rows
    half = z.levels // 2
    kinds = 2 * RADIX - 1
    for at in (0, z.sin):
        lhs_ref[:, at + z.kaps : at + z.sin] = jnp.zeros((2 * half * kinds, z.sin - z.kaps), BF16)
    for r in range(RADIX):
        part = spectra_ref[r * count : (r + 1) * count].astype(F32).reshape(z.kaps, LANES)
        part = jnp.where(kap * RADIX + r <= (period[0:1] - 1) // 2, part, 0.0)
        part = part.astype(BF16).T
        for i in range(2):
            from_cos = part[i * half : (i + 1) * half]
            from_sin = part[z.levels + i * half : z.levels + (i + 1) * half]
            pairs = [(from_cos, from_sin)] if r == 0 else [(from_cos, from_sin), (-from_sin, from_cos)]
            for kind, pair in zip((2 * r - 1, 2 * r) if r else (0,), pairs):
                to = slice((i * kinds + kind) * half, (i * kinds + kind + 1) * half)
                lhs_ref[to, : z.kaps] = pair[0]
                lhs_ref[to, z.sin : z.sin + z.kaps] = pair[1]
    quarter = length // RADIX
    starts = [quarter * j1 for j1 in range(1, RADIX)]
    bases = [pl.multiple_of(s // LANES * LANES, LANES) for s in starts]
    shifts = [s - b for s, b in zip(starts, bases)]
    wide = z.points + LANES
    field_ref[:, wide:] = jnp.zeros((z.levels, z.lons + LANES - wide), BF16)
    keep = [iota((STRIP, LANES), 1) < shift for shift in shifts]
    zero = jnp.zeros((STRIP, LANES), F32)
    for i in range(2):
        rows = slice(i * kinds * half, (i + 1) * kinds * half)
        parts_ref[rows] = dot(lhs_ref[rows], basis_ref[...])
    sent = []
    for at in range(0, z.levels, STRIP):
        rows = slice(at, at + STRIP)
        first = at // half * kinds * half + at % half
        quarters = [[], [], [], []]
        for c in range(z.tiles):
            cos1, cos2, cos3 = [twiddle_ref[r : r + 1, tile(c)] for r in (1, 2, 3)]
            sin1, sin2, sin3 = [twiddle_ref[RADIX + r : RADIX + r + 1, tile(c)] for r in (1, 2, 3)]
            w0, re1, im1, re2, im2, re3, im3 = [
                parts_ref[first + kind * half : first + kind * half + STRIP, tile(c)] for kind in range(kinds)
            ]
            w2 = re2 * cos2 - im2 * sin2
            cross = (re1 * cos1 - im1 * sin1) + (re3 * cos3 - im3 * sin3)
            turn = (re1 * sin1 + im1 * cos1) - (re3 * sin3 + im3 * cos3)
            even, odd = w0 + w2, w0 - w2
            field_ref[rows, tile(c)] = (even + cross).astype(BF16)
            for j1, part in ((1, odd - turn), (2, even - cross), (3, odd + turn)):
                quarters[j1].append(pltpu.roll(part, shifts[j1 - 1], 1))
        field_ref[rows, tile(z.tiles)] = zero.astype(BF16)
        for j1 in range(1, RADIX):
            pieces = zip([zero] + quarters[j1], quarters[j1] + [zero])
            for c, (left, right) in enumerate(pieces):
                lanes = pl.ds(pl.multiple_of(bases[j1 - 1] + c * LANES, LANES), LANES)
                piece = jnp.where(keep[j1 - 1], left, right)
                if c == 0:
                    piece = piece + field_ref[rows, lanes].astype(F32)
                field_ref[rows, lanes] = piece.astype(BF16)
        sent += fetch(
            (field_ref.at[pl.ds(at, STRIP), pl.ds(0, z.lons)],),
            (out_ref.at[0, 0, pl.ds(at, STRIP)],),
            sems.at[pl.ds(at // STRIP, 1)],
        )
    for copy in sent:
        copy.wait()


def body(z, control, row_order, row_length, vertical, amplitude, meridional, balance):
    arguments = (row_order, row_length, control, vertical, amplitude)
    made = (
        jax.ShapeDtypeStruct((z.devices, z.rows, LANES), BF16),
        jax.ShapeDtypeStruct((2 * z.sin, z.points), BF16),
        jax.ShapeDtypeStruct((2 * RADIX + SUBLANES, z.points), F32),
    )
    packets, basis, twiddle = pl.pallas_call(
        functools.partial(analysis_kernel, z),
        out_shape=made,
        in_specs=[HBM] * len(arguments),
        out_specs=(VMEM,) * len(made),
        scratch_shapes=[
            *[pltpu.SMEM(x.shape, x.dtype) for x in arguments[:2]],
            *[pltpu.VMEM(x.shape, x.dtype) for x in arguments[2:]],
            pltpu.SemaphoreType.DMA((len(arguments),)),
            pltpu.VMEM((z.levels, z.lons + LANES), F32),
            pltpu.VMEM((2 * RADIX * z.levels, z.points), BF16),
            pltpu.VMEM((2 * z.heads, z.points), F32),
            pltpu.VMEM((2 * STRIP, z.points), F32),
            pltpu.VMEM((z.waves, LANES), F32),
            pltpu.VMEM((2 * z.kaps, RADIX * LANES), F32),
        ],
        compiler_params=PARAMS,
        name="analysis",
    )(*[pltpu.with_memory_space_constraint(x, pltpu.HBM) for x in arguments])
    matrices = [row_order, *[lax.all_gather(x, "var", axis=0, tiled=True) for x in (meridional, balance)]]
    packets = lax.all_to_all(packets, ("var", "lat"), 0, 0, tiled=True)
    mix, lift = pl.pallas_call(
        functools.partial(matrices_kernel, z),
        out_shape=(
            jax.ShapeDtypeStruct((z.var, z.mixed, z.mixed), BF16),
            jax.ShapeDtypeStruct((z.var - 1, LANES, LANES), BF16),
        ),
        in_specs=[HBM] * len(matrices),
        out_specs=(VMEM, VMEM),
        scratch_shapes=[
            *[(pltpu.SMEM if x.ndim == 1 else pltpu.VMEM)(x.shape, x.dtype) for x in matrices],
            pltpu.SemaphoreType.DMA((len(matrices),)),
        ],
        compiler_params=PARAMS,
        cost_estimate=pl.CostEstimate(flops=10**8, bytes_accessed=10**6, transcendentals=0),
        name="matrices",
    )(*[pltpu.with_memory_space_constraint(x, pltpu.HBM) for x in matrices])
    balanced = pl.pallas_call(
        functools.partial(mixing_kernel, z),
        out_shape=jax.ShapeDtypeStruct((z.var, z.lat, z.rows, LANES), BF16),
        in_specs=[VMEM] * 3,
        out_specs=VMEM,
        compiler_params=PARAMS,
        name="mixing",
    )(packets.reshape(z.var, z.lat, z.rows, LANES), mix, lift)
    balanced = balanced.reshape(z.devices, z.rows, LANES)
    balanced = lax.all_to_all(balanced, ("var", "lat"), 0, 0, tiled=True)
    return pl.pallas_call(
        functools.partial(synthesis_kernel, z),
        out_shape=jax.ShapeDtypeStruct(control.shape, BF16),
        in_specs=[VMEM] * 3,
        out_specs=HBM,
        scratch_shapes=[
            pltpu.SemaphoreType.DMA((z.levels // STRIP,)),
            pltpu.VMEM((z.levels, z.lons + LANES), BF16),
            pltpu.VMEM(((2 * RADIX - 1) * z.levels, 2 * z.sin), BF16),
            pltpu.VMEM(((2 * RADIX - 1) * z.levels, z.points), F32),
        ],
        compiler_params=PARAMS,
        name="synthesis",
    )(balanced, basis, twiddle)


def solution(mesh):
    placed = (
        P("var", "lat", None, None),
        P(),
        P(),
        P("var", None, None),
        P("var", None),
        P("var", None, None),
        P("var", None, None),
    )

    def run(control, row_order, row_length, vertical, amplitude, meridional, balance):
        lat_total, var_total = mesh.shape["lat"], mesh.shape["var"]
        assert control.shape[0] == var_total and control.shape[1] == lat_total
        z = Sizes(lat_total, var_total, control.shape[2], control.shape[3], amplitude.shape[1])
        return jax.shard_map(
            functools.partial(body, z),
            mesh=mesh,
            in_specs=placed,
            out_specs=P("var", "lat", None, None),
            check_vma=False,
        )(control, row_order, row_length, vertical, amplitude, meridional, balance)

    return run
```

```python
import functools
import math

import jax
import jax.numpy as jnp
from jax import lax
from jax.experimental import pallas as pl
from jax.experimental.pallas import tpu as pltpu
from jax.sharding import PartitionSpec as P

RADIX = 4
LANES = 128
SUBLANES = 8
STRIP = 16
F32 = jnp.float32
BF16 = jnp.bfloat16

COS_POLY = (1, -19.7392044, 64.9391174, -85.4501419, 60.1676292, -25.9675999, 6.52865839)
SIN_POLY = (6.28318501, -41.3415909, 81.5999451, -76.6144714, 41.3428841, -12.4712439)

VMEM = pl.BlockSpec(memory_space=pltpu.VMEM)
HBM = pl.BlockSpec(memory_space=pltpu.HBM)
PARAMS = pltpu.CompilerParams(vmem_limit_bytes=32 * 1024 * 1024)


def iota(shape, dim):
    return lax.broadcasted_iota(jnp.int32, shape, dim)


def horner(poly, x):
    total = jnp.full_like(x, poly[-1])
    for term in poly[-2::-1]:
        total = total * x + term
    return total


def cos_sin(turns):
    turns = turns - jnp.round(turns)
    square = turns * turns
    return horner(COS_POLY, square), horner(SIN_POLY, square) * turns


def ceil_div(a, b):
    return -(-a // b)


def round_up(a, b):
    return ceil_div(a, b) * b


def dot(a, b, contract=((1,), (0,))):
    return lax.dot_general(a, b, (contract, ((), ())), preferred_element_type=F32)


class Sizes:
    def __init__(self, lat_total, var_total, levels, lons, waves):
        self.lat, self.var, self.levels, self.lons, self.waves = lat_total, var_total, levels, lons, waves
        self.devices = lat_total * var_total
        self.points = lons // RADIX
        self.tiles = self.points // LANES
        self.block = math.gcd(self.tiles, 2)
        self.kaps = waves // RADIX
        self.rows = round_up(ceil_div(waves, self.devices), SUBLANES)
        assert self.kaps % self.rows == 0 and self.points % LANES == 0 and 2 * levels == LANES and lat_total <= LANES
        self.mixed = lat_total * self.rows
        self.sin = round_up(self.kaps, LANES)
        self.heads = round_up(ceil_div(self.kaps, STRIP), SUBLANES)
        self.params = round_up(levels + lat_total, STRIP)


def own_length(order_ref, length_ref):
    slot = lax.axis_index("lat")
    row = order_ref[slot]
    return slot, row, length_ref[row]


def fetch(sources, targets, sems):
    copies = [pltpu.make_async_copy(s, t, sems.at[i]) for i, (s, t) in enumerate(zip(sources, targets))]
    for copy in copies:
        copy.start()
    return copies


def slot_matrix(z, order_ref, mer_ref):
    slot = iota((z.lat, z.lat), 0)
    row = jnp.zeros((z.lat, z.lat), jnp.int32)
    for t in range(z.lat):
        row = jnp.where(slot == t, order_ref[t], row)
    pick = (row == iota((z.lat, z.lat), 1)).astype(F32).astype(BF16)
    return dot(dot(pick, mer_ref[0]).astype(BF16), pick, ((1,), (1,)))


def tile(c):
    return slice(c * LANES, (c + 1) * LANES)


def analysis_kernel(z, *refs):
    given, made, held = refs[:7], refs[7:11], refs[11:18]
    sems, field_ref, parts_ref, heads_ref, tails_ref, scale_ref, product_ref = refs[18:]
    order_ref, length_ref, control_ref, vert_ref, amp_ref, mer_ref, bal_ref = held
    packet_ref, params_ref, basis_ref, twiddle_ref = made
    copies = fetch(given, held, sems)
    for at in (0, z.sin):
        basis_ref[at + z.kaps : at + z.sin] = jnp.zeros((z.sin - z.kaps, z.points), BF16)
    field_ref[:, z.lons :] = jnp.zeros((z.levels, LANES), F32)
    params_ref[...] = jnp.zeros(params_ref.shape, BF16)
    parts_ref[z.levels : 2 * z.levels] = jnp.zeros((z.levels, z.points), BF16)
    for copy in copies[:2]:
        copy.wait()
    slot, row, length = own_length(order_ref, length_ref)
    quarter = length // RADIX
    period = jnp.full((1, LANES), length, jnp.int32).astype(F32)
    tail = iota((STRIP, LANES), 0).astype(F32)
    head = iota((z.heads, LANES), 0).astype(F32) * STRIP
    tw_row = iota((2 * RADIX, LANES), 0)
    tw_wave = jnp.where(tw_row < RADIX, tw_row, tw_row - RADIX).astype(F32)
    fraction = jnp.full((1, LANES), quarter, jnp.int32).astype(F32)
    for c in range(z.tiles):
        points = c * LANES + iota((1, LANES), 1)
        step = points.astype(F32) / fraction
        tails_ref[:STRIP, tile(c)], tails_ref[STRIP:, tile(c)] = cos_sin(tail * step)
        head_cos, head_sin = cos_sin(head * step)
        heads_ref[: z.heads, tile(c)] = jnp.where(points < quarter, head_cos, 0.0)
        heads_ref[z.heads :, tile(c)] = jnp.where(points < quarter, head_sin, 0.0)
        tw_cos, tw_sin = cos_sin(tw_wave * (points.astype(F32) / period))
        twiddle_ref[: 2 * RADIX, tile(c)] = jnp.where(tw_row < RADIX, tw_cos, tw_sin)
        twiddle_ref[2 * RADIX :, tile(c)] = jnp.broadcast_to(period, (SUBLANES, LANES))
    for copy in copies[2:]:
        copy.wait()
    field_ref[:, : z.lons] = dot(vert_ref[0], control_ref[0, 0])
    starts = [quarter * j1 for j1 in range(1, RADIX)]
    bases = [pl.multiple_of(s // LANES * LANES, LANES) for s in starts]
    shifts = [(LANES - (s - b)) % LANES for s, b in zip(starts, bases)]
    lane = iota((STRIP, LANES), 1)
    keeps = [(lane < shift) | (shift == 0) for shift in shifts]

    def rolled(i, at, c):
        lanes = pl.ds(pl.multiple_of(bases[i] + c * LANES, LANES), LANES)
        return pltpu.roll(field_ref[at : at + STRIP, lanes], shifts[i], 1)

    before = {}
    for block in range(0, z.tiles, z.block):
        for c in range(block, block + z.block):
            tail_cos, tail_sin = tails_ref[:STRIP, tile(c)], tails_ref[STRIP:, tile(c)]
            for at in range(0, z.kaps, STRIP):
                i = at // STRIP
                head_cos, head_sin = heads_ref[i : i + 1, tile(c)], heads_ref[z.heads + i : z.heads + i + 1, tile(c)]
                basis_ref[at : at + STRIP, tile(c)] = (head_cos * tail_cos - head_sin * tail_sin).astype(BF16)
                to = slice(z.sin + at, z.sin + at + STRIP)
                basis_ref[to, tile(c)] = (head_sin * tail_cos + head_cos * tail_sin).astype(BF16)
        for at in range(0, z.levels, STRIP):
            for c in range(block, block + z.block):
                if c == 0:
                    before[at] = [rolled(i, at, 0) for i in range(RADIX - 1)]
                after = [rolled(i, at, c + 1) for i in range(RADIX - 1)]
                second, third, fourth = [jnp.where(k, a, b) for k, a, b in zip(keeps, before[at], after)]
                before[at] = after
                first = field_ref[at : at + STRIP, tile(c)]
                even, odd = first + third, second + fourth
                real, imag, turned = first - third, second - fourth, even - odd
                cos1, cos2, cos3 = [twiddle_ref[r : r + 1, tile(c)] for r in (1, 2, 3)]
                sin1, sin2, sin3 = [twiddle_ref[RADIX + r : RADIX + r + 1, tile(c)] for r in (1, 2, 3)]
                parts = (
                    (even + odd,),
                    (real * cos1 - imag * sin1, real * sin1 + imag * cos1),
                    (turned * cos2, turned * sin2),
                    (real * cos3 + imag * sin3, real * sin3 - imag * cos3),
                )
                for r, pair in enumerate(parts):
                    for half, part in enumerate(pair):
                        to = (2 * r + half) * z.levels + at
                        parts_ref[to : to + STRIP, tile(c)] = part.astype(BF16)
        lanes = slice(block * LANES, (block + z.block) * LANES)
        basis = jnp.concatenate([basis_ref[: z.kaps, lanes], basis_ref[z.sin : z.sin + z.kaps, lanes]], axis=0)
        product = dot(basis, parts_ref[:, lanes], ((1,), (1,)))
        product_ref[...] = product if block == 0 else product_ref[...] + product
    group = LANES // RADIX
    weights = 1.0 / period, 2.0 / period
    for r in range(RADIX):
        picked = iota((group, LANES), 1) == iota((group, LANES), 0) * RADIX + r
        for at in range(0, z.kaps, group):
            lanes = slice(at * RADIX, at * RADIX + LANES)
            amp = jnp.sum(jnp.where(picked, amp_ref[:, lanes], 0.0), axis=1, keepdims=True)
            wave = (at + iota((group, LANES), 0)) * RADIX + r
            weight = jnp.where(wave == 0, *weights) if at + r == 0 else weights[1]
            scale_ref[r * z.kaps + at : r * z.kaps + at + group] = jnp.where(
                wave <= (length - 1) // 2, weight * amp, 0.0
            )
    params_ref[: z.levels] = jnp.concatenate([bal_ref[0], bal_ref[0]], axis=1)
    params_ref[z.levels : z.levels + z.lat, : z.lat] = slot_matrix(z, order_ref, mer_ref).astype(BF16)
    count = z.kaps // z.rows
    sign = jnp.where(iota((1, LANES), 1) < z.levels, -1.0, 1.0).astype(F32)
    for r in range(RADIX):
        lanes = tile(r)
        for i in range(count):
            rows = slice(i * z.rows, (i + 1) * z.rows)
            from_sin = product_ref[z.kaps + i * z.rows : z.kaps + (i + 1) * z.rows, lanes]
            both = product_ref[rows, lanes] + pltpu.roll(from_sin, z.levels, 1) * sign
            scale = scale_ref[r * z.kaps + i * z.rows : r * z.kaps + (i + 1) * z.rows]
            packet_ref[r * count + i] = (both * scale).astype(BF16)
    if z.devices > RADIX * count:
        packet_ref[RADIX * count :] = jnp.zeros((z.devices - RADIX * count, z.rows, LANES), BF16)


def matrices_kernel(z, *refs):
    *given, mix_ref, bal_ref, all_ref = refs
    own = lax.axis_index("var")
    for step, ref in enumerate(given):
        all_ref[(own + step) % z.var] = ref[...]
    size = z.mixed
    to_cols = (iota((z.lat, size), 0) == iota((z.lat, size), 1) // z.rows).astype(F32).astype(BF16)
    same = iota((size, size), 0) % z.rows == iota((size, size), 1) % z.rows
    halves = iota((LANES, LANES), 0) // z.levels == iota((LANES, LANES), 1) // z.levels
    for v in range(z.var):
        meridional = all_ref[v, z.levels :].astype(F32)[: z.lat, : z.lat].astype(BF16)
        slot_cols = dot(meridional, to_cols).astype(BF16)
        mix_ref[v] = jnp.where(same, dot(to_cols, slot_cols, ((0,), (0,))), 0.0).astype(BF16)
        if v > 0:
            balance = all_ref[v, : z.levels].astype(F32)
            balance = jnp.where(halves, jnp.concatenate([balance, balance], axis=0), 0.0)
            bal_ref[v - 1] = balance.T.astype(BF16)


def mixing_kernel(z, packet_ref, mix_ref, bal_ref, out_ref):
    stream = None
    for v in range(z.var):
        coeffs = packet_ref[v].astype(F32).reshape(z.mixed, LANES).astype(BF16)
        blended = dot(mix_ref[v], coeffs)
        if v == 0:
            stream = blended.astype(BF16)
        else:
            blended = blended + dot(stream, bal_ref[v - 1])
        blended = blended.reshape(z.lat, z.rows, LANES)
        for s in range(z.lat):
            out_ref[v, s] = blended[s].astype(BF16)


def masks_kernel(z, twiddle_ref, after_ref, mask_ref):
    del after_ref
    limit = (twiddle_ref[2 * RADIX : 2 * RADIX + 1, :LANES].astype(jnp.int32) - 1) // 2
    for r in range(RADIX):
        wave = iota((z.kaps, LANES), 0) * RADIX + r
        mask_ref[:, tile(r)] = jnp.where(wave <= limit, 1.0, 0.0).astype(BF16)


def synthesis_kernel(z, spectra_ref, basis_ref, twiddle_ref, mask_ref, out_ref, sems, field_ref, lhs_ref, parts_ref):
    period = twiddle_ref[2 * RADIX :, :LANES].astype(jnp.int32)
    length = jnp.max(period)
    count = z.kaps // z.rows
    half = z.levels // 2
    kinds = 2 * RADIX - 1
    for at in (0, z.sin):
        lhs_ref[:, at + z.kaps : at + z.sin] = jnp.zeros((2 * half * kinds, z.sin - z.kaps), BF16)
    for r in range(RADIX):
        part = spectra_ref[r * count : (r + 1) * count].astype(F32).reshape(z.kaps, LANES)
        part = (part.astype(BF16) * mask_ref[:, tile(r)]).T
        for i in range(2):
            from_cos = part[i * half : (i + 1) * half]
            from_sin = part[z.levels + i * half : z.levels + (i + 1) * half]
            pairs = [(from_cos, from_sin)] if r == 0 else [(from_cos, from_sin), (-from_sin, from_cos)]
            for kind, pair in zip((2 * r - 1, 2 * r) if r else (0,), pairs):
                to = slice((i * kinds + kind) * half, (i * kinds + kind + 1) * half)
                lhs_ref[to, : z.kaps] = pair[0]
                lhs_ref[to, z.sin : z.sin + z.kaps] = pair[1]
    quarter = length // RADIX
    starts = [quarter * j1 for j1 in range(1, RADIX)]
    bases = [pl.multiple_of(s // LANES * LANES, LANES) for s in starts]
    shifts = [s - b for s, b in zip(starts, bases)]
    wide = z.points + LANES
    field_ref[:, wide:] = jnp.zeros((z.levels, z.lons + LANES - wide), BF16)
    keep = [iota((STRIP, LANES), 1) < shift for shift in shifts]
    zero = jnp.zeros((STRIP, LANES), F32)
    for i in range(2):
        rows = slice(i * kinds * half, (i + 1) * kinds * half)
        parts_ref[rows] = dot(lhs_ref[rows], basis_ref[...])
    sent = []
    for at in range(0, z.levels, STRIP):
        rows = slice(at, at + STRIP)
        first = at // half * kinds * half + at % half
        quarters = [[], [], [], []]
        for c in range(z.tiles):
            cos1, cos2, cos3 = [twiddle_ref[r : r + 1, tile(c)] for r in (1, 2, 3)]
            sin1, sin2, sin3 = [twiddle_ref[RADIX + r : RADIX + r + 1, tile(c)] for r in (1, 2, 3)]
            w0, re1, im1, re2, im2, re3, im3 = [
                parts_ref[first + kind * half : first + kind * half + STRIP, tile(c)] for kind in range(kinds)
            ]
            w2 = re2 * cos2 - im2 * sin2
            cross = (re1 * cos1 - im1 * sin1) + (re3 * cos3 - im3 * sin3)
            turn = (re1 * sin1 + im1 * cos1) - (re3 * sin3 + im3 * cos3)
            even, odd = w0 + w2, w0 - w2
            field_ref[rows, tile(c)] = (even + cross).astype(BF16)
            for j1, part in ((1, odd - turn), (2, even - cross), (3, odd + turn)):
                quarters[j1].append(pltpu.roll(part, shifts[j1 - 1], 1))
        field_ref[rows, tile(z.tiles)] = zero.astype(BF16)
        for j1 in range(1, RADIX):
            pieces = zip([zero] + quarters[j1], quarters[j1] + [zero])
            for c, (left, right) in enumerate(pieces):
                lanes = pl.ds(pl.multiple_of(bases[j1 - 1] + c * LANES, LANES), LANES)
                piece = jnp.where(keep[j1 - 1], left, right)
                if c == 0:
                    piece = piece + field_ref[rows, lanes].astype(F32)
                field_ref[rows, lanes] = piece.astype(BF16)
        sent += fetch(
            (field_ref.at[pl.ds(at, STRIP), pl.ds(0, z.lons)],),
            (out_ref.at[0, 0, pl.ds(at, STRIP)],),
            sems.at[pl.ds(at // STRIP, 1)],
        )
    for copy in sent:
        copy.wait()


def body(z, control, row_order, row_length, vertical, amplitude, meridional, balance):
    arguments = (row_order, row_length, control, vertical, amplitude, meridional, balance)
    made = (
        jax.ShapeDtypeStruct((z.devices, z.rows, LANES), BF16),
        jax.ShapeDtypeStruct((z.params, LANES), BF16),
        jax.ShapeDtypeStruct((2 * z.sin, z.points), BF16),
        jax.ShapeDtypeStruct((2 * RADIX + SUBLANES, z.points), F32),
    )
    packets, params, basis, twiddle = pl.pallas_call(
        functools.partial(analysis_kernel, z),
        out_shape=made,
        in_specs=[HBM] * len(arguments),
        out_specs=(VMEM,) * len(made),
        scratch_shapes=[
            *[pltpu.SMEM(x.shape, x.dtype) for x in arguments[:2]],
            *[pltpu.VMEM(x.shape, x.dtype) for x in arguments[2:]],
            pltpu.SemaphoreType.DMA((len(arguments),)),
            pltpu.VMEM((z.levels, z.lons + LANES), F32),
            pltpu.VMEM((2 * RADIX * z.levels, z.points), BF16),
            pltpu.VMEM((2 * z.heads, z.points), F32),
            pltpu.VMEM((2 * STRIP, z.points), F32),
            pltpu.VMEM((z.waves, LANES), F32),
            pltpu.VMEM((2 * z.kaps, RADIX * LANES), F32),
        ],
        compiler_params=PARAMS,
        name="analysis",
    )(*[pltpu.with_memory_space_constraint(x, pltpu.HBM) for x in arguments])
    given = [params]
    for step in range(1, z.var):
        given.append(lax.ppermute(params, "var", [((i + step) % z.var, i) for i in range(z.var)]))
    packets = lax.all_to_all(packets, ("var", "lat"), 0, 0, tiled=True)
    mix, lift = pl.pallas_call(
        functools.partial(matrices_kernel, z),
        out_shape=(
            jax.ShapeDtypeStruct((z.var, z.mixed, z.mixed), BF16),
            jax.ShapeDtypeStruct((z.var - 1, LANES, LANES), BF16),
        ),
        in_specs=[VMEM] * z.var,
        out_specs=(VMEM, VMEM),
        scratch_shapes=[pltpu.VMEM((z.var, z.params, LANES), BF16)],
        compiler_params=PARAMS,
        cost_estimate=pl.CostEstimate(flops=10**8, bytes_accessed=10**6, transcendentals=0),
        name="matrices",
    )(*given)
    balanced = pl.pallas_call(
        functools.partial(mixing_kernel, z),
        out_shape=jax.ShapeDtypeStruct((z.var, z.lat, z.rows, LANES), BF16),
        in_specs=[VMEM] * 3,
        out_specs=VMEM,
        compiler_params=PARAMS,
        name="mixing",
    )(packets.reshape(z.var, z.lat, z.rows, LANES), mix, lift)
    balanced = balanced.reshape(z.devices, z.rows, LANES)
    masks = pl.pallas_call(
        functools.partial(masks_kernel, z),
        out_shape=jax.ShapeDtypeStruct((z.kaps, RADIX * LANES), BF16),
        in_specs=[VMEM, pl.BlockSpec(memory_space=pl.ANY)],
        out_specs=VMEM,
        compiler_params=PARAMS,
        cost_estimate=pl.CostEstimate(flops=10**9, bytes_accessed=10**6, transcendentals=0),
        name="masks",
    )(twiddle, balanced)
    balanced = lax.all_to_all(balanced, ("var", "lat"), 0, 0, tiled=True)
    return pl.pallas_call(
        functools.partial(synthesis_kernel, z),
        out_shape=jax.ShapeDtypeStruct(control.shape, BF16),
        in_specs=[VMEM] * 4,
        out_specs=HBM,
        scratch_shapes=[
            pltpu.SemaphoreType.DMA((z.levels // STRIP,)),
            pltpu.VMEM((z.levels, z.lons + LANES), BF16),
            pltpu.VMEM(((2 * RADIX - 1) * z.levels, 2 * z.sin), BF16),
            pltpu.VMEM(((2 * RADIX - 1) * z.levels, z.points), F32),
        ],
        compiler_params=PARAMS,
        name="synthesis",
    )(balanced, basis, twiddle, masks)


def solution(mesh):
    placed = (
        P("var", "lat", None, None),
        P(),
        P(),
        P("var", None, None),
        P("var", None),
        P("var", None, None),
        P("var", None, None),
    )

    def run(control, row_order, row_length, vertical, amplitude, meridional, balance):
        lat_total, var_total = mesh.shape["lat"], mesh.shape["var"]
        assert control.shape[0] == var_total and control.shape[1] == lat_total
        z = Sizes(lat_total, var_total, control.shape[2], control.shape[3], amplitude.shape[1])
        return jax.shard_map(
            functools.partial(body, z),
            mesh=mesh,
            in_specs=placed,
            out_specs=P("var", "lat", None, None),
            check_vma=False,
        )(control, row_order, row_length, vertical, amplitude, meridional, balance)

    return run
```

```python
import functools
import math

import jax
import jax.numpy as jnp
from jax import lax
from jax.experimental import pallas as pl
from jax.experimental.pallas import tpu as pltpu
from jax.sharding import PartitionSpec as P

RADIX = 4
LANES = 128
SUBLANES = 8
STRIP = 16
F32 = jnp.float32
BF16 = jnp.bfloat16

COS_POLY = (1, -19.7392044, 64.9391174, -85.4501419, 60.1676292, -25.9675999, 6.52865839)
SIN_POLY = (6.28318501, -41.3415909, 81.5999451, -76.6144714, 41.3428841, -12.4712439)

VMEM = pl.BlockSpec(memory_space=pltpu.VMEM)
HBM = pl.BlockSpec(memory_space=pltpu.HBM)
PARAMS = pltpu.CompilerParams(vmem_limit_bytes=32 * 1024 * 1024)


def iota(shape, dim):
    return lax.broadcasted_iota(jnp.int32, shape, dim)


def horner(poly, x):
    total = jnp.full_like(x, poly[-1])
    for term in poly[-2::-1]:
        total = total * x + term
    return total


def cos_sin(turns):
    turns = turns - jnp.round(turns)
    square = turns * turns
    return horner(COS_POLY, square), horner(SIN_POLY, square) * turns


def ceil_div(a, b):
    return -(-a // b)


def round_up(a, b):
    return ceil_div(a, b) * b


def dot(a, b, contract=((1,), (0,))):
    return lax.dot_general(a, b, (contract, ((), ())), preferred_element_type=F32)


class Sizes:
    def __init__(self, lat_total, var_total, levels, lons, waves):
        self.lat, self.var, self.levels, self.lons, self.waves = lat_total, var_total, levels, lons, waves
        self.devices = lat_total * var_total
        self.slots = [(lat_total // 4 + slot) % lat_total for slot in range(lat_total)]
        self.points = lons // RADIX
        self.tiles = self.points // LANES
        self.block = math.gcd(self.tiles, 2)
        self.kaps = waves // RADIX
        self.rows = round_up(ceil_div(waves, self.devices), SUBLANES)
        assert self.kaps % self.rows == 0 and self.points % LANES == 0 and 2 * levels == LANES and lat_total <= LANES
        self.mixed = lat_total * self.rows
        self.sin = round_up(self.kaps, LANES)
        self.heads = round_up(ceil_div(self.kaps, STRIP), SUBLANES)
        self.params = round_up(levels + lat_total, STRIP)


def own_length(order_ref, length_ref):
    slot = lax.axis_index("lat")
    row = order_ref[slot]
    return slot, row, length_ref[row]


def fetch(sources, targets, sems):
    copies = [pltpu.make_async_copy(s, t, sems.at[i]) for i, (s, t) in enumerate(zip(sources, targets))]
    for copy in copies:
        copy.start()
    return copies


def slot_matrix(z, order_ref, mer_ref):
    slot = iota((z.lat, z.lat), 0)
    row = jnp.zeros((z.lat, z.lat), jnp.int32)
    for t in range(z.lat):
        row = jnp.where(slot == t, order_ref[z.slots[t]], row)
    pick = (row == iota((z.lat, z.lat), 1)).astype(F32).astype(BF16)
    return dot(dot(pick, mer_ref[0]).astype(BF16), pick, ((1,), (1,)))


def tile(c):
    return slice(c * LANES, (c + 1) * LANES)


def analysis_kernel(z, *refs):
    given, made, held = refs[:7], refs[7:11], refs[11:18]
    sems, field_ref, parts_ref, heads_ref, tails_ref, scale_ref, product_ref = refs[18:]
    order_ref, length_ref, control_ref, vert_ref, amp_ref, mer_ref, bal_ref = held
    packet_ref, params_ref, basis_ref, twiddle_ref = made
    copies = fetch(given, held, sems)
    for at in (0, z.sin):
        basis_ref[at + z.kaps : at + z.sin] = jnp.zeros((z.sin - z.kaps, z.points), BF16)
    field_ref[:, z.lons :] = jnp.zeros((z.levels, LANES), F32)
    params_ref[...] = jnp.zeros(params_ref.shape, BF16)
    parts_ref[z.levels : 2 * z.levels] = jnp.zeros((z.levels, z.points), BF16)
    for copy in copies[:2]:
        copy.wait()
    slot, row, length = own_length(order_ref, length_ref)
    quarter = length // RADIX
    period = jnp.full((1, LANES), length, jnp.int32).astype(F32)
    tail = iota((STRIP, LANES), 0).astype(F32)
    head = iota((z.heads, LANES), 0).astype(F32) * STRIP
    tw_row = iota((2 * RADIX, LANES), 0)
    tw_wave = jnp.where(tw_row < RADIX, tw_row, tw_row - RADIX).astype(F32)
    fraction = jnp.full((1, LANES), quarter, jnp.int32).astype(F32)
    for c in range(z.tiles):
        points = c * LANES + iota((1, LANES), 1)
        step = points.astype(F32) / fraction
        tails_ref[:STRIP, tile(c)], tails_ref[STRIP:, tile(c)] = cos_sin(tail * step)
        head_cos, head_sin = cos_sin(head * step)
        heads_ref[: z.heads, tile(c)] = jnp.where(points < quarter, head_cos, 0.0)
        heads_ref[z.heads :, tile(c)] = jnp.where(points < quarter, head_sin, 0.0)
        tw_cos, tw_sin = cos_sin(tw_wave * (points.astype(F32) / period))
        twiddle_ref[: 2 * RADIX, tile(c)] = jnp.where(tw_row < RADIX, tw_cos, tw_sin)
        twiddle_ref[2 * RADIX :, tile(c)] = jnp.broadcast_to(period, (SUBLANES, LANES))
    for copy in copies[2:]:
        copy.wait()
    field_ref[:, : z.lons] = dot(vert_ref[0], control_ref[0, 0])
    starts = [quarter * j1 for j1 in range(1, RADIX)]
    bases = [pl.multiple_of(s // LANES * LANES, LANES) for s in starts]
    shifts = [(LANES - (s - b)) % LANES for s, b in zip(starts, bases)]
    lane = iota((STRIP, LANES), 1)
    keeps = [(lane < shift) | (shift == 0) for shift in shifts]

    def rolled(i, at, c):
        lanes = pl.ds(pl.multiple_of(bases[i] + c * LANES, LANES), LANES)
        return pltpu.roll(field_ref[at : at + STRIP, lanes], shifts[i], 1)

    before = {}
    for block in range(0, z.tiles, z.block):
        for c in range(block, block + z.block):
            tail_cos, tail_sin = tails_ref[:STRIP, tile(c)], tails_ref[STRIP:, tile(c)]
            for at in range(0, z.kaps, STRIP):
                i = at // STRIP
                head_cos, head_sin = heads_ref[i : i + 1, tile(c)], heads_ref[z.heads + i : z.heads + i + 1, tile(c)]
                basis_ref[at : at + STRIP, tile(c)] = (head_cos * tail_cos - head_sin * tail_sin).astype(BF16)
                to = slice(z.sin + at, z.sin + at + STRIP)
                basis_ref[to, tile(c)] = (head_sin * tail_cos + head_cos * tail_sin).astype(BF16)
        for at in range(0, z.levels, STRIP):
            for c in range(block, block + z.block):
                if c == 0:
                    before[at] = [rolled(i, at, 0) for i in range(RADIX - 1)]
                after = [rolled(i, at, c + 1) for i in range(RADIX - 1)]
                second, third, fourth = [jnp.where(k, a, b) for k, a, b in zip(keeps, before[at], after)]
                before[at] = after
                first = field_ref[at : at + STRIP, tile(c)]
                even, odd = first + third, second + fourth
                real, imag, turned = first - third, second - fourth, even - odd
                cos1, cos2, cos3 = [twiddle_ref[r : r + 1, tile(c)] for r in (1, 2, 3)]
                sin1, sin2, sin3 = [twiddle_ref[RADIX + r : RADIX + r + 1, tile(c)] for r in (1, 2, 3)]
                parts = (
                    (even + odd,),
                    (real * cos1 - imag * sin1, real * sin1 + imag * cos1),
                    (turned * cos2, turned * sin2),
                    (real * cos3 + imag * sin3, real * sin3 - imag * cos3),
                )
                for r, pair in enumerate(parts):
                    for half, part in enumerate(pair):
                        to = (2 * r + half) * z.levels + at
                        parts_ref[to : to + STRIP, tile(c)] = part.astype(BF16)
        lanes = slice(block * LANES, (block + z.block) * LANES)
        basis = jnp.concatenate([basis_ref[: z.kaps, lanes], basis_ref[z.sin : z.sin + z.kaps, lanes]], axis=0)
        product = dot(basis, parts_ref[:, lanes], ((1,), (1,)))
        product_ref[...] = product if block == 0 else product_ref[...] + product
    group = LANES // RADIX
    weights = 1.0 / period, 2.0 / period
    for r in range(RADIX):
        picked = iota((group, LANES), 1) == iota((group, LANES), 0) * RADIX + r
        for at in range(0, z.kaps, group):
            lanes = slice(at * RADIX, at * RADIX + LANES)
            amp = jnp.sum(jnp.where(picked, amp_ref[:, lanes], 0.0), axis=1, keepdims=True)
            wave = (at + iota((group, LANES), 0)) * RADIX + r
            weight = jnp.where(wave == 0, *weights) if at + r == 0 else weights[1]
            scale_ref[r * z.kaps + at : r * z.kaps + at + group] = jnp.where(
                wave <= (length - 1) // 2, weight * amp, 0.0
            )
    params_ref[: z.levels] = jnp.concatenate([bal_ref[0], bal_ref[0]], axis=1)
    params_ref[z.levels : z.levels + z.lat, : z.lat] = slot_matrix(z, order_ref, mer_ref).astype(BF16)
    count = z.kaps // z.rows
    sign = jnp.where(iota((1, LANES), 1) < z.levels, -1.0, 1.0).astype(F32)
    for r in range(RADIX):
        lanes = tile(r)
        for i in range(count):
            rows = slice(i * z.rows, (i + 1) * z.rows)
            from_sin = product_ref[z.kaps + i * z.rows : z.kaps + (i + 1) * z.rows, lanes]
            both = product_ref[rows, lanes] + pltpu.roll(from_sin, z.levels, 1) * sign
            scale = scale_ref[r * z.kaps + i * z.rows : r * z.kaps + (i + 1) * z.rows]
            packet_ref[r * count + i] = (both * scale).astype(BF16)
    if z.devices > RADIX * count:
        packet_ref[RADIX * count :] = jnp.zeros((z.devices - RADIX * count, z.rows, LANES), BF16)


def matrices_kernel(z, *refs):
    *given, mix_ref, bal_ref, all_ref = refs
    own = lax.axis_index("var")
    for step, ref in enumerate(given):
        all_ref[(own + step) % z.var] = ref[...]
    size = z.mixed
    to_cols = (iota((z.lat, size), 0) == iota((z.lat, size), 1) // z.rows).astype(F32).astype(BF16)
    same = iota((size, size), 0) % z.rows == iota((size, size), 1) % z.rows
    halves = iota((LANES, LANES), 0) // z.levels == iota((LANES, LANES), 1) // z.levels
    for v in range(z.var):
        meridional = all_ref[v, z.levels :].astype(F32)[: z.lat, : z.lat].astype(BF16)
        slot_cols = dot(meridional, to_cols).astype(BF16)
        mix_ref[v] = jnp.where(same, dot(to_cols, slot_cols, ((0,), (0,))), 0.0).astype(BF16)
        if v > 0:
            balance = all_ref[v, : z.levels].astype(F32)
            balance = jnp.where(halves, jnp.concatenate([balance, balance], axis=0), 0.0)
            bal_ref[v - 1] = balance.T.astype(BF16)


def mixing_kernel(z, packet_ref, mix_ref, bal_ref, out_ref):
    stream = None
    for v in range(z.var):
        coeffs = packet_ref[v].astype(F32).reshape(z.mixed, LANES).astype(BF16)
        blended = dot(mix_ref[v], coeffs)
        if v == 0:
            stream = blended.astype(BF16)
        else:
            blended = blended + dot(stream, bal_ref[v - 1])
        blended = blended.reshape(z.lat, z.rows, LANES)
        for s in range(z.lat):
            out_ref[v, s] = blended[s].astype(BF16)


def synthesis_kernel(z, spectra_ref, basis_ref, twiddle_ref, out_ref, sems, field_ref, lhs_ref, parts_ref):
    period = twiddle_ref[2 * RADIX :, :LANES].astype(jnp.int32)
    length = jnp.max(period)
    kap = iota((z.kaps, LANES), 0)
    count = z.kaps // z.rows
    half = z.levels // 2
    kinds = 2 * RADIX - 1
    for at in (0, z.sin):
        lhs_ref[:, at + z.kaps : at + z.sin] = jnp.zeros((2 * half * kinds, z.sin - z.kaps), BF16)
    for r in range(RADIX):
        part = spectra_ref[r * count : (r + 1) * count].astype(F32).reshape(z.kaps, LANES)
        part = jnp.where(kap * RADIX + r <= (period[0:1] - 1) // 2, part, 0.0)
        part = part.astype(BF16).T
        for i in range(2):
            from_cos = part[i * half : (i + 1) * half]
            from_sin = part[z.levels + i * half : z.levels + (i + 1) * half]
            pairs = [(from_cos, from_sin)] if r == 0 else [(from_cos, from_sin), (-from_sin, from_cos)]
            for kind, pair in zip((2 * r - 1, 2 * r) if r else (0,), pairs):
                to = slice((i * kinds + kind) * half, (i * kinds + kind + 1) * half)
                lhs_ref[to, : z.kaps] = pair[0]
                lhs_ref[to, z.sin : z.sin + z.kaps] = pair[1]
    quarter = length // RADIX
    starts = [quarter * j1 for j1 in range(1, RADIX)]
    bases = [pl.multiple_of(s // LANES * LANES, LANES) for s in starts]
    shifts = [s - b for s, b in zip(starts, bases)]
    wide = z.points + LANES
    field_ref[:, wide:] = jnp.zeros((z.levels, z.lons + LANES - wide), BF16)
    keep = [iota((STRIP, LANES), 1) < shift for shift in shifts]
    zero = jnp.zeros((STRIP, LANES), F32)
    for i in range(2):
        rows = slice(i * kinds * half, (i + 1) * kinds * half)
        parts_ref[rows] = dot(lhs_ref[rows], basis_ref[...])
    sent = []
    for at in range(0, z.levels, STRIP):
        rows = slice(at, at + STRIP)
        first = at // half * kinds * half + at % half
        quarters = [[], [], [], []]
        for c in range(z.tiles):
            cos1, cos2, cos3 = [twiddle_ref[r : r + 1, tile(c)] for r in (1, 2, 3)]
            sin1, sin2, sin3 = [twiddle_ref[RADIX + r : RADIX + r + 1, tile(c)] for r in (1, 2, 3)]
            w0, re1, im1, re2, im2, re3, im3 = [
                parts_ref[first + kind * half : first + kind * half + STRIP, tile(c)] for kind in range(kinds)
            ]
            w2 = re2 * cos2 - im2 * sin2
            cross = (re1 * cos1 - im1 * sin1) + (re3 * cos3 - im3 * sin3)
            turn = (re1 * sin1 + im1 * cos1) - (re3 * sin3 + im3 * cos3)
            even, odd = w0 + w2, w0 - w2
            field_ref[rows, tile(c)] = (even + cross).astype(BF16)
            for j1, part in ((1, odd - turn), (2, even - cross), (3, odd + turn)):
                quarters[j1].append(pltpu.roll(part, shifts[j1 - 1], 1))
        field_ref[rows, tile(z.tiles)] = zero.astype(BF16)
        for j1 in range(1, RADIX):
            pieces = zip([zero] + quarters[j1], quarters[j1] + [zero])
            for c, (left, right) in enumerate(pieces):
                lanes = pl.ds(pl.multiple_of(bases[j1 - 1] + c * LANES, LANES), LANES)
                piece = jnp.where(keep[j1 - 1], left, right)
                if c == 0:
                    piece = piece + field_ref[rows, lanes].astype(F32)
                field_ref[rows, lanes] = piece.astype(BF16)
        sent += fetch(
            (field_ref.at[pl.ds(at, STRIP), pl.ds(0, z.lons)],),
            (out_ref.at[0, 0, pl.ds(at, STRIP)],),
            sems.at[pl.ds(at // STRIP, 1)],
        )
    for copy in sent:
        copy.wait()


def exchange(z, chunks):
    peers = [v * z.lat + slot for v in range(z.var) for slot in z.slots]
    return lax.all_to_all(chunks, ("var", "lat"), 0, 0, axis_index_groups=[peers], tiled=True)


def body(z, control, row_order, row_length, vertical, amplitude, meridional, balance):
    arguments = (row_order, row_length, control, vertical, amplitude, meridional, balance)
    made = (
        jax.ShapeDtypeStruct((z.devices, z.rows, LANES), BF16),
        jax.ShapeDtypeStruct((z.params, LANES), BF16),
        jax.ShapeDtypeStruct((2 * z.sin, z.points), BF16),
        jax.ShapeDtypeStruct((2 * RADIX + SUBLANES, z.points), F32),
    )
    packets, params, basis, twiddle = pl.pallas_call(
        functools.partial(analysis_kernel, z),
        out_shape=made,
        in_specs=[HBM] * len(arguments),
        out_specs=(VMEM,) * len(made),
        scratch_shapes=[
            *[pltpu.SMEM(x.shape, x.dtype) for x in arguments[:2]],
            *[pltpu.VMEM(x.shape, x.dtype) for x in arguments[2:]],
            pltpu.SemaphoreType.DMA((len(arguments),)),
            pltpu.VMEM((z.levels, z.lons + LANES), F32),
            pltpu.VMEM((2 * RADIX * z.levels, z.points), BF16),
            pltpu.VMEM((2 * z.heads, z.points), F32),
            pltpu.VMEM((2 * STRIP, z.points), F32),
            pltpu.VMEM((z.waves, LANES), F32),
            pltpu.VMEM((2 * z.kaps, RADIX * LANES), F32),
        ],
        compiler_params=PARAMS,
        name="analysis",
    )(*[pltpu.with_memory_space_constraint(x, pltpu.HBM) for x in arguments])
    given = [params]
    for step in range(1, z.var):
        given.append(lax.ppermute(params, "var", [((i + step) % z.var, i) for i in range(z.var)]))
    packets = exchange(z, packets)
    mix, lift = pl.pallas_call(
        functools.partial(matrices_kernel, z),
        out_shape=(
            jax.ShapeDtypeStruct((z.var, z.mixed, z.mixed), BF16),
            jax.ShapeDtypeStruct((z.var - 1, LANES, LANES), BF16),
        ),
        in_specs=[VMEM] * z.var,
        out_specs=(VMEM, VMEM),
        scratch_shapes=[pltpu.VMEM((z.var, z.params, LANES), BF16)],
        compiler_params=PARAMS,
        cost_estimate=pl.CostEstimate(flops=10**8, bytes_accessed=10**6, transcendentals=0),
        name="matrices",
    )(*given)
    balanced = pl.pallas_call(
        functools.partial(mixing_kernel, z),
        out_shape=jax.ShapeDtypeStruct((z.var, z.lat, z.rows, LANES), BF16),
        in_specs=[VMEM] * 3,
        out_specs=VMEM,
        compiler_params=PARAMS,
        name="mixing",
    )(packets.reshape(z.var, z.lat, z.rows, LANES), mix, lift)
    balanced = balanced.reshape(z.devices, z.rows, LANES)
    balanced = exchange(z, balanced)
    return pl.pallas_call(
        functools.partial(synthesis_kernel, z),
        out_shape=jax.ShapeDtypeStruct(control.shape, BF16),
        in_specs=[VMEM] * 3,
        out_specs=HBM,
        scratch_shapes=[
            pltpu.SemaphoreType.DMA((z.levels // STRIP,)),
            pltpu.VMEM((z.levels, z.lons + LANES), BF16),
            pltpu.VMEM(((2 * RADIX - 1) * z.levels, 2 * z.sin), BF16),
            pltpu.VMEM(((2 * RADIX - 1) * z.levels, z.points), F32),
        ],
        compiler_params=PARAMS,
        name="synthesis",
    )(balanced, basis, twiddle)


def solution(mesh):
    placed = (
        P("var", "lat", None, None),
        P(),
        P(),
        P("var", None, None),
        P("var", None),
        P("var", None, None),
        P("var", None, None),
    )

    def run(control, row_order, row_length, vertical, amplitude, meridional, balance):
        lat_total, var_total = mesh.shape["lat"], mesh.shape["var"]
        assert control.shape[0] == var_total and control.shape[1] == lat_total
        z = Sizes(lat_total, var_total, control.shape[2], control.shape[3], amplitude.shape[1])
        return jax.shard_map(
            functools.partial(body, z),
            mesh=mesh,
            in_specs=placed,
            out_specs=P("var", "lat", None, None),
            check_vma=False,
        )(control, row_order, row_length, vertical, amplitude, meridional, balance)

    return run
```

```python
import functools
import math

import jax
import jax.numpy as jnp
from jax import lax
from jax.experimental import pallas as pl
from jax.experimental.pallas import tpu as pltpu
from jax.sharding import PartitionSpec as P

RADIX = 4
LANES = 128
SUBLANES = 8
STRIP = 16
F32 = jnp.float32
BF16 = jnp.bfloat16

COS_POLY = (1, -19.7392044, 64.9391174, -85.4501419, 60.1676292, -25.9675999, 6.52865839)
SIN_POLY = (6.28318501, -41.3415909, 81.5999451, -76.6144714, 41.3428841, -12.4712439)

VMEM = pl.BlockSpec(memory_space=pltpu.VMEM)
HBM = pl.BlockSpec(memory_space=pltpu.HBM)
PARAMS = pltpu.CompilerParams(vmem_limit_bytes=32 * 1024 * 1024)


def iota(shape, dim):
    return lax.broadcasted_iota(jnp.int32, shape, dim)


def horner(poly, x):
    total = jnp.full_like(x, poly[-1])
    for term in poly[-2::-1]:
        total = total * x + term
    return total


def cos_sin(turns):
    turns = turns - jnp.round(turns)
    square = turns * turns
    return horner(COS_POLY, square), horner(SIN_POLY, square) * turns


def ceil_div(a, b):
    return -(-a // b)


def round_up(a, b):
    return ceil_div(a, b) * b


def dot(a, b, contract=((1,), (0,))):
    return lax.dot_general(a, b, (contract, ((), ())), preferred_element_type=F32)


class Sizes:
    def __init__(self, lat_total, var_total, levels, lons, waves):
        self.lat, self.var, self.levels, self.lons, self.waves = lat_total, var_total, levels, lons, waves
        self.devices = lat_total * var_total
        self.points = lons // RADIX
        self.tiles = self.points // LANES
        self.block = math.gcd(self.tiles, 2)
        self.kaps = waves // RADIX
        self.rows = round_up(ceil_div(waves, self.devices), SUBLANES)
        self.mixed = lat_total * self.rows
        assert self.kaps % (3 * STRIP) == 0 and self.mixed % STRIP == 0 and self.points % LANES == 0
        assert 2 * levels == LANES and lat_total <= LANES
        self.sin = round_up(self.kaps, LANES)
        self.heads = round_up(ceil_div(self.kaps, STRIP), SUBLANES)
        self.params = round_up(levels + lat_total, STRIP)


def own_length(order_ref, length_ref):
    slot = lax.axis_index("lat")
    row = order_ref[slot]
    return slot, row, length_ref[row]


def fetch(sources, targets, sems):
    copies = [pltpu.make_async_copy(s, t, sems.at[i]) for i, (s, t) in enumerate(zip(sources, targets))]
    for copy in copies:
        copy.start()
    return copies


def slot_matrix(z, order_ref, mer_ref):
    slot = iota((z.lat, z.lat), 0)
    row = jnp.zeros((z.lat, z.lat), jnp.int32)
    for t in range(z.lat):
        row = jnp.where(slot == t, order_ref[t], row)
    pick = (row == iota((z.lat, z.lat), 1)).astype(F32).astype(BF16)
    return dot(dot(pick, mer_ref[0]).astype(BF16), pick, ((1,), (1,)))


def tile(c):
    return slice(c * LANES, (c + 1) * LANES)


def analysis_kernel(z, *refs):
    given, made, held = refs[:7], refs[7:11], refs[11:18]
    sems, field_ref, parts_ref, heads_ref, tails_ref, scale_ref, product_ref = refs[18:]
    order_ref, length_ref, control_ref, vert_ref, amp_ref, mer_ref, bal_ref = held
    packet_ref, params_ref, basis_ref, twiddle_ref = made
    copies = fetch(given, held, sems)
    for at in (0, z.sin):
        basis_ref[at + z.kaps : at + z.sin] = jnp.zeros((z.sin - z.kaps, z.points), BF16)
    field_ref[:, z.lons :] = jnp.zeros((z.levels, LANES), F32)
    params_ref[...] = jnp.zeros(params_ref.shape, BF16)
    parts_ref[z.levels : 2 * z.levels] = jnp.zeros((z.levels, z.points), BF16)
    for copy in copies[:2]:
        copy.wait()
    slot, row, length = own_length(order_ref, length_ref)
    quarter = length // RADIX
    period = jnp.full((1, LANES), length, jnp.int32).astype(F32)
    tail = iota((STRIP, LANES), 0).astype(F32)
    head = iota((z.heads, LANES), 0).astype(F32) * STRIP
    tw_row = iota((2 * RADIX, LANES), 0)
    tw_wave = jnp.where(tw_row < RADIX, tw_row, tw_row - RADIX).astype(F32)
    fraction = jnp.full((1, LANES), quarter, jnp.int32).astype(F32)
    for c in range(z.tiles):
        points = c * LANES + iota((1, LANES), 1)
        step = points.astype(F32) / fraction
        tails_ref[:STRIP, tile(c)], tails_ref[STRIP:, tile(c)] = cos_sin(tail * step)
        head_cos, head_sin = cos_sin(head * step)
        heads_ref[: z.heads, tile(c)] = jnp.where(points < quarter, head_cos, 0.0)
        heads_ref[z.heads :, tile(c)] = jnp.where(points < quarter, head_sin, 0.0)
        tw_cos, tw_sin = cos_sin(tw_wave * (points.astype(F32) / period))
        twiddle_ref[: 2 * RADIX, tile(c)] = jnp.where(tw_row < RADIX, tw_cos, tw_sin)
        twiddle_ref[2 * RADIX :, tile(c)] = jnp.broadcast_to(period, (SUBLANES, LANES))
    for copy in copies[2:]:
        copy.wait()
    field_ref[:, : z.lons] = dot(vert_ref[0], control_ref[0, 0])
    starts = [quarter * j1 for j1 in range(1, RADIX)]
    bases = [pl.multiple_of(s // LANES * LANES, LANES) for s in starts]
    shifts = [(LANES - (s - b)) % LANES for s, b in zip(starts, bases)]
    lane = iota((STRIP, LANES), 1)
    keeps = [(lane < shift) | (shift == 0) for shift in shifts]

    def rolled(i, at, c):
        lanes = pl.ds(pl.multiple_of(bases[i] + c * LANES, LANES), LANES)
        return pltpu.roll(field_ref[at : at + STRIP, lanes], shifts[i], 1)

    before = {}
    for block in range(0, z.tiles, z.block):
        for c in range(block, block + z.block):
            tail_cos, tail_sin = tails_ref[:STRIP, tile(c)], tails_ref[STRIP:, tile(c)]
            for at in range(0, z.kaps, STRIP):
                i = at // STRIP
                head_cos, head_sin = heads_ref[i : i + 1, tile(c)], heads_ref[z.heads + i : z.heads + i + 1, tile(c)]
                basis_ref[at : at + STRIP, tile(c)] = (head_cos * tail_cos - head_sin * tail_sin).astype(BF16)
                to = slice(z.sin + at, z.sin + at + STRIP)
                basis_ref[to, tile(c)] = (head_sin * tail_cos + head_cos * tail_sin).astype(BF16)
        for at in range(0, z.levels, STRIP):
            for c in range(block, block + z.block):
                if c == 0:
                    before[at] = [rolled(i, at, 0) for i in range(RADIX - 1)]
                after = [rolled(i, at, c + 1) for i in range(RADIX - 1)]
                second, third, fourth = [jnp.where(k, a, b) for k, a, b in zip(keeps, before[at], after)]
                before[at] = after
                first = field_ref[at : at + STRIP, tile(c)]
                even, odd = first + third, second + fourth
                real, imag, turned = first - third, second - fourth, even - odd
                cos1, cos2, cos3 = [twiddle_ref[r : r + 1, tile(c)] for r in (1, 2, 3)]
                sin1, sin2, sin3 = [twiddle_ref[RADIX + r : RADIX + r + 1, tile(c)] for r in (1, 2, 3)]
                parts = (
                    (even + odd,),
                    (real * cos1 - imag * sin1, real * sin1 + imag * cos1),
                    (turned * cos2, turned * sin2),
                    (real * cos3 + imag * sin3, real * sin3 - imag * cos3),
                )
                for r, pair in enumerate(parts):
                    for half, part in enumerate(pair):
                        to = (2 * r + half) * z.levels + at
                        parts_ref[to : to + STRIP, tile(c)] = part.astype(BF16)
        lanes = slice(block * LANES, (block + z.block) * LANES)
        basis = jnp.concatenate([basis_ref[: z.kaps, lanes], basis_ref[z.sin : z.sin + z.kaps, lanes]], axis=0)
        product = dot(basis, parts_ref[:, lanes], ((1,), (1,)))
        product_ref[...] = product if block == 0 else product_ref[...] + product
    group = LANES // RADIX
    weights = 1.0 / period, 2.0 / period
    for r in range(RADIX):
        picked = iota((group, LANES), 1) == iota((group, LANES), 0) * RADIX + r
        for at in range(0, z.kaps, group):
            lanes = slice(at * RADIX, at * RADIX + LANES)
            amp = jnp.sum(jnp.where(picked, amp_ref[:, lanes], 0.0), axis=1, keepdims=True)
            wave = (at + iota((group, LANES), 0)) * RADIX + r
            weight = jnp.where(wave == 0, *weights) if at + r == 0 else weights[1]
            scale_ref[r * z.kaps + at : r * z.kaps + at + group] = jnp.where(
                wave <= (length - 1) // 2, weight * amp, 0.0
            )
    params_ref[: z.levels] = jnp.concatenate([bal_ref[0], bal_ref[0]], axis=1)
    params_ref[z.levels : z.levels + z.lat, : z.lat] = slot_matrix(z, order_ref, mer_ref).astype(BF16)
    sign = jnp.where(iota((1, LANES), 1) < z.levels, -1.0, 1.0).astype(F32)
    for r in range(RADIX):
        for at in range(0, z.kaps, 3 * STRIP):
            rows = slice(at, at + 3 * STRIP)
            from_sin = product_ref[z.kaps + at : z.kaps + at + 3 * STRIP, tile(r)]
            both = product_ref[rows, tile(r)] + pltpu.roll(from_sin, z.levels, 1) * sign
            to = slice(r * z.kaps + at, r * z.kaps + at + 3 * STRIP)
            packet_ref[to] = (both * scale_ref[to]).astype(BF16)
    rest = z.devices * z.rows - z.waves
    if rest:
        packet_ref[z.waves :] = jnp.zeros((rest, LANES), BF16)


def matrices_kernel(z, *refs):
    *given, mix_ref, bal_ref, all_ref = refs
    own = lax.axis_index("var")
    for step, ref in enumerate(given):
        all_ref[(own + step) % z.var] = ref[...]
    size = z.mixed
    to_cols = (iota((z.lat, size), 0) == iota((z.lat, size), 1) // z.rows).astype(F32).astype(BF16)
    same = iota((size, size), 0) % z.rows == iota((size, size), 1) % z.rows
    halves = iota((LANES, LANES), 0) // z.levels == iota((LANES, LANES), 1) // z.levels
    for v in range(z.var):
        meridional = all_ref[v, z.levels :].astype(F32)[: z.lat, : z.lat].astype(BF16)
        slot_cols = dot(meridional, to_cols).astype(BF16)
        mix_ref[v] = jnp.where(same, dot(to_cols, slot_cols, ((0,), (0,))), 0.0).astype(BF16)
        if v > 0:
            balance = all_ref[v, : z.levels].astype(F32)
            balance = jnp.where(halves, jnp.concatenate([balance, balance], axis=0), 0.0)
            bal_ref[v - 1] = balance.T.astype(BF16)


def mixing_kernel(z, packet_ref, mix_ref, bal_ref, out_ref):
    stream = None
    for v in range(z.var):
        rows = slice(v * z.mixed, (v + 1) * z.mixed)
        blended = dot(mix_ref[v], packet_ref[rows])
        if v == 0:
            stream = blended.astype(BF16)
        else:
            blended = blended + dot(stream, bal_ref[v - 1])
        out_ref[rows] = blended.astype(BF16)


def synthesis_kernel(z, spectra_ref, basis_ref, twiddle_ref, out_ref, sems, field_ref, lhs_ref, parts_ref):
    period = twiddle_ref[2 * RADIX :, :LANES].astype(jnp.int32)
    length = jnp.max(period)
    kap = iota((z.kaps, LANES), 0)
    half = z.levels // 2
    kinds = 2 * RADIX - 1
    for at in (0, z.sin):
        lhs_ref[:, at + z.kaps : at + z.sin] = jnp.zeros((2 * half * kinds, z.sin - z.kaps), BF16)
    for r in range(RADIX):
        part = spectra_ref[r * z.kaps : (r + 1) * z.kaps].astype(F32)
        part = jnp.where(kap * RADIX + r <= (period[0:1] - 1) // 2, part, 0.0)
        part = part.astype(BF16).T
        for i in range(2):
            from_cos = part[i * half : (i + 1) * half]
            from_sin = part[z.levels + i * half : z.levels + (i + 1) * half]
            pairs = [(from_cos, from_sin)] if r == 0 else [(from_cos, from_sin), (-from_sin, from_cos)]
            for kind, pair in zip((2 * r - 1, 2 * r) if r else (0,), pairs):
                to = slice((i * kinds + kind) * half, (i * kinds + kind + 1) * half)
                lhs_ref[to, : z.kaps] = pair[0]
                lhs_ref[to, z.sin : z.sin + z.kaps] = pair[1]
    quarter = length // RADIX
    starts = [quarter * j1 for j1 in range(1, RADIX)]
    bases = [pl.multiple_of(s // LANES * LANES, LANES) for s in starts]
    shifts = [s - b for s, b in zip(starts, bases)]
    wide = z.points + LANES
    field_ref[:, wide:] = jnp.zeros((z.levels, z.lons + LANES - wide), BF16)
    keep = [iota((STRIP, LANES), 1) < shift for shift in shifts]
    zero = jnp.zeros((STRIP, LANES), F32)
    for i in range(2):
        rows = slice(i * kinds * half, (i + 1) * kinds * half)
        parts_ref[rows] = dot(lhs_ref[rows], basis_ref[...])
    sent = []
    for at in range(0, z.levels, STRIP):
        rows = slice(at, at + STRIP)
        first = at // half * kinds * half + at % half
        quarters = [[], [], [], []]
        for c in range(z.tiles):
            cos1, cos2, cos3 = [twiddle_ref[r : r + 1, tile(c)] for r in (1, 2, 3)]
            sin1, sin2, sin3 = [twiddle_ref[RADIX + r : RADIX + r + 1, tile(c)] for r in (1, 2, 3)]
            w0, re1, im1, re2, im2, re3, im3 = [
                parts_ref[first + kind * half : first + kind * half + STRIP, tile(c)] for kind in range(kinds)
            ]
            w2 = re2 * cos2 - im2 * sin2
            cross = (re1 * cos1 - im1 * sin1) + (re3 * cos3 - im3 * sin3)
            turn = (re1 * sin1 + im1 * cos1) - (re3 * sin3 + im3 * cos3)
            even, odd = w0 + w2, w0 - w2
            field_ref[rows, tile(c)] = (even + cross).astype(BF16)
            for j1, part in ((1, odd - turn), (2, even - cross), (3, odd + turn)):
                quarters[j1].append(pltpu.roll(part, shifts[j1 - 1], 1))
        field_ref[rows, tile(z.tiles)] = zero.astype(BF16)
        for j1 in range(1, RADIX):
            pieces = zip([zero] + quarters[j1], quarters[j1] + [zero])
            for c, (left, right) in enumerate(pieces):
                lanes = pl.ds(pl.multiple_of(bases[j1 - 1] + c * LANES, LANES), LANES)
                piece = jnp.where(keep[j1 - 1], left, right)
                if c == 0:
                    piece = piece + field_ref[rows, lanes].astype(F32)
                field_ref[rows, lanes] = piece.astype(BF16)
        sent += fetch(
            (field_ref.at[pl.ds(at, STRIP), pl.ds(0, z.lons)],),
            (out_ref.at[0, 0, pl.ds(at, STRIP)],),
            sems.at[pl.ds(at // STRIP, 1)],
        )
    for copy in sent:
        copy.wait()


def exchange(z, spectra):
    chunks = spectra.reshape(z.devices, z.rows, LANES)
    return lax.all_to_all(chunks, ("var", "lat"), 0, 0, tiled=True).reshape(spectra.shape)


def body(z, control, row_order, row_length, vertical, amplitude, meridional, balance):
    arguments = (row_order, row_length, control, vertical, amplitude, meridional, balance)
    made = (
        jax.ShapeDtypeStruct((z.devices * z.rows, LANES), BF16),
        jax.ShapeDtypeStruct((z.params, LANES), BF16),
        jax.ShapeDtypeStruct((2 * z.sin, z.points), BF16),
        jax.ShapeDtypeStruct((2 * RADIX + SUBLANES, z.points), F32),
    )
    packets, params, basis, twiddle = pl.pallas_call(
        functools.partial(analysis_kernel, z),
        out_shape=made,
        in_specs=[HBM] * len(arguments),
        out_specs=(VMEM,) * len(made),
        scratch_shapes=[
            *[pltpu.SMEM(x.shape, x.dtype) for x in arguments[:2]],
            *[pltpu.VMEM(x.shape, x.dtype) for x in arguments[2:]],
            pltpu.SemaphoreType.DMA((len(arguments),)),
            pltpu.VMEM((z.levels, z.lons + LANES), F32),
            pltpu.VMEM((2 * RADIX * z.levels, z.points), BF16),
            pltpu.VMEM((2 * z.heads, z.points), F32),
            pltpu.VMEM((2 * STRIP, z.points), F32),
            pltpu.VMEM((z.waves, LANES), F32),
            pltpu.VMEM((2 * z.kaps, RADIX * LANES), F32),
        ],
        compiler_params=PARAMS,
        name="analysis",
    )(*[pltpu.with_memory_space_constraint(x, pltpu.HBM) for x in arguments])
    given = [params]
    for step in range(1, z.var):
        given.append(lax.ppermute(params, "var", [((i + step) % z.var, i) for i in range(z.var)]))
    packets = exchange(z, packets)
    mix, lift = pl.pallas_call(
        functools.partial(matrices_kernel, z),
        out_shape=(
            jax.ShapeDtypeStruct((z.var, z.mixed, z.mixed), BF16),
            jax.ShapeDtypeStruct((z.var - 1, LANES, LANES), BF16),
        ),
        in_specs=[VMEM] * z.var,
        out_specs=(VMEM, VMEM),
        scratch_shapes=[pltpu.VMEM((z.var, z.params, LANES), BF16)],
        compiler_params=PARAMS,
        cost_estimate=pl.CostEstimate(flops=10**8, bytes_accessed=10**6, transcendentals=0),
        name="matrices",
    )(*given)
    balanced = pl.pallas_call(
        functools.partial(mixing_kernel, z),
        out_shape=jax.ShapeDtypeStruct(packets.shape, BF16),
        in_specs=[VMEM] * 3,
        out_specs=VMEM,
        compiler_params=PARAMS,
        name="mixing",
    )(packets, mix, lift)
    balanced = exchange(z, balanced)
    return pl.pallas_call(
        functools.partial(synthesis_kernel, z),
        out_shape=jax.ShapeDtypeStruct(control.shape, BF16),
        in_specs=[VMEM] * 3,
        out_specs=HBM,
        scratch_shapes=[
            pltpu.SemaphoreType.DMA((z.levels // STRIP,)),
            pltpu.VMEM((z.levels, z.lons + LANES), BF16),
            pltpu.VMEM(((2 * RADIX - 1) * z.levels, 2 * z.sin), BF16),
            pltpu.VMEM(((2 * RADIX - 1) * z.levels, z.points), F32),
        ],
        compiler_params=PARAMS,
        name="synthesis",
    )(balanced, basis, twiddle)


def solution(mesh):
    placed = (
        P("var", "lat", None, None),
        P(),
        P(),
        P("var", None, None),
        P("var", None),
        P("var", None, None),
        P("var", None, None),
    )

    def run(control, row_order, row_length, vertical, amplitude, meridional, balance):
        lat_total, var_total = mesh.shape["lat"], mesh.shape["var"]
        assert control.shape[0] == var_total and control.shape[1] == lat_total
        z = Sizes(lat_total, var_total, control.shape[2], control.shape[3], amplitude.shape[1])
        return jax.shard_map(
            functools.partial(body, z),
            mesh=mesh,
            in_specs=placed,
            out_specs=P("var", "lat", None, None),
            check_vma=False,
        )(control, row_order, row_length, vertical, amplitude, meridional, balance)

    return run
```

```python
import functools
import math

import jax
import jax.numpy as jnp
from jax import lax
from jax.experimental import pallas as pl
from jax.experimental.pallas import tpu as pltpu
from jax.sharding import PartitionSpec as P

RADIX = 4
LANES = 128
SUBLANES = 8
STRIP = 16
F32 = jnp.float32
BF16 = jnp.bfloat16

COS_POLY = (1, -19.7392044, 64.9391174, -85.4501419, 60.1676292, -25.9675999, 6.52865839)
SIN_POLY = (6.28318501, -41.3415909, 81.5999451, -76.6144714, 41.3428841, -12.4712439)

VMEM = pl.BlockSpec(memory_space=pltpu.VMEM)
HBM = pl.BlockSpec(memory_space=pltpu.HBM)
PARAMS = pltpu.CompilerParams(vmem_limit_bytes=32 * 1024 * 1024)


def iota(shape, dim):
    return lax.broadcasted_iota(jnp.int32, shape, dim)


def horner(poly, x):
    total = jnp.full_like(x, poly[-1])
    for term in poly[-2::-1]:
        total = total * x + term
    return total


def cos_sin(turns):
    turns = turns - jnp.round(turns)
    square = turns * turns
    return horner(COS_POLY, square), horner(SIN_POLY, square) * turns


def ceil_div(a, b):
    return -(-a // b)


def round_up(a, b):
    return ceil_div(a, b) * b


def dot(a, b, contract=((1,), (0,))):
    return lax.dot_general(a, b, (contract, ((), ())), preferred_element_type=F32)


class Sizes:
    def __init__(self, lat_total, var_total, levels, lons, waves):
        self.lat, self.var, self.levels, self.lons, self.waves = lat_total, var_total, levels, lons, waves
        self.devices = lat_total * var_total
        self.points = lons // RADIX
        self.tiles = self.points // LANES
        self.block = math.gcd(self.tiles, 2)
        self.kaps = waves // RADIX
        self.rows = round_up(ceil_div(waves, self.devices), SUBLANES)
        assert self.kaps % self.rows == 0 and self.points % LANES == 0 and 2 * levels == LANES and lat_total <= LANES
        self.mixed = lat_total * self.rows
        self.sin = round_up(self.kaps, LANES)
        self.heads = round_up(ceil_div(self.kaps, STRIP), SUBLANES)
        self.params = round_up(levels + lat_total, STRIP)


def own_length(order_ref, length_ref):
    slot = lax.axis_index("lat")
    row = order_ref[slot]
    return slot, row, length_ref[row]


def fetch(sources, targets, sems):
    copies = [pltpu.make_async_copy(s, t, sems.at[i]) for i, (s, t) in enumerate(zip(sources, targets))]
    for copy in copies:
        copy.start()
    return copies


def slot_matrix(z, order_ref, mer_ref):
    slot = iota((z.lat, z.lat), 0)
    row = jnp.zeros((z.lat, z.lat), jnp.int32)
    for t in range(z.lat):
        row = jnp.where(slot == t, order_ref[t], row)
    pick = (row == iota((z.lat, z.lat), 1)).astype(F32).astype(BF16)
    return dot(dot(pick, mer_ref[0]).astype(BF16), pick, ((1,), (1,)))


def tile(c):
    return slice(c * LANES, (c + 1) * LANES)


def analysis_kernel(z, *refs):
    given, made, held = refs[:7], refs[7:11], refs[11:18]
    sems, field_ref, parts_ref, heads_ref, tails_ref, scale_ref, product_ref = refs[18:]
    order_ref, length_ref, control_ref, vert_ref, amp_ref, mer_ref, bal_ref = held
    packet_ref, params_ref, basis_ref, twiddle_ref = made
    copies = fetch(given, held, sems)
    for at in (0, z.sin):
        basis_ref[at + z.kaps : at + z.sin] = jnp.zeros((z.sin - z.kaps, z.points), BF16)
    field_ref[:, z.lons :] = jnp.zeros((z.levels, LANES), F32)
    params_ref[...] = jnp.zeros(params_ref.shape, BF16)
    parts_ref[z.levels : 2 * z.levels] = jnp.zeros((z.levels, z.points), BF16)
    for copy in copies[:2]:
        copy.wait()
    slot, row, length = own_length(order_ref, length_ref)
    quarter = length // RADIX
    period = jnp.full((1, LANES), length, jnp.int32).astype(F32)
    tail = iota((STRIP, LANES), 0).astype(F32)
    head = iota((z.heads, LANES), 0).astype(F32) * STRIP
    tw_row = iota((2 * RADIX, LANES), 0)
    tw_wave = jnp.where(tw_row < RADIX, tw_row, tw_row - RADIX).astype(F32)
    fraction = jnp.full((1, LANES), quarter, jnp.int32).astype(F32)
    for c in range(z.tiles):
        points = c * LANES + iota((1, LANES), 1)
        step = points.astype(F32) / fraction
        tails_ref[:STRIP, tile(c)], tails_ref[STRIP:, tile(c)] = cos_sin(tail * step)
        head_cos, head_sin = cos_sin(head * step)
        heads_ref[: z.heads, tile(c)] = jnp.where(points < quarter, head_cos, 0.0)
        heads_ref[z.heads :, tile(c)] = jnp.where(points < quarter, head_sin, 0.0)
        tw_cos, tw_sin = cos_sin(tw_wave * (points.astype(F32) / period))
        twiddle_ref[: 2 * RADIX, tile(c)] = jnp.where(tw_row < RADIX, tw_cos, tw_sin)
        twiddle_ref[2 * RADIX :, tile(c)] = jnp.broadcast_to(period, (SUBLANES, LANES))
    for copy in copies[2:]:
        copy.wait()
    field_ref[:, : z.lons] = dot(vert_ref[0], control_ref[0, 0])
    starts = [quarter * j1 for j1 in range(1, RADIX)]
    bases = [pl.multiple_of(s // LANES * LANES, LANES) for s in starts]
    shifts = [(LANES - (s - b)) % LANES for s, b in zip(starts, bases)]
    lane = iota((STRIP, LANES), 1)
    keeps = [(lane < shift) | (shift == 0) for shift in shifts]

    def rolled(i, at, c):
        lanes = pl.ds(pl.multiple_of(bases[i] + c * LANES, LANES), LANES)
        return pltpu.roll(field_ref[at : at + STRIP, lanes], shifts[i], 1)

    before = {}
    for block in range(0, z.tiles, z.block):
        for c in range(block, block + z.block):
            tail_cos, tail_sin = tails_ref[:STRIP, tile(c)], tails_ref[STRIP:, tile(c)]
            for at in range(0, z.kaps, STRIP):
                i = at // STRIP
                head_cos, head_sin = heads_ref[i : i + 1, tile(c)], heads_ref[z.heads + i : z.heads + i + 1, tile(c)]
                basis_ref[at : at + STRIP, tile(c)] = (head_cos * tail_cos - head_sin * tail_sin).astype(BF16)
                to = slice(z.sin + at, z.sin + at + STRIP)
                basis_ref[to, tile(c)] = (head_sin * tail_cos + head_cos * tail_sin).astype(BF16)
        for at in range(0, z.levels, STRIP):
            for c in range(block, block + z.block):
                if c == 0:
                    before[at] = [rolled(i, at, 0) for i in range(RADIX - 1)]
                after = [rolled(i, at, c + 1) for i in range(RADIX - 1)]
                second, third, fourth = [jnp.where(k, a, b) for k, a, b in zip(keeps, before[at], after)]
                before[at] = after
                first = field_ref[at : at + STRIP, tile(c)]
                even, odd = first + third, second + fourth
                real, imag, turned = first - third, second - fourth, even - odd
                cos1, cos2, cos3 = [twiddle_ref[r : r + 1, tile(c)] for r in (1, 2, 3)]
                sin1, sin2, sin3 = [twiddle_ref[RADIX + r : RADIX + r + 1, tile(c)] for r in (1, 2, 3)]
                parts = (
                    (even + odd,),
                    (real * cos1 - imag * sin1, real * sin1 + imag * cos1),
                    (turned * cos2, turned * sin2),
                    (real * cos3 + imag * sin3, real * sin3 - imag * cos3),
                )
                for r, pair in enumerate(parts):
                    for half, part in enumerate(pair):
                        to = (2 * r + half) * z.levels + at
                        parts_ref[to : to + STRIP, tile(c)] = part.astype(BF16)
        lanes = slice(block * LANES, (block + z.block) * LANES)
        basis = jnp.concatenate([basis_ref[: z.kaps, lanes], basis_ref[z.sin : z.sin + z.kaps, lanes]], axis=0)
        product = dot(basis, parts_ref[:, lanes], ((1,), (1,)))
        product_ref[...] = product if block == 0 else product_ref[...] + product
    group = LANES // RADIX
    weights = 1.0 / period, 2.0 / period
    for r in range(RADIX):
        picked = iota((group, LANES), 1) == iota((group, LANES), 0) * RADIX + r
        for at in range(0, z.kaps, group):
            lanes = slice(at * RADIX, at * RADIX + LANES)
            amp = jnp.sum(jnp.where(picked, amp_ref[:, lanes], 0.0), axis=1, keepdims=True)
            wave = (at + iota((group, LANES), 0)) * RADIX + r
            weight = jnp.where(wave == 0, *weights) if at + r == 0 else weights[1]
            scale_ref[r * z.kaps + at : r * z.kaps + at + group] = jnp.where(
                wave <= (length - 1) // 2, weight * amp, 0.0
            )
    params_ref[: z.levels] = jnp.concatenate([bal_ref[0], bal_ref[0]], axis=1)
    params_ref[z.levels : z.levels + z.lat, : z.lat] = slot_matrix(z, order_ref, mer_ref).astype(BF16)
    count = z.kaps // z.rows
    sign = jnp.where(iota((1, LANES), 1) < z.levels, -1.0, 1.0).astype(F32)
    for r in range(RADIX):
        lanes = tile(r)
        for i in range(count):
            rows = slice(i * z.rows, (i + 1) * z.rows)
            from_sin = product_ref[z.kaps + i * z.rows : z.kaps + (i + 1) * z.rows, lanes]
            both = product_ref[rows, lanes] + pltpu.roll(from_sin, z.levels, 1) * sign
            scale = scale_ref[r * z.kaps + i * z.rows : r * z.kaps + (i + 1) * z.rows]
            packet_ref[r * count + i] = (both * scale).astype(BF16)
    if z.devices > RADIX * count:
        packet_ref[RADIX * count :] = jnp.zeros((z.devices - RADIX * count, z.rows, LANES), BF16)


def matrices_kernel(z, *refs):
    *given, mix_ref, bal_ref, all_ref = refs
    own = lax.axis_index("var")
    for step, ref in enumerate(given):
        all_ref[(own + step) % z.var] = ref[...]
    size = z.mixed
    to_cols = (iota((z.lat, size), 0) == iota((z.lat, size), 1) // z.rows).astype(F32).astype(BF16)
    same = iota((size, size), 0) % z.rows == iota((size, size), 1) % z.rows
    halves = iota((LANES, LANES), 0) // z.levels == iota((LANES, LANES), 1) // z.levels
    for v in range(z.var):
        meridional = all_ref[v, z.levels :].astype(F32)[: z.lat, : z.lat].astype(BF16)
        slot_cols = dot(meridional, to_cols).astype(BF16)
        mix_ref[v] = jnp.where(same, dot(to_cols, slot_cols, ((0,), (0,))), 0.0).astype(BF16)
        if v > 0:
            balance = all_ref[v, : z.levels].astype(F32)
            balance = jnp.where(halves, jnp.concatenate([balance, balance], axis=0), 0.0)
            bal_ref[v - 1] = balance.T.astype(BF16)


def mixing_kernel(z, packet_ref, mix_ref, bal_ref, out_ref):
    stream = None
    for v in range(z.var):
        coeffs = packet_ref[v].astype(F32).reshape(z.mixed, LANES).astype(BF16)
        blended = dot(mix_ref[v], coeffs)
        if v == 0:
            stream = blended.astype(BF16)
        else:
            blended = blended + dot(stream, bal_ref[v - 1])
        blended = blended.reshape(z.lat, z.rows, LANES)
        for s in range(z.lat):
            out_ref[v, s] = blended[s].astype(BF16)


def synthesis_kernel(z, spectra_ref, basis_ref, twiddle_ref, out_ref, sems, field_ref, lhs_ref, parts_ref):
    period = twiddle_ref[2 * RADIX :, :LANES].astype(jnp.int32)
    length = jnp.max(period)
    kap = iota((z.kaps, LANES), 0)
    count = z.kaps // z.rows
    kinds = 2 * RADIX - 1
    for at in (0, z.sin):
        lhs_ref[:, at + z.kaps : at + z.sin] = jnp.zeros((kinds * z.levels, z.sin - z.kaps), BF16)
    for r in range(RADIX):
        part = spectra_ref[r * count : (r + 1) * count].astype(F32).reshape(z.kaps, LANES)
        part = jnp.where(kap * RADIX + r <= (period[0:1] - 1) // 2, part, 0.0)
        part = part.astype(BF16).T
        from_cos, from_sin = part[: z.levels], part[z.levels :]
        pairs = [(from_cos, from_sin)] if r == 0 else [(from_cos, from_sin), (-from_sin, from_cos)]
        for kind, pair in zip((2 * r - 1, 2 * r) if r else (0,), pairs):
            to = slice(kind * z.levels, (kind + 1) * z.levels)
            lhs_ref[to, : z.kaps] = pair[0]
            lhs_ref[to, z.sin : z.sin + z.kaps] = pair[1]
    quarter = length // RADIX
    starts = [quarter * j1 for j1 in range(1, RADIX)]
    bases = [pl.multiple_of(s // LANES * LANES, LANES) for s in starts]
    shifts = [s - b for s, b in zip(starts, bases)]
    wide = z.points + LANES
    field_ref[:, wide:] = jnp.zeros((z.levels, z.lons + LANES - wide), BF16)
    keep = [iota((STRIP, LANES), 1) < shift for shift in shifts]
    zero = jnp.zeros((STRIP, LANES), F32)
    parts_ref[...] = dot(lhs_ref[...], basis_ref[...])
    sent = []
    for at in range(0, z.levels, STRIP):
        rows = slice(at, at + STRIP)
        quarters = [[], [], [], []]
        for c in range(z.tiles):
            cos1, cos2, cos3 = [twiddle_ref[r : r + 1, tile(c)] for r in (1, 2, 3)]
            sin1, sin2, sin3 = [twiddle_ref[RADIX + r : RADIX + r + 1, tile(c)] for r in (1, 2, 3)]
            w0, re1, im1, re2, im2, re3, im3 = [
                parts_ref[kind * z.levels + at : kind * z.levels + at + STRIP, tile(c)] for kind in range(kinds)
            ]
            w2 = re2 * cos2 - im2 * sin2
            cross = (re1 * cos1 - im1 * sin1) + (re3 * cos3 - im3 * sin3)
            turn = (re1 * sin1 + im1 * cos1) - (re3 * sin3 + im3 * cos3)
            even, odd = w0 + w2, w0 - w2
            field_ref[rows, tile(c)] = (even + cross).astype(BF16)
            for j1, part in ((1, odd - turn), (2, even - cross), (3, odd + turn)):
                quarters[j1].append(pltpu.roll(part, shifts[j1 - 1], 1))
        field_ref[rows, tile(z.tiles)] = zero.astype(BF16)
        for j1 in range(1, RADIX):
            pieces = zip([zero] + quarters[j1], quarters[j1] + [zero])
            for c, (left, right) in enumerate(pieces):
                lanes = pl.ds(pl.multiple_of(bases[j1 - 1] + c * LANES, LANES), LANES)
                piece = jnp.where(keep[j1 - 1], left, right)
                if c == 0:
                    piece = piece + field_ref[rows, lanes].astype(F32)
                field_ref[rows, lanes] = piece.astype(BF16)
        sent += fetch(
            (field_ref.at[pl.ds(at, STRIP), pl.ds(0, z.lons)],),
            (out_ref.at[0, 0, pl.ds(at, STRIP)],),
            sems.at[pl.ds(at // STRIP, 1)],
        )
    for copy in sent:
        copy.wait()


def body(z, control, row_order, row_length, vertical, amplitude, meridional, balance):
    arguments = (row_order, row_length, control, vertical, amplitude, meridional, balance)
    made = (
        jax.ShapeDtypeStruct((z.devices, z.rows, LANES), BF16),
        jax.ShapeDtypeStruct((z.params, LANES), BF16),
        jax.ShapeDtypeStruct((2 * z.sin, z.points), BF16),
        jax.ShapeDtypeStruct((2 * RADIX + SUBLANES, z.points), F32),
    )
    packets, params, basis, twiddle = pl.pallas_call(
        functools.partial(analysis_kernel, z),
        out_shape=made,
        in_specs=[HBM] * len(arguments),
        out_specs=(VMEM,) * len(made),
        scratch_shapes=[
            *[pltpu.SMEM(x.shape, x.dtype) for x in arguments[:2]],
            *[pltpu.VMEM(x.shape, x.dtype) for x in arguments[2:]],
            pltpu.SemaphoreType.DMA((len(arguments),)),
            pltpu.VMEM((z.levels, z.lons + LANES), F32),
            pltpu.VMEM((2 * RADIX * z.levels, z.points), BF16),
            pltpu.VMEM((2 * z.heads, z.points), F32),
            pltpu.VMEM((2 * STRIP, z.points), F32),
            pltpu.VMEM((z.waves, LANES), F32),
            pltpu.VMEM((2 * z.kaps, RADIX * LANES), F32),
        ],
        compiler_params=PARAMS,
        name="analysis",
    )(*[pltpu.with_memory_space_constraint(x, pltpu.HBM) for x in arguments])
    given = [params]
    for step in range(1, z.var):
        given.append(lax.ppermute(params, "var", [((i + step) % z.var, i) for i in range(z.var)]))
    packets = lax.all_to_all(packets, ("var", "lat"), 0, 0, tiled=True)
    mix, lift = pl.pallas_call(
        functools.partial(matrices_kernel, z),
        out_shape=(
            jax.ShapeDtypeStruct((z.var, z.mixed, z.mixed), BF16),
            jax.ShapeDtypeStruct((z.var - 1, LANES, LANES), BF16),
        ),
        in_specs=[VMEM] * z.var,
        out_specs=(VMEM, VMEM),
        scratch_shapes=[pltpu.VMEM((z.var, z.params, LANES), BF16)],
        compiler_params=PARAMS,
        cost_estimate=pl.CostEstimate(flops=10**8, bytes_accessed=10**6, transcendentals=0),
        name="matrices",
    )(*given)
    balanced = pl.pallas_call(
        functools.partial(mixing_kernel, z),
        out_shape=jax.ShapeDtypeStruct((z.var, z.lat, z.rows, LANES), BF16),
        in_specs=[VMEM] * 3,
        out_specs=VMEM,
        compiler_params=PARAMS,
        name="mixing",
    )(packets.reshape(z.var, z.lat, z.rows, LANES), mix, lift)
    balanced = balanced.reshape(z.devices, z.rows, LANES)
    balanced = lax.all_to_all(balanced, ("var", "lat"), 0, 0, tiled=True)
    return pl.pallas_call(
        functools.partial(synthesis_kernel, z),
        out_shape=jax.ShapeDtypeStruct(control.shape, BF16),
        in_specs=[VMEM] * 3,
        out_specs=HBM,
        scratch_shapes=[
            pltpu.SemaphoreType.DMA((z.levels // STRIP,)),
            pltpu.VMEM((z.levels, z.lons + LANES), BF16),
            pltpu.VMEM(((2 * RADIX - 1) * z.levels, 2 * z.sin), BF16),
            pltpu.VMEM(((2 * RADIX - 1) * z.levels, z.points), F32),
        ],
        compiler_params=PARAMS,
        name="synthesis",
    )(balanced, basis, twiddle)


def solution(mesh):
    placed = (
        P("var", "lat", None, None),
        P(),
        P(),
        P("var", None, None),
        P("var", None),
        P("var", None, None),
        P("var", None, None),
    )

    def run(control, row_order, row_length, vertical, amplitude, meridional, balance):
        lat_total, var_total = mesh.shape["lat"], mesh.shape["var"]
        assert control.shape[0] == var_total and control.shape[1] == lat_total
        z = Sizes(lat_total, var_total, control.shape[2], control.shape[3], amplitude.shape[1])
        return jax.shard_map(
            functools.partial(body, z),
            mesh=mesh,
            in_specs=placed,
            out_specs=P("var", "lat", None, None),
            check_vma=False,
        )(control, row_order, row_length, vertical, amplitude, meridional, balance)

    return run
```

```python
import functools
import math

import jax
import jax.numpy as jnp
from jax import lax
from jax.experimental import pallas as pl
from jax.experimental.pallas import tpu as pltpu
from jax.sharding import PartitionSpec as P

RADIX = 4
LANES = 128
SUBLANES = 8
STRIP = 16
F32 = jnp.float32
BF16 = jnp.bfloat16

COS_POLY = (1, -19.7392044, 64.9391174, -85.4501419, 60.1676292, -25.9675999, 6.52865839)
SIN_POLY = (6.28318501, -41.3415909, 81.5999451, -76.6144714, 41.3428841, -12.4712439)

VMEM = pl.BlockSpec(memory_space=pltpu.VMEM)
HBM = pl.BlockSpec(memory_space=pltpu.HBM)
PARAMS = pltpu.CompilerParams(vmem_limit_bytes=32 * 1024 * 1024)


def iota(shape, dim):
    return lax.broadcasted_iota(jnp.int32, shape, dim)


def horner(poly, x):
    total = jnp.full_like(x, poly[-1])
    for term in poly[-2::-1]:
        total = total * x + term
    return total


def cos_sin(turns):
    turns = turns - jnp.round(turns)
    square = turns * turns
    return horner(COS_POLY, square), horner(SIN_POLY, square) * turns


def ceil_div(a, b):
    return -(-a // b)


def round_up(a, b):
    return ceil_div(a, b) * b


def dot(a, b, contract=((1,), (0,))):
    return lax.dot_general(a, b, (contract, ((), ())), preferred_element_type=F32)


class Sizes:
    def __init__(self, lat_total, var_total, levels, lons, waves):
        self.lat, self.var, self.levels, self.lons, self.waves = lat_total, var_total, levels, lons, waves
        self.devices = lat_total * var_total
        self.points = lons // RADIX
        self.tiles = self.points // LANES
        self.block = math.gcd(self.tiles, 2)
        self.kaps = waves // RADIX
        self.rows = round_up(ceil_div(waves, self.devices), SUBLANES)
        assert self.kaps % self.rows == 0 and self.points % LANES == 0 and 2 * levels == LANES and lat_total <= LANES
        self.mixed = lat_total * self.rows
        self.sin = round_up(self.kaps, LANES)
        self.heads = round_up(ceil_div(self.kaps, STRIP), SUBLANES)
        self.params = round_up(levels + lat_total, STRIP)


def own_length(order_ref, length_ref):
    slot = lax.axis_index("lat")
    row = order_ref[slot]
    return slot, row, length_ref[row]


def fetch(sources, targets, sems):
    copies = [pltpu.make_async_copy(s, t, sems.at[i]) for i, (s, t) in enumerate(zip(sources, targets))]
    for copy in copies:
        copy.start()
    return copies


def slot_matrix(z, order_ref, mer_ref):
    slot = iota((z.lat, z.lat), 0)
    row = jnp.zeros((z.lat, z.lat), jnp.int32)
    for t in range(z.lat):
        row = jnp.where(slot == t, order_ref[t], row)
    pick = (row == iota((z.lat, z.lat), 1)).astype(F32).astype(BF16)
    return dot(dot(pick, mer_ref[0]).astype(BF16), pick, ((1,), (1,)))


def lanes_below(bound):
    lane = iota((STRIP, LANES), 1).astype(F32).astype(BF16)
    return lane < jnp.full((STRIP, LANES), bound, jnp.int32).astype(F32).astype(BF16)


def tile(c):
    return slice(c * LANES, (c + 1) * LANES)


def analysis_kernel(z, *refs):
    given, made, held = refs[:7], refs[7:11], refs[11:18]
    sems, field_ref, parts_ref, heads_ref, tails_ref, scale_ref, product_ref = refs[18:]
    order_ref, length_ref, control_ref, vert_ref, amp_ref, mer_ref, bal_ref = held
    packet_ref, params_ref, basis_ref, twiddle_ref = made
    copies = fetch(given, held, sems)
    for at in (0, z.sin):
        basis_ref[at + z.kaps : at + z.sin] = jnp.zeros((z.sin - z.kaps, z.points), BF16)
    field_ref[:, z.lons :] = jnp.zeros((z.levels, LANES), BF16)
    params_ref[...] = jnp.zeros(params_ref.shape, BF16)
    parts_ref[z.levels : 2 * z.levels] = jnp.zeros((z.levels, z.points), BF16)
    for copy in copies[:2]:
        copy.wait()
    slot, row, length = own_length(order_ref, length_ref)
    quarter = length // RADIX
    period = jnp.full((1, LANES), length, jnp.int32).astype(F32)
    tail = iota((STRIP, LANES), 0).astype(F32)
    head = iota((z.heads, LANES), 0).astype(F32) * STRIP
    tw_row = iota((2 * RADIX, LANES), 0)
    tw_wave = jnp.where(tw_row < RADIX, tw_row, tw_row - RADIX).astype(F32)
    fraction = jnp.full((1, LANES), quarter, jnp.int32).astype(F32)
    for c in range(z.tiles):
        points = c * LANES + iota((1, LANES), 1)
        step = points.astype(F32) / fraction
        tails_ref[:STRIP, tile(c)], tails_ref[STRIP:, tile(c)] = cos_sin(tail * step)
        head_cos, head_sin = cos_sin(head * step)
        heads_ref[: z.heads, tile(c)] = jnp.where(points < quarter, head_cos, 0.0)
        heads_ref[z.heads :, tile(c)] = jnp.where(points < quarter, head_sin, 0.0)
        tw_cos, tw_sin = cos_sin(tw_wave * (points.astype(F32) / period))
        twiddle_ref[: 2 * RADIX, tile(c)] = jnp.where(tw_row < RADIX, tw_cos, tw_sin)
        twiddle_ref[2 * RADIX :, tile(c)] = jnp.broadcast_to(period, (SUBLANES, LANES))
    for copy in copies[2:]:
        copy.wait()
    field_ref[:, : z.lons] = dot(vert_ref[0], control_ref[0, 0]).astype(BF16)
    starts = [quarter * j1 for j1 in range(1, RADIX)]
    bases = [pl.multiple_of(s // LANES * LANES, LANES) for s in starts]
    shifts = [(LANES - (s - b)) % LANES for s, b in zip(starts, bases)]
    keeps = [lanes_below(jnp.where(shift == 0, LANES, shift)) for shift in shifts]

    def rolled(i, at, c):
        lanes = pl.ds(pl.multiple_of(bases[i] + c * LANES, LANES), LANES)
        return pltpu.roll(field_ref[at : at + STRIP, lanes], shifts[i], 1)

    before = {}
    for block in range(0, z.tiles, z.block):
        for c in range(block, block + z.block):
            tail_cos, tail_sin = tails_ref[:STRIP, tile(c)], tails_ref[STRIP:, tile(c)]
            for at in range(0, z.kaps, STRIP):
                i = at // STRIP
                head_cos, head_sin = heads_ref[i : i + 1, tile(c)], heads_ref[z.heads + i : z.heads + i + 1, tile(c)]
                basis_ref[at : at + STRIP, tile(c)] = (head_cos * tail_cos - head_sin * tail_sin).astype(BF16)
                to = slice(z.sin + at, z.sin + at + STRIP)
                basis_ref[to, tile(c)] = (head_sin * tail_cos + head_cos * tail_sin).astype(BF16)
        for at in range(0, z.levels, STRIP):
            for c in range(block, block + z.block):
                if c == 0:
                    before[at] = [rolled(i, at, 0) for i in range(RADIX - 1)]
                after = [rolled(i, at, c + 1) for i in range(RADIX - 1)]
                quarters = [jnp.where(k, a, b) for k, a, b in zip(keeps, before[at], after)]
                before[at] = after
                quarters = [field_ref[at : at + STRIP, tile(c)], *quarters]
                first, second, third, fourth = [x.astype(F32) for x in quarters]
                even, odd = first + third, second + fourth
                real, imag, turned = first - third, second - fourth, even - odd
                cos1, cos2, cos3 = [twiddle_ref[r : r + 1, tile(c)] for r in (1, 2, 3)]
                sin1, sin2, sin3 = [twiddle_ref[RADIX + r : RADIX + r + 1, tile(c)] for r in (1, 2, 3)]
                parts = (
                    (even + odd,),
                    (real * cos1 - imag * sin1, real * sin1 + imag * cos1),
                    (turned * cos2, turned * sin2),
                    (real * cos3 + imag * sin3, real * sin3 - imag * cos3),
                )
                for r, pair in enumerate(parts):
                    for half, part in enumerate(pair):
                        to = (2 * r + half) * z.levels + at
                        parts_ref[to : to + STRIP, tile(c)] = part.astype(BF16)
        lanes = slice(block * LANES, (block + z.block) * LANES)
        basis = jnp.concatenate([basis_ref[: z.kaps, lanes], basis_ref[z.sin : z.sin + z.kaps, lanes]], axis=0)
        product = dot(basis, parts_ref[:, lanes], ((1,), (1,)))
        product_ref[...] = product if block == 0 else product_ref[...] + product
    group = LANES // RADIX
    weights = 1.0 / period, 2.0 / period
    for r in range(RADIX):
        picked = iota((group, LANES), 1) == iota((group, LANES), 0) * RADIX + r
        for at in range(0, z.kaps, group):
            lanes = slice(at * RADIX, at * RADIX + LANES)
            amp = jnp.sum(jnp.where(picked, amp_ref[:, lanes], 0.0), axis=1, keepdims=True)
            wave = (at + iota((group, LANES), 0)) * RADIX + r
            weight = jnp.where(wave == 0, *weights) if at + r == 0 else weights[1]
            scale_ref[r * z.kaps + at : r * z.kaps + at + group] = jnp.where(
                wave <= (length - 1) // 2, weight * amp, 0.0
            )
    params_ref[: z.levels] = jnp.concatenate([bal_ref[0], bal_ref[0]], axis=1)
    params_ref[z.levels : z.levels + z.lat, : z.lat] = slot_matrix(z, order_ref, mer_ref).astype(BF16)
    count = z.kaps // z.rows
    sign = jnp.where(iota((1, LANES), 1) < z.levels, -1.0, 1.0).astype(F32)
    for r in range(RADIX):
        lanes = tile(r)
        for i in range(count):
            rows = slice(i * z.rows, (i + 1) * z.rows)
            from_sin = product_ref[z.kaps + i * z.rows : z.kaps + (i + 1) * z.rows, lanes]
            both = product_ref[rows, lanes] + pltpu.roll(from_sin, z.levels, 1) * sign
            scale = scale_ref[r * z.kaps + i * z.rows : r * z.kaps + (i + 1) * z.rows]
            packet_ref[r * count + i] = (both * scale).astype(BF16)
    if z.devices > RADIX * count:
        packet_ref[RADIX * count :] = jnp.zeros((z.devices - RADIX * count, z.rows, LANES), BF16)


def matrices_kernel(z, *refs):
    *given, mix_ref, bal_ref, all_ref = refs
    own = lax.axis_index("var")
    for step, ref in enumerate(given):
        all_ref[(own + step) % z.var] = ref[...]
    size = z.mixed
    to_cols = (iota((z.lat, size), 0) == iota((z.lat, size), 1) // z.rows).astype(F32).astype(BF16)
    same = iota((size, size), 0) % z.rows == iota((size, size), 1) % z.rows
    halves = iota((LANES, LANES), 0) // z.levels == iota((LANES, LANES), 1) // z.levels
    for v in range(z.var):
        meridional = all_ref[v, z.levels :].astype(F32)[: z.lat, : z.lat].astype(BF16)
        slot_cols = dot(meridional, to_cols).astype(BF16)
        mix_ref[v] = jnp.where(same, dot(to_cols, slot_cols, ((0,), (0,))), 0.0).astype(BF16)
        if v > 0:
            balance = all_ref[v, : z.levels].astype(F32)
            balance = jnp.where(halves, jnp.concatenate([balance, balance], axis=0), 0.0)
            bal_ref[v - 1] = balance.T.astype(BF16)


def mixing_kernel(z, packet_ref, mix_ref, bal_ref, out_ref):
    stream = None
    for v in range(z.var):
        coeffs = packet_ref[v].astype(F32).reshape(z.mixed, LANES).astype(BF16)
        blended = dot(mix_ref[v], coeffs)
        if v == 0:
            stream = blended.astype(BF16)
        else:
            blended = blended + dot(stream, bal_ref[v - 1])
        blended = blended.reshape(z.lat, z.rows, LANES)
        for s in range(z.lat):
            out_ref[v, s] = blended[s].astype(BF16)


def synthesis_kernel(z, spectra_ref, basis_ref, twiddle_ref, out_ref, sems, field_ref, lhs_ref, parts_ref):
    period = twiddle_ref[2 * RADIX :, :LANES].astype(jnp.int32)
    length = jnp.max(period)
    kap = iota((z.kaps, LANES), 0)
    count = z.kaps // z.rows
    half = z.levels // 2
    kinds = 2 * RADIX - 1
    for at in (0, z.sin):
        lhs_ref[:, at + z.kaps : at + z.sin] = jnp.zeros((2 * half * kinds, z.sin - z.kaps), BF16)
    for r in range(RADIX):
        part = spectra_ref[r * count : (r + 1) * count].astype(F32).reshape(z.kaps, LANES)
        part = jnp.where(kap * RADIX + r <= (period[0:1] - 1) // 2, part, 0.0)
        part = part.astype(BF16).T
        for i in range(2):
            from_cos = part[i * half : (i + 1) * half]
            from_sin = part[z.levels + i * half : z.levels + (i + 1) * half]
            pairs = [(from_cos, from_sin)] if r == 0 else [(from_cos, from_sin), (-from_sin, from_cos)]
            for kind, pair in zip((2 * r - 1, 2 * r) if r else (0,), pairs):
                to = slice((i * kinds + kind) * half, (i * kinds + kind + 1) * half)
                lhs_ref[to, : z.kaps] = pair[0]
                lhs_ref[to, z.sin : z.sin + z.kaps] = pair[1]
    quarter = length // RADIX
    starts = [quarter * j1 for j1 in range(1, RADIX)]
    bases = [pl.multiple_of(s // LANES * LANES, LANES) for s in starts]
    shifts = [s - b for s, b in zip(starts, bases)]
    wide = z.points + LANES
    field_ref[:, wide:] = jnp.zeros((z.levels, z.lons + LANES - wide), BF16)
    keep = [iota((STRIP, LANES), 1) < shift for shift in shifts]
    zero = jnp.zeros((STRIP, LANES), F32)
    for i in range(2):
        rows = slice(i * kinds * half, (i + 1) * kinds * half)
        parts_ref[rows] = dot(lhs_ref[rows], basis_ref[...])
    sent = []
    for at in range(0, z.levels, STRIP):
        rows = slice(at, at + STRIP)
        first = at // half * kinds * half + at % half
        quarters = [[], [], [], []]
        for c in range(z.tiles):
            cos1, cos2, cos3 = [twiddle_ref[r : r + 1, tile(c)] for r in (1, 2, 3)]
            sin1, sin2, sin3 = [twiddle_ref[RADIX + r : RADIX + r + 1, tile(c)] for r in (1, 2, 3)]
            w0, re1, im1, re2, im2, re3, im3 = [
                parts_ref[first + kind * half : first + kind * half + STRIP, tile(c)] for kind in range(kinds)
            ]
            w2 = re2 * cos2 - im2 * sin2
            cross = (re1 * cos1 - im1 * sin1) + (re3 * cos3 - im3 * sin3)
            turn = (re1 * sin1 + im1 * cos1) - (re3 * sin3 + im3 * cos3)
            even, odd = w0 + w2, w0 - w2
            field_ref[rows, tile(c)] = (even + cross).astype(BF16)
            for j1, part in ((1, odd - turn), (2, even - cross), (3, odd + turn)):
                quarters[j1].append(pltpu.roll(part, shifts[j1 - 1], 1))
        field_ref[rows, tile(z.tiles)] = zero.astype(BF16)
        for j1 in range(1, RADIX):
            pieces = zip([zero] + quarters[j1], quarters[j1] + [zero])
            for c, (left, right) in enumerate(pieces):
                lanes = pl.ds(pl.multiple_of(bases[j1 - 1] + c * LANES, LANES), LANES)
                piece = jnp.where(keep[j1 - 1], left, right)
                if c == 0:
                    piece = piece + field_ref[rows, lanes].astype(F32)
                field_ref[rows, lanes] = piece.astype(BF16)
        sent += fetch(
            (field_ref.at[pl.ds(at, STRIP), pl.ds(0, z.lons)],),
            (out_ref.at[0, 0, pl.ds(at, STRIP)],),
            sems.at[pl.ds(at // STRIP, 1)],
        )
    for copy in sent:
        copy.wait()


def body(z, control, row_order, row_length, vertical, amplitude, meridional, balance):
    arguments = (row_order, row_length, control, vertical, amplitude, meridional, balance)
    made = (
        jax.ShapeDtypeStruct((z.devices, z.rows, LANES), BF16),
        jax.ShapeDtypeStruct((z.params, LANES), BF16),
        jax.ShapeDtypeStruct((2 * z.sin, z.points), BF16),
        jax.ShapeDtypeStruct((2 * RADIX + SUBLANES, z.points), F32),
    )
    packets, params, basis, twiddle = pl.pallas_call(
        functools.partial(analysis_kernel, z),
        out_shape=made,
        in_specs=[HBM] * len(arguments),
        out_specs=(VMEM,) * len(made),
        scratch_shapes=[
            *[pltpu.SMEM(x.shape, x.dtype) for x in arguments[:2]],
            *[pltpu.VMEM(x.shape, x.dtype) for x in arguments[2:]],
            pltpu.SemaphoreType.DMA((len(arguments),)),
            pltpu.VMEM((z.levels, z.lons + LANES), BF16),
            pltpu.VMEM((2 * RADIX * z.levels, z.points), BF16),
            pltpu.VMEM((2 * z.heads, z.points), F32),
            pltpu.VMEM((2 * STRIP, z.points), F32),
            pltpu.VMEM((z.waves, LANES), F32),
            pltpu.VMEM((2 * z.kaps, RADIX * LANES), F32),
        ],
        compiler_params=PARAMS,
        name="analysis",
    )(*[pltpu.with_memory_space_constraint(x, pltpu.HBM) for x in arguments])
    given = [params]
    for step in range(1, z.var):
        given.append(lax.ppermute(params, "var", [((i + step) % z.var, i) for i in range(z.var)]))
    packets = lax.all_to_all(packets, ("var", "lat"), 0, 0, tiled=True)
    mix, lift = pl.pallas_call(
        functools.partial(matrices_kernel, z),
        out_shape=(
            jax.ShapeDtypeStruct((z.var, z.mixed, z.mixed), BF16),
            jax.ShapeDtypeStruct((z.var - 1, LANES, LANES), BF16),
        ),
        in_specs=[VMEM] * z.var,
        out_specs=(VMEM, VMEM),
        scratch_shapes=[pltpu.VMEM((z.var, z.params, LANES), BF16)],
        compiler_params=PARAMS,
        cost_estimate=pl.CostEstimate(flops=10**8, bytes_accessed=10**6, transcendentals=0),
        name="matrices",
    )(*given)
    balanced = pl.pallas_call(
        functools.partial(mixing_kernel, z),
        out_shape=jax.ShapeDtypeStruct((z.var, z.lat, z.rows, LANES), BF16),
        in_specs=[VMEM] * 3,
        out_specs=VMEM,
        compiler_params=PARAMS,
        name="mixing",
    )(packets.reshape(z.var, z.lat, z.rows, LANES), mix, lift)
    balanced = balanced.reshape(z.devices, z.rows, LANES)
    balanced = lax.all_to_all(balanced, ("var", "lat"), 0, 0, tiled=True)
    return pl.pallas_call(
        functools.partial(synthesis_kernel, z),
        out_shape=jax.ShapeDtypeStruct(control.shape, BF16),
        in_specs=[VMEM] * 3,
        out_specs=HBM,
        scratch_shapes=[
            pltpu.SemaphoreType.DMA((z.levels // STRIP,)),
            pltpu.VMEM((z.levels, z.lons + LANES), BF16),
            pltpu.VMEM(((2 * RADIX - 1) * z.levels, 2 * z.sin), BF16),
            pltpu.VMEM(((2 * RADIX - 1) * z.levels, z.points), F32),
        ],
        compiler_params=PARAMS,
        name="synthesis",
    )(balanced, basis, twiddle)


def solution(mesh):
    placed = (
        P("var", "lat", None, None),
        P(),
        P(),
        P("var", None, None),
        P("var", None),
        P("var", None, None),
        P("var", None, None),
    )

    def run(control, row_order, row_length, vertical, amplitude, meridional, balance):
        lat_total, var_total = mesh.shape["lat"], mesh.shape["var"]
        assert control.shape[0] == var_total and control.shape[1] == lat_total
        z = Sizes(lat_total, var_total, control.shape[2], control.shape[3], amplitude.shape[1])
        return jax.shard_map(
            functools.partial(body, z),
            mesh=mesh,
            in_specs=placed,
            out_specs=P("var", "lat", None, None),
            check_vma=False,
        )(control, row_order, row_length, vertical, amplitude, meridional, balance)

    return run
```

```python
import functools
import math

import jax
import jax.numpy as jnp
from jax import lax
from jax.experimental import pallas as pl
from jax.experimental.pallas import tpu as pltpu
from jax.sharding import PartitionSpec as P

RADIX = 4
LANES = 128
SUBLANES = 8
STRIP = 16
F32 = jnp.float32
BF16 = jnp.bfloat16

COS_POLY = (1, -19.7392044, 64.9391174, -85.4501419, 60.1676292, -25.9675999, 6.52865839)
SIN_POLY = (6.28318501, -41.3415909, 81.5999451, -76.6144714, 41.3428841, -12.4712439)

VMEM = pl.BlockSpec(memory_space=pltpu.VMEM)
HBM = pl.BlockSpec(memory_space=pltpu.HBM)
PARAMS = pltpu.CompilerParams(vmem_limit_bytes=32 * 1024 * 1024)


def iota(shape, dim):
    return lax.broadcasted_iota(jnp.int32, shape, dim)


def horner(poly, x):
    total = jnp.full_like(x, poly[-1])
    for term in poly[-2::-1]:
        total = total * x + term
    return total


def cos_sin(turns):
    turns = turns - jnp.round(turns)
    square = turns * turns
    return horner(COS_POLY, square), horner(SIN_POLY, square) * turns


def ceil_div(a, b):
    return -(-a // b)


def round_up(a, b):
    return ceil_div(a, b) * b


def dot(a, b, contract=((1,), (0,))):
    return lax.dot_general(a, b, (contract, ((), ())), preferred_element_type=F32)


class Sizes:
    def __init__(self, lat_total, var_total, levels, lons, waves):
        self.lat, self.var, self.levels, self.lons, self.waves = lat_total, var_total, levels, lons, waves
        self.devices = lat_total * var_total
        self.points = lons // RADIX
        self.tiles = self.points // LANES
        self.block = math.gcd(self.tiles, 2)
        self.kaps = waves // RADIX
        self.rows = round_up(ceil_div(waves, self.devices), SUBLANES)
        assert self.kaps % self.rows == 0 and self.points % LANES == 0 and 2 * levels == LANES and lat_total <= LANES
        self.mixed = lat_total * self.rows
        self.sin = round_up(self.kaps, LANES)
        self.heads = round_up(ceil_div(self.kaps, STRIP), SUBLANES)
        self.params = round_up(levels + lat_total, STRIP)


def own_length(order_ref, length_ref):
    slot = lax.axis_index("lat")
    row = order_ref[slot]
    return slot, row, length_ref[row]


def fetch(sources, targets, sems):
    copies = [pltpu.make_async_copy(s, t, sems.at[i]) for i, (s, t) in enumerate(zip(sources, targets))]
    for copy in copies:
        copy.start()
    return copies


def slot_matrix(z, order_ref, mer_ref):
    def picks(count):
        slot = iota((count, z.lat), 0)
        row = jnp.full((count, z.lat), -1, jnp.int32)
        for t in range(z.lat):
            row = jnp.where(slot == t, order_ref[t], row)
        return (row == iota((count, z.lat), 1)).astype(F32).astype(BF16)

    rows = dot(picks(z.params - z.levels), mer_ref[0]).astype(BF16)
    return dot(rows, picks(LANES), ((1,), (1,)))


def tile(c):
    return slice(c * LANES, (c + 1) * LANES)


def analysis_kernel(z, *refs):
    given, made, held = refs[:7], refs[7:11], refs[11:18]
    sems, field_ref, parts_ref, heads_ref, tails_ref, scale_ref, product_ref = refs[18:]
    order_ref, length_ref, control_ref, vert_ref, amp_ref, mer_ref, bal_ref = held
    packet_ref, params_ref, basis_ref, twiddle_ref = made
    copies = fetch(given, held, sems)
    for at in (0, z.sin):
        basis_ref[at + z.kaps : at + z.sin] = jnp.zeros((z.sin - z.kaps, z.points), BF16)
    field_ref[:, z.lons :] = jnp.zeros((z.levels, LANES), F32)
    parts_ref[z.levels : 2 * z.levels] = jnp.zeros((z.levels, z.points), BF16)
    for copy in copies[:2]:
        copy.wait()
    slot, row, length = own_length(order_ref, length_ref)
    quarter = length // RADIX
    period = jnp.full((1, LANES), length, jnp.int32).astype(F32)
    tail = iota((STRIP, LANES), 0).astype(F32)
    head = iota((z.heads, LANES), 0).astype(F32) * STRIP
    tw_row = iota((2 * RADIX, LANES), 0)
    tw_wave = jnp.where(tw_row < RADIX, tw_row, tw_row - RADIX).astype(F32)
    fraction = jnp.full((1, LANES), quarter, jnp.int32).astype(F32)
    for c in range(z.tiles):
        points = c * LANES + iota((1, LANES), 1)
        step = points.astype(F32) / fraction
        tails_ref[:STRIP, tile(c)], tails_ref[STRIP:, tile(c)] = cos_sin(tail * step)
        head_cos, head_sin = cos_sin(head * step)
        heads_ref[: z.heads, tile(c)] = jnp.where(points < quarter, head_cos, 0.0)
        heads_ref[z.heads :, tile(c)] = jnp.where(points < quarter, head_sin, 0.0)
        tw_cos, tw_sin = cos_sin(tw_wave * (points.astype(F32) / period))
        twiddle_ref[: 2 * RADIX, tile(c)] = jnp.where(tw_row < RADIX, tw_cos, tw_sin)
        twiddle_ref[2 * RADIX :, tile(c)] = jnp.broadcast_to(period, (SUBLANES, LANES))
    for copy in copies[2:]:
        copy.wait()
    field_ref[:, : z.lons] = dot(vert_ref[0], control_ref[0, 0])
    starts = [quarter * j1 for j1 in range(1, RADIX)]
    bases = [pl.multiple_of(s // LANES * LANES, LANES) for s in starts]
    shifts = [(LANES - (s - b)) % LANES for s, b in zip(starts, bases)]
    lane = iota((STRIP, LANES), 1)
    keeps = [(lane < shift) | (shift == 0) for shift in shifts]

    def rolled(i, at, c):
        lanes = pl.ds(pl.multiple_of(bases[i] + c * LANES, LANES), LANES)
        return pltpu.roll(field_ref[at : at + STRIP, lanes], shifts[i], 1)

    before = {}
    for block in range(0, z.tiles, z.block):
        for c in range(block, block + z.block):
            tail_cos, tail_sin = tails_ref[:STRIP, tile(c)], tails_ref[STRIP:, tile(c)]
            for at in range(0, z.kaps, STRIP):
                i = at // STRIP
                head_cos, head_sin = heads_ref[i : i + 1, tile(c)], heads_ref[z.heads + i : z.heads + i + 1, tile(c)]
                basis_ref[at : at + STRIP, tile(c)] = (head_cos * tail_cos - head_sin * tail_sin).astype(BF16)
                to = slice(z.sin + at, z.sin + at + STRIP)
                basis_ref[to, tile(c)] = (head_sin * tail_cos + head_cos * tail_sin).astype(BF16)
        for at in range(0, z.levels, STRIP):
            for c in range(block, block + z.block):
                if c == 0:
                    before[at] = [rolled(i, at, 0) for i in range(RADIX - 1)]
                after = [rolled(i, at, c + 1) for i in range(RADIX - 1)]
                second, third, fourth = [jnp.where(k, a, b) for k, a, b in zip(keeps, before[at], after)]
                before[at] = after
                first = field_ref[at : at + STRIP, tile(c)]
                even, odd = first + third, second + fourth
                real, imag, turned = first - third, second - fourth, even - odd
                cos1, cos2, cos3 = [twiddle_ref[r : r + 1, tile(c)] for r in (1, 2, 3)]
                sin1, sin2, sin3 = [twiddle_ref[RADIX + r : RADIX + r + 1, tile(c)] for r in (1, 2, 3)]
                parts = (
                    (even + odd,),
                    (real * cos1 - imag * sin1, real * sin1 + imag * cos1),
                    (turned * cos2, turned * sin2),
                    (real * cos3 + imag * sin3, real * sin3 - imag * cos3),
                )
                for r, pair in enumerate(parts):
                    for half, part in enumerate(pair):
                        to = (2 * r + half) * z.levels + at
                        parts_ref[to : to + STRIP, tile(c)] = part.astype(BF16)
        lanes = slice(block * LANES, (block + z.block) * LANES)
        basis = jnp.concatenate([basis_ref[: z.kaps, lanes], basis_ref[z.sin : z.sin + z.kaps, lanes]], axis=0)
        product = dot(basis, parts_ref[:, lanes], ((1,), (1,)))
        product_ref[...] = product if block == 0 else product_ref[...] + product
    group = LANES // RADIX
    weights = 1.0 / period, 2.0 / period
    for r in range(RADIX):
        picked = iota((group, LANES), 1) == iota((group, LANES), 0) * RADIX + r
        for at in range(0, z.kaps, group):
            lanes = slice(at * RADIX, at * RADIX + LANES)
            amp = jnp.sum(jnp.where(picked, amp_ref[:, lanes], 0.0), axis=1, keepdims=True)
            wave = (at + iota((group, LANES), 0)) * RADIX + r
            weight = jnp.where(wave == 0, *weights) if at + r == 0 else weights[1]
            scale_ref[r * z.kaps + at : r * z.kaps + at + group] = jnp.where(
                wave <= (length - 1) // 2, weight * amp, 0.0
            )
    params_ref[: z.levels] = jnp.concatenate([bal_ref[0], bal_ref[0]], axis=1)
    params_ref[z.levels :] = slot_matrix(z, order_ref, mer_ref).astype(BF16)
    count = z.kaps // z.rows
    sign = jnp.where(iota((1, LANES), 1) < z.levels, -1.0, 1.0).astype(F32)
    for r in range(RADIX):
        lanes = tile(r)
        for i in range(count):
            rows = slice(i * z.rows, (i + 1) * z.rows)
            from_sin = product_ref[z.kaps + i * z.rows : z.kaps + (i + 1) * z.rows, lanes]
            both = product_ref[rows, lanes] + pltpu.roll(from_sin, z.levels, 1) * sign
            scale = scale_ref[r * z.kaps + i * z.rows : r * z.kaps + (i + 1) * z.rows]
            packet_ref[r * count + i] = (both * scale).astype(BF16)
    if z.devices > RADIX * count:
        packet_ref[RADIX * count :] = jnp.zeros((z.devices - RADIX * count, z.rows, LANES), BF16)


def matrices_kernel(z, *refs):
    *given, mix_ref, bal_ref, all_ref = refs
    own = lax.axis_index("var")
    for step, ref in enumerate(given):
        all_ref[(own + step) % z.var] = ref[...]
    size = z.mixed
    to_cols = (iota((z.lat, size), 0) == iota((z.lat, size), 1) // z.rows).astype(F32).astype(BF16)
    same = iota((size, size), 0) % z.rows == iota((size, size), 1) % z.rows
    halves = iota((LANES, LANES), 0) // z.levels == iota((LANES, LANES), 1) // z.levels
    for v in range(z.var):
        meridional = all_ref[v, z.levels :].astype(F32)[: z.lat, : z.lat].astype(BF16)
        slot_cols = dot(meridional, to_cols).astype(BF16)
        mix_ref[v] = jnp.where(same, dot(to_cols, slot_cols, ((0,), (0,))), 0.0).astype(BF16)
        if v > 0:
            balance = all_ref[v, : z.levels].astype(F32)
            balance = jnp.where(halves, jnp.concatenate([balance, balance], axis=0), 0.0)
            bal_ref[v - 1] = balance.T.astype(BF16)


def mixing_kernel(z, packet_ref, mix_ref, bal_ref, out_ref):
    stream = None
    for v in range(z.var):
        coeffs = packet_ref[v].astype(F32).reshape(z.mixed, LANES).astype(BF16)
        blended = dot(mix_ref[v], coeffs)
        if v == 0:
            stream = blended.astype(BF16)
        else:
            blended = blended + dot(stream, bal_ref[v - 1])
        blended = blended.reshape(z.lat, z.rows, LANES)
        for s in range(z.lat):
            out_ref[v, s] = blended[s].astype(BF16)


def synthesis_kernel(z, spectra_ref, basis_ref, twiddle_ref, out_ref, sems, field_ref, lhs_ref, parts_ref):
    period = twiddle_ref[2 * RADIX :, :LANES].astype(jnp.int32)
    length = jnp.max(period)
    kap = iota((z.kaps, LANES), 0)
    count = z.kaps // z.rows
    half = z.levels // 2
    kinds = 2 * RADIX - 1
    for at in (0, z.sin):
        lhs_ref[:, at + z.kaps : at + z.sin] = jnp.zeros((2 * half * kinds, z.sin - z.kaps), BF16)
    for r in range(RADIX):
        part = spectra_ref[r * count : (r + 1) * count].astype(F32).reshape(z.kaps, LANES)
        part = jnp.where(kap * RADIX + r <= (period[0:1] - 1) // 2, part, 0.0)
        part = part.astype(BF16).T
        for i in range(2):
            from_cos = part[i * half : (i + 1) * half]
            from_sin = part[z.levels + i * half : z.levels + (i + 1) * half]
            pairs = [(from_cos, from_sin)] if r == 0 else [(from_cos, from_sin), (-from_sin, from_cos)]
            for kind, pair in zip((2 * r - 1, 2 * r) if r else (0,), pairs):
                to = slice((i * kinds + kind) * half, (i * kinds + kind + 1) * half)
                lhs_ref[to, : z.kaps] = pair[0]
                lhs_ref[to, z.sin : z.sin + z.kaps] = pair[1]
    quarter = length // RADIX
    starts = [quarter * j1 for j1 in range(1, RADIX)]
    bases = [pl.multiple_of(s // LANES * LANES, LANES) for s in starts]
    shifts = [s - b for s, b in zip(starts, bases)]
    wide = z.points + LANES
    field_ref[:, wide:] = jnp.zeros((z.levels, z.lons + LANES - wide), BF16)
    keep = [iota((STRIP, LANES), 1) < shift for shift in shifts]
    zero = jnp.zeros((STRIP, LANES), F32)
    for i in range(2):
        rows = slice(i * kinds * half, (i + 1) * kinds * half)
        parts_ref[rows] = dot(lhs_ref[rows], basis_ref[...])
    sent = []
    for at in range(0, z.levels, STRIP):
        rows = slice(at, at + STRIP)
        first = at // half * kinds * half + at % half
        quarters = [[], [], [], []]
        for c in range(z.tiles):
            cos1, cos2, cos3 = [twiddle_ref[r : r + 1, tile(c)] for r in (1, 2, 3)]
            sin1, sin2, sin3 = [twiddle_ref[RADIX + r : RADIX + r + 1, tile(c)] for r in (1, 2, 3)]
            w0, re1, im1, re2, im2, re3, im3 = [
                parts_ref[first + kind * half : first + kind * half + STRIP, tile(c)] for kind in range(kinds)
            ]
            w2 = re2 * cos2 - im2 * sin2
            cross = (re1 * cos1 - im1 * sin1) + (re3 * cos3 - im3 * sin3)
            turn = (re1 * sin1 + im1 * cos1) - (re3 * sin3 + im3 * cos3)
            even, odd = w0 + w2, w0 - w2
            field_ref[rows, tile(c)] = (even + cross).astype(BF16)
            for j1, part in ((1, odd - turn), (2, even - cross), (3, odd + turn)):
                quarters[j1].append(pltpu.roll(part, shifts[j1 - 1], 1))
        field_ref[rows, tile(z.tiles)] = zero.astype(BF16)
        for j1 in range(1, RADIX):
            pieces = zip([zero] + quarters[j1], quarters[j1] + [zero])
            for c, (left, right) in enumerate(pieces):
                lanes = pl.ds(pl.multiple_of(bases[j1 - 1] + c * LANES, LANES), LANES)
                piece = jnp.where(keep[j1 - 1], left, right)
                if c == 0:
                    piece = piece + field_ref[rows, lanes].astype(F32)
                field_ref[rows, lanes] = piece.astype(BF16)
        sent += fetch(
            (field_ref.at[pl.ds(at, STRIP), pl.ds(0, z.lons)],),
            (out_ref.at[0, 0, pl.ds(at, STRIP)],),
            sems.at[pl.ds(at // STRIP, 1)],
        )
    for copy in sent:
        copy.wait()


def body(z, control, row_order, row_length, vertical, amplitude, meridional, balance):
    arguments = (row_order, row_length, control, vertical, amplitude, meridional, balance)
    made = (
        jax.ShapeDtypeStruct((z.devices, z.rows, LANES), BF16),
        jax.ShapeDtypeStruct((z.params, LANES), BF16),
        jax.ShapeDtypeStruct((2 * z.sin, z.points), BF16),
        jax.ShapeDtypeStruct((2 * RADIX + SUBLANES, z.points), F32),
    )
    packets, params, basis, twiddle = pl.pallas_call(
        functools.partial(analysis_kernel, z),
        out_shape=made,
        in_specs=[HBM] * len(arguments),
        out_specs=(VMEM,) * len(made),
        scratch_shapes=[
            *[pltpu.SMEM(x.shape, x.dtype) for x in arguments[:2]],
            *[pltpu.VMEM(x.shape, x.dtype) for x in arguments[2:]],
            pltpu.SemaphoreType.DMA((len(arguments),)),
            pltpu.VMEM((z.levels, z.lons + LANES), F32),
            pltpu.VMEM((2 * RADIX * z.levels, z.points), BF16),
            pltpu.VMEM((2 * z.heads, z.points), F32),
            pltpu.VMEM((2 * STRIP, z.points), F32),
            pltpu.VMEM((z.waves, LANES), F32),
            pltpu.VMEM((2 * z.kaps, RADIX * LANES), F32),
        ],
        compiler_params=PARAMS,
        name="analysis",
    )(*[pltpu.with_memory_space_constraint(x, pltpu.HBM) for x in arguments])
    given = [params]
    for step in range(1, z.var):
        given.append(lax.ppermute(params, "var", [((i + step) % z.var, i) for i in range(z.var)]))
    packets = lax.all_to_all(packets, ("var", "lat"), 0, 0, tiled=True)
    mix, lift = pl.pallas_call(
        functools.partial(matrices_kernel, z),
        out_shape=(
            jax.ShapeDtypeStruct((z.var, z.mixed, z.mixed), BF16),
            jax.ShapeDtypeStruct((z.var - 1, LANES, LANES), BF16),
        ),
        in_specs=[VMEM] * z.var,
        out_specs=(VMEM, VMEM),
        scratch_shapes=[pltpu.VMEM((z.var, z.params, LANES), BF16)],
        compiler_params=PARAMS,
        cost_estimate=pl.CostEstimate(flops=10**8, bytes_accessed=10**6, transcendentals=0),
        name="matrices",
    )(*given)
    balanced = pl.pallas_call(
        functools.partial(mixing_kernel, z),
        out_shape=jax.ShapeDtypeStruct((z.var, z.lat, z.rows, LANES), BF16),
        in_specs=[VMEM] * 3,
        out_specs=VMEM,
        compiler_params=PARAMS,
        name="mixing",
    )(packets.reshape(z.var, z.lat, z.rows, LANES), mix, lift)
    balanced = balanced.reshape(z.devices, z.rows, LANES)
    balanced = lax.all_to_all(balanced, ("var", "lat"), 0, 0, tiled=True)
    return pl.pallas_call(
        functools.partial(synthesis_kernel, z),
        out_shape=jax.ShapeDtypeStruct(control.shape, BF16),
        in_specs=[VMEM] * 3,
        out_specs=HBM,
        scratch_shapes=[
            pltpu.SemaphoreType.DMA((z.levels // STRIP,)),
            pltpu.VMEM((z.levels, z.lons + LANES), BF16),
            pltpu.VMEM(((2 * RADIX - 1) * z.levels, 2 * z.sin), BF16),
            pltpu.VMEM(((2 * RADIX - 1) * z.levels, z.points), F32),
        ],
        compiler_params=PARAMS,
        name="synthesis",
    )(balanced, basis, twiddle)


def solution(mesh):
    placed = (
        P("var", "lat", None, None),
        P(),
        P(),
        P("var", None, None),
        P("var", None),
        P("var", None, None),
        P("var", None, None),
    )

    def run(control, row_order, row_length, vertical, amplitude, meridional, balance):
        lat_total, var_total = mesh.shape["lat"], mesh.shape["var"]
        assert control.shape[0] == var_total and control.shape[1] == lat_total
        z = Sizes(lat_total, var_total, control.shape[2], control.shape[3], amplitude.shape[1])
        return jax.shard_map(
            functools.partial(body, z),
            mesh=mesh,
            in_specs=placed,
            out_specs=P("var", "lat", None, None),
            check_vma=False,
        )(control, row_order, row_length, vertical, amplitude, meridional, balance)

    return run
```

```python
import functools
import math

import jax
import jax.numpy as jnp
from jax import lax
from jax.experimental import pallas as pl
from jax.experimental.pallas import tpu as pltpu
from jax.sharding import PartitionSpec as P

RADIX = 4
LANES = 128
SUBLANES = 8
STRIP = 16
F32 = jnp.float32
BF16 = jnp.bfloat16

COS_POLY = (1, -19.7392044, 64.9391174, -85.4501419, 60.1676292, -25.9675999, 6.52865839)
SIN_POLY = (6.28318501, -41.3415909, 81.5999451, -76.6144714, 41.3428841, -12.4712439)

VMEM = pl.BlockSpec(memory_space=pltpu.VMEM)
HBM = pl.BlockSpec(memory_space=pltpu.HBM)
PARAMS = pltpu.CompilerParams(vmem_limit_bytes=32 * 1024 * 1024)


def iota(shape, dim):
    return lax.broadcasted_iota(jnp.int32, shape, dim)


def horner(poly, x):
    total = jnp.full_like(x, poly[-1])
    for term in poly[-2::-1]:
        total = total * x + term
    return total


def cos_sin(turns):
    turns = turns - jnp.round(turns)
    square = turns * turns
    return horner(COS_POLY, square), horner(SIN_POLY, square) * turns


def ceil_div(a, b):
    return -(-a // b)


def round_up(a, b):
    return ceil_div(a, b) * b


def dot(a, b, contract=((1,), (0,))):
    return lax.dot_general(a, b, (contract, ((), ())), preferred_element_type=F32)


class Sizes:
    def __init__(self, lat_total, var_total, levels, lons, waves):
        self.lat, self.var, self.levels, self.lons, self.waves = lat_total, var_total, levels, lons, waves
        self.devices = lat_total * var_total
        self.slots = list(range(lat_total))[::-1]
        self.points = lons // RADIX
        self.tiles = self.points // LANES
        self.block = math.gcd(self.tiles, 2)
        self.kaps = waves // RADIX
        self.rows = round_up(ceil_div(waves, self.devices), SUBLANES)
        assert self.kaps % self.rows == 0 and self.points % LANES == 0 and 2 * levels == LANES and lat_total <= LANES
        self.mixed = lat_total * self.rows
        self.sin = round_up(self.kaps, LANES)
        self.heads = round_up(ceil_div(self.kaps, STRIP), SUBLANES)
        self.params = round_up(levels + lat_total, STRIP)


def own_length(order_ref, length_ref):
    slot = lax.axis_index("lat")
    row = order_ref[slot]
    return slot, row, length_ref[row]


def fetch(sources, targets, sems):
    copies = [pltpu.make_async_copy(s, t, sems.at[i]) for i, (s, t) in enumerate(zip(sources, targets))]
    for copy in copies:
        copy.start()
    return copies


def slot_matrix(z, order_ref, mer_ref):
    def picks(count):
        slot = iota((count, z.lat), 0)
        row = jnp.full((count, z.lat), -1, jnp.int32)
        for t in range(z.lat):
            row = jnp.where(slot == t, order_ref[z.slots[t]], row)
        return (row == iota((count, z.lat), 1)).astype(F32).astype(BF16)

    rows = dot(picks(z.params - z.levels), mer_ref[0]).astype(BF16)
    return dot(rows, picks(LANES), ((1,), (1,)))


def tile(c):
    return slice(c * LANES, (c + 1) * LANES)


def analysis_kernel(z, *refs):
    given, made, held = refs[:7], refs[7:11], refs[11:18]
    sems, field_ref, parts_ref, heads_ref, tails_ref, scale_ref, product_ref = refs[18:]
    order_ref, length_ref, control_ref, vert_ref, amp_ref, mer_ref, bal_ref = held
    packet_ref, params_ref, basis_ref, twiddle_ref = made
    copies = fetch(given, held, sems)
    for at in (0, z.sin):
        basis_ref[at + z.kaps : at + z.sin] = jnp.zeros((z.sin - z.kaps, z.points), BF16)
    field_ref[:, z.lons :] = jnp.zeros((z.levels, LANES), F32)
    parts_ref[z.levels : 2 * z.levels] = jnp.zeros((z.levels, z.points), BF16)
    for copy in copies[:2]:
        copy.wait()
    slot, row, length = own_length(order_ref, length_ref)
    quarter = length // RADIX
    period = jnp.full((1, LANES), length, jnp.int32).astype(F32)
    tail = iota((STRIP, LANES), 0).astype(F32)
    head = iota((z.heads, LANES), 0).astype(F32) * STRIP
    tw_row = iota((2 * RADIX, LANES), 0)
    tw_wave = jnp.where(tw_row < RADIX, tw_row, tw_row - RADIX).astype(F32)
    fraction = jnp.full((1, LANES), quarter, jnp.int32).astype(F32)
    for c in range(z.tiles):
        points = c * LANES + iota((1, LANES), 1)
        step = points.astype(F32) / fraction
        tails_ref[:STRIP, tile(c)], tails_ref[STRIP:, tile(c)] = cos_sin(tail * step)
        head_cos, head_sin = cos_sin(head * step)
        heads_ref[: z.heads, tile(c)] = jnp.where(points < quarter, head_cos, 0.0)
        heads_ref[z.heads :, tile(c)] = jnp.where(points < quarter, head_sin, 0.0)
        tw_cos, tw_sin = cos_sin(tw_wave * (points.astype(F32) / period))
        twiddle_ref[: 2 * RADIX, tile(c)] = jnp.where(tw_row < RADIX, tw_cos, tw_sin)
        twiddle_ref[2 * RADIX :, tile(c)] = jnp.broadcast_to(period, (SUBLANES, LANES))
    for copy in copies[2:]:
        copy.wait()
    field_ref[:, : z.lons] = dot(vert_ref[0], control_ref[0, 0])
    starts = [quarter * j1 for j1 in range(1, RADIX)]
    bases = [pl.multiple_of(s // LANES * LANES, LANES) for s in starts]
    shifts = [(LANES - (s - b)) % LANES for s, b in zip(starts, bases)]
    lane = iota((STRIP, LANES), 1)
    keeps = [(lane < shift) | (shift == 0) for shift in shifts]

    def rolled(i, at, c):
        lanes = pl.ds(pl.multiple_of(bases[i] + c * LANES, LANES), LANES)
        return pltpu.roll(field_ref[at : at + STRIP, lanes], shifts[i], 1)

    before = {}
    for block in range(0, z.tiles, z.block):
        for c in range(block, block + z.block):
            tail_cos, tail_sin = tails_ref[:STRIP, tile(c)], tails_ref[STRIP:, tile(c)]
            for at in range(0, z.kaps, STRIP):
                i = at // STRIP
                head_cos, head_sin = heads_ref[i : i + 1, tile(c)], heads_ref[z.heads + i : z.heads + i + 1, tile(c)]
                basis_ref[at : at + STRIP, tile(c)] = (head_cos * tail_cos - head_sin * tail_sin).astype(BF16)
                to = slice(z.sin + at, z.sin + at + STRIP)
                basis_ref[to, tile(c)] = (head_sin * tail_cos + head_cos * tail_sin).astype(BF16)
        for at in range(0, z.levels, STRIP):
            for c in range(block, block + z.block):
                if c == 0:
                    before[at] = [rolled(i, at, 0) for i in range(RADIX - 1)]
                after = [rolled(i, at, c + 1) for i in range(RADIX - 1)]
                second, third, fourth = [jnp.where(k, a, b) for k, a, b in zip(keeps, before[at], after)]
                before[at] = after
                first = field_ref[at : at + STRIP, tile(c)]
                even, odd = first + third, second + fourth
                real, imag, turned = first - third, second - fourth, even - odd
                cos1, cos2, cos3 = [twiddle_ref[r : r + 1, tile(c)] for r in (1, 2, 3)]
                sin1, sin2, sin3 = [twiddle_ref[RADIX + r : RADIX + r + 1, tile(c)] for r in (1, 2, 3)]
                parts = (
                    (even + odd,),
                    (real * cos1 - imag * sin1, real * sin1 + imag * cos1),
                    (turned * cos2, turned * sin2),
                    (real * cos3 + imag * sin3, real * sin3 - imag * cos3),
                )
                for r, pair in enumerate(parts):
                    for half, part in enumerate(pair):
                        to = (2 * r + half) * z.levels + at
                        parts_ref[to : to + STRIP, tile(c)] = part.astype(BF16)
        lanes = slice(block * LANES, (block + z.block) * LANES)
        basis = jnp.concatenate([basis_ref[: z.kaps, lanes], basis_ref[z.sin : z.sin + z.kaps, lanes]], axis=0)
        product = dot(basis, parts_ref[:, lanes], ((1,), (1,)))
        product_ref[...] = product if block == 0 else product_ref[...] + product
    group = LANES // RADIX
    weights = 1.0 / period, 2.0 / period
    for r in range(RADIX):
        picked = iota((group, LANES), 1) == iota((group, LANES), 0) * RADIX + r
        for at in range(0, z.kaps, group):
            lanes = slice(at * RADIX, at * RADIX + LANES)
            amp = jnp.sum(jnp.where(picked, amp_ref[:, lanes], 0.0), axis=1, keepdims=True)
            wave = (at + iota((group, LANES), 0)) * RADIX + r
            weight = jnp.where(wave == 0, *weights) if at + r == 0 else weights[1]
            scale_ref[r * z.kaps + at : r * z.kaps + at + group] = jnp.where(
                wave <= (length - 1) // 2, weight * amp, 0.0
            )
    params_ref[: z.levels] = jnp.concatenate([bal_ref[0], bal_ref[0]], axis=1)
    params_ref[z.levels :] = slot_matrix(z, order_ref, mer_ref).astype(BF16)
    count = z.kaps // z.rows
    sign = jnp.where(iota((1, LANES), 1) < z.levels, -1.0, 1.0).astype(F32)
    for r in range(RADIX):
        lanes = tile(r)
        for i in range(count):
            rows = slice(i * z.rows, (i + 1) * z.rows)
            from_sin = product_ref[z.kaps + i * z.rows : z.kaps + (i + 1) * z.rows, lanes]
            both = product_ref[rows, lanes] + pltpu.roll(from_sin, z.levels, 1) * sign
            scale = scale_ref[r * z.kaps + i * z.rows : r * z.kaps + (i + 1) * z.rows]
            packet_ref[r * count + i] = (both * scale).astype(BF16)
    if z.devices > RADIX * count:
        packet_ref[RADIX * count :] = jnp.zeros((z.devices - RADIX * count, z.rows, LANES), BF16)


def matrices_kernel(z, *refs):
    *given, mix_ref, bal_ref, all_ref = refs
    own = lax.axis_index("var")
    for step, ref in enumerate(given):
        all_ref[(own + step) % z.var] = ref[...]
    size = z.mixed
    to_cols = (iota((z.lat, size), 0) == iota((z.lat, size), 1) // z.rows).astype(F32).astype(BF16)
    same = iota((size, size), 0) % z.rows == iota((size, size), 1) % z.rows
    halves = iota((LANES, LANES), 0) // z.levels == iota((LANES, LANES), 1) // z.levels
    for v in range(z.var):
        meridional = all_ref[v, z.levels :].astype(F32)[: z.lat, : z.lat].astype(BF16)
        slot_cols = dot(meridional, to_cols).astype(BF16)
        mix_ref[v] = jnp.where(same, dot(to_cols, slot_cols, ((0,), (0,))), 0.0).astype(BF16)
        if v > 0:
            balance = all_ref[v, : z.levels].astype(F32)
            balance = jnp.where(halves, jnp.concatenate([balance, balance], axis=0), 0.0)
            bal_ref[v - 1] = balance.T.astype(BF16)


def mixing_kernel(z, packet_ref, mix_ref, bal_ref, out_ref):
    stream = None
    for v in range(z.var):
        coeffs = packet_ref[:, v].astype(F32).reshape(z.mixed, LANES).astype(BF16)
        blended = dot(mix_ref[v], coeffs)
        if v == 0:
            stream = blended.astype(BF16)
        else:
            blended = blended + dot(stream, bal_ref[v - 1])
        blended = blended.reshape(z.lat, z.rows, LANES)
        for s in range(z.lat):
            out_ref[s, v] = blended[s].astype(BF16)


def synthesis_kernel(z, spectra_ref, basis_ref, twiddle_ref, out_ref, sems, field_ref, lhs_ref, parts_ref):
    period = twiddle_ref[2 * RADIX :, :LANES].astype(jnp.int32)
    length = jnp.max(period)
    kap = iota((z.kaps, LANES), 0)
    count = z.kaps // z.rows
    half = z.levels // 2
    kinds = 2 * RADIX - 1
    for at in (0, z.sin):
        lhs_ref[:, at + z.kaps : at + z.sin] = jnp.zeros((2 * half * kinds, z.sin - z.kaps), BF16)
    for r in range(RADIX):
        part = spectra_ref[r * count : (r + 1) * count].astype(F32).reshape(z.kaps, LANES)
        part = jnp.where(kap * RADIX + r <= (period[0:1] - 1) // 2, part, 0.0)
        part = part.astype(BF16).T
        for i in range(2):
            from_cos = part[i * half : (i + 1) * half]
            from_sin = part[z.levels + i * half : z.levels + (i + 1) * half]
            pairs = [(from_cos, from_sin)] if r == 0 else [(from_cos, from_sin), (-from_sin, from_cos)]
            for kind, pair in zip((2 * r - 1, 2 * r) if r else (0,), pairs):
                to = slice((i * kinds + kind) * half, (i * kinds + kind + 1) * half)
                lhs_ref[to, : z.kaps] = pair[0]
                lhs_ref[to, z.sin : z.sin + z.kaps] = pair[1]
    quarter = length // RADIX
    starts = [quarter * j1 for j1 in range(1, RADIX)]
    bases = [pl.multiple_of(s // LANES * LANES, LANES) for s in starts]
    shifts = [s - b for s, b in zip(starts, bases)]
    wide = z.points + LANES
    field_ref[:, wide:] = jnp.zeros((z.levels, z.lons + LANES - wide), BF16)
    keep = [iota((STRIP, LANES), 1) < shift for shift in shifts]
    zero = jnp.zeros((STRIP, LANES), F32)
    for i in range(2):
        rows = slice(i * kinds * half, (i + 1) * kinds * half)
        parts_ref[rows] = dot(lhs_ref[rows], basis_ref[...])
    sent = []
    for at in range(0, z.levels, STRIP):
        rows = slice(at, at + STRIP)
        first = at // half * kinds * half + at % half
        quarters = [[], [], [], []]
        for c in range(z.tiles):
            cos1, cos2, cos3 = [twiddle_ref[r : r + 1, tile(c)] for r in (1, 2, 3)]
            sin1, sin2, sin3 = [twiddle_ref[RADIX + r : RADIX + r + 1, tile(c)] for r in (1, 2, 3)]
            w0, re1, im1, re2, im2, re3, im3 = [
                parts_ref[first + kind * half : first + kind * half + STRIP, tile(c)] for kind in range(kinds)
            ]
            w2 = re2 * cos2 - im2 * sin2
            cross = (re1 * cos1 - im1 * sin1) + (re3 * cos3 - im3 * sin3)
            turn = (re1 * sin1 + im1 * cos1) - (re3 * sin3 + im3 * cos3)
            even, odd = w0 + w2, w0 - w2
            field_ref[rows, tile(c)] = (even + cross).astype(BF16)
            for j1, part in ((1, odd - turn), (2, even - cross), (3, odd + turn)):
                quarters[j1].append(pltpu.roll(part, shifts[j1 - 1], 1))
        field_ref[rows, tile(z.tiles)] = zero.astype(BF16)
        for j1 in range(1, RADIX):
            pieces = zip([zero] + quarters[j1], quarters[j1] + [zero])
            for c, (left, right) in enumerate(pieces):
                lanes = pl.ds(pl.multiple_of(bases[j1 - 1] + c * LANES, LANES), LANES)
                piece = jnp.where(keep[j1 - 1], left, right)
                if c == 0:
                    piece = piece + field_ref[rows, lanes].astype(F32)
                field_ref[rows, lanes] = piece.astype(BF16)
        sent += fetch(
            (field_ref.at[pl.ds(at, STRIP), pl.ds(0, z.lons)],),
            (out_ref.at[0, 0, pl.ds(at, STRIP)],),
            sems.at[pl.ds(at // STRIP, 1)],
        )
    for copy in sent:
        copy.wait()


def exchange(z, chunks):
    peers = [v * z.lat + slot for slot in z.slots for v in range(z.var)]
    return lax.all_to_all(chunks, ("var", "lat"), 0, 0, axis_index_groups=[peers], tiled=True)


def body(z, control, row_order, row_length, vertical, amplitude, meridional, balance):
    arguments = (row_order, row_length, control, vertical, amplitude, meridional, balance)
    made = (
        jax.ShapeDtypeStruct((z.devices, z.rows, LANES), BF16),
        jax.ShapeDtypeStruct((z.params, LANES), BF16),
        jax.ShapeDtypeStruct((2 * z.sin, z.points), BF16),
        jax.ShapeDtypeStruct((2 * RADIX + SUBLANES, z.points), F32),
    )
    packets, params, basis, twiddle = pl.pallas_call(
        functools.partial(analysis_kernel, z),
        out_shape=made,
        in_specs=[HBM] * len(arguments),
        out_specs=(VMEM,) * len(made),
        scratch_shapes=[
            *[pltpu.SMEM(x.shape, x.dtype) for x in arguments[:2]],
            *[pltpu.VMEM(x.shape, x.dtype) for x in arguments[2:]],
            pltpu.SemaphoreType.DMA((len(arguments),)),
            pltpu.VMEM((z.levels, z.lons + LANES), F32),
            pltpu.VMEM((2 * RADIX * z.levels, z.points), BF16),
            pltpu.VMEM((2 * z.heads, z.points), F32),
            pltpu.VMEM((2 * STRIP, z.points), F32),
            pltpu.VMEM((z.waves, LANES), F32),
            pltpu.VMEM((2 * z.kaps, RADIX * LANES), F32),
        ],
        compiler_params=PARAMS,
        name="analysis",
    )(*[pltpu.with_memory_space_constraint(x, pltpu.HBM) for x in arguments])
    given = [params]
    for step in range(1, z.var):
        given.append(lax.ppermute(params, "var", [((i + step) % z.var, i) for i in range(z.var)]))
    packets = exchange(z, packets)
    mix, lift = pl.pallas_call(
        functools.partial(matrices_kernel, z),
        out_shape=(
            jax.ShapeDtypeStruct((z.var, z.mixed, z.mixed), BF16),
            jax.ShapeDtypeStruct((z.var - 1, LANES, LANES), BF16),
        ),
        in_specs=[VMEM] * z.var,
        out_specs=(VMEM, VMEM),
        scratch_shapes=[pltpu.VMEM((z.var, z.params, LANES), BF16)],
        compiler_params=PARAMS,
        cost_estimate=pl.CostEstimate(flops=10**8, bytes_accessed=10**6, transcendentals=0),
        name="matrices",
    )(*given)
    balanced = pl.pallas_call(
        functools.partial(mixing_kernel, z),
        out_shape=jax.ShapeDtypeStruct((z.lat, z.var, z.rows, LANES), BF16),
        in_specs=[VMEM] * 3,
        out_specs=VMEM,
        compiler_params=PARAMS,
        name="mixing",
    )(packets.reshape(z.lat, z.var, z.rows, LANES), mix, lift)
    balanced = balanced.reshape(z.devices, z.rows, LANES)
    balanced = exchange(z, balanced)
    return pl.pallas_call(
        functools.partial(synthesis_kernel, z),
        out_shape=jax.ShapeDtypeStruct(control.shape, BF16),
        in_specs=[VMEM] * 3,
        out_specs=HBM,
        scratch_shapes=[
            pltpu.SemaphoreType.DMA((z.levels // STRIP,)),
            pltpu.VMEM((z.levels, z.lons + LANES), BF16),
            pltpu.VMEM(((2 * RADIX - 1) * z.levels, 2 * z.sin), BF16),
            pltpu.VMEM(((2 * RADIX - 1) * z.levels, z.points), F32),
        ],
        compiler_params=PARAMS,
        name="synthesis",
    )(balanced, basis, twiddle)


def solution(mesh):
    placed = (
        P("var", "lat", None, None),
        P(),
        P(),
        P("var", None, None),
        P("var", None),
        P("var", None, None),
        P("var", None, None),
    )

    def run(control, row_order, row_length, vertical, amplitude, meridional, balance):
        lat_total, var_total = mesh.shape["lat"], mesh.shape["var"]
        assert control.shape[0] == var_total and control.shape[1] == lat_total
        z = Sizes(lat_total, var_total, control.shape[2], control.shape[3], amplitude.shape[1])
        return jax.shard_map(
            functools.partial(body, z),
            mesh=mesh,
            in_specs=placed,
            out_specs=P("var", "lat", None, None),
            check_vma=False,
        )(control, row_order, row_length, vertical, amplitude, meridional, balance)

    return run
```

```python
import functools
import math

import jax
import jax.numpy as jnp
from jax import lax
from jax.experimental import pallas as pl
from jax.experimental.pallas import tpu as pltpu
from jax.sharding import PartitionSpec as P

RADIX = 4
LANES = 128
SUBLANES = 8
STRIP = 16
F32 = jnp.float32
BF16 = jnp.bfloat16

COS_POLY = (1, -19.7392044, 64.9391174, -85.4501419, 60.1676292, -25.9675999, 6.52865839)
SIN_POLY = (6.28318501, -41.3415909, 81.5999451, -76.6144714, 41.3428841, -12.4712439)

VMEM = pl.BlockSpec(memory_space=pltpu.VMEM)
HBM = pl.BlockSpec(memory_space=pltpu.HBM)
PARAMS = pltpu.CompilerParams(vmem_limit_bytes=32 * 1024 * 1024)


def iota(shape, dim):
    return lax.broadcasted_iota(jnp.int32, shape, dim)


def horner(poly, x):
    total = jnp.full_like(x, poly[-1])
    for term in poly[-2::-1]:
        total = total * x + term
    return total


def cos_sin(turns):
    turns = turns - jnp.round(turns)
    square = turns * turns
    return horner(COS_POLY, square), horner(SIN_POLY, square) * turns


def ceil_div(a, b):
    return -(-a // b)


def round_up(a, b):
    return ceil_div(a, b) * b


def dot(a, b, contract=((1,), (0,))):
    return lax.dot_general(a, b, (contract, ((), ())), preferred_element_type=F32)


class Sizes:
    def __init__(self, lat_total, var_total, levels, lons, waves):
        self.lat, self.var, self.levels, self.lons, self.waves = lat_total, var_total, levels, lons, waves
        self.devices = lat_total * var_total
        self.points = lons // RADIX
        self.tiles = self.points // LANES
        self.block = math.gcd(self.tiles, 2)
        self.kaps = waves // RADIX
        self.rows = round_up(ceil_div(waves, self.devices), SUBLANES)
        assert self.kaps % self.rows == 0 and self.points % LANES == 0 and 2 * levels == LANES and lat_total <= LANES
        self.mixed = lat_total * self.rows
        self.sin = round_up(self.kaps, LANES)
        self.heads = round_up(ceil_div(self.kaps, STRIP), SUBLANES)
        self.params = round_up(levels + lat_total, STRIP)


def own_length(order_ref, length_ref):
    slot = lax.axis_index("lat")
    row = order_ref[slot]
    return slot, row, length_ref[row]


def fetch(sources, targets, sems, priorities=None):
    copies = [pltpu.make_async_copy(s, t, sems.at[i]) for i, (s, t) in enumerate(zip(sources, targets))]
    for i, copy in enumerate(copies):
        copy.start(priority=priorities[i] if priorities else 0)
    return copies


def slot_matrix(z, order_ref, mer_ref):
    def picks(count):
        slot = iota((count, z.lat), 0)
        row = jnp.full((count, z.lat), -1, jnp.int32)
        for t in range(z.lat):
            row = jnp.where(slot == t, order_ref[t], row)
        return (row == iota((count, z.lat), 1)).astype(F32).astype(BF16)

    rows = dot(picks(z.params - z.levels), mer_ref[0]).astype(BF16)
    return dot(rows, picks(LANES), ((1,), (1,)))


def tile(c):
    return slice(c * LANES, (c + 1) * LANES)


def analysis_kernel(z, *refs):
    given, made, held = refs[:7], refs[7:11], refs[11:18]
    sems, field_ref, parts_ref, heads_ref, tails_ref, scale_ref, product_ref = refs[18:]
    order_ref, length_ref, control_ref, vert_ref, amp_ref, mer_ref, bal_ref = held
    packet_ref, params_ref, basis_ref, twiddle_ref = made
    strips = [pl.ds(at, STRIP) for at in range(0, z.levels, STRIP)]
    copies = fetch(
        [*given[:2], *[given[2].at[0, 0, strip] for strip in strips], *given[3:]],
        [*held[:2], *[control_ref.at[0, 0, strip] for strip in strips], *held[3:]],
        sems,
        [0, 1, *[i % 2 for i in range(len(strips))], *[i % 2 for i in range(len(given) - 3)]],
    )
    for at in (0, z.sin):
        basis_ref[at + z.kaps : at + z.sin] = jnp.zeros((z.sin - z.kaps, z.points), BF16)
    field_ref[:, z.lons :] = jnp.zeros((z.levels, LANES), F32)
    parts_ref[z.levels : 2 * z.levels] = jnp.zeros((z.levels, z.points), BF16)
    for copy in copies[:2]:
        copy.wait()
    slot, row, length = own_length(order_ref, length_ref)
    quarter = length // RADIX
    period = jnp.full((1, LANES), length, jnp.int32).astype(F32)
    tail = iota((STRIP, LANES), 0).astype(F32)
    head = iota((z.heads, LANES), 0).astype(F32) * STRIP
    tw_row = iota((2 * RADIX, LANES), 0)
    tw_wave = jnp.where(tw_row < RADIX, tw_row, tw_row - RADIX).astype(F32)
    fraction = jnp.full((1, LANES), quarter, jnp.int32).astype(F32)
    for c in range(z.tiles):
        points = c * LANES + iota((1, LANES), 1)
        step = points.astype(F32) / fraction
        tails_ref[:STRIP, tile(c)], tails_ref[STRIP:, tile(c)] = cos_sin(tail * step)
        head_cos, head_sin = cos_sin(head * step)
        heads_ref[: z.heads, tile(c)] = jnp.where(points < quarter, head_cos, 0.0)
        heads_ref[z.heads :, tile(c)] = jnp.where(points < quarter, head_sin, 0.0)
        tw_cos, tw_sin = cos_sin(tw_wave * (points.astype(F32) / period))
        twiddle_ref[: 2 * RADIX, tile(c)] = jnp.where(tw_row < RADIX, tw_cos, tw_sin)
        twiddle_ref[2 * RADIX :, tile(c)] = jnp.broadcast_to(period, (SUBLANES, LANES))
    for copy in copies[2:]:
        copy.wait()
    field_ref[:, : z.lons] = dot(vert_ref[0], control_ref[0, 0])
    starts = [quarter * j1 for j1 in range(1, RADIX)]
    bases = [pl.multiple_of(s // LANES * LANES, LANES) for s in starts]
    shifts = [(LANES - (s - b)) % LANES for s, b in zip(starts, bases)]
    lane = iota((STRIP, LANES), 1)
    keeps = [(lane < shift) | (shift == 0) for shift in shifts]

    def rolled(i, at, c):
        lanes = pl.ds(pl.multiple_of(bases[i] + c * LANES, LANES), LANES)
        return pltpu.roll(field_ref[at : at + STRIP, lanes], shifts[i], 1)

    before = {}
    for block in range(0, z.tiles, z.block):
        for c in range(block, block + z.block):
            tail_cos, tail_sin = tails_ref[:STRIP, tile(c)], tails_ref[STRIP:, tile(c)]
            for at in range(0, z.kaps, STRIP):
                i = at // STRIP
                head_cos, head_sin = heads_ref[i : i + 1, tile(c)], heads_ref[z.heads + i : z.heads + i + 1, tile(c)]
                basis_ref[at : at + STRIP, tile(c)] = (head_cos * tail_cos - head_sin * tail_sin).astype(BF16)
                to = slice(z.sin + at, z.sin + at + STRIP)
                basis_ref[to, tile(c)] = (head_sin * tail_cos + head_cos * tail_sin).astype(BF16)
        for at in range(0, z.levels, STRIP):
            for c in range(block, block + z.block):
                if c == 0:
                    before[at] = [rolled(i, at, 0) for i in range(RADIX - 1)]
                after = [rolled(i, at, c + 1) for i in range(RADIX - 1)]
                second, third, fourth = [jnp.where(k, a, b) for k, a, b in zip(keeps, before[at], after)]
                before[at] = after
                first = field_ref[at : at + STRIP, tile(c)]
                even, odd = first + third, second + fourth
                real, imag, turned = first - third, second - fourth, even - odd
                cos1, cos2, cos3 = [twiddle_ref[r : r + 1, tile(c)] for r in (1, 2, 3)]
                sin1, sin2, sin3 = [twiddle_ref[RADIX + r : RADIX + r + 1, tile(c)] for r in (1, 2, 3)]
                parts = (
                    (even + odd,),
                    (real * cos1 - imag * sin1, real * sin1 + imag * cos1),
                    (turned * cos2, turned * sin2),
                    (real * cos3 + imag * sin3, real * sin3 - imag * cos3),
                )
                for r, pair in enumerate(parts):
                    for half, part in enumerate(pair):
                        to = (2 * r + half) * z.levels + at
                        parts_ref[to : to + STRIP, tile(c)] = part.astype(BF16)
        lanes = slice(block * LANES, (block + z.block) * LANES)
        basis = jnp.concatenate([basis_ref[: z.kaps, lanes], basis_ref[z.sin : z.sin + z.kaps, lanes]], axis=0)
        product = dot(basis, parts_ref[:, lanes], ((1,), (1,)))
        product_ref[...] = product if block == 0 else product_ref[...] + product
    group = LANES // RADIX
    weights = 1.0 / period, 2.0 / period
    for r in range(RADIX):
        picked = iota((group, LANES), 1) == iota((group, LANES), 0) * RADIX + r
        for at in range(0, z.kaps, group):
            lanes = slice(at * RADIX, at * RADIX + LANES)
            amp = jnp.sum(jnp.where(picked, amp_ref[:, lanes], 0.0), axis=1, keepdims=True)
            wave = (at + iota((group, LANES), 0)) * RADIX + r
            weight = jnp.where(wave == 0, *weights) if at + r == 0 else weights[1]
            scale_ref[r * z.kaps + at : r * z.kaps + at + group] = jnp.where(
                wave <= (length - 1) // 2, weight * amp, 0.0
            )
    params_ref[: z.levels] = jnp.concatenate([bal_ref[0], bal_ref[0]], axis=1)
    params_ref[z.levels :] = slot_matrix(z, order_ref, mer_ref).astype(BF16)
    count = z.kaps // z.rows
    sign = jnp.where(iota((1, LANES), 1) < z.levels, -1.0, 1.0).astype(F32)
    for r in range(RADIX):
        lanes = tile(r)
        for i in range(count):
            rows = slice(i * z.rows, (i + 1) * z.rows)
            from_sin = product_ref[z.kaps + i * z.rows : z.kaps + (i + 1) * z.rows, lanes]
            both = product_ref[rows, lanes] + pltpu.roll(from_sin, z.levels, 1) * sign
            scale = scale_ref[r * z.kaps + i * z.rows : r * z.kaps + (i + 1) * z.rows]
            packet_ref[r * count + i] = (both * scale).astype(BF16)
    if z.devices > RADIX * count:
        packet_ref[RADIX * count :] = jnp.zeros((z.devices - RADIX * count, z.rows, LANES), BF16)


def matrices_kernel(z, *refs):
    *given, mix_ref, bal_ref, all_ref = refs
    own = lax.axis_index("var")
    for step, ref in enumerate(given):
        all_ref[(own + step) % z.var] = ref[...]
    size = z.mixed
    to_cols = (iota((z.lat, size), 0) == iota((z.lat, size), 1) // z.rows).astype(F32).astype(BF16)
    same = iota((size, size), 0) % z.rows == iota((size, size), 1) % z.rows
    halves = iota((LANES, LANES), 0) // z.levels == iota((LANES, LANES), 1) // z.levels
    for v in range(z.var):
        meridional = all_ref[v, z.levels :].astype(F32)[: z.lat, : z.lat].astype(BF16)
        slot_cols = dot(meridional, to_cols).astype(BF16)
        mix_ref[v] = jnp.where(same, dot(to_cols, slot_cols, ((0,), (0,))), 0.0).astype(BF16)
        if v > 0:
            balance = all_ref[v, : z.levels].astype(F32)
            balance = jnp.where(halves, jnp.concatenate([balance, balance], axis=0), 0.0)
            bal_ref[v - 1] = balance.T.astype(BF16)


def mixing_kernel(z, packet_ref, mix_ref, bal_ref, out_ref):
    stream = None
    for v in range(z.var):
        coeffs = packet_ref[v].astype(F32).reshape(z.mixed, LANES).astype(BF16)
        blended = dot(mix_ref[v], coeffs)
        if v == 0:
            stream = blended.astype(BF16)
        else:
            blended = blended + dot(stream, bal_ref[v - 1])
        blended = blended.reshape(z.lat, z.rows, LANES)
        for s in range(z.lat):
            out_ref[v, s] = blended[s].astype(BF16)


def synthesis_kernel(z, spectra_ref, basis_ref, twiddle_ref, out_ref, sems, field_ref, lhs_ref, parts_ref):
    period = twiddle_ref[2 * RADIX :, :LANES].astype(jnp.int32)
    length = jnp.max(period)
    kap = iota((z.kaps, LANES), 0)
    count = z.kaps // z.rows
    half = z.levels // 2
    kinds = 2 * RADIX - 1
    for at in (0, z.sin):
        lhs_ref[:, at + z.kaps : at + z.sin] = jnp.zeros((2 * half * kinds, z.sin - z.kaps), BF16)
    for r in range(RADIX):
        part = spectra_ref[r * count : (r + 1) * count].astype(F32).reshape(z.kaps, LANES)
        part = jnp.where(kap * RADIX + r <= (period[0:1] - 1) // 2, part, 0.0)
        part = part.astype(BF16).T
        for i in range(2):
            from_cos = part[i * half : (i + 1) * half]
            from_sin = part[z.levels + i * half : z.levels + (i + 1) * half]
            pairs = [(from_cos, from_sin)] if r == 0 else [(from_cos, from_sin), (-from_sin, from_cos)]
            for kind, pair in zip((2 * r - 1, 2 * r) if r else (0,), pairs):
                to = slice((i * kinds + kind) * half, (i * kinds + kind + 1) * half)
                lhs_ref[to, : z.kaps] = pair[0]
                lhs_ref[to, z.sin : z.sin + z.kaps] = pair[1]
    quarter = length // RADIX
    starts = [quarter * j1 for j1 in range(1, RADIX)]
    bases = [pl.multiple_of(s // LANES * LANES, LANES) for s in starts]
    shifts = [s - b for s, b in zip(starts, bases)]
    wide = z.points + LANES
    field_ref[:, wide:] = jnp.zeros((z.levels, z.lons + LANES - wide), BF16)
    keep = [iota((STRIP, LANES), 1) < shift for shift in shifts]
    zero = jnp.zeros((STRIP, LANES), F32)
    for i in range(2):
        rows = slice(i * kinds * half, (i + 1) * kinds * half)
        parts_ref[rows] = dot(lhs_ref[rows], basis_ref[...])
    sent = []
    for at in range(0, z.levels, STRIP):
        rows = slice(at, at + STRIP)
        first = at // half * kinds * half + at % half
        quarters = [[], [], [], []]
        for c in range(z.tiles):
            cos1, cos2, cos3 = [twiddle_ref[r : r + 1, tile(c)] for r in (1, 2, 3)]
            sin1, sin2, sin3 = [twiddle_ref[RADIX + r : RADIX + r + 1, tile(c)] for r in (1, 2, 3)]
            w0, re1, im1, re2, im2, re3, im3 = [
                parts_ref[first + kind * half : first + kind * half + STRIP, tile(c)] for kind in range(kinds)
            ]
            w2 = re2 * cos2 - im2 * sin2
            cross = (re1 * cos1 - im1 * sin1) + (re3 * cos3 - im3 * sin3)
            turn = (re1 * sin1 + im1 * cos1) - (re3 * sin3 + im3 * cos3)
            even, odd = w0 + w2, w0 - w2
            field_ref[rows, tile(c)] = (even + cross).astype(BF16)
            for j1, part in ((1, odd - turn), (2, even - cross), (3, odd + turn)):
                quarters[j1].append(pltpu.roll(part, shifts[j1 - 1], 1))
        field_ref[rows, tile(z.tiles)] = zero.astype(BF16)
        for j1 in range(1, RADIX):
            pieces = zip([zero] + quarters[j1], quarters[j1] + [zero])
            for c, (left, right) in enumerate(pieces):
                lanes = pl.ds(pl.multiple_of(bases[j1 - 1] + c * LANES, LANES), LANES)
                piece = jnp.where(keep[j1 - 1], left, right)
                if c == 0:
                    piece = piece + field_ref[rows, lanes].astype(F32)
                field_ref[rows, lanes] = piece.astype(BF16)
        sent += fetch(
            (field_ref.at[pl.ds(at, STRIP), pl.ds(0, z.lons)],),
            (out_ref.at[0, 0, pl.ds(at, STRIP)],),
            sems.at[pl.ds(at // STRIP, 1)],
        )
    for copy in sent:
        copy.wait()


def body(z, control, row_order, row_length, vertical, amplitude, meridional, balance):
    arguments = (row_order, row_length, control, vertical, amplitude, meridional, balance)
    made = (
        jax.ShapeDtypeStruct((z.devices, z.rows, LANES), BF16),
        jax.ShapeDtypeStruct((z.params, LANES), BF16),
        jax.ShapeDtypeStruct((2 * z.sin, z.points), BF16),
        jax.ShapeDtypeStruct((2 * RADIX + SUBLANES, z.points), F32),
    )
    packets, params, basis, twiddle = pl.pallas_call(
        functools.partial(analysis_kernel, z),
        out_shape=made,
        in_specs=[HBM] * len(arguments),
        out_specs=(VMEM,) * len(made),
        scratch_shapes=[
            *[pltpu.SMEM(x.shape, x.dtype) for x in arguments[:2]],
            *[pltpu.VMEM(x.shape, x.dtype) for x in arguments[2:]],
            pltpu.SemaphoreType.DMA((len(arguments) - 1 + z.levels // STRIP,)),
            pltpu.VMEM((z.levels, z.lons + LANES), F32),
            pltpu.VMEM((2 * RADIX * z.levels, z.points), BF16),
            pltpu.VMEM((2 * z.heads, z.points), F32),
            pltpu.VMEM((2 * STRIP, z.points), F32),
            pltpu.VMEM((z.waves, LANES), F32),
            pltpu.VMEM((2 * z.kaps, RADIX * LANES), F32),
        ],
        compiler_params=PARAMS,
        name="analysis",
    )(*[pltpu.with_memory_space_constraint(x, pltpu.HBM) for x in arguments])
    given = [params]
    for step in range(1, z.var):
        given.append(lax.ppermute(params, "var", [((i + step) % z.var, i) for i in range(z.var)]))
    packets = lax.all_to_all(packets, ("var", "lat"), 0, 0, tiled=True)
    mix, lift = pl.pallas_call(
        functools.partial(matrices_kernel, z),
        out_shape=(
            jax.ShapeDtypeStruct((z.var, z.mixed, z.mixed), BF16),
            jax.ShapeDtypeStruct((z.var - 1, LANES, LANES), BF16),
        ),
        in_specs=[VMEM] * z.var,
        out_specs=(VMEM, VMEM),
        scratch_shapes=[pltpu.VMEM((z.var, z.params, LANES), BF16)],
        compiler_params=PARAMS,
        cost_estimate=pl.CostEstimate(flops=10**8, bytes_accessed=10**6, transcendentals=0),
        name="matrices",
    )(*given)
    balanced = pl.pallas_call(
        functools.partial(mixing_kernel, z),
        out_shape=jax.ShapeDtypeStruct((z.var, z.lat, z.rows, LANES), BF16),
        in_specs=[VMEM] * 3,
        out_specs=VMEM,
        compiler_params=PARAMS,
        name="mixing",
    )(packets.reshape(z.var, z.lat, z.rows, LANES), mix, lift)
    balanced = balanced.reshape(z.devices, z.rows, LANES)
    balanced = lax.all_to_all(balanced, ("var", "lat"), 0, 0, tiled=True)
    return pl.pallas_call(
        functools.partial(synthesis_kernel, z),
        out_shape=jax.ShapeDtypeStruct(control.shape, BF16),
        in_specs=[VMEM] * 3,
        out_specs=HBM,
        scratch_shapes=[
            pltpu.SemaphoreType.DMA((z.levels // STRIP,)),
            pltpu.VMEM((z.levels, z.lons + LANES), BF16),
            pltpu.VMEM(((2 * RADIX - 1) * z.levels, 2 * z.sin), BF16),
            pltpu.VMEM(((2 * RADIX - 1) * z.levels, z.points), F32),
        ],
        compiler_params=PARAMS,
        name="synthesis",
    )(balanced, basis, twiddle)


def solution(mesh):
    placed = (
        P("var", "lat", None, None),
        P(),
        P(),
        P("var", None, None),
        P("var", None),
        P("var", None, None),
        P("var", None, None),
    )

    def run(control, row_order, row_length, vertical, amplitude, meridional, balance):
        lat_total, var_total = mesh.shape["lat"], mesh.shape["var"]
        assert control.shape[0] == var_total and control.shape[1] == lat_total
        z = Sizes(lat_total, var_total, control.shape[2], control.shape[3], amplitude.shape[1])
        return jax.shard_map(
            functools.partial(body, z),
            mesh=mesh,
            in_specs=placed,
            out_specs=P("var", "lat", None, None),
            check_vma=False,
        )(control, row_order, row_length, vertical, amplitude, meridional, balance)

    return run
```

```python
import functools
import math

import jax
import jax.numpy as jnp
from jax import lax
from jax.experimental import pallas as pl
from jax.experimental.pallas import tpu as pltpu
from jax.sharding import PartitionSpec as P

RADIX = 4
LANES = 128
SUBLANES = 8
STRIP = 16
F32 = jnp.float32
BF16 = jnp.bfloat16

COS_POLY = (1, -19.7392044, 64.9391174, -85.4501419, 60.1676292, -25.9675999, 6.52865839)
SIN_POLY = (6.28318501, -41.3415909, 81.5999451, -76.6144714, 41.3428841, -12.4712439)

VMEM = pl.BlockSpec(memory_space=pltpu.VMEM)
HBM = pl.BlockSpec(memory_space=pltpu.HBM)
PARAMS = pltpu.CompilerParams(vmem_limit_bytes=32 * 1024 * 1024)


def iota(shape, dim):
    return lax.broadcasted_iota(jnp.int32, shape, dim)


def horner(poly, x):
    total = jnp.full_like(x, poly[-1])
    for term in poly[-2::-1]:
        total = total * x + term
    return total


def cos_sin(turns):
    turns = turns - jnp.round(turns)
    square = turns * turns
    return horner(COS_POLY, square), horner(SIN_POLY, square) * turns


def ceil_div(a, b):
    return -(-a // b)


def round_up(a, b):
    return ceil_div(a, b) * b


def dot(a, b, contract=((1,), (0,))):
    return lax.dot_general(a, b, (contract, ((), ())), preferred_element_type=F32)


class Sizes:
    def __init__(self, lat_total, var_total, levels, lons, waves):
        self.lat, self.var, self.levels, self.lons, self.waves = lat_total, var_total, levels, lons, waves
        self.devices = lat_total * var_total
        self.points = lons // RADIX
        self.tiles = self.points // LANES
        self.block = math.gcd(self.tiles, 2)
        self.kaps = waves // RADIX
        self.rows = round_up(ceil_div(waves, self.devices), SUBLANES)
        assert self.kaps % self.rows == 0 and self.points % LANES == 0 and 2 * levels == LANES and lat_total <= LANES
        self.mixed = lat_total * self.rows
        self.sin = round_up(self.kaps, LANES)
        self.heads = round_up(ceil_div(self.kaps, STRIP), SUBLANES)
        self.params = round_up(levels + lat_total, STRIP)


def own_length(order_ref, length_ref):
    slot = lax.axis_index("lat")
    row = order_ref[slot]
    return slot, row, length_ref[row]


def fetch(sources, targets, sems):
    copies = [pltpu.make_async_copy(s, t, sems.at[i]) for i, (s, t) in enumerate(zip(sources, targets))]
    for copy in copies:
        copy.start()
    return copies


def slot_matrix(z, order_ref, mer_ref):
    def picks(count):
        slot = iota((count, z.lat), 0)
        row = jnp.full((count, z.lat), -1, jnp.int32)
        for t in range(z.lat):
            row = jnp.where(slot == t, order_ref[t], row)
        return (row == iota((count, z.lat), 1)).astype(F32).astype(BF16)

    rows = dot(picks(z.params - z.levels), mer_ref[0]).astype(BF16)
    return dot(rows, picks(LANES), ((1,), (1,)))


def tile(c):
    return slice(c * LANES, (c + 1) * LANES)


def analysis_kernel(z, *refs):
    given, made, held = refs[:7], refs[7:11], refs[11:18]
    sems, field_ref, parts_ref, heads_ref, tails_ref, scale_ref, product_ref = refs[18:]
    order_ref, length_ref, control_ref, vert_ref, amp_ref, mer_ref, bal_ref = held
    packet_ref, params_ref, basis_ref, twiddle_ref = made
    copies = fetch(given, held, sems)
    for at in (0, z.sin):
        basis_ref[at + z.kaps : at + z.sin] = jnp.zeros((z.sin - z.kaps, z.points), BF16)
    field_ref[:, z.lons :] = jnp.zeros((z.levels, LANES), F32)
    parts_ref[z.levels : 2 * z.levels] = jnp.zeros((z.levels, z.points), BF16)
    for copy in copies[:2]:
        copy.wait()
    slot, row, length = own_length(order_ref, length_ref)
    quarter = length // RADIX
    period = jnp.full((1, LANES), length, jnp.int32).astype(F32)
    tail = iota((STRIP, LANES), 0).astype(F32)
    head = iota((z.heads, LANES), 0).astype(F32) * STRIP
    tw_row = iota((2 * RADIX, LANES), 0)
    tw_wave = jnp.where(tw_row < RADIX, tw_row, tw_row - RADIX).astype(F32)
    fraction = jnp.full((1, LANES), quarter, jnp.int32).astype(F32)
    for c in range(z.tiles):
        points = c * LANES + iota((1, LANES), 1)
        step = points.astype(F32) / fraction
        tails_ref[:STRIP, tile(c)], tails_ref[STRIP:, tile(c)] = cos_sin(tail * step)
        head_cos, head_sin = cos_sin(head * step)
        heads_ref[: z.heads, tile(c)] = jnp.where(points < quarter, head_cos, 0.0)
        heads_ref[z.heads :, tile(c)] = jnp.where(points < quarter, head_sin, 0.0)
        tw_cos, tw_sin = cos_sin(tw_wave * (points.astype(F32) / period))
        twiddle_ref[: 2 * RADIX, tile(c)] = jnp.where(tw_row < RADIX, tw_cos, tw_sin)
        twiddle_ref[2 * RADIX :, tile(c)] = jnp.broadcast_to(period, (SUBLANES, LANES))
    for c in range(z.tiles):
        tail_cos, tail_sin = tails_ref[:STRIP, tile(c)], tails_ref[STRIP:, tile(c)]
        for at in range(0, z.kaps, STRIP):
            i = at // STRIP
            head_cos, head_sin = heads_ref[i : i + 1, tile(c)], heads_ref[z.heads + i : z.heads + i + 1, tile(c)]
            basis_ref[at : at + STRIP, tile(c)] = (head_cos * tail_cos - head_sin * tail_sin).astype(BF16)
            to = slice(z.sin + at, z.sin + at + STRIP)
            basis_ref[to, tile(c)] = (head_sin * tail_cos + head_cos * tail_sin).astype(BF16)
    for copy in copies[4:]:
        copy.wait()
    group = LANES // RADIX
    weights = 1.0 / period, 2.0 / period
    for r in range(RADIX):
        picked = iota((group, LANES), 1) == iota((group, LANES), 0) * RADIX + r
        for at in range(0, z.kaps, group):
            lanes = slice(at * RADIX, at * RADIX + LANES)
            amp = jnp.sum(jnp.where(picked, amp_ref[:, lanes], 0.0), axis=1, keepdims=True)
            wave = (at + iota((group, LANES), 0)) * RADIX + r
            weight = jnp.where(wave == 0, *weights) if at + r == 0 else weights[1]
            scale_ref[r * z.kaps + at : r * z.kaps + at + group] = jnp.where(
                wave <= (length - 1) // 2, weight * amp, 0.0
            )
    params_ref[: z.levels] = jnp.concatenate([bal_ref[0], bal_ref[0]], axis=1)
    params_ref[z.levels :] = slot_matrix(z, order_ref, mer_ref).astype(BF16)
    for copy in copies[2:4]:
        copy.wait()
    field_ref[:, : z.lons] = dot(vert_ref[0], control_ref[0, 0])
    starts = [quarter * j1 for j1 in range(1, RADIX)]
    bases = [pl.multiple_of(s // LANES * LANES, LANES) for s in starts]
    shifts = [(LANES - (s - b)) % LANES for s, b in zip(starts, bases)]
    lane = iota((STRIP, LANES), 1)
    keeps = [(lane < shift) | (shift == 0) for shift in shifts]

    def rolled(i, at, c):
        lanes = pl.ds(pl.multiple_of(bases[i] + c * LANES, LANES), LANES)
        return pltpu.roll(field_ref[at : at + STRIP, lanes], shifts[i], 1)

    before = {}
    for block in range(0, z.tiles, z.block):
        for at in range(0, z.levels, STRIP):
            for c in range(block, block + z.block):
                if c == 0:
                    before[at] = [rolled(i, at, 0) for i in range(RADIX - 1)]
                after = [rolled(i, at, c + 1) for i in range(RADIX - 1)]
                second, third, fourth = [jnp.where(k, a, b) for k, a, b in zip(keeps, before[at], after)]
                before[at] = after
                first = field_ref[at : at + STRIP, tile(c)]
                even, odd = first + third, second + fourth
                real, imag, turned = first - third, second - fourth, even - odd
                cos1, cos2, cos3 = [twiddle_ref[r : r + 1, tile(c)] for r in (1, 2, 3)]
                sin1, sin2, sin3 = [twiddle_ref[RADIX + r : RADIX + r + 1, tile(c)] for r in (1, 2, 3)]
                parts = (
                    (even + odd,),
                    (real * cos1 - imag * sin1, real * sin1 + imag * cos1),
                    (turned * cos2, turned * sin2),
                    (real * cos3 + imag * sin3, real * sin3 - imag * cos3),
                )
                for r, pair in enumerate(parts):
                    for half, part in enumerate(pair):
                        to = (2 * r + half) * z.levels + at
                        parts_ref[to : to + STRIP, tile(c)] = part.astype(BF16)
        lanes = slice(block * LANES, (block + z.block) * LANES)
        basis = jnp.concatenate([basis_ref[: z.kaps, lanes], basis_ref[z.sin : z.sin + z.kaps, lanes]], axis=0)
        product = dot(basis, parts_ref[:, lanes], ((1,), (1,)))
        product_ref[...] = product if block == 0 else product_ref[...] + product
    count = z.kaps // z.rows
    sign = jnp.where(iota((1, LANES), 1) < z.levels, -1.0, 1.0).astype(F32)
    for r in range(RADIX):
        lanes = tile(r)
        for i in range(count):
            rows = slice(i * z.rows, (i + 1) * z.rows)
            from_sin = product_ref[z.kaps + i * z.rows : z.kaps + (i + 1) * z.rows, lanes]
            both = product_ref[rows, lanes] + pltpu.roll(from_sin, z.levels, 1) * sign
            scale = scale_ref[r * z.kaps + i * z.rows : r * z.kaps + (i + 1) * z.rows]
            packet_ref[r * count + i] = (both * scale).astype(BF16)
    if z.devices > RADIX * count:
        packet_ref[RADIX * count :] = jnp.zeros((z.devices - RADIX * count, z.rows, LANES), BF16)


def matrices_kernel(z, *refs):
    *given, mix_ref, bal_ref, all_ref = refs
    own = lax.axis_index("var")
    for step, ref in enumerate(given):
        all_ref[(own + step) % z.var] = ref[...]
    size = z.mixed
    to_cols = (iota((z.lat, size), 0) == iota((z.lat, size), 1) // z.rows).astype(F32).astype(BF16)
    same = iota((size, size), 0) % z.rows == iota((size, size), 1) % z.rows
    halves = iota((LANES, LANES), 0) // z.levels == iota((LANES, LANES), 1) // z.levels
    for v in range(z.var):
        meridional = all_ref[v, z.levels :].astype(F32)[: z.lat, : z.lat].astype(BF16)
        slot_cols = dot(meridional, to_cols).astype(BF16)
        mix_ref[v] = jnp.where(same, dot(to_cols, slot_cols, ((0,), (0,))), 0.0).astype(BF16)
        if v > 0:
            balance = all_ref[v, : z.levels].astype(F32)
            balance = jnp.where(halves, jnp.concatenate([balance, balance], axis=0), 0.0)
            bal_ref[v - 1] = balance.T.astype(BF16)


def mixing_kernel(z, packet_ref, mix_ref, bal_ref, out_ref):
    stream = None
    for v in range(z.var):
        coeffs = packet_ref[v].astype(F32).reshape(z.mixed, LANES).astype(BF16)
        blended = dot(mix_ref[v], coeffs)
        if v == 0:
            stream = blended.astype(BF16)
        else:
            blended = blended + dot(stream, bal_ref[v - 1])
        blended = blended.reshape(z.lat, z.rows, LANES)
        for s in range(z.lat):
            out_ref[v, s] = blended[s].astype(BF16)


def synthesis_kernel(z, spectra_ref, basis_ref, twiddle_ref, out_ref, sems, field_ref, lhs_ref, parts_ref):
    period = twiddle_ref[2 * RADIX :, :LANES].astype(jnp.int32)
    length = jnp.max(period)
    kap = iota((z.kaps, LANES), 0)
    count = z.kaps // z.rows
    half = z.levels // 2
    kinds = 2 * RADIX - 1
    for at in (0, z.sin):
        lhs_ref[:, at + z.kaps : at + z.sin] = jnp.zeros((2 * half * kinds, z.sin - z.kaps), BF16)
    for r in range(RADIX):
        part = spectra_ref[r * count : (r + 1) * count].astype(F32).reshape(z.kaps, LANES)
        part = jnp.where(kap * RADIX + r <= (period[0:1] - 1) // 2, part, 0.0)
        part = part.astype(BF16).T
        for i in range(2):
            from_cos = part[i * half : (i + 1) * half]
            from_sin = part[z.levels + i * half : z.levels + (i + 1) * half]
            pairs = [(from_cos, from_sin)] if r == 0 else [(from_cos, from_sin), (-from_sin, from_cos)]
            for kind, pair in zip((2 * r - 1, 2 * r) if r else (0,), pairs):
                to = slice((i * kinds + kind) * half, (i * kinds + kind + 1) * half)
                lhs_ref[to, : z.kaps] = pair[0]
                lhs_ref[to, z.sin : z.sin + z.kaps] = pair[1]
    quarter = length // RADIX
    starts = [quarter * j1 for j1 in range(1, RADIX)]
    bases = [pl.multiple_of(s // LANES * LANES, LANES) for s in starts]
    shifts = [s - b for s, b in zip(starts, bases)]
    wide = z.points + LANES
    field_ref[:, wide:] = jnp.zeros((z.levels, z.lons + LANES - wide), BF16)
    keep = [iota((STRIP, LANES), 1) < shift for shift in shifts]
    zero = jnp.zeros((STRIP, LANES), F32)
    for i in range(2):
        rows = slice(i * kinds * half, (i + 1) * kinds * half)
        parts_ref[rows] = dot(lhs_ref[rows], basis_ref[...])
    sent = []
    for at in range(0, z.levels, STRIP):
        rows = slice(at, at + STRIP)
        first = at // half * kinds * half + at % half
        quarters = [[], [], [], []]
        for c in range(z.tiles):
            cos1, cos2, cos3 = [twiddle_ref[r : r + 1, tile(c)] for r in (1, 2, 3)]
            sin1, sin2, sin3 = [twiddle_ref[RADIX + r : RADIX + r + 1, tile(c)] for r in (1, 2, 3)]
            w0, re1, im1, re2, im2, re3, im3 = [
                parts_ref[first + kind * half : first + kind * half + STRIP, tile(c)] for kind in range(kinds)
            ]
            w2 = re2 * cos2 - im2 * sin2
            cross = (re1 * cos1 - im1 * sin1) + (re3 * cos3 - im3 * sin3)
            turn = (re1 * sin1 + im1 * cos1) - (re3 * sin3 + im3 * cos3)
            even, odd = w0 + w2, w0 - w2
            field_ref[rows, tile(c)] = (even + cross).astype(BF16)
            for j1, part in ((1, odd - turn), (2, even - cross), (3, odd + turn)):
                quarters[j1].append(pltpu.roll(part, shifts[j1 - 1], 1))
        field_ref[rows, tile(z.tiles)] = zero.astype(BF16)
        for j1 in range(1, RADIX):
            pieces = zip([zero] + quarters[j1], quarters[j1] + [zero])
            for c, (left, right) in enumerate(pieces):
                lanes = pl.ds(pl.multiple_of(bases[j1 - 1] + c * LANES, LANES), LANES)
                piece = jnp.where(keep[j1 - 1], left, right)
                if c == 0:
                    piece = piece + field_ref[rows, lanes].astype(F32)
                field_ref[rows, lanes] = piece.astype(BF16)
        sent += fetch(
            (field_ref.at[pl.ds(at, STRIP), pl.ds(0, z.lons)],),
            (out_ref.at[0, 0, pl.ds(at, STRIP)],),
            sems.at[pl.ds(at // STRIP, 1)],
        )
    for copy in sent:
        copy.wait()


def body(z, control, row_order, row_length, vertical, amplitude, meridional, balance):
    arguments = (row_order, row_length, control, vertical, amplitude, meridional, balance)
    made = (
        jax.ShapeDtypeStruct((z.devices, z.rows, LANES), BF16),
        jax.ShapeDtypeStruct((z.params, LANES), BF16),
        jax.ShapeDtypeStruct((2 * z.sin, z.points), BF16),
        jax.ShapeDtypeStruct((2 * RADIX + SUBLANES, z.points), F32),
    )
    packets, params, basis, twiddle = pl.pallas_call(
        functools.partial(analysis_kernel, z),
        out_shape=made,
        in_specs=[HBM] * len(arguments),
        out_specs=(VMEM,) * len(made),
        scratch_shapes=[
            *[pltpu.SMEM(x.shape, x.dtype) for x in arguments[:2]],
            *[pltpu.VMEM(x.shape, x.dtype) for x in arguments[2:]],
            pltpu.SemaphoreType.DMA((len(arguments),)),
            pltpu.VMEM((z.levels, z.lons + LANES), F32),
            pltpu.VMEM((2 * RADIX * z.levels, z.points), BF16),
            pltpu.VMEM((2 * z.heads, z.points), F32),
            pltpu.VMEM((2 * STRIP, z.points), F32),
            pltpu.VMEM((z.waves, LANES), F32),
            pltpu.VMEM((2 * z.kaps, RADIX * LANES), F32),
        ],
        compiler_params=PARAMS,
        name="analysis",
    )(*[pltpu.with_memory_space_constraint(x, pltpu.HBM) for x in arguments])
    given = [params]
    for step in range(1, z.var):
        given.append(lax.ppermute(params, "var", [((i + step) % z.var, i) for i in range(z.var)]))
    packets = lax.all_to_all(packets, ("var", "lat"), 0, 0, tiled=True)
    mix, lift = pl.pallas_call(
        functools.partial(matrices_kernel, z),
        out_shape=(
            jax.ShapeDtypeStruct((z.var, z.mixed, z.mixed), BF16),
            jax.ShapeDtypeStruct((z.var - 1, LANES, LANES), BF16),
        ),
        in_specs=[VMEM] * z.var,
        out_specs=(VMEM, VMEM),
        scratch_shapes=[pltpu.VMEM((z.var, z.params, LANES), BF16)],
        compiler_params=PARAMS,
        cost_estimate=pl.CostEstimate(flops=10**8, bytes_accessed=10**6, transcendentals=0),
        name="matrices",
    )(*given)
    balanced = pl.pallas_call(
        functools.partial(mixing_kernel, z),
        out_shape=jax.ShapeDtypeStruct((z.var, z.lat, z.rows, LANES), BF16),
        in_specs=[VMEM] * 3,
        out_specs=VMEM,
        compiler_params=PARAMS,
        name="mixing",
    )(packets.reshape(z.var, z.lat, z.rows, LANES), mix, lift)
    balanced = balanced.reshape(z.devices, z.rows, LANES)
    balanced = lax.all_to_all(balanced, ("var", "lat"), 0, 0, tiled=True)
    return pl.pallas_call(
        functools.partial(synthesis_kernel, z),
        out_shape=jax.ShapeDtypeStruct(control.shape, BF16),
        in_specs=[VMEM] * 3,
        out_specs=HBM,
        scratch_shapes=[
            pltpu.SemaphoreType.DMA((z.levels // STRIP,)),
            pltpu.VMEM((z.levels, z.lons + LANES), BF16),
            pltpu.VMEM(((2 * RADIX - 1) * z.levels, 2 * z.sin), BF16),
            pltpu.VMEM(((2 * RADIX - 1) * z.levels, z.points), F32),
        ],
        compiler_params=PARAMS,
        name="synthesis",
    )(balanced, basis, twiddle)


def solution(mesh):
    placed = (
        P("var", "lat", None, None),
        P(),
        P(),
        P("var", None, None),
        P("var", None),
        P("var", None, None),
        P("var", None, None),
    )

    def run(control, row_order, row_length, vertical, amplitude, meridional, balance):
        lat_total, var_total = mesh.shape["lat"], mesh.shape["var"]
        assert control.shape[0] == var_total and control.shape[1] == lat_total
        z = Sizes(lat_total, var_total, control.shape[2], control.shape[3], amplitude.shape[1])
        return jax.shard_map(
            functools.partial(body, z),
            mesh=mesh,
            in_specs=placed,
            out_specs=P("var", "lat", None, None),
            check_vma=False,
        )(control, row_order, row_length, vertical, amplitude, meridional, balance)

    return run
```

```python
import functools
import math

import jax
import jax.numpy as jnp
from jax import lax
from jax.experimental import pallas as pl
from jax.experimental.pallas import tpu as pltpu
from jax.sharding import PartitionSpec as P

RADIX = 4
LANES = 128
SUBLANES = 8
STRIP = 16
F32 = jnp.float32
BF16 = jnp.bfloat16

COS_POLY = (1, -19.7392044, 64.9391174, -85.4501419, 60.1676292, -25.9675999, 6.52865839)
SIN_POLY = (6.28318501, -41.3415909, 81.5999451, -76.6144714, 41.3428841, -12.4712439)

VMEM = pl.BlockSpec(memory_space=pltpu.VMEM)
HBM = pl.BlockSpec(memory_space=pltpu.HBM)
PARAMS = pltpu.CompilerParams(vmem_limit_bytes=32 * 1024 * 1024)


def iota(shape, dim):
    return lax.broadcasted_iota(jnp.int32, shape, dim)


def horner(poly, x):
    total = jnp.full_like(x, poly[-1])
    for term in poly[-2::-1]:
        total = total * x + term
    return total


def cos_sin(turns):
    turns = turns - jnp.round(turns)
    square = turns * turns
    return horner(COS_POLY, square), horner(SIN_POLY, square) * turns


def ceil_div(a, b):
    return -(-a // b)


def round_up(a, b):
    return ceil_div(a, b) * b


def dot(a, b, contract=((1,), (0,))):
    return lax.dot_general(a, b, (contract, ((), ())), preferred_element_type=F32)


class Sizes:
    def __init__(self, lat_total, var_total, levels, lons, waves):
        self.lat, self.var, self.levels, self.lons, self.waves = lat_total, var_total, levels, lons, waves
        self.devices = lat_total * var_total
        self.points = lons // RADIX
        self.tiles = self.points // LANES
        self.block = math.gcd(self.tiles, 2)
        self.kaps = waves // RADIX
        self.rows = round_up(ceil_div(waves, self.devices), SUBLANES)
        assert self.kaps % self.rows == 0 and self.points % LANES == 0 and 2 * levels == LANES and lat_total <= LANES
        self.mixed = lat_total * self.rows
        self.sin = round_up(self.kaps, LANES)
        self.heads = round_up(ceil_div(self.kaps, STRIP), SUBLANES)
        self.params = round_up(levels + lat_total, STRIP)


def own_length(order_ref, length_ref):
    slot = lax.axis_index("lat")
    row = order_ref[slot]
    return slot, row, length_ref[row]


def fetch(sources, targets, sems):
    copies = [pltpu.make_async_copy(s, t, sems.at[i]) for i, (s, t) in enumerate(zip(sources, targets))]
    for copy in copies:
        copy.start()
    return copies


def slot_matrix(z, order_ref, mer_ref):
    def picks(count):
        slot = iota((count, z.lat), 0)
        row = jnp.full((count, z.lat), -1, jnp.int32)
        for t in range(z.lat):
            row = jnp.where(slot == t, order_ref[t], row)
        return (row == iota((count, z.lat), 1)).astype(F32).astype(BF16)

    rows = dot(picks(z.params - z.levels), mer_ref[0]).astype(BF16)
    return dot(rows, picks(LANES), ((1,), (1,)))


def tile(c):
    return slice(c * LANES, (c + 1) * LANES)


def analysis_kernel(z, *refs):
    given, made, held = refs[:7], refs[7:11], refs[11:18]
    sems, field_ref, parts_ref, heads_ref, tails_ref, scale_ref, product_ref = refs[18:]
    order_ref, length_ref, control_ref, vert_ref, amp_ref, mer_ref, bal_ref = held
    packet_ref, params_ref, basis_ref, twiddle_ref = made
    copies = fetch(given, held, sems)
    for at in (0, z.sin):
        basis_ref[at + z.kaps : at + z.sin] = jnp.zeros((z.sin - z.kaps, z.points), BF16)
    field_ref[:, z.lons :] = jnp.zeros((z.levels, LANES), F32)
    parts_ref[z.levels : 2 * z.levels] = jnp.zeros((z.levels, z.points), BF16)
    for copy in copies:
        copy.wait()
    field_ref[:, : z.lons] = dot(vert_ref[0], control_ref[0, 0])
    slot, row, length = own_length(order_ref, length_ref)
    quarter = length // RADIX
    period = jnp.full((1, LANES), length, jnp.int32).astype(F32)
    tail = iota((STRIP, LANES), 0).astype(F32)
    head = iota((z.heads, LANES), 0).astype(F32) * STRIP
    tw_row = iota((2 * RADIX, LANES), 0)
    tw_wave = jnp.where(tw_row < RADIX, tw_row, tw_row - RADIX).astype(F32)
    fraction = jnp.full((1, LANES), quarter, jnp.int32).astype(F32)
    for c in range(z.tiles):
        points = c * LANES + iota((1, LANES), 1)
        step = points.astype(F32) / fraction
        tails_ref[:STRIP, tile(c)], tails_ref[STRIP:, tile(c)] = cos_sin(tail * step)
        head_cos, head_sin = cos_sin(head * step)
        heads_ref[: z.heads, tile(c)] = jnp.where(points < quarter, head_cos, 0.0)
        heads_ref[z.heads :, tile(c)] = jnp.where(points < quarter, head_sin, 0.0)
        tw_cos, tw_sin = cos_sin(tw_wave * (points.astype(F32) / period))
        twiddle_ref[: 2 * RADIX, tile(c)] = jnp.where(tw_row < RADIX, tw_cos, tw_sin)
        twiddle_ref[2 * RADIX :, tile(c)] = jnp.broadcast_to(period, (SUBLANES, LANES))
    starts = [quarter * j1 for j1 in range(1, RADIX)]
    bases = [pl.multiple_of(s // LANES * LANES, LANES) for s in starts]
    shifts = [(LANES - (s - b)) % LANES for s, b in zip(starts, bases)]
    lane = iota((STRIP, LANES), 1)
    keeps = [(lane < shift) | (shift == 0) for shift in shifts]

    def rolled(i, at, c):
        lanes = pl.ds(pl.multiple_of(bases[i] + c * LANES, LANES), LANES)
        return pltpu.roll(field_ref[at : at + STRIP, lanes], shifts[i], 1)

    before = {}
    for block in range(0, z.tiles, z.block):
        for c in range(block, block + z.block):
            tail_cos, tail_sin = tails_ref[:STRIP, tile(c)], tails_ref[STRIP:, tile(c)]
            for at in range(0, z.kaps, STRIP):
                i = at // STRIP
                head_cos, head_sin = heads_ref[i : i + 1, tile(c)], heads_ref[z.heads + i : z.heads + i + 1, tile(c)]
                basis_ref[at : at + STRIP, tile(c)] = (head_cos * tail_cos - head_sin * tail_sin).astype(BF16)
                to = slice(z.sin + at, z.sin + at + STRIP)
                basis_ref[to, tile(c)] = (head_sin * tail_cos + head_cos * tail_sin).astype(BF16)
        for at in range(0, z.levels, STRIP):
            for c in range(block, block + z.block):
                if c == 0:
                    before[at] = [rolled(i, at, 0) for i in range(RADIX - 1)]
                after = [rolled(i, at, c + 1) for i in range(RADIX - 1)]
                second, third, fourth = [jnp.where(k, a, b) for k, a, b in zip(keeps, before[at], after)]
                before[at] = after
                first = field_ref[at : at + STRIP, tile(c)]
                even, odd = first + third, second + fourth
                real, imag, turned = first - third, second - fourth, even - odd
                cos1, cos2, cos3 = [twiddle_ref[r : r + 1, tile(c)] for r in (1, 2, 3)]
                sin1, sin2, sin3 = [twiddle_ref[RADIX + r : RADIX + r + 1, tile(c)] for r in (1, 2, 3)]
                parts = (
                    (even + odd,),
                    (real * cos1 - imag * sin1, real * sin1 + imag * cos1),
                    (turned * cos2, turned * sin2),
                    (real * cos3 + imag * sin3, real * sin3 - imag * cos3),
                )
                for r, pair in enumerate(parts):
                    for half, part in enumerate(pair):
                        to = (2 * r + half) * z.levels + at
                        parts_ref[to : to + STRIP, tile(c)] = part.astype(BF16)
        lanes = slice(block * LANES, (block + z.block) * LANES)
        basis = jnp.concatenate([basis_ref[: z.kaps, lanes], basis_ref[z.sin : z.sin + z.kaps, lanes]], axis=0)
        product = dot(basis, parts_ref[:, lanes], ((1,), (1,)))
        product_ref[...] = product if block == 0 else product_ref[...] + product
    group = LANES // RADIX
    weights = 1.0 / period, 2.0 / period
    for r in range(RADIX):
        picked = iota((group, LANES), 1) == iota((group, LANES), 0) * RADIX + r
        for at in range(0, z.kaps, group):
            lanes = slice(at * RADIX, at * RADIX + LANES)
            amp = jnp.sum(jnp.where(picked, amp_ref[:, lanes], 0.0), axis=1, keepdims=True)
            wave = (at + iota((group, LANES), 0)) * RADIX + r
            weight = jnp.where(wave == 0, *weights) if at + r == 0 else weights[1]
            scale_ref[r * z.kaps + at : r * z.kaps + at + group] = jnp.where(
                wave <= (length - 1) // 2, weight * amp, 0.0
            )
    params_ref[: z.levels] = jnp.concatenate([bal_ref[0], bal_ref[0]], axis=1)
    params_ref[z.levels :] = slot_matrix(z, order_ref, mer_ref).astype(BF16)
    count = z.kaps // z.rows
    sign = jnp.where(iota((1, LANES), 1) < z.levels, -1.0, 1.0).astype(F32)
    for r in range(RADIX):
        lanes = tile(r)
        for i in range(count):
            rows = slice(i * z.rows, (i + 1) * z.rows)
            from_sin = product_ref[z.kaps + i * z.rows : z.kaps + (i + 1) * z.rows, lanes]
            both = product_ref[rows, lanes] + pltpu.roll(from_sin, z.levels, 1) * sign
            scale = scale_ref[r * z.kaps + i * z.rows : r * z.kaps + (i + 1) * z.rows]
            packet_ref[r * count + i] = (both * scale).astype(BF16)
    if z.devices > RADIX * count:
        packet_ref[RADIX * count :] = jnp.zeros((z.devices - RADIX * count, z.rows, LANES), BF16)


def matrices_kernel(z, *refs):
    *given, mix_ref, bal_ref, all_ref = refs
    own = lax.axis_index("var")
    for step, ref in enumerate(given):
        all_ref[(own + step) % z.var] = ref[...]
    size = z.mixed
    to_cols = (iota((z.lat, size), 0) == iota((z.lat, size), 1) // z.rows).astype(F32).astype(BF16)
    same = iota((size, size), 0) % z.rows == iota((size, size), 1) % z.rows
    halves = iota((LANES, LANES), 0) // z.levels == iota((LANES, LANES), 1) // z.levels
    for v in range(z.var):
        meridional = all_ref[v, z.levels :].astype(F32)[: z.lat, : z.lat].astype(BF16)
        slot_cols = dot(meridional, to_cols).astype(BF16)
        mix_ref[v] = jnp.where(same, dot(to_cols, slot_cols, ((0,), (0,))), 0.0).astype(BF16)
        if v > 0:
            balance = all_ref[v, : z.levels].astype(F32)
            balance = jnp.where(halves, jnp.concatenate([balance, balance], axis=0), 0.0)
            bal_ref[v - 1] = balance.T.astype(BF16)


def mixing_kernel(z, packet_ref, mix_ref, bal_ref, out_ref):
    stream = None
    for v in range(z.var):
        coeffs = packet_ref[v].astype(F32).reshape(z.mixed, LANES).astype(BF16)
        blended = dot(mix_ref[v], coeffs)
        if v == 0:
            stream = blended.astype(BF16)
        else:
            blended = blended + dot(stream, bal_ref[v - 1])
        blended = blended.reshape(z.lat, z.rows, LANES)
        for s in range(z.lat):
            out_ref[v, s] = blended[s].astype(BF16)


def synthesis_kernel(z, spectra_ref, basis_ref, twiddle_ref, out_ref, sems, field_ref, lhs_ref, parts_ref):
    period = twiddle_ref[2 * RADIX :, :LANES].astype(jnp.int32)
    length = jnp.max(period)
    kap = iota((z.kaps, LANES), 0)
    count = z.kaps // z.rows
    half = z.levels // 2
    kinds = 2 * RADIX - 1
    for at in (0, z.sin):
        lhs_ref[:, at + z.kaps : at + z.sin] = jnp.zeros((2 * half * kinds, z.sin - z.kaps), BF16)
    for r in range(RADIX):
        part = spectra_ref[r * count : (r + 1) * count].astype(F32).reshape(z.kaps, LANES)
        part = jnp.where(kap * RADIX + r <= (period[0:1] - 1) // 2, part, 0.0)
        part = part.astype(BF16).T
        for i in range(2):
            from_cos = part[i * half : (i + 1) * half]
            from_sin = part[z.levels + i * half : z.levels + (i + 1) * half]
            pairs = [(from_cos, from_sin)] if r == 0 else [(from_cos, from_sin), (-from_sin, from_cos)]
            for kind, pair in zip((2 * r - 1, 2 * r) if r else (0,), pairs):
                to = slice((i * kinds + kind) * half, (i * kinds + kind + 1) * half)
                lhs_ref[to, : z.kaps] = pair[0]
                lhs_ref[to, z.sin : z.sin + z.kaps] = pair[1]
    quarter = length // RADIX
    starts = [quarter * j1 for j1 in range(1, RADIX)]
    bases = [pl.multiple_of(s // LANES * LANES, LANES) for s in starts]
    shifts = [s - b for s, b in zip(starts, bases)]
    wide = z.points + LANES
    field_ref[:, wide:] = jnp.zeros((z.levels, z.lons + LANES - wide), BF16)
    keep = [iota((STRIP, LANES), 1) < shift for shift in shifts]
    zero = jnp.zeros((STRIP, LANES), F32)
    for i in range(2):
        rows = slice(i * kinds * half, (i + 1) * kinds * half)
        parts_ref[rows] = dot(lhs_ref[rows], basis_ref[...])
    sent = []
    for at in range(0, z.levels, STRIP):
        rows = slice(at, at + STRIP)
        first = at // half * kinds * half + at % half
        quarters = [[], [], [], []]
        for c in range(z.tiles):
            cos1, cos2, cos3 = [twiddle_ref[r : r + 1, tile(c)] for r in (1, 2, 3)]
            sin1, sin2, sin3 = [twiddle_ref[RADIX + r : RADIX + r + 1, tile(c)] for r in (1, 2, 3)]
            w0, re1, im1, re2, im2, re3, im3 = [
                parts_ref[first + kind * half : first + kind * half + STRIP, tile(c)] for kind in range(kinds)
            ]
            w2 = re2 * cos2 - im2 * sin2
            cross = (re1 * cos1 - im1 * sin1) + (re3 * cos3 - im3 * sin3)
            turn = (re1 * sin1 + im1 * cos1) - (re3 * sin3 + im3 * cos3)
            even, odd = w0 + w2, w0 - w2
            field_ref[rows, tile(c)] = (even + cross).astype(BF16)
            for j1, part in ((1, odd - turn), (2, even - cross), (3, odd + turn)):
                quarters[j1].append(pltpu.roll(part, shifts[j1 - 1], 1))
        field_ref[rows, tile(z.tiles)] = zero.astype(BF16)
        for j1 in range(1, RADIX):
            pieces = zip([zero] + quarters[j1], quarters[j1] + [zero])
            for c, (left, right) in enumerate(pieces):
                lanes = pl.ds(pl.multiple_of(bases[j1 - 1] + c * LANES, LANES), LANES)
                piece = jnp.where(keep[j1 - 1], left, right)
                if c == 0:
                    piece = piece + field_ref[rows, lanes].astype(F32)
                field_ref[rows, lanes] = piece.astype(BF16)
        sent += fetch(
            (field_ref.at[pl.ds(at, STRIP), pl.ds(0, z.lons)],),
            (out_ref.at[0, 0, pl.ds(at, STRIP)],),
            sems.at[pl.ds(at // STRIP, 1)],
        )
    for copy in sent:
        copy.wait()


def body(z, control, row_order, row_length, vertical, amplitude, meridional, balance):
    arguments = (row_order, row_length, control, vertical, amplitude, meridional, balance)
    made = (
        jax.ShapeDtypeStruct((z.devices, z.rows, LANES), BF16),
        jax.ShapeDtypeStruct((z.params, LANES), BF16),
        jax.ShapeDtypeStruct((2 * z.sin, z.points), BF16),
        jax.ShapeDtypeStruct((2 * RADIX + SUBLANES, z.points), F32),
    )
    packets, params, basis, twiddle = pl.pallas_call(
        functools.partial(analysis_kernel, z),
        out_shape=made,
        in_specs=[HBM] * len(arguments),
        out_specs=(VMEM,) * len(made),
        scratch_shapes=[
            *[pltpu.SMEM(x.shape, x.dtype) for x in arguments[:2]],
            *[pltpu.VMEM(x.shape, x.dtype) for x in arguments[2:]],
            pltpu.SemaphoreType.DMA((len(arguments),)),
            pltpu.VMEM((z.levels, z.lons + LANES), F32),
            pltpu.VMEM((2 * RADIX * z.levels, z.points), BF16),
            pltpu.VMEM((2 * z.heads, z.points), F32),
            pltpu.VMEM((2 * STRIP, z.points), F32),
            pltpu.VMEM((z.waves, LANES), F32),
            pltpu.VMEM((2 * z.kaps, RADIX * LANES), F32),
        ],
        compiler_params=PARAMS,
        name="analysis",
    )(*[pltpu.with_memory_space_constraint(x, pltpu.HBM) for x in arguments])
    given = [params]
    for step in range(1, z.var):
        given.append(lax.ppermute(params, "var", [((i + step) % z.var, i) for i in range(z.var)]))
    packets = lax.all_to_all(packets, ("var", "lat"), 0, 0, tiled=True)
    mix, lift = pl.pallas_call(
        functools.partial(matrices_kernel, z),
        out_shape=(
            jax.ShapeDtypeStruct((z.var, z.mixed, z.mixed), BF16),
            jax.ShapeDtypeStruct((z.var - 1, LANES, LANES), BF16),
        ),
        in_specs=[VMEM] * z.var,
        out_specs=(VMEM, VMEM),
        scratch_shapes=[pltpu.VMEM((z.var, z.params, LANES), BF16)],
        compiler_params=PARAMS,
        cost_estimate=pl.CostEstimate(flops=10**8, bytes_accessed=10**6, transcendentals=0),
        name="matrices",
    )(*given)
    balanced = pl.pallas_call(
        functools.partial(mixing_kernel, z),
        out_shape=jax.ShapeDtypeStruct((z.var, z.lat, z.rows, LANES), BF16),
        in_specs=[VMEM] * 3,
        out_specs=VMEM,
        compiler_params=PARAMS,
        name="mixing",
    )(packets.reshape(z.var, z.lat, z.rows, LANES), mix, lift)
    balanced = balanced.reshape(z.devices, z.rows, LANES)
    balanced = lax.all_to_all(balanced, ("var", "lat"), 0, 0, tiled=True)
    return pl.pallas_call(
        functools.partial(synthesis_kernel, z),
        out_shape=jax.ShapeDtypeStruct(control.shape, BF16),
        in_specs=[VMEM] * 3,
        out_specs=HBM,
        scratch_shapes=[
            pltpu.SemaphoreType.DMA((z.levels // STRIP,)),
            pltpu.VMEM((z.levels, z.lons + LANES), BF16),
            pltpu.VMEM(((2 * RADIX - 1) * z.levels, 2 * z.sin), BF16),
            pltpu.VMEM(((2 * RADIX - 1) * z.levels, z.points), F32),
        ],
        compiler_params=PARAMS,
        name="synthesis",
    )(balanced, basis, twiddle)


def solution(mesh):
    placed = (
        P("var", "lat", None, None),
        P(),
        P(),
        P("var", None, None),
        P("var", None),
        P("var", None, None),
        P("var", None, None),
    )

    def run(control, row_order, row_length, vertical, amplitude, meridional, balance):
        lat_total, var_total = mesh.shape["lat"], mesh.shape["var"]
        assert control.shape[0] == var_total and control.shape[1] == lat_total
        z = Sizes(lat_total, var_total, control.shape[2], control.shape[3], amplitude.shape[1])
        return jax.shard_map(
            functools.partial(body, z),
            mesh=mesh,
            in_specs=placed,
            out_specs=P("var", "lat", None, None),
            check_vma=False,
        )(control, row_order, row_length, vertical, amplitude, meridional, balance)

    return run
```

```python
import functools
import math

import jax
import jax.numpy as jnp
from jax import lax
from jax.experimental import pallas as pl
from jax.experimental.pallas import tpu as pltpu
from jax.sharding import PartitionSpec as P

RADIX = 4
LANES = 128
SUBLANES = 8
STRIP = 16
F32 = jnp.float32
BF16 = jnp.bfloat16

COS_POLY = (1, -19.7392044, 64.9391174, -85.4501419, 60.1676292, -25.9675999, 6.52865839)
SIN_POLY = (6.28318501, -41.3415909, 81.5999451, -76.6144714, 41.3428841, -12.4712439)

VMEM = pl.BlockSpec(memory_space=pltpu.VMEM)
HBM = pl.BlockSpec(memory_space=pltpu.HBM)
PARAMS = pltpu.CompilerParams(vmem_limit_bytes=32 * 1024 * 1024)


def iota(shape, dim):
    return lax.broadcasted_iota(jnp.int32, shape, dim)


def horner(poly, x):
    total = jnp.full_like(x, poly[-1])
    for term in poly[-2::-1]:
        total = total * x + term
    return total


def cos_sin(turns):
    turns = turns - jnp.round(turns)
    square = turns * turns
    return horner(COS_POLY, square), horner(SIN_POLY, square) * turns


def ceil_div(a, b):
    return -(-a // b)


def round_up(a, b):
    return ceil_div(a, b) * b


def dot(a, b, contract=((1,), (0,))):
    return lax.dot_general(a, b, (contract, ((), ())), preferred_element_type=F32)


class Sizes:
    def __init__(self, lat_total, var_total, levels, lons, waves):
        self.lat, self.var, self.levels, self.lons, self.waves = lat_total, var_total, levels, lons, waves
        self.devices = lat_total * var_total
        self.points = lons // RADIX
        self.tiles = self.points // LANES
        self.block = math.gcd(self.tiles, 2)
        self.kaps = waves // RADIX
        self.rows = round_up(ceil_div(waves, self.devices), SUBLANES)
        assert self.kaps % self.rows == 0 and self.points % LANES == 0 and 2 * levels == LANES and lat_total <= LANES
        self.mixed = lat_total * self.rows
        self.sin = round_up(self.kaps, LANES)
        self.heads = round_up(ceil_div(self.kaps, STRIP), SUBLANES)
        self.params = round_up(levels + lat_total, STRIP)


def own_length(order_ref, length_ref):
    slot = lax.axis_index("lat")
    row = order_ref[slot]
    return slot, row, length_ref[row]


def fetch(sources, targets, sems):
    copies = [pltpu.make_async_copy(s, t, sems.at[i]) for i, (s, t) in enumerate(zip(sources, targets))]
    for copy in copies:
        copy.start()
    return copies


def slot_matrix(z, order_ref, mer_ref):
    def picks(count):
        slot = iota((count, z.lat), 0)
        row = jnp.full((count, z.lat), -1, jnp.int32)
        for t in range(z.lat):
            row = jnp.where(slot == t, order_ref[t], row)
        return (row == iota((count, z.lat), 1)).astype(F32).astype(BF16)

    rows = dot(picks(z.params - z.levels), mer_ref[0]).astype(BF16)
    return dot(rows, picks(LANES), ((1,), (1,)))


def tile(c):
    return slice(c * LANES, (c + 1) * LANES)


def analysis_kernel(z, *refs):
    given, made, held = refs[:7], refs[7:11], refs[11:18]
    sems, field_ref, parts_ref, heads_ref, tails_ref, scale_ref, product_ref = refs[18:]
    order_ref, length_ref, control_ref, vert_ref, amp_ref, mer_ref, bal_ref = held
    packet_ref, params_ref, basis_ref, twiddle_ref = made
    copies = fetch(given, held, sems)
    for at in (0, z.sin):
        basis_ref[at + z.kaps : at + z.sin] = jnp.zeros((z.sin - z.kaps, z.points), BF16)
    field_ref[:, z.lons :] = jnp.zeros((z.levels, LANES), F32)
    for copy in copies[:2]:
        copy.wait()
    slot, row, length = own_length(order_ref, length_ref)
    quarter = length // RADIX
    period = jnp.full((1, LANES), length, jnp.int32).astype(F32)
    tail = iota((STRIP, LANES), 0).astype(F32)
    head = iota((z.heads, LANES), 0).astype(F32) * STRIP
    tw_row = iota((2 * RADIX, LANES), 0)
    tw_wave = jnp.where(tw_row < RADIX, tw_row, tw_row - RADIX).astype(F32)
    fraction = jnp.full((1, LANES), quarter, jnp.int32).astype(F32)
    for c in range(z.tiles):
        points = c * LANES + iota((1, LANES), 1)
        step = points.astype(F32) / fraction
        tails_ref[:STRIP, tile(c)], tails_ref[STRIP:, tile(c)] = cos_sin(tail * step)
        head_cos, head_sin = cos_sin(head * step)
        heads_ref[: z.heads, tile(c)] = jnp.where(points < quarter, head_cos, 0.0)
        heads_ref[z.heads :, tile(c)] = jnp.where(points < quarter, head_sin, 0.0)
        tw_cos, tw_sin = cos_sin(tw_wave * (points.astype(F32) / period))
        twiddle_ref[: 2 * RADIX, tile(c)] = jnp.where(tw_row < RADIX, tw_cos, tw_sin)
        twiddle_ref[2 * RADIX :, tile(c)] = jnp.broadcast_to(period, (SUBLANES, LANES))
    for copy in copies[2:]:
        copy.wait()
    field_ref[:, : z.lons] = dot(vert_ref[0], control_ref[0, 0])
    starts = [quarter * j1 for j1 in range(1, RADIX)]
    bases = [pl.multiple_of(s // LANES * LANES, LANES) for s in starts]
    shifts = [(LANES - (s - b)) % LANES for s, b in zip(starts, bases)]
    lane = iota((STRIP, LANES), 1)
    keeps = [(lane < shift) | (shift == 0) for shift in shifts]

    def rolled(i, at, c):
        lanes = pl.ds(pl.multiple_of(bases[i] + c * LANES, LANES), LANES)
        return pltpu.roll(field_ref[at : at + STRIP, lanes], shifts[i], 1)

    before = {}
    kinds = 2 * RADIX - 1
    for block in range(0, z.tiles, z.block):
        for c in range(block, block + z.block):
            tail_cos, tail_sin = tails_ref[:STRIP, tile(c)], tails_ref[STRIP:, tile(c)]
            for at in range(0, z.kaps, STRIP):
                i = at // STRIP
                head_cos, head_sin = heads_ref[i : i + 1, tile(c)], heads_ref[z.heads + i : z.heads + i + 1, tile(c)]
                basis_ref[at : at + STRIP, tile(c)] = (head_cos * tail_cos - head_sin * tail_sin).astype(BF16)
                to = slice(z.sin + at, z.sin + at + STRIP)
                basis_ref[to, tile(c)] = (head_sin * tail_cos + head_cos * tail_sin).astype(BF16)
        for at in range(0, z.levels, STRIP):
            for c in range(block, block + z.block):
                if c == 0:
                    before[at] = [rolled(i, at, 0) for i in range(RADIX - 1)]
                after = [rolled(i, at, c + 1) for i in range(RADIX - 1)]
                second, third, fourth = [jnp.where(k, a, b) for k, a, b in zip(keeps, before[at], after)]
                before[at] = after
                first = field_ref[at : at + STRIP, tile(c)]
                even, odd = first + third, second + fourth
                real, imag, turned = first - third, second - fourth, even - odd
                cos1, cos2, cos3 = [twiddle_ref[r : r + 1, tile(c)] for r in (1, 2, 3)]
                sin1, sin2, sin3 = [twiddle_ref[RADIX + r : RADIX + r + 1, tile(c)] for r in (1, 2, 3)]
                parts = (
                    (even + odd,),
                    (real * cos1 - imag * sin1, real * sin1 + imag * cos1),
                    (turned * cos2, turned * sin2),
                    (real * cos3 + imag * sin3, real * sin3 - imag * cos3),
                )
                for r, pair in enumerate(parts):
                    for half, part in enumerate(pair):
                        to = ((2 * r - 2 if r else 2 * RADIX - 2) + half) * z.levels + at
                        parts_ref[to : to + STRIP, tile(c)] = part.astype(BF16)
        lanes = slice(block * LANES, (block + z.block) * LANES)
        basis = jnp.concatenate([basis_ref[: z.kaps, lanes], basis_ref[z.sin : z.sin + z.kaps, lanes]], axis=0)
        product = dot(basis, parts_ref[:, lanes], ((1,), (1,)))
        used = slice(0, kinds * z.levels)
        product_ref[:, used] = product if block == 0 else product_ref[:, used] + product
    group = LANES // RADIX
    weights = 1.0 / period, 2.0 / period
    for r in range(RADIX):
        picked = iota((group, LANES), 1) == iota((group, LANES), 0) * RADIX + r
        for at in range(0, z.kaps, group):
            lanes = slice(at * RADIX, at * RADIX + LANES)
            amp = jnp.sum(jnp.where(picked, amp_ref[:, lanes], 0.0), axis=1, keepdims=True)
            wave = (at + iota((group, LANES), 0)) * RADIX + r
            weight = jnp.where(wave == 0, *weights) if at + r == 0 else weights[1]
            scale_ref[r * z.kaps + at : r * z.kaps + at + group] = jnp.where(
                wave <= (length - 1) // 2, weight * amp, 0.0
            )
    params_ref[: z.levels] = jnp.concatenate([bal_ref[0], bal_ref[0]], axis=1)
    params_ref[z.levels :] = slot_matrix(z, order_ref, mer_ref).astype(BF16)
    count = z.kaps // z.rows
    sign = jnp.where(iota((1, LANES), 1) < z.levels, -1.0, 1.0).astype(F32)
    for r in range(RADIX):
        lanes = tile(r - 1 if r else RADIX - 1)
        for i in range(count):
            rows = slice(i * z.rows, (i + 1) * z.rows)
            from_sin = product_ref[z.kaps + i * z.rows : z.kaps + (i + 1) * z.rows, lanes]
            from_cos, from_sin = product_ref[rows, lanes], pltpu.roll(from_sin, z.levels, 1)
            both = from_cos + from_sin * sign if r else jnp.where(sign < 0, from_cos, from_sin)
            scale = scale_ref[r * z.kaps + i * z.rows : r * z.kaps + (i + 1) * z.rows]
            packet_ref[r * count + i] = (both * scale).astype(BF16)
    if z.devices > RADIX * count:
        packet_ref[RADIX * count :] = jnp.zeros((z.devices - RADIX * count, z.rows, LANES), BF16)


def matrices_kernel(z, *refs):
    *given, mix_ref, bal_ref, all_ref = refs
    own = lax.axis_index("var")
    for step, ref in enumerate(given):
        all_ref[(own + step) % z.var] = ref[...]
    size = z.mixed
    to_cols = (iota((z.lat, size), 0) == iota((z.lat, size), 1) // z.rows).astype(F32).astype(BF16)
    same = iota((size, size), 0) % z.rows == iota((size, size), 1) % z.rows
    halves = iota((LANES, LANES), 0) // z.levels == iota((LANES, LANES), 1) // z.levels
    for v in range(z.var):
        meridional = all_ref[v, z.levels :].astype(F32)[: z.lat, : z.lat].astype(BF16)
        slot_cols = dot(meridional, to_cols).astype(BF16)
        mix_ref[v] = jnp.where(same, dot(to_cols, slot_cols, ((0,), (0,))), 0.0).astype(BF16)
        if v > 0:
            balance = all_ref[v, : z.levels].astype(F32)
            balance = jnp.where(halves, jnp.concatenate([balance, balance], axis=0), 0.0)
            bal_ref[v - 1] = balance.T.astype(BF16)


def mixing_kernel(z, packet_ref, mix_ref, bal_ref, out_ref):
    stream = None
    for v in range(z.var):
        coeffs = packet_ref[v].astype(F32).reshape(z.mixed, LANES).astype(BF16)
        blended = dot(mix_ref[v], coeffs)
        if v == 0:
            stream = blended.astype(BF16)
        else:
            blended = blended + dot(stream, bal_ref[v - 1])
        blended = blended.reshape(z.lat, z.rows, LANES)
        for s in range(z.lat):
            out_ref[v, s] = blended[s].astype(BF16)


def synthesis_kernel(z, spectra_ref, basis_ref, twiddle_ref, out_ref, sems, field_ref, lhs_ref, parts_ref):
    period = twiddle_ref[2 * RADIX :, :LANES].astype(jnp.int32)
    length = jnp.max(period)
    kap = iota((z.kaps, LANES), 0)
    count = z.kaps // z.rows
    half = z.levels // 2
    kinds = 2 * RADIX - 1
    for at in (0, z.sin):
        lhs_ref[:, at + z.kaps : at + z.sin] = jnp.zeros((2 * half * kinds, z.sin - z.kaps), BF16)
    for r in range(RADIX):
        part = spectra_ref[r * count : (r + 1) * count].astype(F32).reshape(z.kaps, LANES)
        part = jnp.where(kap * RADIX + r <= (period[0:1] - 1) // 2, part, 0.0)
        part = part.astype(BF16).T
        for i in range(2):
            from_cos = part[i * half : (i + 1) * half]
            from_sin = part[z.levels + i * half : z.levels + (i + 1) * half]
            pairs = [(from_cos, from_sin)] if r == 0 else [(from_cos, from_sin), (-from_sin, from_cos)]
            for kind, pair in zip((2 * r - 1, 2 * r) if r else (0,), pairs):
                to = slice((i * kinds + kind) * half, (i * kinds + kind + 1) * half)
                lhs_ref[to, : z.kaps] = pair[0]
                lhs_ref[to, z.sin : z.sin + z.kaps] = pair[1]
    quarter = length // RADIX
    starts = [quarter * j1 for j1 in range(1, RADIX)]
    bases = [pl.multiple_of(s // LANES * LANES, LANES) for s in starts]
    shifts = [s - b for s, b in zip(starts, bases)]
    wide = z.points + LANES
    field_ref[:, wide:] = jnp.zeros((z.levels, z.lons + LANES - wide), BF16)
    keep = [iota((STRIP, LANES), 1) < shift for shift in shifts]
    zero = jnp.zeros((STRIP, LANES), F32)
    for i in range(2):
        rows = slice(i * kinds * half, (i + 1) * kinds * half)
        parts_ref[rows] = dot(lhs_ref[rows], basis_ref[...])
    sent = []
    for at in range(0, z.levels, STRIP):
        rows = slice(at, at + STRIP)
        first = at // half * kinds * half + at % half
        quarters = [[], [], [], []]
        for c in range(z.tiles):
            cos1, cos2, cos3 = [twiddle_ref[r : r + 1, tile(c)] for r in (1, 2, 3)]
            sin1, sin2, sin3 = [twiddle_ref[RADIX + r : RADIX + r + 1, tile(c)] for r in (1, 2, 3)]
            w0, re1, im1, re2, im2, re3, im3 = [
                parts_ref[first + kind * half : first + kind * half + STRIP, tile(c)] for kind in range(kinds)
            ]
            w2 = re2 * cos2 - im2 * sin2
            cross = (re1 * cos1 - im1 * sin1) + (re3 * cos3 - im3 * sin3)
            turn = (re1 * sin1 + im1 * cos1) - (re3 * sin3 + im3 * cos3)
            even, odd = w0 + w2, w0 - w2
            field_ref[rows, tile(c)] = (even + cross).astype(BF16)
            for j1, part in ((1, odd - turn), (2, even - cross), (3, odd + turn)):
                quarters[j1].append(pltpu.roll(part, shifts[j1 - 1], 1))
        field_ref[rows, tile(z.tiles)] = zero.astype(BF16)
        for j1 in range(1, RADIX):
            pieces = zip([zero] + quarters[j1], quarters[j1] + [zero])
            for c, (left, right) in enumerate(pieces):
                lanes = pl.ds(pl.multiple_of(bases[j1 - 1] + c * LANES, LANES), LANES)
                piece = jnp.where(keep[j1 - 1], left, right)
                if c == 0:
                    piece = piece + field_ref[rows, lanes].astype(F32)
                field_ref[rows, lanes] = piece.astype(BF16)
        sent += fetch(
            (field_ref.at[pl.ds(at, STRIP), pl.ds(0, z.lons)],),
            (out_ref.at[0, 0, pl.ds(at, STRIP)],),
            sems.at[pl.ds(at // STRIP, 1)],
        )
    for copy in sent:
        copy.wait()


def body(z, control, row_order, row_length, vertical, amplitude, meridional, balance):
    arguments = (row_order, row_length, control, vertical, amplitude, meridional, balance)
    made = (
        jax.ShapeDtypeStruct((z.devices, z.rows, LANES), BF16),
        jax.ShapeDtypeStruct((z.params, LANES), BF16),
        jax.ShapeDtypeStruct((2 * z.sin, z.points), BF16),
        jax.ShapeDtypeStruct((2 * RADIX + SUBLANES, z.points), F32),
    )
    packets, params, basis, twiddle = pl.pallas_call(
        functools.partial(analysis_kernel, z),
        out_shape=made,
        in_specs=[HBM] * len(arguments),
        out_specs=(VMEM,) * len(made),
        scratch_shapes=[
            *[pltpu.SMEM(x.shape, x.dtype) for x in arguments[:2]],
            *[pltpu.VMEM(x.shape, x.dtype) for x in arguments[2:]],
            pltpu.SemaphoreType.DMA((len(arguments),)),
            pltpu.VMEM((z.levels, z.lons + LANES), F32),
            pltpu.VMEM(((2 * RADIX - 1) * z.levels, z.points), BF16),
            pltpu.VMEM((2 * z.heads, z.points), F32),
            pltpu.VMEM((2 * STRIP, z.points), F32),
            pltpu.VMEM((z.waves, LANES), F32),
            pltpu.VMEM((2 * z.kaps, RADIX * LANES), F32),
        ],
        compiler_params=PARAMS,
        name="analysis",
    )(*[pltpu.with_memory_space_constraint(x, pltpu.HBM) for x in arguments])
    given = [params]
    for step in range(1, z.var):
        given.append(lax.ppermute(params, "var", [((i + step) % z.var, i) for i in range(z.var)]))
    packets = lax.all_to_all(packets, ("var", "lat"), 0, 0, tiled=True)
    mix, lift = pl.pallas_call(
        functools.partial(matrices_kernel, z),
        out_shape=(
            jax.ShapeDtypeStruct((z.var, z.mixed, z.mixed), BF16),
            jax.ShapeDtypeStruct((z.var - 1, LANES, LANES), BF16),
        ),
        in_specs=[VMEM] * z.var,
        out_specs=(VMEM, VMEM),
        scratch_shapes=[pltpu.VMEM((z.var, z.params, LANES), BF16)],
        compiler_params=PARAMS,
        cost_estimate=pl.CostEstimate(flops=10**8, bytes_accessed=10**6, transcendentals=0),
        name="matrices",
    )(*given)
    balanced = pl.pallas_call(
        functools.partial(mixing_kernel, z),
        out_shape=jax.ShapeDtypeStruct((z.var, z.lat, z.rows, LANES), BF16),
        in_specs=[VMEM] * 3,
        out_specs=VMEM,
        compiler_params=PARAMS,
        name="mixing",
    )(packets.reshape(z.var, z.lat, z.rows, LANES), mix, lift)
    balanced = balanced.reshape(z.devices, z.rows, LANES)
    balanced = lax.all_to_all(balanced, ("var", "lat"), 0, 0, tiled=True)
    return pl.pallas_call(
        functools.partial(synthesis_kernel, z),
        out_shape=jax.ShapeDtypeStruct(control.shape, BF16),
        in_specs=[VMEM] * 3,
        out_specs=HBM,
        scratch_shapes=[
            pltpu.SemaphoreType.DMA((z.levels // STRIP,)),
            pltpu.VMEM((z.levels, z.lons + LANES), BF16),
            pltpu.VMEM(((2 * RADIX - 1) * z.levels, 2 * z.sin), BF16),
            pltpu.VMEM(((2 * RADIX - 1) * z.levels, z.points), F32),
        ],
        compiler_params=PARAMS,
        name="synthesis",
    )(balanced, basis, twiddle)


def solution(mesh):
    placed = (
        P("var", "lat", None, None),
        P(),
        P(),
        P("var", None, None),
        P("var", None),
        P("var", None, None),
        P("var", None, None),
    )

    def run(control, row_order, row_length, vertical, amplitude, meridional, balance):
        lat_total, var_total = mesh.shape["lat"], mesh.shape["var"]
        assert control.shape[0] == var_total and control.shape[1] == lat_total
        z = Sizes(lat_total, var_total, control.shape[2], control.shape[3], amplitude.shape[1])
        return jax.shard_map(
            functools.partial(body, z),
            mesh=mesh,
            in_specs=placed,
            out_specs=P("var", "lat", None, None),
            check_vma=False,
        )(control, row_order, row_length, vertical, amplitude, meridional, balance)

    return run
```

```python
import functools
import math

import jax
import jax.numpy as jnp
from jax import lax
from jax.experimental import pallas as pl
from jax.experimental.pallas import tpu as pltpu
from jax.sharding import PartitionSpec as P

RADIX = 4
LANES = 128
SUBLANES = 8
STRIP = 16
F32 = jnp.float32
BF16 = jnp.bfloat16

COS_POLY = (1, -19.7392044, 64.9391174, -85.4501419, 60.1676292, -25.9675999, 6.52865839)
SIN_POLY = (6.28318501, -41.3415909, 81.5999451, -76.6144714, 41.3428841, -12.4712439)

VMEM = pl.BlockSpec(memory_space=pltpu.VMEM)
HBM = pl.BlockSpec(memory_space=pltpu.HBM)
PARAMS = pltpu.CompilerParams(vmem_limit_bytes=32 * 1024 * 1024)


def iota(shape, dim):
    return lax.broadcasted_iota(jnp.int32, shape, dim)


def horner(poly, x):
    total = jnp.full_like(x, poly[-1])
    for term in poly[-2::-1]:
        total = total * x + term
    return total


def cos_sin(turns):
    turns = turns - jnp.round(turns)
    square = turns * turns
    return horner(COS_POLY, square), horner(SIN_POLY, square) * turns


def ceil_div(a, b):
    return -(-a // b)


def round_up(a, b):
    return ceil_div(a, b) * b


def dot(a, b, contract=((1,), (0,))):
    return lax.dot_general(a, b, (contract, ((), ())), preferred_element_type=F32)


class Sizes:
    def __init__(self, lat_total, var_total, levels, lons, waves):
        self.lat, self.var, self.levels, self.lons, self.waves = lat_total, var_total, levels, lons, waves
        self.devices = lat_total * var_total
        self.points = lons // RADIX
        self.tiles = self.points // LANES
        self.block = math.gcd(self.tiles, 2)
        self.kaps = waves // RADIX
        self.rows = round_up(ceil_div(waves, self.devices), SUBLANES)
        assert self.kaps % self.rows == 0 and self.points % LANES == 0 and 2 * levels == LANES and lat_total <= LANES
        self.mixed = lat_total * self.rows
        self.sin = round_up(self.kaps, LANES)
        self.heads = round_up(ceil_div(self.kaps, STRIP), SUBLANES)
        self.params = round_up(levels + lat_total, STRIP)


def own_length(order_ref, length_ref):
    slot = lax.axis_index("lat")
    row = order_ref[slot]
    return slot, row, length_ref[row]


def fetch(sources, targets, sems):
    copies = [pltpu.make_async_copy(s, t, sems.at[i]) for i, (s, t) in enumerate(zip(sources, targets))]
    for copy in copies:
        copy.start()
    return copies


def slot_matrix(z, order_ref, mer_ref):
    def picks(count):
        slot = iota((count, z.lat), 0)
        row = jnp.full((count, z.lat), -1, jnp.int32)
        for t in range(z.lat):
            row = jnp.where(slot == t, order_ref[t], row)
        return (row == iota((count, z.lat), 1)).astype(F32).astype(BF16)

    rows = dot(picks(z.params - z.levels), mer_ref[0]).astype(BF16)
    return dot(rows, picks(LANES), ((1,), (1,)))


def lanes_below(bound):
    lane = iota((STRIP, LANES), 1).astype(F32).astype(BF16)
    return lane < jnp.full((STRIP, LANES), bound, jnp.int32).astype(F32).astype(BF16)


def tile(c):
    return slice(c * LANES, (c + 1) * LANES)


def analysis_kernel(z, *refs):
    given, made, held = refs[:7], refs[7:11], refs[11:18]
    sems, field_ref, parts_ref, heads_ref, tails_ref, scale_ref, product_ref = refs[18:]
    order_ref, length_ref, control_ref, vert_ref, amp_ref, mer_ref, bal_ref = held
    packet_ref, params_ref, basis_ref, twiddle_ref = made
    copies = fetch(given, held, sems)
    for at in (0, z.sin):
        basis_ref[at + z.kaps : at + z.sin] = jnp.zeros((z.sin - z.kaps, z.points), BF16)
    field_ref[:, z.lons :] = jnp.zeros((z.levels, LANES), BF16)
    for copy in copies[:2]:
        copy.wait()
    slot, row, length = own_length(order_ref, length_ref)
    quarter = length // RADIX
    period = jnp.full((1, LANES), length, jnp.int32).astype(F32)
    tail = iota((STRIP, LANES), 0).astype(F32)
    head = iota((z.heads, LANES), 0).astype(F32) * STRIP
    tw_row = iota((2 * RADIX, LANES), 0)
    tw_wave = jnp.where(tw_row < RADIX, tw_row, tw_row - RADIX).astype(F32)
    fraction = jnp.full((1, LANES), quarter, jnp.int32).astype(F32)
    for c in range(z.tiles):
        points = c * LANES + iota((1, LANES), 1)
        step = points.astype(F32) / fraction
        tails_ref[:STRIP, tile(c)], tails_ref[STRIP:, tile(c)] = cos_sin(tail * step)
        head_cos, head_sin = cos_sin(head * step)
        heads_ref[: z.heads, tile(c)] = jnp.where(points < quarter, head_cos, 0.0)
        heads_ref[z.heads :, tile(c)] = jnp.where(points < quarter, head_sin, 0.0)
        tw_cos, tw_sin = cos_sin(tw_wave * (points.astype(F32) / period))
        twiddle_ref[: 2 * RADIX, tile(c)] = jnp.where(tw_row < RADIX, tw_cos, tw_sin)
        twiddle_ref[2 * RADIX :, tile(c)] = jnp.broadcast_to(period, (SUBLANES, LANES))
    for copy in copies[2:]:
        copy.wait()
    field_ref[:, : z.lons] = dot(vert_ref[0], control_ref[0, 0]).astype(BF16)
    starts = [quarter * j1 for j1 in range(1, RADIX)]
    bases = [pl.multiple_of(s // LANES * LANES, LANES) for s in starts]
    shifts = [(LANES - (s - b)) % LANES for s, b in zip(starts, bases)]
    keeps = [lanes_below(jnp.where(shift == 0, LANES, shift)) for shift in shifts]

    def rolled(i, at, c):
        lanes = pl.ds(pl.multiple_of(bases[i] + c * LANES, LANES), LANES)
        return pltpu.roll(field_ref[at : at + STRIP, lanes], shifts[i], 1)

    before = {}
    kinds = 2 * RADIX - 1
    for block in range(0, z.tiles, z.block):
        for c in range(block, block + z.block):
            tail_cos, tail_sin = tails_ref[:STRIP, tile(c)], tails_ref[STRIP:, tile(c)]
            for at in range(0, z.kaps, STRIP):
                i = at // STRIP
                head_cos, head_sin = heads_ref[i : i + 1, tile(c)], heads_ref[z.heads + i : z.heads + i + 1, tile(c)]
                basis_ref[at : at + STRIP, tile(c)] = (head_cos * tail_cos - head_sin * tail_sin).astype(BF16)
                to = slice(z.sin + at, z.sin + at + STRIP)
                basis_ref[to, tile(c)] = (head_sin * tail_cos + head_cos * tail_sin).astype(BF16)
        for at in range(0, z.levels, STRIP):
            for c in range(block, block + z.block):
                if c == 0:
                    before[at] = [rolled(i, at, 0) for i in range(RADIX - 1)]
                after = [rolled(i, at, c + 1) for i in range(RADIX - 1)]
                quarters = [jnp.where(k, a, b) for k, a, b in zip(keeps, before[at], after)]
                before[at] = after
                quarters = [field_ref[at : at + STRIP, tile(c)], *quarters]
                first, second, third, fourth = [x.astype(F32) for x in quarters]
                even, odd = first + third, second + fourth
                real, imag, turned = first - third, second - fourth, even - odd
                cos1, cos2, cos3 = [twiddle_ref[r : r + 1, tile(c)] for r in (1, 2, 3)]
                sin1, sin2, sin3 = [twiddle_ref[RADIX + r : RADIX + r + 1, tile(c)] for r in (1, 2, 3)]
                parts = (
                    (even + odd,),
                    (real * cos1 - imag * sin1, real * sin1 + imag * cos1),
                    (turned * cos2, turned * sin2),
                    (real * cos3 + imag * sin3, real * sin3 - imag * cos3),
                )
                for r, pair in enumerate(parts):
                    for half, part in enumerate(pair):
                        to = ((2 * r - 2 if r else 2 * RADIX - 2) + half) * z.levels + at
                        parts_ref[to : to + STRIP, tile(c)] = part.astype(BF16)
        lanes = slice(block * LANES, (block + z.block) * LANES)
        basis = jnp.concatenate([basis_ref[: z.kaps, lanes], basis_ref[z.sin : z.sin + z.kaps, lanes]], axis=0)
        product = dot(basis, parts_ref[:, lanes], ((1,), (1,)))
        used = slice(0, kinds * z.levels)
        product_ref[:, used] = product if block == 0 else product_ref[:, used] + product
    group = LANES // RADIX
    weights = 1.0 / period, 2.0 / period
    for r in range(RADIX):
        picked = iota((group, LANES), 1) == iota((group, LANES), 0) * RADIX + r
        for at in range(0, z.kaps, group):
            lanes = slice(at * RADIX, at * RADIX + LANES)
            amp = jnp.sum(jnp.where(picked, amp_ref[:, lanes], 0.0), axis=1, keepdims=True)
            wave = (at + iota((group, LANES), 0)) * RADIX + r
            weight = jnp.where(wave == 0, *weights) if at + r == 0 else weights[1]
            scale_ref[r * z.kaps + at : r * z.kaps + at + group] = jnp.where(
                wave <= (length - 1) // 2, weight * amp, 0.0
            )
    params_ref[: z.levels] = jnp.concatenate([bal_ref[0], bal_ref[0]], axis=1)
    params_ref[z.levels :] = slot_matrix(z, order_ref, mer_ref).astype(BF16)
    count = z.kaps // z.rows
    sign = jnp.where(iota((1, LANES), 1) < z.levels, -1.0, 1.0).astype(F32)
    for r in range(RADIX):
        lanes = tile(r - 1 if r else RADIX - 1)
        for i in range(count):
            rows = slice(i * z.rows, (i + 1) * z.rows)
            from_sin = product_ref[z.kaps + i * z.rows : z.kaps + (i + 1) * z.rows, lanes]
            from_cos, from_sin = product_ref[rows, lanes], pltpu.roll(from_sin, z.levels, 1)
            both = from_cos + from_sin * sign if r else jnp.where(sign < 0, from_cos, from_sin)
            scale = scale_ref[r * z.kaps + i * z.rows : r * z.kaps + (i + 1) * z.rows]
            packet_ref[r * count + i] = (both * scale).astype(BF16)
    if z.devices > RADIX * count:
        packet_ref[RADIX * count :] = jnp.zeros((z.devices - RADIX * count, z.rows, LANES), BF16)


def matrices_kernel(z, *refs):
    *given, mix_ref, bal_ref, all_ref = refs
    own = lax.axis_index("var")
    for step, ref in enumerate(given):
        all_ref[(own + step) % z.var] = ref[...]
    size = z.mixed
    to_cols = (iota((z.lat, size), 0) == iota((z.lat, size), 1) // z.rows).astype(F32).astype(BF16)
    same = iota((size, size), 0) % z.rows == iota((size, size), 1) % z.rows
    halves = iota((LANES, LANES), 0) // z.levels == iota((LANES, LANES), 1) // z.levels
    for v in range(z.var):
        meridional = all_ref[v, z.levels :].astype(F32)[: z.lat, : z.lat].astype(BF16)
        slot_cols = dot(meridional, to_cols).astype(BF16)
        mix_ref[v] = jnp.where(same, dot(to_cols, slot_cols, ((0,), (0,))), 0.0).astype(BF16)
        if v > 0:
            balance = all_ref[v, : z.levels].astype(F32)
            balance = jnp.where(halves, jnp.concatenate([balance, balance], axis=0), 0.0)
            bal_ref[v - 1] = balance.T.astype(BF16)


def mixing_kernel(z, packet_ref, mix_ref, bal_ref, out_ref):
    stream = None
    for v in range(z.var):
        coeffs = packet_ref[v].astype(F32).reshape(z.mixed, LANES).astype(BF16)
        blended = dot(mix_ref[v], coeffs)
        if v == 0:
            stream = blended.astype(BF16)
        else:
            blended = blended + dot(stream, bal_ref[v - 1])
        blended = blended.reshape(z.lat, z.rows, LANES)
        for s in range(z.lat):
            out_ref[v, s] = blended[s].astype(BF16)


def synthesis_kernel(z, spectra_ref, basis_ref, twiddle_ref, out_ref, sems, field_ref, lhs_ref, parts_ref):
    period = twiddle_ref[2 * RADIX :, :LANES].astype(jnp.int32)
    length = jnp.max(period)
    kap = iota((z.kaps, LANES), 0)
    count = z.kaps // z.rows
    half = z.levels // 2
    kinds = 2 * RADIX - 1
    for at in (0, z.sin):
        lhs_ref[:, at + z.kaps : at + z.sin] = jnp.zeros((2 * half * kinds, z.sin - z.kaps), BF16)
    for r in range(RADIX):
        part = spectra_ref[r * count : (r + 1) * count].astype(F32).reshape(z.kaps, LANES)
        part = jnp.where(kap * RADIX + r <= (period[0:1] - 1) // 2, part, 0.0)
        part = part.astype(BF16).T
        for i in range(2):
            from_cos = part[i * half : (i + 1) * half]
            from_sin = part[z.levels + i * half : z.levels + (i + 1) * half]
            pairs = [(from_cos, from_sin)] if r == 0 else [(from_cos, from_sin), (-from_sin, from_cos)]
            for kind, pair in zip((2 * r - 1, 2 * r) if r else (0,), pairs):
                to = slice((i * kinds + kind) * half, (i * kinds + kind + 1) * half)
                lhs_ref[to, : z.kaps] = pair[0]
                lhs_ref[to, z.sin : z.sin + z.kaps] = pair[1]
    quarter = length // RADIX
    starts = [quarter * j1 for j1 in range(1, RADIX)]
    bases = [pl.multiple_of(s // LANES * LANES, LANES) for s in starts]
    shifts = [s - b for s, b in zip(starts, bases)]
    wide = z.points + LANES
    field_ref[:, wide:] = jnp.zeros((z.levels, z.lons + LANES - wide), BF16)
    keep = [iota((STRIP, LANES), 1) < shift for shift in shifts]
    zero = jnp.zeros((STRIP, LANES), F32)
    for i in range(2):
        rows = slice(i * kinds * half, (i + 1) * kinds * half)
        parts_ref[rows] = dot(lhs_ref[rows], basis_ref[...])
    sent = []
    for at in range(0, z.levels, STRIP):
        rows = slice(at, at + STRIP)
        first = at // half * kinds * half + at % half
        quarters = [[], [], [], []]
        for c in range(z.tiles):
            cos1, cos2, cos3 = [twiddle_ref[r : r + 1, tile(c)] for r in (1, 2, 3)]
            sin1, sin2, sin3 = [twiddle_ref[RADIX + r : RADIX + r + 1, tile(c)] for r in (1, 2, 3)]
            w0, re1, im1, re2, im2, re3, im3 = [
                parts_ref[first + kind * half : first + kind * half + STRIP, tile(c)] for kind in range(kinds)
            ]
            w2 = re2 * cos2 - im2 * sin2
            cross = (re1 * cos1 - im1 * sin1) + (re3 * cos3 - im3 * sin3)
            turn = (re1 * sin1 + im1 * cos1) - (re3 * sin3 + im3 * cos3)
            even, odd = w0 + w2, w0 - w2
            field_ref[rows, tile(c)] = (even + cross).astype(BF16)
            for j1, part in ((1, odd - turn), (2, even - cross), (3, odd + turn)):
                quarters[j1].append(pltpu.roll(part, shifts[j1 - 1], 1))
        field_ref[rows, tile(z.tiles)] = zero.astype(BF16)
        for j1 in range(1, RADIX):
            pieces = zip([zero] + quarters[j1], quarters[j1] + [zero])
            for c, (left, right) in enumerate(pieces):
                lanes = pl.ds(pl.multiple_of(bases[j1 - 1] + c * LANES, LANES), LANES)
                piece = jnp.where(keep[j1 - 1], left, right)
                if c == 0:
                    piece = piece + field_ref[rows, lanes].astype(F32)
                field_ref[rows, lanes] = piece.astype(BF16)
        sent += fetch(
            (field_ref.at[pl.ds(at, STRIP), pl.ds(0, z.lons)],),
            (out_ref.at[0, 0, pl.ds(at, STRIP)],),
            sems.at[pl.ds(at // STRIP, 1)],
        )
    for copy in sent:
        copy.wait()


def body(z, control, row_order, row_length, vertical, amplitude, meridional, balance):
    arguments = (row_order, row_length, control, vertical, amplitude, meridional, balance)
    made = (
        jax.ShapeDtypeStruct((z.devices, z.rows, LANES), BF16),
        jax.ShapeDtypeStruct((z.params, LANES), BF16),
        jax.ShapeDtypeStruct((2 * z.sin, z.points), BF16),
        jax.ShapeDtypeStruct((2 * RADIX + SUBLANES, z.points), F32),
    )
    packets, params, basis, twiddle = pl.pallas_call(
        functools.partial(analysis_kernel, z),
        out_shape=made,
        in_specs=[HBM] * len(arguments),
        out_specs=(VMEM,) * len(made),
        scratch_shapes=[
            *[pltpu.SMEM(x.shape, x.dtype) for x in arguments[:2]],
            *[pltpu.VMEM(x.shape, x.dtype) for x in arguments[2:]],
            pltpu.SemaphoreType.DMA((len(arguments),)),
            pltpu.VMEM((z.levels, z.lons + LANES), BF16),
            pltpu.VMEM(((2 * RADIX - 1) * z.levels, z.points), BF16),
            pltpu.VMEM((2 * z.heads, z.points), F32),
            pltpu.VMEM((2 * STRIP, z.points), F32),
            pltpu.VMEM((z.waves, LANES), F32),
            pltpu.VMEM((2 * z.kaps, RADIX * LANES), F32),
        ],
        compiler_params=PARAMS,
        name="analysis",
    )(*[pltpu.with_memory_space_constraint(x, pltpu.HBM) for x in arguments])
    given = [params]
    for step in range(1, z.var):
        given.append(lax.ppermute(params, "var", [((i + step) % z.var, i) for i in range(z.var)]))
    packets = lax.all_to_all(packets, ("var", "lat"), 0, 0, tiled=True)
    mix, lift = pl.pallas_call(
        functools.partial(matrices_kernel, z),
        out_shape=(
            jax.ShapeDtypeStruct((z.var, z.mixed, z.mixed), BF16),
            jax.ShapeDtypeStruct((z.var - 1, LANES, LANES), BF16),
        ),
        in_specs=[VMEM] * z.var,
        out_specs=(VMEM, VMEM),
        scratch_shapes=[pltpu.VMEM((z.var, z.params, LANES), BF16)],
        compiler_params=PARAMS,
        cost_estimate=pl.CostEstimate(flops=10**8, bytes_accessed=10**6, transcendentals=0),
        name="matrices",
    )(*given)
    balanced = pl.pallas_call(
        functools.partial(mixing_kernel, z),
        out_shape=jax.ShapeDtypeStruct((z.var, z.lat, z.rows, LANES), BF16),
        in_specs=[VMEM] * 3,
        out_specs=VMEM,
        compiler_params=PARAMS,
        name="mixing",
    )(packets.reshape(z.var, z.lat, z.rows, LANES), mix, lift)
    balanced = balanced.reshape(z.devices, z.rows, LANES)
    balanced = lax.all_to_all(balanced, ("var", "lat"), 0, 0, tiled=True)
    return pl.pallas_call(
        functools.partial(synthesis_kernel, z),
        out_shape=jax.ShapeDtypeStruct(control.shape, BF16),
        in_specs=[VMEM] * 3,
        out_specs=HBM,
        scratch_shapes=[
            pltpu.SemaphoreType.DMA((z.levels // STRIP,)),
            pltpu.VMEM((z.levels, z.lons + LANES), BF16),
            pltpu.VMEM(((2 * RADIX - 1) * z.levels, 2 * z.sin), BF16),
            pltpu.VMEM(((2 * RADIX - 1) * z.levels, z.points), F32),
        ],
        compiler_params=PARAMS,
        name="synthesis",
    )(balanced, basis, twiddle)


def solution(mesh):
    placed = (
        P("var", "lat", None, None),
        P(),
        P(),
        P("var", None, None),
        P("var", None),
        P("var", None, None),
        P("var", None, None),
    )

    def run(control, row_order, row_length, vertical, amplitude, meridional, balance):
        lat_total, var_total = mesh.shape["lat"], mesh.shape["var"]
        assert control.shape[0] == var_total and control.shape[1] == lat_total
        z = Sizes(lat_total, var_total, control.shape[2], control.shape[3], amplitude.shape[1])
        return jax.shard_map(
            functools.partial(body, z),
            mesh=mesh,
            in_specs=placed,
            out_specs=P("var", "lat", None, None),
            check_vma=False,
        )(control, row_order, row_length, vertical, amplitude, meridional, balance)

    return run
```
